32 devices in a mesh: img: 8 (over y, x, core), row: 4 (over z).
Axes of the slice: x: 2, y: 2, z: 4, core: 2. Of those that a mesh axis runs over, the one named last changes fastest.
Arguments:
- x_in: bfloat16 [16, 24, 24, 1024], P('img', 'row'), may hold values from -6 to 6
- pre_reduce: bfloat16 [1024, 1024], replicated, may hold values from -0.1875 to 0.1875
- pre_conv: bfloat16 [3, 3, 1024], replicated, may hold values from -2 to 2
- pre_expand: bfloat16 [1024, 1024], replicated, may hold values from -0.1875 to 0.1875
- pre_mid_gain: float32 [2, 1024], replicated, may hold values from 0.25 to 1.75
- pre_mid_shift: float32 [2, 1024], replicated, may hold values from -3 to 3
- pre_out_gain: float32 [1024], replicated, may hold values from 0.25 to 1.75
- pre_out_shift: float32 [1024], replicated, may hold values from -3 to 3
- post_reduce: bfloat16 [1024, 1024], replicated, may hold values from -0.1875 to 0.1875
- post_conv: bfloat16 [3, 3, 1024], replicated, may hold values from -2 to 2
- post_expand: bfloat16 [1024, 1024], replicated, may hold values from -0.1875 to 0.1875
- post_mid_gain: float32 [2, 1024], replicated, may hold values from 0.25 to 1.75
- post_mid_shift: float32 [2, 1024], replicated, may hold values from -3 to 3
- post_out_gain: float32 [1024], replicated, may hold values from 0.25 to 1.75
- post_out_shift: float32 [1024], replicated, may hold values from -3 to 3
- read_weight: bfloat16 [1024, 4096], P(None, 'row'), may hold values from -0.1875 to 0.1875
- read_bias: float32 [4096], P('row'), may hold values from -3 to 3
- cotangent: bfloat16 [16, 12, 12, 4096], P('img', None, None, 'row'), may hold values from -6 to 6
Outputs:
- readout: bfloat16 [16, 12, 12, 4096], P('img', None, None, 'row')
- x_grad: bfloat16 [16, 24, 24, 1024], P('img', 'row')
- pre_reduce_grad: float32 [1024, 1024], replicated
- pre_conv_grad: float32 [3, 3, 1024], replicated
- pre_expand_grad: float32 [1024, 1024], replicated
- pre_mid_gain_grad: float32 [2, 1024], replicated
- pre_mid_shift_grad: float32 [2, 1024], replicated
- pre_out_gain_grad: float32 [1024], replicated
- pre_out_shift_grad: float32 [1024], replicated
- post_reduce_grad: float32 [1024, 1024], replicated
- post_conv_grad: float32 [3, 3, 1024], replicated
- post_expand_grad: float32 [1024, 1024], replicated
- post_mid_gain_grad: float32 [2, 1024], replicated
- post_mid_shift_grad: float32 [2, 1024], replicated
- post_out_gain_grad: float32 [1024], replicated
- post_out_shift_grad: float32 [1024], replicated
- read_weight_grad: float32 [1024, 4096], P(None, 'row')
- read_bias_grad: float32 [4096], P('row')
The draws below stay inside these ranges and needn't reach their ends.
All inputs are finite; a program needn't handle non-finite values.
Results may differ from the reference program's by a relative error of at most 0.02.
Values may be sent and summed in bfloat16 or wider, within the bound.
No kernel may reach another device: no remote copies, remote signals or barrier semaphores. Data moves between devices by JAX's collectives and lax.ppermute only.
A program may use at most 128 MiB of HBM per device.

```python
import jax
import jax.numpy as jnp
from jax import lax

WIDTH = 1024
OUT = 4096
GRID = 24
MID = 1024
IMG_DEV = 2
IMAGES = 16
N_IMG = 8


def shard_levels(rng, shape, pieces, least, largest):
    factor_of, own = 1.0, jax.random.fold_in(rng, 6)
    for axis_at, parts in pieces:
        draws = jnp.exp(jax.random.uniform(jax.random.fold_in(own, axis_at), (parts,), jnp.float32, least / len(pieces), largest / len(pieces)))
        factor_of = factor_of * jnp.repeat(draws, shape[axis_at] // parts).reshape([-1 if axis == axis_at else 1 for axis in range(len(shape))])
    return factor_of


def noise(stream_key, shape, width, reach, split=(), held_as=jnp.bfloat16):
    entries = jax.random.normal(stream_key, shape, jnp.float32) * width
    if len(split) > 0:
        entries = shard_levels(stream_key, shape, split, -0.22, 0.18) * entries
    return jnp.clip(entries, min=-reach, max=reach).astype(held_as)


def setup_inputs(seed: int = 0) -> dict:
    streams_of = jax.random.split(jax.random.key(seed), 19)
    return {
        "x_in": noise(streams_of[0], (IMAGES, GRID, GRID, WIDTH), 1.0, 6.0, ((0, 8), (1, 4))),
        "pre_reduce": noise(streams_of[1], (WIDTH, MID), WIDTH ** -0.5, 0.1875),
        "pre_conv": noise(streams_of[2], (3, 3, MID), 9 ** -0.5, 2.0),
        "pre_expand": noise(streams_of[3], (MID, WIDTH), MID ** -0.5, 0.1875),
        "pre_mid_gain": jnp.clip(1.0 + 0.15 * jax.random.normal(streams_of[4], (2, MID), jnp.float32), 0.25, 1.75),
        "pre_mid_shift": noise(streams_of[5], (2, MID), 0.5, 3.0, (), jnp.float32),
        "pre_out_gain": jnp.clip(1.0 + 0.15 * jax.random.normal(streams_of[6], (WIDTH,), jnp.float32), 0.25, 1.75),
        "pre_out_shift": noise(streams_of[7], (WIDTH,), 0.5, 3.0, (), jnp.float32),
        "post_reduce": noise(streams_of[8], (WIDTH, MID), WIDTH ** -0.5, 0.1875),
        "post_conv": noise(streams_of[9], (3, 3, MID), 9 ** -0.5, 2.0),
        "post_expand": noise(streams_of[10], (MID, WIDTH), MID ** -0.5, 0.1875),
        "post_mid_gain": jnp.clip(1.0 + 0.15 * jax.random.normal(streams_of[11], (2, MID), jnp.float32), 0.25, 1.75),
        "post_mid_shift": noise(streams_of[12], (2, MID), 0.5, 3.0, (), jnp.float32),
        "post_out_gain": jnp.clip(1.0 + 0.15 * jax.random.normal(streams_of[13], (WIDTH,), jnp.float32), 0.25, 1.75),
        "post_out_shift": noise(streams_of[14], (WIDTH,), 0.5, 3.0, (), jnp.float32),
        "read_weight": noise(streams_of[15], (WIDTH, OUT), WIDTH ** -0.5, 0.1875, ((1, 4),)),
        "read_bias": noise(streams_of[16], (OUT,), 0.5, 3.0, ((0, 4),), jnp.float32),
        "cotangent": noise(streams_of[17], (IMAGES, GRID // 2, GRID // 2, OUT), 1.0, 6.0, ((0, 8), (3, 4))),
    }


@jax.custom_vjp
def low(v):
    return lax.optimization_barrier(v.astype(jnp.bfloat16)).astype(jnp.float32)

@jax.custom_vjp
def low_back(v):
    return v

def low_keep(v):
    return (low(v), None)

def low_pass(kept, grad):
    return (grad,)

def back_keep(v):
    return (v, None)

def back_low(kept, grad):
    return (low(grad),)
low.defvjp(low_keep, low_pass)
low_back.defvjp(back_keep, back_low)
EPSILON = 1e-06
HIGH = lax.Precision.HIGHEST

def layer_norm(value, gain, shift):
    centred = value - lax.optimization_barrier(jnp.mean(value, axis=-1, keepdims=True))
    spread = lax.optimization_barrier(jnp.mean(centred * centred, axis=-1, keepdims=True))
    return centred * lax.rsqrt(spread + EPSILON) * gain + shift

def depthwise(field, kernel):
    return lax.conv_general_dilated(field, kernel[:, :, None, :], (1, 1), ((1, 1), (1, 1)), dimension_numbers=('NHWC', 'HWIO', 'NHWC'), feature_group_count=field.shape[-1], precision=HIGH)

def bottleneck(inputs, reduce_w, conv_w, expand_w, mid_gain, mid_shift, out_gain, out_shift):
    reduced = low_back(jnp.einsum('bhwc,cm->bhwm', low(inputs), reduce_w, precision=HIGH))
    first = low(jax.nn.silu(layer_norm(reduced, mid_gain[0], mid_shift[0])))
    conv_out = low_back(depthwise(first, conv_w))
    second = low(jax.nn.silu(layer_norm(conv_out, mid_gain[1], mid_shift[1])))
    expanded = low_back(jnp.einsum('bhwm,mc->bhwc', second, expand_w, precision=HIGH))
    return jax.nn.silu(inputs + layer_norm(expanded, out_gain, out_shift))

def forward(images, *params):
    block_one = bottleneck(images, *params[0:7])
    count, side = (block_one.shape[0], block_one.shape[1])
    pooled = block_one.reshape(count, side // 2, 2, side // 2, 2, block_one.shape[3]).mean(axis=(2, 4))
    block_two = bottleneck(pooled, *params[7:14])
    pre_act = low_back(jnp.einsum('bhwc,co->bhwo', low(block_two), params[14], precision=HIGH) + params[15])
    return jax.nn.gelu(pre_act, approximate=False)

def reference(x_in, pre_reduce, pre_conv, pre_expand, pre_mid_gain, pre_mid_shift, pre_out_gain, pre_out_shift, post_reduce, post_conv, post_expand, post_mid_gain, post_mid_shift, post_out_gain, post_out_shift, read_weight, read_bias, cotangent):
    weights = tuple((w.astype(jnp.float32) for w in (pre_reduce, pre_conv, pre_expand, pre_mid_gain, pre_mid_shift, pre_out_gain, pre_out_shift, post_reduce, post_conv, post_expand, post_mid_gain, post_mid_shift, post_out_gain, post_out_shift, read_weight, read_bias)))
    group_x = x_in.reshape(N_IMG, IMG_DEV, GRID, GRID, WIDTH)
    group_c = cotangent.reshape(N_IMG, IMG_DEV, GRID // 2, GRID // 2, OUT)

    def step(totals, pair):
        images, cot = pair
        result, pull = jax.vjp(forward, images.astype(jnp.float32), *weights)
        grads = pull(cot.astype(jnp.float32))
        totals = tuple((a + b for a, b in zip(totals, grads[1:])))
        return (totals, (result.astype(jnp.bfloat16), grads[0].astype(jnp.bfloat16)))
    zeros = tuple((jnp.zeros(w.shape, jnp.float32) for w in weights))
    totals, (outputs, x_grads) = lax.scan(step, zeros, (group_x, group_c))
    readout = outputs.reshape(IMAGES, GRID // 2, GRID // 2, OUT)
    x_grad = x_grads.reshape(IMAGES, GRID, GRID, WIDTH)
    return (readout, x_grad, totals[0], totals[1], totals[2], totals[3], totals[4], totals[5], totals[6], totals[7], totals[8], totals[9], totals[10], totals[11], totals[12], totals[13], totals[14], totals[15])
```

```python
import jax
import jax.numpy as jnp
from jax import lax
from jax.sharding import PartitionSpec as P

EPSILON = 1e-06
SQRT_HALF = 0.7071067811865476
INV_SQRT_TWO_PI = 0.3989422804014327


def with_halo(value, sides, width):
    for axis, dim in sides:
        size, length = (lax.axis_size(axis), value.shape[dim])
        up = [(i, (i + 1) % size) for i in range(size - 1)]
        down = [(j, i) for i, j in up]
        last = lax.slice_in_dim(value, length - width, length, axis=dim)
        leading = lax.slice_in_dim(value, 0, width, axis=dim)
        before = lax.ppermute(last, axis, up)
        after = lax.ppermute(leading, axis, down)
        value = jnp.concatenate([before, value, after], axis=dim)
    return value


def norm_forward(value, gain, shift):
    centred = value - jnp.mean(value, axis=-1, keepdims=True)
    factor = lax.rsqrt(jnp.mean(centred * centred, axis=-1, keepdims=True) + EPSILON)
    normed = centred * factor
    return (normed * gain + shift, normed, factor)


def norm_backward(grad_out, normed, factor, gain):
    scaled = grad_out * gain
    d_value = factor * (
        scaled
        - jnp.mean(scaled, axis=-1, keepdims=True)
        - normed * jnp.mean(scaled * normed, axis=-1, keepdims=True)
    )
    return (d_value, jnp.sum(grad_out * normed, axis=(0, 1, 2)), jnp.sum(grad_out, axis=(0, 1, 2)))


def silu_grad(grad, value):
    sigma = jax.nn.sigmoid(value)
    return grad * sigma * (1.0 + value * (1.0 - sigma))


def depth_conv(padded, kernel):
    rows = padded.shape[1] - 2
    cols = padded.shape[2]
    wide = jnp.pad(padded, ((0, 0), (0, 0), (1, 1), (0, 0))).astype(jnp.float32)
    total = jnp.zeros((padded.shape[0], rows, cols, padded.shape[3]), jnp.float32)
    for top in range(3):
        for left in range(3):
            total = total + wide[:, top : top + rows, left : left + cols, :] * kernel[top, left]
    return total


def depth_conv_back(padded, beside_all, kernel):
    rows = padded.shape[1] - 2
    cols = padded.shape[2]
    wide = jnp.pad(padded, ((0, 0), (0, 0), (1, 1), (0, 0))).astype(jnp.float32)
    grad_wide = jnp.pad(beside_all, ((0, 0), (0, 0), (1, 1), (0, 0))).astype(jnp.float32)
    centre = grad_wide[:, 1 : 1 + rows, 1 : 1 + cols, :]
    taps = []
    grad_first = jnp.zeros(centre.shape, jnp.float32)
    for top in range(3):
        for left in range(3):
            taps.append(
                jnp.sum(wide[:, top : top + rows, left : left + cols, :] * centre, axis=(0, 1, 2))
            )
            grad_first = (
                grad_first
                + grad_wide[:, 2 - top : 2 - top + rows, 2 - left : 2 - left + cols, :]
                * kernel[top, left]
            )
    return (jnp.stack(taps).reshape(3, 3, kernel.shape[2]), grad_first)


def pre_rows(field):
    return with_halo(field, (("row", 1),), 1)


def post_rows(field):
    return with_halo(field, (("row", 1),), 1)


def pre_back_rows(field):
    return with_halo(field, (("row", 1),), 1)


def post_back_rows(field):
    return with_halo(field, (("row", 1),), 1)


def block_forward(inputs, params, fetch_rows):
    reduce_w, conv_w, expand_w, mid_gain, mid_shift, out_gain, out_shift = params
    in_low = inputs.astype(jnp.bfloat16)
    reduced = jnp.einsum("bhwc,cm->bhwm", in_low, reduce_w, preferred_element_type=jnp.float32)
    norm_a, normed_a, factor_a = norm_forward(reduced, mid_gain[0], mid_shift[0])
    first = jax.nn.silu(norm_a).astype(jnp.bfloat16)
    padded = fetch_rows(first)
    conv_out = depth_conv(padded, conv_w.astype(jnp.float32))
    norm_b, normed_b, factor_b = norm_forward(conv_out, mid_gain[1], mid_shift[1])
    second = jax.nn.silu(norm_b).astype(jnp.bfloat16)
    expanded = jnp.einsum("bhwm,mc->bhwc", second, expand_w, preferred_element_type=jnp.float32)
    norm_c, normed_c, factor_c = norm_forward(expanded, out_gain, out_shift)
    summed = inputs + norm_c
    kept = (
        in_low,
        norm_a,
        normed_a,
        factor_a,
        padded,
        norm_b,
        normed_b,
        factor_b,
        second,
        normed_c,
        factor_c,
        summed,
    )
    return (jax.nn.silu(summed), kept)


def block_backward(grad_out, kept, params, fetch_back):
    reduce_w, conv_w, expand_w, mid_gain, mid_shift, out_gain, out_shift = params
    (
        in_low,
        norm_a,
        normed_a,
        factor_a,
        padded,
        norm_b,
        normed_b,
        factor_b,
        second,
        normed_c,
        factor_c,
        summed,
    ) = kept
    grad_sum = silu_grad(grad_out, summed)
    grad_exp, d_out_gain, d_out_shift = norm_backward(grad_sum, normed_c, factor_c, out_gain)
    grad_exp_low = grad_exp.astype(jnp.bfloat16)
    d_expand = jnp.einsum("bhwm,bhwc->mc", second, grad_exp_low, preferred_element_type=jnp.float32)
    grad_second = jnp.einsum(
        "bhwc,mc->bhwm", grad_exp_low, expand_w, preferred_element_type=jnp.float32
    )
    grad_conv, d_gain_b, d_shift_b = norm_backward(
        silu_grad(grad_second, norm_b), normed_b, factor_b, mid_gain[1]
    )
    beside_all = fetch_back(grad_conv.astype(jnp.bfloat16))
    d_kernel, grad_first = depth_conv_back(padded, beside_all, conv_w.astype(jnp.float32))
    grad_red, d_gain_a, d_shift_a = norm_backward(
        silu_grad(grad_first, norm_a), normed_a, factor_a, mid_gain[0]
    )
    grad_red_low = grad_red.astype(jnp.bfloat16)
    d_reduce = jnp.einsum("bhwc,bhwm->cm", in_low, grad_red_low, preferred_element_type=jnp.float32)
    grad_in = grad_sum + jnp.einsum(
        "bhwm,cm->bhwc", grad_red_low, reduce_w, preferred_element_type=jnp.float32
    )
    grads = (
        d_reduce,
        d_kernel,
        d_expand,
        jnp.stack([d_gain_a, d_gain_b]),
        jnp.stack([d_shift_a, d_shift_b]),
        d_out_gain,
        d_out_shift,
    )
    return (grad_in, grads)


def scatter_sum(field, axis):
    size = lax.axis_size(axis)
    pieces = field.reshape((size, field.shape[0] // size) + field.shape[1:])
    pieces = lax.all_to_all(pieces, axis, 0, 0, tiled=True)
    return jnp.sum(pieces.astype(jnp.float32), axis=0)


def swap_sum(field):
    rows = field.shape[0] // 2
    mine = lax.axis_index("half")
    keep = lax.dynamic_slice_in_dim(field, mine * rows, rows, axis=0)
    give = lax.dynamic_slice_in_dim(field, (1 - mine) * rows, rows, axis=0)
    got = lax.ppermute(give, "half", [(0, 1), (1, 0)])
    return keep.astype(jnp.float32) + got.astype(jnp.float32)


def total_direct(field):
    low = jnp.bfloat16
    part = swap_sum(field.astype(low)).astype(low)
    part = scatter_sum(part, "im").astype(low)
    part = scatter_sum(part, "row").astype(low)
    part = lax.all_gather(part, "row", axis=0, tiled=True)
    part = lax.all_gather(part, "im", axis=0, tiled=True)
    return lax.all_gather(part, "half", axis=0, tiled=True).astype(jnp.float32)


def total_offload(field, axes):
    part = field.astype(jnp.bfloat16)
    for axis in axes:
        part = lax.psum_scatter(part, axis, scatter_dimension=0, tiled=True)
    for axis in axes[::-1]:
        part = lax.all_gather(part, axis, axis=0, tiled=True)
    return part.astype(jnp.float32)


def total_small(parts):
    flat = jnp.concatenate([part.reshape(-1, part.shape[-1]) for part in parts], axis=0)
    flat = lax.psum(lax.psum(flat, ("im", "half")), "row")
    whole, at = ([], 0)
    for part in parts:
        rows = part.size // part.shape[-1]
        whole.append(flat[at : at + rows].reshape(part.shape))
        at += rows
    return whole


def shards(
    x_in,
    pre_reduce,
    pre_conv,
    pre_expand,
    pre_mid_gain,
    pre_mid_shift,
    pre_out_gain,
    pre_out_shift,
    post_reduce,
    post_conv,
    post_expand,
    post_mid_gain,
    post_mid_shift,
    post_out_gain,
    post_out_shift,
    read_weight,
    read_bias,
    cotangent,
):
    pre_params = (
        pre_reduce,
        pre_conv,
        pre_expand,
        pre_mid_gain,
        pre_mid_shift,
        pre_out_gain,
        pre_out_shift,
    )
    post_params = (
        post_reduce,
        post_conv,
        post_expand,
        post_mid_gain,
        post_mid_shift,
        post_out_gain,
        post_out_shift,
    )
    images = x_in.astype(jnp.float32)
    count, strip, side, width = images.shape
    block_one, pre_kept = block_forward(images, pre_params, pre_rows)
    pooled = block_one.reshape(count, strip // 2, 2, side // 2, 2, width).mean(axis=(2, 4))
    block_two, post_kept = block_forward(pooled, post_params, post_rows)
    whole = lax.all_gather(block_two.astype(jnp.bfloat16), "row", axis=1, tiled=True)
    pre_act = (
        jnp.einsum("bhwc,co->bhwo", whole, read_weight, preferred_element_type=jnp.float32)
        + read_bias
    )
    readout = jax.nn.gelu(pre_act, approximate=False).astype(jnp.bfloat16)
    normal_cdf = 0.5 * (1.0 + lax.erf(pre_act * SQRT_HALF))
    density = jnp.exp(-0.5 * pre_act * pre_act) * INV_SQRT_TWO_PI
    grad_pre = (cotangent.astype(jnp.float32) * (normal_cdf + pre_act * density)).astype(
        jnp.bfloat16
    )
    d_read_w = jnp.einsum("bhwc,bhwo->co", whole, grad_pre, preferred_element_type=jnp.float32)
    d_read_b = jnp.sum(grad_pre.astype(jnp.float32), axis=(0, 1, 2))
    read_w_total = total_offload(d_read_w, (("im", "half"),))
    read_b_total = lax.psum(d_read_b, ("im", "half"))
    terms = jnp.einsum("bhwo,co->bhwc", grad_pre, read_weight, preferred_element_type=jnp.float32)
    strips = lax.axis_size("row")
    terms = terms.astype(jnp.bfloat16).reshape(count, strips, strip // 2, side // 2, width)
    terms = jnp.swapaxes(terms, 0, 1)
    terms = lax.all_to_all(terms, "row", 0, 0, tiled=True)
    grad_two = jnp.sum(terms.astype(jnp.float32), axis=0)
    grad_pooled, post_grads = block_backward(grad_two, post_kept, post_params, post_back_rows)
    post_big = total_offload(
        jnp.concatenate([post_grads[0], post_grads[2]], axis=0), (("im", "half"), "row")
    )
    grad_one = jnp.broadcast_to(
        (0.25 * grad_pooled)[:, :, None, :, None, :], (count, strip // 2, 2, side // 2, 2, width)
    ).reshape(count, strip, side, width)
    grad_in, pre_grads = block_backward(grad_one, pre_kept, pre_params, pre_back_rows)
    pre_expand_total = total_direct(pre_grads[2])
    pre_reduce_total = total_direct(pre_grads[0])
    post_small = total_small([post_grads[1]] + list(post_grads[3:]))
    pre_small = total_small([pre_grads[1]] + list(pre_grads[3:]))
    return (
        readout,
        grad_in.astype(jnp.bfloat16),
        pre_reduce_total,
        pre_small[0],
        pre_expand_total,
        pre_small[1],
        pre_small[2],
        pre_small[3],
        pre_small[4],
        post_big[:width],
        post_small[0],
        post_big[width:],
        post_small[1],
        post_small[2],
        post_small[3],
        post_small[4],
        read_w_total,
        read_b_total,
    )


def solution(mesh):
    images, strips = mesh.devices.shape
    split = jax.sharding.Mesh(
        mesh.devices.reshape(images // 2, 2, strips), ("im", "half", "row")
    )
    img = ("im", "half")
    return jax.shard_map(
        shards,
        mesh=split,
        in_specs=(P(img, "row", None, None),)
        + (P(),) * 14
        + (P(None, "row"), P("row"), P(img, None, None, "row")),
        out_specs=(P(img, None, None, "row"), P(img, "row", None, None))
        + (P(),) * 14
        + (P(None, "row"), P("row")),
        check_vma=False,
    )
```

```python
import jax
import jax.numpy as jnp
from jax import lax
from jax.sharding import PartitionSpec as P

EPSILON = 1e-06
SQRT_HALF = 0.7071067811865476
INV_SQRT_TWO_PI = 0.3989422804014327
LOW = jnp.bfloat16
IMG = ("im", "half")


def with_halo(value):
    size, length = (lax.axis_size("row"), value.shape[1])
    up = [(i, (i + 1) % size) for i in range(size - 1)]
    down = [(j, i) for i, j in up]
    last = lax.slice_in_dim(value, length - 1, length, axis=1)
    leading = lax.slice_in_dim(value, 0, 1, axis=1)
    before = lax.ppermute(last, "row", up)
    after = lax.ppermute(leading, "row", down)
    return jnp.concatenate([before, value, after], axis=1)


def norm_forward(value, gain, shift):
    centred = value - jnp.mean(value, axis=-1, keepdims=True)
    factor = lax.rsqrt(jnp.mean(centred * centred, axis=-1, keepdims=True) + EPSILON)
    normed = centred * factor
    return (normed * gain + shift, normed, factor)


def norm_backward(grad_out, normed, factor, gain):
    scaled = grad_out * gain
    d_value = factor * (
        scaled
        - jnp.mean(scaled, axis=-1, keepdims=True)
        - normed * jnp.mean(scaled * normed, axis=-1, keepdims=True)
    )
    return (d_value, jnp.sum(grad_out * normed, axis=(0, 1, 2)), jnp.sum(grad_out, axis=(0, 1, 2)))


def silu_grad(grad, value):
    sigma = jax.nn.sigmoid(value)
    return grad * sigma * (1.0 + value * (1.0 - sigma))


def depth_conv(padded, kernel):
    rows = padded.shape[1] - 2
    cols = padded.shape[2]
    wide = jnp.pad(padded, ((0, 0), (0, 0), (1, 1), (0, 0))).astype(jnp.float32)
    total = jnp.zeros((padded.shape[0], rows, cols, padded.shape[3]), jnp.float32)
    for top in range(3):
        for left in range(3):
            total = total + wide[:, top : top + rows, left : left + cols, :] * kernel[top, left]
    return total


def depth_conv_back(padded, beside_all, kernel):
    rows = padded.shape[1] - 2
    cols = padded.shape[2]
    wide = jnp.pad(padded, ((0, 0), (0, 0), (1, 1), (0, 0))).astype(jnp.float32)
    grad_wide = jnp.pad(beside_all, ((0, 0), (0, 0), (1, 1), (0, 0))).astype(jnp.float32)
    centre = grad_wide[:, 1 : 1 + rows, 1 : 1 + cols, :]
    taps = []
    grad_first = jnp.zeros(centre.shape, jnp.float32)
    for top in range(3):
        for left in range(3):
            taps.append(
                jnp.sum(wide[:, top : top + rows, left : left + cols, :] * centre, axis=(0, 1, 2))
            )
            grad_first = (
                grad_first
                + grad_wide[:, 2 - top : 2 - top + rows, 2 - left : 2 - left + cols, :]
                * kernel[top, left]
            )
    return (jnp.stack(taps), grad_first)


def block_forward(inputs, params):
    reduce_w, conv_w, expand_w, mid_gain, mid_shift, out_gain, out_shift = params
    in_low = inputs.astype(LOW)
    reduced = jnp.einsum("bhwc,cm->bhwm", in_low, reduce_w, preferred_element_type=jnp.float32)
    norm_a, normed_a, factor_a = norm_forward(reduced, mid_gain[0], mid_shift[0])
    first = jax.nn.silu(norm_a).astype(LOW)
    padded = with_halo(first)
    conv_out = depth_conv(padded, conv_w.astype(jnp.float32))
    norm_b, normed_b, factor_b = norm_forward(conv_out, mid_gain[1], mid_shift[1])
    second = jax.nn.silu(norm_b).astype(LOW)
    expanded = jnp.einsum("bhwm,mc->bhwc", second, expand_w, preferred_element_type=jnp.float32)
    norm_c, normed_c, factor_c = norm_forward(expanded, out_gain, out_shift)
    summed = inputs + norm_c
    kept = (
        norm_a,
        normed_a,
        factor_a,
        padded,
        norm_b,
        normed_b,
        factor_b,
        normed_c,
        factor_c,
        summed,
    )
    return (jax.nn.silu(summed), in_low, second, kept)


def block_backward(grad_out, kept, params):
    reduce_w, conv_w, expand_w, mid_gain, mid_shift, out_gain, out_shift = params
    (
        norm_a,
        normed_a,
        factor_a,
        padded,
        norm_b,
        normed_b,
        factor_b,
        normed_c,
        factor_c,
        summed,
    ) = kept
    grad_sum = silu_grad(grad_out, summed)
    grad_exp, d_out_gain, d_out_shift = norm_backward(grad_sum, normed_c, factor_c, out_gain)
    grad_exp_low = grad_exp.astype(LOW)
    grad_second = jnp.einsum(
        "bhwc,mc->bhwm", grad_exp_low, expand_w, preferred_element_type=jnp.float32
    )
    grad_conv, d_gain_b, d_shift_b = norm_backward(
        silu_grad(grad_second, norm_b), normed_b, factor_b, mid_gain[1]
    )
    beside_all = with_halo(grad_conv.astype(LOW))
    d_kernel, grad_first = depth_conv_back(padded, beside_all, conv_w.astype(jnp.float32))
    grad_red, d_gain_a, d_shift_a = norm_backward(
        silu_grad(grad_first, norm_a), normed_a, factor_a, mid_gain[0]
    )
    grad_red_low = grad_red.astype(LOW)
    grad_in = grad_sum + jnp.einsum(
        "bhwm,cm->bhwc", grad_red_low, reduce_w, preferred_element_type=jnp.float32
    )
    small = jnp.concatenate(
        [
            d_kernel,
            jnp.stack([d_gain_a, d_gain_b, d_shift_a, d_shift_b, d_out_gain, d_out_shift]),
        ]
    )
    return (grad_in, grad_exp_low, grad_red_low, small)


def flat(field):
    return field.reshape(-1, field.shape[-1])


def swap(field):
    return lax.ppermute(field, "half", [(0, 1), (1, 0)])


def pair_columns(field):
    rows = flat(field)
    width = rows.shape[1] // 2
    mine = lax.axis_index("half")
    keep = lax.dynamic_slice_in_dim(rows, mine * width, width, axis=1)
    give = lax.dynamic_slice_in_dim(rows, (1 - mine) * width, width, axis=1)
    return jnp.concatenate([keep, swap(give)], axis=0)


def pair_rows(field):
    rows = flat(field)
    return jnp.concatenate([rows, swap(rows)], axis=0)


def outer(left, right):
    return jnp.einsum("tm,tc->mc", left, right, preferred_element_type=jnp.float32).astype(LOW)


def scatter_sum(field, axis, dim=0):
    size = lax.axis_size(axis)
    pieces = field.reshape((size, field.shape[0] // size) + field.shape[1:])
    pieces = lax.all_to_all(pieces, axis, 0, 0, tiled=True)
    return jnp.sum(pieces.astype(jnp.float32), axis=0).astype(LOW)


def spread(field, axis):
    size = lax.axis_size(axis)
    pieces = jnp.broadcast_to(field[None], (size,) + field.shape)
    pieces = lax.all_to_all(pieces, axis, 0, 0, tiled=True)
    return pieces.reshape((-1,) + field.shape[1:])


def total_pair(left, right):
    part = outer(left, right)
    part = scatter_sum(part, "im")
    part = scatter_sum(part, "row")
    part = spread(part, "row")
    part = spread(part, "im")
    other = swap(part)
    first = lax.axis_index("half") == 0
    return jnp.concatenate(
        [jnp.where(first, part, other), jnp.where(first, other, part)], axis=0
    ).astype(jnp.float32)


def my_columns(field):
    count = lax.axis_size(IMG)
    width = field.shape[1] // count
    return lax.dynamic_slice_in_dim(field, lax.axis_index(IMG) * width, width, axis=1)


def gather_img(field):
    return lax.all_gather(flat(field), IMG, axis=0, tiled=True)


def shards(
    x_in,
    pre_reduce,
    pre_conv,
    pre_expand,
    pre_mid_gain,
    pre_mid_shift,
    pre_out_gain,
    pre_out_shift,
    post_reduce,
    post_conv,
    post_expand,
    post_mid_gain,
    post_mid_shift,
    post_out_gain,
    post_out_shift,
    read_weight,
    read_bias,
    cotangent,
):
    pre_params = (
        pre_reduce,
        pre_conv,
        pre_expand,
        pre_mid_gain,
        pre_mid_shift,
        pre_out_gain,
        pre_out_shift,
    )
    post_params = (
        post_reduce,
        post_conv,
        post_expand,
        post_mid_gain,
        post_mid_shift,
        post_out_gain,
        post_out_shift,
    )
    images = x_in.astype(jnp.float32)
    count, strip, side, width = images.shape
    strips = lax.axis_size("row")
    block_one, pre_in, pre_second, pre_kept = block_forward(images, pre_params)
    pooled = block_one.reshape(count, strip // 2, 2, side // 2, 2, width).mean(axis=(2, 4))
    block_two, post_in, post_second, post_kept = block_forward(pooled, post_params)
    whole = lax.all_gather(block_two.astype(LOW), "row", axis=1, tiled=True)
    pre_in_pair = pair_columns(pre_in)
    pre_second_pair = pair_columns(pre_second)
    post_in_all = my_columns(gather_img(post_in))
    post_second_all = my_columns(gather_img(post_second))
    pre_act = (
        jnp.einsum("bhwc,co->bhwo", whole, read_weight, preferred_element_type=jnp.float32)
        + read_bias
    )
    readout = jax.nn.gelu(pre_act, approximate=False).astype(LOW)
    normal_cdf = 0.5 * (1.0 + lax.erf(pre_act * SQRT_HALF))
    density = jnp.exp(-0.5 * pre_act * pre_act) * INV_SQRT_TWO_PI
    grad_pre = (cotangent.astype(jnp.float32) * (normal_cdf + pre_act * density)).astype(LOW)
    terms = jnp.einsum("bhwo,co->bhwc", grad_pre, read_weight, preferred_element_type=jnp.float32)
    terms = terms.astype(LOW).reshape(count, strips, strip // 2, side // 2, width)
    terms = lax.all_to_all(jnp.swapaxes(terms, 0, 1), "row", 0, 0, tiled=True)
    d_read_w = outer(flat(whole), flat(grad_pre))
    d_read_b = jnp.sum(grad_pre.astype(jnp.float32), axis=(0, 1, 2))
    read_part = lax.psum_scatter(d_read_w, IMG, scatter_dimension=0, tiled=True)
    read_total = lax.all_gather(read_part, IMG, axis=0, tiled=True).astype(jnp.float32)
    grad_two = jnp.sum(terms.astype(jnp.float32), axis=0)
    grad_pooled, post_ge, post_gr, post_small = block_backward(grad_two, post_kept, post_params)
    post_part = jnp.stack(
        [
            outer(post_in_all, gather_img(post_gr)),
            outer(post_second_all, gather_img(post_ge)),
        ],
        axis=1,
    )
    post_part = spread(scatter_sum(post_part, "row"), "row")
    post_total = lax.all_gather(post_part, IMG, axis=0, tiled=True).astype(jnp.float32)
    grad_one = jnp.broadcast_to(
        (0.25 * grad_pooled)[:, :, None, :, None, :], (count, strip // 2, 2, side // 2, 2, width)
    ).reshape(count, strip, side, width)
    grad_in, pre_ge, pre_gr, pre_small = block_backward(grad_one, pre_kept, pre_params)
    pre_expand_total = total_pair(pre_second_pair, pair_rows(pre_ge))
    pre_reduce_total = total_pair(pre_in_pair, pair_rows(pre_gr))
    small = jnp.concatenate([pre_small, post_small, d_read_b[None], d_read_b[None]]).astype(LOW)
    small = lax.all_gather(small, IMG + ("row",), axis=0, tiled=False).astype(jnp.float32)
    small = small.reshape((-1, strips) + small.shape[1:])
    small_total = jnp.sum(small[:, :, :30], axis=(0, 1))
    read_b_total = jnp.sum(
        lax.dynamic_index_in_dim(small[:, :, 30], lax.axis_index("row"), 1, False), axis=0
    )

    def small_grads(rows):
        return (
            rows[:9].reshape(3, 3, -1),
            rows[9:11],
            rows[11:13],
            rows[13],
            rows[14],
        )

    pre_conv_g, pre_gain_g, pre_shift_g, pre_og_g, pre_os_g = small_grads(small_total[:15])
    post_conv_g, post_gain_g, post_shift_g, post_og_g, post_os_g = small_grads(small_total[15:])
    return (
        readout,
        grad_in.astype(LOW),
        pre_reduce_total,
        pre_conv_g,
        pre_expand_total,
        pre_gain_g,
        pre_shift_g,
        pre_og_g,
        pre_os_g,
        post_total[:, 0],
        post_conv_g,
        post_total[:, 1],
        post_gain_g,
        post_shift_g,
        post_og_g,
        post_os_g,
        read_total,
        read_b_total,
    )


def solution(mesh):
    images, strips = mesh.devices.shape
    split = jax.sharding.Mesh(
        mesh.devices.reshape(images // 2, 2, strips), ("im", "half", "row")
    )
    return jax.shard_map(
        shards,
        mesh=split,
        in_specs=(P(IMG, "row", None, None),)
        + (P(),) * 14
        + (P(None, "row"), P("row"), P(IMG, None, None, "row")),
        out_specs=(P(IMG, None, None, "row"), P(IMG, "row", None, None))
        + (P(),) * 14
        + (P(None, "row"), P("row")),
        check_vma=False,
    )
```

```python
import jax
import jax.numpy as jnp
from jax import lax
from jax.sharding import PartitionSpec as P

EPSILON = 1e-06
SQRT_HALF = 0.7071067811865476
INV_SQRT_TWO_PI = 0.3989422804014327
LOW = jnp.bfloat16
IMG = ("im", "half")


def with_halo(value):
    size, length = (lax.axis_size("row"), value.shape[1])
    up = [(i, (i + 1) % size) for i in range(size - 1)]
    down = [(j, i) for i, j in up]
    last = lax.slice_in_dim(value, length - 1, length, axis=1)
    leading = lax.slice_in_dim(value, 0, 1, axis=1)
    before = lax.ppermute(last, "row", up)
    after = lax.ppermute(leading, "row", down)
    return jnp.concatenate([before, value, after], axis=1)


def norm_forward(value, gain, shift):
    centred = value - jnp.mean(value, axis=-1, keepdims=True)
    factor = lax.rsqrt(jnp.mean(centred * centred, axis=-1, keepdims=True) + EPSILON)
    normed = centred * factor
    return (normed * gain + shift, normed, factor)


def norm_backward(grad_out, normed, factor, gain):
    scaled = grad_out * gain
    d_value = factor * (
        scaled
        - jnp.mean(scaled, axis=-1, keepdims=True)
        - normed * jnp.mean(scaled * normed, axis=-1, keepdims=True)
    )
    return (d_value, jnp.sum(grad_out * normed, axis=(0, 1, 2)), jnp.sum(grad_out, axis=(0, 1, 2)))


def silu_grad(grad, value):
    sigma = jax.nn.sigmoid(value)
    return grad * sigma * (1.0 + value * (1.0 - sigma))


def depth_conv(padded, kernel):
    rows = padded.shape[1] - 2
    cols = padded.shape[2]
    wide = jnp.pad(padded, ((0, 0), (0, 0), (1, 1), (0, 0))).astype(jnp.float32)
    total = jnp.zeros((padded.shape[0], rows, cols, padded.shape[3]), jnp.float32)
    for top in range(3):
        for left in range(3):
            total = total + wide[:, top : top + rows, left : left + cols, :] * kernel[top, left]
    return total


def depth_conv_back(padded, beside_all, kernel):
    rows = padded.shape[1] - 2
    cols = padded.shape[2]
    wide = jnp.pad(padded, ((0, 0), (0, 0), (1, 1), (0, 0))).astype(jnp.float32)
    grad_wide = jnp.pad(beside_all, ((0, 0), (0, 0), (1, 1), (0, 0))).astype(jnp.float32)
    centre = grad_wide[:, 1 : 1 + rows, 1 : 1 + cols, :]
    taps = []
    grad_first = jnp.zeros(centre.shape, jnp.float32)
    for top in range(3):
        for left in range(3):
            taps.append(
                jnp.sum(wide[:, top : top + rows, left : left + cols, :] * centre, axis=(0, 1, 2))
            )
            grad_first = (
                grad_first
                + grad_wide[:, 2 - top : 2 - top + rows, 2 - left : 2 - left + cols, :]
                * kernel[top, left]
            )
    return (jnp.stack(taps), grad_first)


def block_forward(inputs, params, beside=None):
    reduce_w, conv_w, expand_w, mid_gain, mid_shift, out_gain, out_shift = params
    in_low = inputs.astype(LOW)
    reduced = jnp.einsum("bhwc,cm->bhwm", in_low, reduce_w, preferred_element_type=jnp.float32)
    norm_a, normed_a, factor_a = norm_forward(reduced, mid_gain[0], mid_shift[0])
    first = jax.nn.silu(norm_a).astype(LOW)
    padded = with_halo(first)
    if beside is not None:
        padded, beside = tie(padded, beside)
    conv_out = depth_conv(padded, conv_w.astype(jnp.float32))
    norm_b, normed_b, factor_b = norm_forward(conv_out, mid_gain[1], mid_shift[1])
    second = jax.nn.silu(norm_b).astype(LOW)
    expanded = jnp.einsum("bhwm,mc->bhwc", second, expand_w, preferred_element_type=jnp.float32)
    norm_c, normed_c, factor_c = norm_forward(expanded, out_gain, out_shift)
    summed = inputs + norm_c
    kept = (
        norm_a,
        normed_a,
        factor_a,
        padded,
        norm_b,
        normed_b,
        factor_b,
        normed_c,
        factor_c,
        summed,
    )
    return (jax.nn.silu(summed), in_low, second, kept, beside)


def backward_expand(grad_out, kept, params):
    grad_sum = silu_grad(grad_out, kept[9])
    grad_exp, d_gain, d_shift = norm_backward(grad_sum, kept[7], kept[8], params[5])
    return (grad_sum, grad_exp.astype(LOW), (d_gain, d_shift))


def backward_mid(grad_exp_low, kept, params):
    grad_second = jnp.einsum(
        "bhwc,mc->bhwm", grad_exp_low, params[2], preferred_element_type=jnp.float32
    )
    grad_conv, d_gain, d_shift = norm_backward(
        silu_grad(grad_second, kept[4]), kept[5], kept[6], params[3][1]
    )
    return (grad_conv.astype(LOW), (d_gain, d_shift))


def backward_reduce(beside_all, kept, params):
    d_kernel, grad_first = depth_conv_back(kept[3], beside_all, params[1].astype(jnp.float32))
    grad_red, d_gain, d_shift = norm_backward(
        silu_grad(grad_first, kept[0]), kept[1], kept[2], params[3][0]
    )
    return (grad_red.astype(LOW), d_kernel, (d_gain, d_shift))


def backward_in(grad_sum, grad_red_low, params):
    return grad_sum + jnp.einsum(
        "bhwm,cm->bhwc", grad_red_low, params[0], preferred_element_type=jnp.float32
    )


def small_rows(d_kernel, mid_a, mid_b, out):
    return jnp.concatenate(
        [d_kernel, jnp.stack([mid_a[0], mid_b[0], mid_a[1], mid_b[1], out[0], out[1]])]
    )


def swap(field):
    return lax.ppermute(field, "half", [(0, 1), (1, 0)])


def tie(*values):
    return lax.optimization_barrier(values)


def pair_columns(field):
    width = field.shape[-1] // 2
    mine = lax.axis_index("half")
    keep = lax.dynamic_slice_in_dim(field, mine * width, width, axis=3)
    give = lax.dynamic_slice_in_dim(field, (1 - mine) * width, width, axis=3)
    return jnp.concatenate([keep, swap(give)], axis=0)


def pair_rows(field):
    return jnp.concatenate([field, swap(field)], axis=0)


def outer(left, right):
    return jnp.einsum("bhwm,bhwc->mc", left, right, preferred_element_type=jnp.float32).astype(LOW)


def exchange(pieces, axis):
    return lax.all_to_all(pieces, axis, 0, 0, tiled=True)


def spread(field, axis):
    size = lax.axis_size(axis)
    return exchange(jnp.broadcast_to(field[None], (size,) + field.shape), axis)


def sum_low(pieces):
    return jnp.sum(pieces.astype(jnp.float32), axis=0).astype(LOW)


def split_rows(field, axis):
    size = lax.axis_size(axis)
    return field.reshape(
        field.shape[:-2] + (size, field.shape[-2] // size, field.shape[-1])
    )


def scatter_plane(half_grad):
    return sum_low(exchange(split_rows(half_grad, "im"), "im"))


def scatter_row(parts):
    pieces = jnp.stack([split_rows(part, "row") for part in parts], axis=1)
    return sum_low(exchange(pieces, "row"))


def assemble(part, other, at):
    first = lax.axis_index("half") == 0
    top, bottom = (jnp.where(first, part, other), jnp.where(first, other, part))
    width = part.shape[-1]
    return jnp.concatenate(
        [top[:, :, at].reshape(-1, width), bottom[:, :, at].reshape(-1, width)], axis=0
    ).astype(jnp.float32)


def shards(
    x_in,
    pre_reduce,
    pre_conv,
    pre_expand,
    pre_mid_gain,
    pre_mid_shift,
    pre_out_gain,
    pre_out_shift,
    post_reduce,
    post_conv,
    post_expand,
    post_mid_gain,
    post_mid_shift,
    post_out_gain,
    post_out_shift,
    read_weight,
    read_bias,
    cotangent,
):
    pre_params = (
        pre_reduce,
        pre_conv,
        pre_expand,
        pre_mid_gain,
        pre_mid_shift,
        pre_out_gain,
        pre_out_shift,
    )
    post_params = (
        post_reduce,
        post_conv,
        post_expand,
        post_mid_gain,
        post_mid_shift,
        post_out_gain,
        post_out_shift,
    )
    images = x_in.astype(jnp.float32)
    count, strip, side, width = images.shape
    strips = lax.axis_size("row")
    block_one, pre_in, pre_second, pre_kept, pre_in_pair = block_forward(
        images, pre_params, pair_columns(x_in)
    )
    pooled = block_one.reshape(count, strip // 2, 2, side // 2, 2, width).mean(axis=(2, 4))
    block_two, post_in, post_second, post_kept, pre_second_pair = block_forward(
        pooled, post_params, pair_columns(pre_second)
    )
    plane = lax.axis_size("im")
    whole = jnp.moveaxis(spread(block_two.astype(LOW), "row"), 0, 1)
    whole = whole.reshape(count, side // 2, side // 2, width)
    lefts = jnp.stack([post_in, post_second])
    lefts = lefts.reshape(lefts.shape[:-1] + (2, plane, width // (2 * plane)))
    lefts = exchange(jnp.moveaxis(lefts, -2, 0), "im")
    whole, lefts = tie(whole, lefts)
    pre_act = (
        jnp.einsum("bhwc,co->bhwo", whole, read_weight, preferred_element_type=jnp.float32)
        + read_bias
    )
    readout = jax.nn.gelu(pre_act, approximate=False).astype(LOW)
    normal_cdf = 0.5 * (1.0 + lax.erf(pre_act * SQRT_HALF))
    density = jnp.exp(-0.5 * pre_act * pre_act) * INV_SQRT_TWO_PI
    grad_pre = (cotangent.astype(jnp.float32) * (normal_cdf + pre_act * density)).astype(LOW)
    terms = jnp.einsum("bhwo,co->bhwc", grad_pre, read_weight, preferred_element_type=jnp.float32)
    terms = terms.astype(LOW).reshape(count, strips, strip // 2, side // 2, width)
    terms = exchange(jnp.swapaxes(terms, 0, 1), "row")
    d_read_w = outer(whole, grad_pre)
    d_read_b = jnp.sum(grad_pre.astype(jnp.float32), axis=(0, 1, 2))
    terms, d_read_w = tie(terms, d_read_w)
    read_part = lax.psum_scatter(d_read_w, IMG, scatter_dimension=0, tiled=True)
    grad_two = jnp.sum(terms.astype(jnp.float32), axis=0)
    post_gs, post_ge, post_out = backward_expand(grad_two, post_kept, post_params)
    post_gc, post_mid = backward_mid(post_ge, post_kept, post_params)
    post_gr, post_taps, post_first = backward_reduce(with_halo(post_gc), post_kept, post_params)
    rights = spread(jnp.stack([post_gr, post_ge]), "im")
    grad_pooled = backward_in(post_gs, post_gr, post_params)
    grad_one = jnp.broadcast_to(
        (0.25 * grad_pooled)[:, :, None, :, None, :], (count, strip // 2, 2, side // 2, 2, width)
    ).reshape(count, strip, side, width)
    pre_gs, pre_ge, pre_out = backward_expand(grad_one, pre_kept, pre_params)
    pre_ge, rights = tie(pre_ge, rights)
    post_half = jnp.einsum(
        "inbhwam,inbhwc->anmc", lefts, rights, preferred_element_type=jnp.float32
    ).astype(LOW)
    mine = lax.axis_index("half")
    post_keep = lax.dynamic_index_in_dim(post_half, mine, 0, False)
    post_got = swap(lax.dynamic_index_in_dim(post_half, 1 - mine, 0, False))
    pre_ge_pair = pair_rows(pre_ge)
    pre_gc, pre_mid = backward_mid(pre_ge, pre_kept, pre_params)
    pre_beside, pre_ge_pair, post_got, read_part = tie(
        with_halo(pre_gc), pre_ge_pair, post_got, read_part
    )
    read_total = lax.all_gather(read_part, IMG, axis=0, tiled=True)
    post_part = (post_keep.astype(jnp.float32) + post_got.astype(jnp.float32)).astype(LOW)
    post_part = scatter_row([post_part[0], post_part[1]])
    expand_part = scatter_plane(outer(pre_second_pair, pre_ge_pair))
    pre_gr, pre_taps, pre_first = backward_reduce(pre_beside, pre_kept, pre_params)
    pre_gr_pair, post_part, expand_part = tie(pair_rows(pre_gr), post_part, expand_part)
    reduce_part = scatter_plane(outer(pre_in_pair, pre_gr_pair))
    post_part = spread(post_part, "row")
    expand_part = scatter_row([expand_part])
    reduce_part, post_part, expand_part = tie(reduce_part, post_part, expand_part)
    post_part = spread(post_part, "im")
    expand_part = spread(expand_part, "row")
    reduce_part = scatter_row([reduce_part])
    expand_part, reduce_part = tie(expand_part, reduce_part)
    reduce_part = spread(reduce_part, "row")
    expand_part = spread(expand_part, "im")
    reduce_part, expand_part, post_part, read_total = tie(
        reduce_part, expand_part, post_part, read_total
    )
    reduce_part = spread(reduce_part, "im")
    post_other = swap(post_part)
    expand_other = swap(expand_part)
    reduce_other = swap(reduce_part)
    post_reduce_g = assemble(post_part, post_other, 0)
    post_expand_g = assemble(post_part, post_other, 1)
    pre_expand_g = assemble(expand_part, expand_other, 0)
    pre_reduce_g = assemble(reduce_part, reduce_other, 0)
    grad_in = backward_in(pre_gs, pre_gr, pre_params)
    pre_small = small_rows(pre_taps, pre_first, pre_mid, pre_out)
    post_small = small_rows(post_taps, post_first, post_mid, post_out)
    small = jnp.concatenate([pre_small, post_small]).astype(LOW)
    small = lax.all_gather(small, "row", axis=0, tiled=False)
    small = jnp.concatenate([sum_low(small), d_read_b[None].astype(LOW)])
    small = lax.all_gather(small, IMG, axis=0, tiled=False)
    small_total = jnp.sum(small.astype(jnp.float32), axis=0)
    read_b_total = small_total[30]

    def small_grads(rows):
        return (
            rows[:9].reshape(3, 3, -1),
            rows[9:11],
            rows[11:13],
            rows[13],
            rows[14],
        )

    pre_conv_g, pre_gain_g, pre_shift_g, pre_og_g, pre_os_g = small_grads(small_total[:15])
    post_conv_g, post_gain_g, post_shift_g, post_og_g, post_os_g = small_grads(small_total[15:30])
    return (
        readout,
        grad_in.astype(LOW),
        pre_reduce_g,
        pre_conv_g,
        pre_expand_g,
        pre_gain_g,
        pre_shift_g,
        pre_og_g,
        pre_os_g,
        post_reduce_g,
        post_conv_g,
        post_expand_g,
        post_gain_g,
        post_shift_g,
        post_og_g,
        post_os_g,
        read_total.astype(jnp.float32),
        read_b_total,
    )


def solution(mesh):
    images, strips = mesh.devices.shape
    split = jax.sharding.Mesh(
        mesh.devices.reshape(images // 2, 2, strips), ("im", "half", "row")
    )
    return jax.shard_map(
        shards,
        mesh=split,
        in_specs=(P(IMG, "row", None, None),)
        + (P(),) * 14
        + (P(None, "row"), P("row"), P(IMG, None, None, "row")),
        out_specs=(P(IMG, None, None, "row"), P(IMG, "row", None, None))
        + (P(),) * 14
        + (P(None, "row"), P("row")),
        check_vma=False,
    )
```

```python
import jax
import jax.numpy as jnp
from jax import lax
from jax.sharding import PartitionSpec as P

EPSILON = 1e-06
SQRT_HALF = 0.7071067811865476
INV_SQRT_TWO_PI = 0.3989422804014327
LOW = jnp.bfloat16
IMG = ("im", "half")


def with_halo(value):
    size, length = (lax.axis_size("row"), value.shape[1])
    up = [(i, (i + 1) % size) for i in range(size - 1)]
    down = [(j, i) for i, j in up]
    last = lax.slice_in_dim(value, length - 1, length, axis=1)
    leading = lax.slice_in_dim(value, 0, 1, axis=1)
    before = lax.ppermute(last, "row", up)
    after = lax.ppermute(leading, "row", down)
    return jnp.concatenate([before, value, after], axis=1)


def norm_forward(value, gain, shift):
    centred = value - jnp.mean(value, axis=-1, keepdims=True)
    factor = lax.rsqrt(jnp.mean(centred * centred, axis=-1, keepdims=True) + EPSILON)
    normed = centred * factor
    return (normed * gain + shift, normed, factor)


def norm_backward(grad_out, normed, factor, gain):
    scaled = grad_out * gain
    d_value = factor * (
        scaled
        - jnp.mean(scaled, axis=-1, keepdims=True)
        - normed * jnp.mean(scaled * normed, axis=-1, keepdims=True)
    )
    return (d_value, jnp.sum(grad_out * normed, axis=(0, 1, 2)), jnp.sum(grad_out, axis=(0, 1, 2)))


def silu_grad(grad, value):
    sigma = jax.nn.sigmoid(value)
    return grad * sigma * (1.0 + value * (1.0 - sigma))


def depth_conv(padded, kernel):
    rows = padded.shape[1] - 2
    cols = padded.shape[2]
    wide = jnp.pad(padded, ((0, 0), (0, 0), (1, 1), (0, 0))).astype(jnp.float32)
    total = jnp.zeros((padded.shape[0], rows, cols, padded.shape[3]), jnp.float32)
    for top in range(3):
        for left in range(3):
            total = total + wide[:, top : top + rows, left : left + cols, :] * kernel[top, left]
    return total


def depth_conv_back(padded, beside_all, kernel):
    rows = padded.shape[1] - 2
    cols = padded.shape[2]
    wide = jnp.pad(padded, ((0, 0), (0, 0), (1, 1), (0, 0))).astype(jnp.float32)
    grad_wide = jnp.pad(beside_all, ((0, 0), (0, 0), (1, 1), (0, 0))).astype(jnp.float32)
    centre = grad_wide[:, 1 : 1 + rows, 1 : 1 + cols, :]
    taps = []
    grad_first = jnp.zeros(centre.shape, jnp.float32)
    for top in range(3):
        for left in range(3):
            taps.append(
                jnp.sum(wide[:, top : top + rows, left : left + cols, :] * centre, axis=(0, 1, 2))
            )
            grad_first = (
                grad_first
                + grad_wide[:, 2 - top : 2 - top + rows, 2 - left : 2 - left + cols, :]
                * kernel[top, left]
            )
    return (jnp.stack(taps), grad_first)


def block_forward(inputs, params, beside=None):
    reduce_w, conv_w, expand_w, mid_gain, mid_shift, out_gain, out_shift = params
    in_low = inputs.astype(LOW)
    reduced = jnp.einsum("bhwc,cm->bhwm", in_low, reduce_w, preferred_element_type=jnp.float32)
    norm_a, normed_a, factor_a = norm_forward(reduced, mid_gain[0], mid_shift[0])
    first = jax.nn.silu(norm_a).astype(LOW)
    padded = with_halo(first)
    if beside is not None:
        padded, beside = tie(padded, beside)
    conv_out = depth_conv(padded, conv_w.astype(jnp.float32))
    norm_b, normed_b, factor_b = norm_forward(conv_out, mid_gain[1], mid_shift[1])
    second = jax.nn.silu(norm_b).astype(LOW)
    expanded = jnp.einsum("bhwm,mc->bhwc", second, expand_w, preferred_element_type=jnp.float32)
    norm_c, normed_c, factor_c = norm_forward(expanded, out_gain, out_shift)
    summed = inputs + norm_c
    kept = (
        norm_a,
        normed_a,
        factor_a,
        padded,
        norm_b,
        normed_b,
        factor_b,
        normed_c,
        factor_c,
        summed,
    )
    return (jax.nn.silu(summed), in_low, second, kept, beside)


def backward_expand(grad_out, kept, params):
    grad_sum = silu_grad(grad_out, kept[9])
    grad_exp, d_gain, d_shift = norm_backward(grad_sum, kept[7], kept[8], params[5])
    return (grad_sum, grad_exp.astype(LOW), (d_gain, d_shift))


def backward_mid(grad_exp_low, kept, params):
    grad_second = jnp.einsum(
        "bhwc,mc->bhwm", grad_exp_low, params[2], preferred_element_type=jnp.float32
    )
    grad_conv, d_gain, d_shift = norm_backward(
        silu_grad(grad_second, kept[4]), kept[5], kept[6], params[3][1]
    )
    return (grad_conv.astype(LOW), (d_gain, d_shift))


def backward_reduce(beside_all, kept, params):
    d_kernel, grad_first = depth_conv_back(kept[3], beside_all, params[1].astype(jnp.float32))
    grad_red, d_gain, d_shift = norm_backward(
        silu_grad(grad_first, kept[0]), kept[1], kept[2], params[3][0]
    )
    return (grad_red.astype(LOW), d_kernel, (d_gain, d_shift))


def backward_in(grad_sum, grad_red_low, params):
    return grad_sum + jnp.einsum(
        "bhwm,cm->bhwc", grad_red_low, params[0], preferred_element_type=jnp.float32
    )


def small_rows(d_kernel, mid_a, mid_b, out):
    return jnp.concatenate(
        [d_kernel, jnp.stack([mid_a[0], mid_b[0], mid_a[1], mid_b[1], out[0], out[1]])]
    )


def swap(field):
    return lax.ppermute(field, "half", [(0, 1), (1, 0)])


def tie(*values):
    return lax.optimization_barrier(values)


def pair_columns(field):
    width = field.shape[-1] // 2
    mine = lax.axis_index("half")
    keep = lax.dynamic_slice_in_dim(field, mine * width, width, axis=3)
    give = lax.dynamic_slice_in_dim(field, (1 - mine) * width, width, axis=3)
    return jnp.concatenate([keep, swap(give)], axis=0)


def pair_rows(field):
    return jnp.concatenate([field, swap(field)], axis=0)


def outer(left, right):
    return jnp.einsum("bhwm,bhwc->mc", left, right, preferred_element_type=jnp.float32).astype(LOW)


def exchange(pieces, axis):
    return lax.all_to_all(pieces, axis, 0, 0, tiled=True)


def spread(field, axis):
    size = lax.axis_size(axis)
    return exchange(jnp.broadcast_to(field[None], (size,) + field.shape), axis)


def sum_low(pieces):
    return jnp.sum(pieces.astype(jnp.float32), axis=0).astype(LOW)


def split_rows(field, axis):
    size = lax.axis_size(axis)
    return field.reshape(
        field.shape[:-2] + (size, field.shape[-2] // size, field.shape[-1])
    )


def scatter_plane(half_grad):
    return sum_low(exchange(split_rows(half_grad, "im"), "im"))


def scatter_steps(pieces):
    size = pieces.shape[0]
    if size > 4:
        return sum_low(exchange(pieces, "im"))
    mine = lax.axis_index("im")
    total = lax.dynamic_index_in_dim(pieces, mine, 0, False).astype(jnp.float32)
    for step in range(1, size):
        give = lax.dynamic_index_in_dim(pieces, mine ^ step, 0, False)
        got = lax.ppermute(give, "im", [(at, at ^ step) for at in range(size)])
        total = total + got.astype(jnp.float32)
    return total.astype(LOW)


def scatter_plane_steps(half_grad):
    return scatter_steps(split_rows(half_grad, "im"))


def gather_halves(part):
    return lax.all_gather(part, ("half", "im"), axis=0, tiled=True)


def scatter_row(parts):
    pieces = jnp.stack([split_rows(part, "row") for part in parts], axis=1)
    return sum_low(exchange(pieces, "row"))


def assemble(part, other, at):
    first = lax.axis_index("half") == 0
    top, bottom = (jnp.where(first, part, other), jnp.where(first, other, part))
    width = part.shape[-1]
    return jnp.concatenate(
        [top[:, :, at].reshape(-1, width), bottom[:, :, at].reshape(-1, width)], axis=0
    ).astype(jnp.float32)


def shards(
    x_in,
    pre_reduce,
    pre_conv,
    pre_expand,
    pre_mid_gain,
    pre_mid_shift,
    pre_out_gain,
    pre_out_shift,
    post_reduce,
    post_conv,
    post_expand,
    post_mid_gain,
    post_mid_shift,
    post_out_gain,
    post_out_shift,
    read_weight,
    read_bias,
    cotangent,
):
    pre_params = (
        pre_reduce,
        pre_conv,
        pre_expand,
        pre_mid_gain,
        pre_mid_shift,
        pre_out_gain,
        pre_out_shift,
    )
    post_params = (
        post_reduce,
        post_conv,
        post_expand,
        post_mid_gain,
        post_mid_shift,
        post_out_gain,
        post_out_shift,
    )
    images = x_in.astype(jnp.float32)
    count, strip, side, width = images.shape
    strips = lax.axis_size("row")
    block_one, pre_in, pre_second, pre_kept, pre_in_pair = block_forward(
        images, pre_params, pair_columns(x_in)
    )
    rows_one = block_one.reshape(count, strip // 2, 2, side, width)
    rows_one = 0.25 * (rows_one[:, :, 0] + rows_one[:, :, 1])
    pooled = rows_one.reshape(count, strip // 2, side // 2, 2, width).sum(axis=3)
    block_two, post_in, post_second, post_kept, pre_second_pair = block_forward(
        pooled, post_params, pair_columns(pre_second)
    )
    whole = lax.all_gather(block_two.astype(LOW), "row", axis=1, tiled=True)
    post_in_pair = pair_columns(post_in)
    post_second_pair = pair_columns(post_second)
    pre_act = (
        jnp.einsum("bhwc,co->bhwo", whole, read_weight, preferred_element_type=jnp.float32)
        + read_bias
    )
    readout = jax.nn.gelu(pre_act, approximate=False).astype(LOW)
    normal_cdf = 0.5 * (1.0 + lax.erf(pre_act * SQRT_HALF))
    density = jnp.exp(-0.5 * pre_act * pre_act) * INV_SQRT_TWO_PI
    grad_pre = (cotangent.astype(jnp.float32) * (normal_cdf + pre_act * density)).astype(LOW)
    terms = jnp.einsum("bhwo,co->bhwc", grad_pre, read_weight, preferred_element_type=jnp.float32)
    terms = terms.astype(LOW).reshape(count, strips, strip // 2, side // 2, width)
    terms = exchange(jnp.swapaxes(terms, 0, 1), "row")
    read_half = outer(pair_columns(whole), pair_rows(grad_pre))
    d_read_b = jnp.sum(grad_pre.astype(jnp.float32), axis=(0, 1, 2))
    read_part = scatter_plane_steps(read_half)
    grad_two = jnp.sum(terms.astype(jnp.float32), axis=0)
    post_gs, post_ge, post_out = backward_expand(grad_two, post_kept, post_params)
    post_gc, post_mid = backward_mid(post_ge, post_kept, post_params)
    post_beside, read_part, post_in_pair, post_second_pair = tie(
        with_halo(post_gc), read_part, post_in_pair, post_second_pair
    )
    read_total = gather_halves(read_part)
    post_gr, post_taps, post_first = backward_reduce(post_beside, post_kept, post_params)
    post_pair = pair_rows(jnp.stack([post_gr, post_ge], axis=1))
    grad_pooled = backward_in(post_gs, post_gr, post_params)
    grad_one = jnp.broadcast_to(
        (0.25 * grad_pooled)[:, :, :, None, :], (count, strip // 2, side // 2, 2, width)
    ).reshape(count, strip // 2, 1, side, width)
    grad_one = jnp.broadcast_to(grad_one, (count, strip // 2, 2, side, width))
    grad_one = grad_one.reshape(count, strip, side, width)
    grad_one, post_pair = tie(grad_one, post_pair)
    post_half = jnp.concatenate(
        [
            split_rows(outer(post_in_pair, post_pair[:, 0]), "im"),
            split_rows(outer(post_second_pair, post_pair[:, 1]), "im"),
        ],
        axis=1,
    )
    post_part = scatter_steps(post_half)
    pre_gs, pre_ge, pre_out = backward_expand(grad_one, pre_kept, pre_params)
    pre_ge_pair = pair_rows(pre_ge)
    pre_gc, pre_mid = backward_mid(pre_ge, pre_kept, pre_params)
    pre_beside, pre_ge_pair, post_part = tie(with_halo(pre_gc), pre_ge_pair, post_part)
    post_part = lax.psum_scatter(
        jnp.moveaxis(
            post_part.reshape(2, strips, -1, width), 1, 0
        ).reshape(-1, width),
        "row",
        scatter_dimension=0,
        tiled=True,
    )
    post_total = lax.all_gather(post_part, "row", axis=0, tiled=True)
    post_total = gather_halves(post_total)
    expand_part = scatter_plane(outer(pre_second_pair, pre_ge_pair))
    pre_gr, pre_taps, pre_first = backward_reduce(pre_beside, pre_kept, pre_params)
    pre_gr_pair, expand_part = tie(pair_rows(pre_gr), expand_part)
    reduce_part = scatter_plane(outer(pre_in_pair, pre_gr_pair))
    part = spread(scatter_row([expand_part, reduce_part]), "row")
    part = spread(part, "im")
    other = swap(part)
    pre_expand_g = assemble(part, other, 0)
    pre_reduce_g = assemble(part, other, 1)
    post_total = post_total.reshape(2, -1, strips, 2, post_part.shape[0] // 2, width)
    post_reduce_g = post_total[:, :, :, 0].reshape(-1, width).astype(jnp.float32)
    post_expand_g = post_total[:, :, :, 1].reshape(-1, width).astype(jnp.float32)
    grad_in = backward_in(pre_gs, pre_gr, pre_params)
    pre_small = small_rows(pre_taps, pre_first, pre_mid, pre_out)
    post_small = small_rows(post_taps, post_first, post_mid, post_out)
    small = jnp.concatenate([pre_small, post_small]).astype(LOW)
    small = lax.all_gather(small, "row", axis=0, tiled=False)
    small = jnp.concatenate([sum_low(small), d_read_b[None].astype(LOW)])
    small = lax.all_gather(small, IMG, axis=0, tiled=False)
    small_total = jnp.sum(small.astype(jnp.float32), axis=0)
    read_b_total = small_total[30]

    def small_grads(rows):
        return (
            rows[:9].reshape(3, 3, -1),
            rows[9:11],
            rows[11:13],
            rows[13],
            rows[14],
        )

    pre_conv_g, pre_gain_g, pre_shift_g, pre_og_g, pre_os_g = small_grads(small_total[:15])
    post_conv_g, post_gain_g, post_shift_g, post_og_g, post_os_g = small_grads(small_total[15:30])
    return (
        readout,
        grad_in.astype(LOW),
        pre_reduce_g,
        pre_conv_g,
        pre_expand_g,
        pre_gain_g,
        pre_shift_g,
        pre_og_g,
        pre_os_g,
        post_reduce_g,
        post_conv_g,
        post_expand_g,
        post_gain_g,
        post_shift_g,
        post_og_g,
        post_os_g,
        read_total.astype(jnp.float32),
        read_b_total,
    )


def solution(mesh):
    images, strips = mesh.devices.shape
    split = jax.sharding.Mesh(
        mesh.devices.reshape(images // 2, 2, strips), ("im", "half", "row")
    )
    return jax.shard_map(
        shards,
        mesh=split,
        in_specs=(P(IMG, "row", None, None),)
        + (P(),) * 14
        + (P(None, "row"), P("row"), P(IMG, None, None, "row")),
        out_specs=(P(IMG, None, None, "row"), P(IMG, "row", None, None))
        + (P(),) * 14
        + (P(None, "row"), P("row")),
        check_vma=False,
    )
```

```python
import functools

import jax
import jax.numpy as jnp
from jax import lax
from jax.experimental import pallas as pl
from jax.experimental.pallas import tpu as pltpu
from jax.sharding import PartitionSpec as P

EPSILON = 1e-06
SQRT_HALF = 0.7071067811865476
INV_SQRT_TWO_PI = 0.3989422804014327
LOW = jnp.bfloat16
FULL = jnp.float32
IMG = ("im", "half")
TILE = 256
SLAB = 16
LANES = 128
VMEM_BYTES = 48 * 1024 * 1024


def tie(*values):
    return lax.optimization_barrier(values)


def norm(value):
    centred = value - jnp.mean(value, axis=-1, keepdims=True)
    factor = lax.rsqrt(jnp.mean(centred * centred, axis=-1, keepdims=True) + EPSILON)
    return (centred * factor, factor)


def norm_back(grad, normed, factor, gain):
    scaled = grad * gain
    return factor * (
        scaled
        - jnp.mean(scaled, axis=-1, keepdims=True)
        - normed * jnp.mean(scaled * normed, axis=-1, keepdims=True)
    )


def gate(value):
    return 0.5 * jnp.tanh(0.5 * value) + 0.5


def silu(value):
    return value * gate(value)


def silu_back(grad, value):
    sigma = gate(value)
    return grad * sigma * (1.0 + value * (1.0 - sigma))


def fold(value):
    return jnp.sum(value.reshape(-1, 8, value.shape[-1]), axis=0)


def live(rows, cols):
    at = lax.broadcasted_iota(jnp.int32, (rows, 1), 0)
    return lax.rem(at, SLAB) < cols


def from_left(value):
    at = lax.broadcasted_iota(jnp.int32, (value.shape[0], 1), 0)
    return jnp.where(at == 0, 0.0, pltpu.roll(value, 1, 0))


def from_right(value):
    last = value.shape[0] - 1
    at = lax.broadcasted_iota(jnp.int32, (value.shape[0], 1), 0)
    return jnp.where(at == last, 0.0, pltpu.roll(value, last, 0))


def matmul(left_ref, right_ref, out_ref):
    @pl.loop(0, right_ref.shape[1] // TILE)
    def _(at):
        cols = pl.ds(pl.multiple_of(at * TILE, TILE), TILE)
        out_ref[:, cols] = jnp.dot(
            left_ref[...], right_ref[:, cols], preferred_element_type=FULL
        )


def matmul_back(left_ref, right_ref, out_ref):
    @pl.loop(0, right_ref.shape[0] // TILE)
    def _(at):
        cols = pl.ds(pl.multiple_of(at * TILE, TILE), TILE)
        out_ref[:, cols] = lax.dot_general(
            left_ref[...],
            right_ref[cols, :],
            (((1,), (1,)), ((), ())),
            preferred_element_type=FULL,
        ).astype(out_ref.dtype)


def rows_of(at, size):
    return pl.ds(pl.multiple_of(at * size, SLAB), size)


def fill_halo(pad_ref, low_ref, before_ref, after_ref):
    count, rows, cols, width = pad_ref.shape
    rows = rows - 2
    for image in range(count):
        pad_ref[image, 0] = before_ref[image].astype(FULL)
        pad_ref[image, rows + 1] = after_ref[image].astype(FULL)

    size = cols if cols % SLAB == 0 else 2 * cols
    per = size // cols
    each = rows // per

    @pl.loop(0, count * each)
    def _(at):
        part = low_ref[rows_of(at, size), :].astype(FULL).reshape(per, cols, width)
        pad_ref[at // each, pl.ds(1 + per * lax.rem(at, each), per)] = part


def conv_row(pad_ref, taps, image, row):
    lines = [pad_ref[image, row + top] for top in range(3)]
    sums = [
        lines[0] * taps[left] + lines[1] * taps[3 + left] + lines[2] * taps[6 + left]
        for left in range(3)
    ]
    return from_left(sums[0]) + sums[1] + from_right(sums[2])


def conv_back_row(pad_ref, grad_ref, taps, taps_ref, image, row):
    lines = [grad_ref[image, row + top] for top in range(3)]
    sums = [
        lines[2] * taps[left] + lines[1] * taps[3 + left] + lines[0] * taps[6 + left]
        for left in range(3)
    ]
    shifted = [from_right(lines[1]), lines[1], from_left(lines[1])]
    for top in range(3):
        source = pad_ref[image, row + top]
        for left in range(3):
            taps_ref[3 * top + left] += fold(source * shifted[left])
    return from_right(sums[0]) + sums[1] + from_left(sums[2])


def narrow(pair, value):
    side = value.shape[0]
    parts = []
    for at in range(value.shape[1] // LANES):
        pair[pl.ds(at * side, side), :] = value[:, at * LANES : (at + 1) * LANES]
        parts.append(
            pair[pl.ds(at * side, side // 2, stride=2), :]
            + pair[pl.ds(at * side + 1, side // 2, stride=2), :]
        )
    return jnp.concatenate(parts, axis=1)


def widen(pair, value):
    cols = value.shape[0]
    parts = []
    for at in range(value.shape[1] // LANES):
        part = value[:, at * LANES : (at + 1) * LANES]
        pair[pl.ds(2 * cols * at, cols, stride=2), :] = part
        pair[pl.ds(2 * cols * at + 1, cols, stride=2), :] = part
        parts.append(pair[pl.ds(2 * cols * at, 2 * cols), :])
    return jnp.concatenate(parts, axis=1)


def tap_rows(conv_ref):
    return [conv_ref[pl.ds(at, 1), :] for at in range(9)]


def finish(small_ref, sums_ref, at, place):
    small_ref[pl.ds(place, 1), :] = jnp.sum(sums_ref[at], axis=0, keepdims=True)


def pre_reduce_kernel(
    x_ref, w_ref, gain_ref, shift_ref, first_ref, top_ref, bottom_ref, normed_ref, factor_ref, red
):
    count, side, width = top_ref.shape
    size = 2 * side
    steps = x_ref.shape[0] // size
    matmul(x_ref, w_ref, red)
    gain, shift = (gain_ref[pl.ds(0, 1), :], shift_ref[pl.ds(0, 1), :])

    @pl.loop(0, steps)
    def _(at):
        rows = rows_of(at, size)
        normed, factor = norm(red[rows, :])
        normed_ref[rows, :] = normed
        factor_ref[rows, :] = factor
        first_ref[rows, :] = silu(normed * gain + shift).astype(LOW)

    each = steps // count
    for image in range(count):
        head = first_ref[pl.ds(image * each * size, size), :].astype(FULL)
        tail = first_ref[pl.ds((image * each + each - 1) * size, size), :].astype(FULL)
        top_ref[image] = head[:side].astype(LOW)
        bottom_ref[image] = tail[side:].astype(LOW)


def pre_rest_kernel(
    x_ref,
    first_ref,
    before_ref,
    after_ref,
    conv_ref,
    expand_ref,
    gain_ref,
    shift_ref,
    out_gain_ref,
    out_shift_ref,
    reduce_ref,
    post_gain_ref,
    post_shift_ref,
    second_ref,
    normed_b_ref,
    factor_b_ref,
    normed_c_ref,
    factor_c_ref,
    summed_ref,
    pooled_ref,
    pooled_low_ref,
    post_first_ref,
    post_top_ref,
    post_bottom_ref,
    post_normed_ref,
    post_factor_ref,
    pad,
    exp,
    pair,
    red,
):
    count, strip, side, width = pad.shape
    strip = strip - 2
    size = 2 * side
    each = strip // 2
    fill_halo(pad, first_ref, before_ref, after_ref)
    taps = tap_rows(conv_ref)
    gain, shift = (gain_ref[pl.ds(1, 1), :], shift_ref[pl.ds(1, 1), :])

    @pl.loop(0, count * each)
    def _(at):
        rows = rows_of(at, size)
        image, row = (at // each, 2 * lax.rem(at, each))
        conv = jnp.concatenate(
            [conv_row(pad, taps, image, row), conv_row(pad, taps, image, row + 1)], axis=0
        )
        normed, factor = norm(conv)
        normed_b_ref[rows, :] = normed
        factor_b_ref[rows, :] = factor
        second_ref[rows, :] = silu(normed * gain + shift).astype(LOW)

    matmul(second_ref, expand_ref, exp)
    out_gain, out_shift = (out_gain_ref[...], out_shift_ref[...])
    cols = side // 2
    for at in range(count * each):
        rows = pl.ds(at * size, size)
        normed, factor = norm(exp[rows, :])
        normed_c_ref[rows, :] = normed
        factor_c_ref[rows, :] = factor
        summed = x_ref[rows, :].astype(FULL) + normed * out_gain + out_shift
        summed_ref[rows, :] = summed
        block = silu(summed)
        half = narrow(pair, block[:side] + block[side:])
        pooled_ref[pl.ds(at * SLAB, cols), :] = 0.25 * half
        pooled_ref[pl.ds(at * SLAB + cols, SLAB - cols), :] = jnp.zeros(
            (SLAB - cols, width), FULL
        )
    pooled_low_ref[...] = pooled_ref[...].astype(LOW)
    matmul(pooled_low_ref, reduce_ref, red)
    normed, factor = norm(red[...])
    post_normed_ref[...] = normed
    post_factor_ref[...] = factor
    first = silu(normed * post_gain_ref[pl.ds(0, 1), :] + post_shift_ref[pl.ds(0, 1), :])
    post_first_ref[...] = jnp.where(live(red.shape[0], cols), first, 0.0).astype(LOW)
    for image in range(count):
        post_top_ref[image] = post_first_ref[pl.ds(image * each * SLAB, SLAB), :]
        post_bottom_ref[image] = post_first_ref[pl.ds((image * each + each - 1) * SLAB, SLAB), :]


def post_rest_kernel(
    pooled_ref,
    first_ref,
    before_ref,
    after_ref,
    conv_ref,
    expand_ref,
    gain_ref,
    shift_ref,
    out_gain_ref,
    out_shift_ref,
    block_ref,
    second_ref,
    normed_b_ref,
    factor_b_ref,
    normed_c_ref,
    factor_c_ref,
    summed_ref,
    pad,
    exp,
    compact,
    *,
    cols
):
    count, rows, _, width = pad.shape
    rows = rows - 2
    fill_halo(pad, first_ref, before_ref, after_ref)
    taps = tap_rows(conv_ref)
    gain, shift = (gain_ref[pl.ds(1, 1), :], shift_ref[pl.ds(1, 1), :])

    @pl.loop(0, count * rows)
    def _(at):
        place = rows_of(at, SLAB)
        normed, factor = norm(conv_row(pad, taps, at // rows, lax.rem(at, rows)))
        normed_b_ref[place, :] = normed
        factor_b_ref[place, :] = factor
        second_ref[place, :] = silu(normed * gain + shift).astype(LOW)

    matmul(second_ref, expand_ref, exp)
    normed, factor = norm(exp[...])
    normed_c_ref[...] = normed
    factor_c_ref[...] = factor
    summed = pooled_ref[...] + normed * out_gain_ref[...] + out_shift_ref[...]
    summed_ref[...] = summed
    exp[...] = silu(summed)
    for at in range(count * rows):
        compact[pl.ds(at * cols, cols), :] = exp[pl.ds(at * SLAB, cols), :]
    block_ref[...] = compact[...].astype(LOW)


def readout_kernel(
    whole_ref, w_ref, bias_ref, cot_ref, out_ref, grad_ref, terms_ref, bias_grad_ref
):
    @pl.loop(0, w_ref.shape[1] // TILE)
    def _(at):
        cols = pl.ds(pl.multiple_of(at * TILE, TILE), TILE)
        act = jnp.dot(whole_ref[...], w_ref[:, cols], preferred_element_type=FULL)
        act = act + bias_ref[:, cols]
        cdf = 0.5 * (1.0 + lax.erf(act * SQRT_HALF))
        density = jnp.exp(-0.5 * act * act) * INV_SQRT_TWO_PI
        out_ref[:, cols] = (act * cdf).astype(LOW)
        grad = (cot_ref[:, cols].astype(FULL) * (cdf + act * density)).astype(LOW)
        grad_ref[:, cols] = grad
        bias_grad_ref[:, cols] = jnp.sum(grad.astype(FULL), axis=0, keepdims=True)

    matmul_back(grad_ref, w_ref, terms_ref)


def post_back_kernel(
    pieces_ref,
    expand_ref,
    gain_ref,
    shift_ref,
    out_gain_ref,
    normed_b_ref,
    factor_b_ref,
    normed_c_ref,
    factor_c_ref,
    summed_ref,
    grad_sum_ref,
    grad_exp_ref,
    grad_conv_ref,
    top_ref,
    bottom_ref,
    small_ref,
    compact,
    spread_out,
    sec,
    *,
    cols
):
    count = top_ref.shape[0]
    tokens, width = grad_sum_ref.shape
    each = tokens // SLAB // count
    total = pieces_ref[0].astype(FULL)
    for at in range(1, pieces_ref.shape[0]):
        total = total + pieces_ref[at].astype(FULL)
    compact[...] = total
    spread_out[...] = jnp.zeros((tokens, width), FULL)
    for at in range(tokens // SLAB):
        spread_out[pl.ds(at * SLAB, cols), :] = compact[pl.ds(at * cols, cols), :]
    grad_sum = silu_back(spread_out[...], summed_ref[...])
    grad_sum_ref[...] = grad_sum
    normed = normed_c_ref[...]
    grad_exp_ref[...] = norm_back(grad_sum, normed, factor_c_ref[...], out_gain_ref[...]).astype(
        LOW
    )
    small_ref[pl.ds(2, 1), :] = jnp.sum(grad_sum * normed, axis=0, keepdims=True)
    small_ref[pl.ds(3, 1), :] = jnp.sum(grad_sum, axis=0, keepdims=True)
    matmul_back(grad_exp_ref, expand_ref, sec)
    gain, shift = (gain_ref[pl.ds(1, 1), :], shift_ref[pl.ds(1, 1), :])
    normed = normed_b_ref[...]
    grad = silu_back(sec[...], normed * gain + shift)
    grad_conv_ref[...] = norm_back(grad, normed, factor_b_ref[...], gain).astype(LOW)
    small_ref[pl.ds(0, 1), :] = jnp.sum(grad * normed, axis=0, keepdims=True)
    small_ref[pl.ds(1, 1), :] = jnp.sum(grad, axis=0, keepdims=True)
    for image in range(count):
        top_ref[image] = grad_conv_ref[pl.ds(image * each * SLAB, SLAB), :]
        bottom_ref[image] = grad_conv_ref[pl.ds((image * each + each - 1) * SLAB, SLAB), :]


def middle_back_kernel(
    grad_conv_ref,
    before_ref,
    after_ref,
    first_ref,
    first_before_ref,
    first_after_ref,
    post_conv_ref,
    post_reduce_ref,
    post_gain_ref,
    post_shift_ref,
    post_normed_ref,
    post_factor_ref,
    post_grad_sum_ref,
    expand_ref,
    gain_ref,
    shift_ref,
    out_gain_ref,
    normed_b_ref,
    factor_b_ref,
    normed_c_ref,
    factor_c_ref,
    summed_ref,
    post_grad_red_ref,
    grad_sum_ref,
    grad_exp_ref,
    pre_grad_conv_ref,
    top_ref,
    bottom_ref,
    post_small_ref,
    small_ref,
    pad,
    grad_pad,
    taps_sum,
    grad_in,
    pair,
    sec,
    sums,
    *,
    cols
):
    count, side, width = top_ref.shape
    fill_halo(grad_pad, grad_conv_ref, before_ref, after_ref)
    fill_halo(pad, first_ref, first_before_ref, first_after_ref)
    taps = tap_rows(post_conv_ref)
    taps_sum[...] = jnp.zeros_like(taps_sum)
    sums[...] = jnp.zeros_like(sums)
    gain, shift = (post_gain_ref[pl.ds(0, 1), :], post_shift_ref[pl.ds(0, 1), :])
    each = post_grad_sum_ref.shape[0] // SLAB // count

    @pl.loop(0, count * each)
    def _(at):
        place = rows_of(at, SLAB)
        grad = conv_back_row(pad, grad_pad, taps, taps_sum, at // each, lax.rem(at, each))
        normed = post_normed_ref[place, :]
        grad = jnp.where(live(SLAB, cols), silu_back(grad, normed * gain + shift), 0.0)
        sums[0] += fold(grad * normed)
        sums[1] += fold(grad)
        post_grad_red_ref[place, :] = norm_back(
            grad, normed, post_factor_ref[place, :], gain
        ).astype(LOW)

    for at in range(9):
        finish(post_small_ref, taps_sum, at, at)
    finish(post_small_ref, sums, 0, 9)
    finish(post_small_ref, sums, 1, 10)
    matmul_back(post_grad_red_ref, post_reduce_ref, grad_in)
    sums[...] = jnp.zeros_like(sums)
    size = 2 * side
    out_gain = out_gain_ref[...]
    for at in range(count * each):
        rows = pl.ds(at * size, size)
        place = pl.ds(at * SLAB, cols)
        grad = 0.25 * (post_grad_sum_ref[place, :] + grad_in[place, :])
        grad = widen(pair, grad)
        grad = jnp.concatenate([grad, grad], axis=0)
        grad_sum = silu_back(grad, summed_ref[rows, :])
        grad_sum_ref[rows, :] = grad_sum
        normed = normed_c_ref[rows, :]
        sums[0] += fold(grad_sum * normed)
        sums[1] += fold(grad_sum)
        grad_exp_ref[rows, :] = norm_back(
            grad_sum, normed, factor_c_ref[rows, :], out_gain
        ).astype(LOW)
    finish(small_ref, sums, 0, 2)
    finish(small_ref, sums, 1, 3)
    matmul_back(grad_exp_ref, expand_ref, sec)
    sums[...] = jnp.zeros_like(sums)
    gain_b, shift_b = (gain_ref[pl.ds(1, 1), :], shift_ref[pl.ds(1, 1), :])

    @pl.loop(0, count * each)
    def _(at):
        rows = rows_of(at, size)
        normed = normed_b_ref[rows, :]
        grad = silu_back(sec[rows, :], normed * gain_b + shift_b)
        sums[0] += fold(grad * normed)
        sums[1] += fold(grad)
        pre_grad_conv_ref[rows, :] = norm_back(
            grad, normed, factor_b_ref[rows, :], gain_b
        ).astype(LOW)

    finish(small_ref, sums, 0, 0)
    finish(small_ref, sums, 1, 1)
    for image in range(count):
        head = pre_grad_conv_ref[pl.ds(image * each * size, size), :].astype(FULL)
        tail = pre_grad_conv_ref[pl.ds((image * each + each - 1) * size, size), :].astype(FULL)
        top_ref[image] = head[:side].astype(LOW)
        bottom_ref[image] = tail[side:].astype(LOW)


def pre_back_kernel(
    grad_conv_ref,
    before_ref,
    after_ref,
    first_ref,
    first_before_ref,
    first_after_ref,
    conv_ref,
    gain_ref,
    shift_ref,
    normed_ref,
    factor_ref,
    grad_red_ref,
    small_ref,
    pad,
    grad_pad,
    taps_sum,
    sums,
):
    count, strip, side, width = pad.shape
    strip = strip - 2
    size = 2 * side
    each = strip // 2
    fill_halo(grad_pad, grad_conv_ref, before_ref, after_ref)
    fill_halo(pad, first_ref, first_before_ref, first_after_ref)
    taps = tap_rows(conv_ref)
    taps_sum[...] = jnp.zeros_like(taps_sum)
    sums[...] = jnp.zeros_like(sums)
    gain, shift = (gain_ref[pl.ds(0, 1), :], shift_ref[pl.ds(0, 1), :])

    @pl.loop(0, count * each)
    def _(at):
        rows = rows_of(at, size)
        image, row = (at // each, 2 * lax.rem(at, each))
        grad = jnp.concatenate(
            [
                conv_back_row(pad, grad_pad, taps, taps_sum, image, row),
                conv_back_row(pad, grad_pad, taps, taps_sum, image, row + 1),
            ],
            axis=0,
        )
        normed = normed_ref[rows, :]
        grad = silu_back(grad, normed * gain + shift)
        sums[0] += fold(grad * normed)
        sums[1] += fold(grad)
        grad_red_ref[rows, :] = norm_back(grad, normed, factor_ref[rows, :], gain).astype(LOW)

    for at in range(9):
        finish(small_ref, taps_sum, at, at)
    finish(small_ref, sums, 0, 9)
    finish(small_ref, sums, 1, 10)


def like(*shape, dtype=FULL):
    return jax.ShapeDtypeStruct(shape, dtype)


def call(kernel, outs, scratch, flops, *args):
    moved = sum(arg.size * arg.dtype.itemsize for arg in args)
    moved += sum(out.size * out.dtype.itemsize for out in outs)
    return pl.pallas_call(
        kernel,
        out_shape=outs,
        in_specs=[pl.BlockSpec(memory_space=pltpu.VMEM)] * len(args),
        out_specs=[pl.BlockSpec(memory_space=pltpu.VMEM)] * len(outs),
        scratch_shapes=[pltpu.VMEM(shape, FULL) for shape in scratch],
        compiler_params=pltpu.CompilerParams(vmem_limit_bytes=VMEM_BYTES),
        cost_estimate=pl.CostEstimate(flops=flops, bytes_accessed=moved, transcendentals=0),
    )(*args)


def edges(top, bottom):
    size = lax.axis_size("row")
    up = [(at, at + 1) for at in range(size - 1)]
    down = [(at + 1, at) for at in range(size - 1)]
    return (lax.ppermute(bottom, "row", up), lax.ppermute(top, "row", down))


def swap(field):
    return lax.ppermute(field, "half", [(0, 1), (1, 0)])


def pair_columns(field):
    width = field.shape[-1] // 2
    mine = lax.axis_index("half")
    keep = lax.dynamic_slice_in_dim(field, mine * width, width, axis=1)
    give = lax.dynamic_slice_in_dim(field, (1 - mine) * width, width, axis=1)
    return jnp.concatenate([keep, swap(give)], axis=0)


def pair_rows(field):
    return jnp.concatenate([field, swap(field)], axis=0)


def outer(left, right):
    return jnp.einsum("tm,tc->mc", left, right, preferred_element_type=FULL).astype(LOW)


def exchange(pieces, axis):
    return lax.all_to_all(pieces, axis, 0, 0, tiled=True)


def spread(field, axis):
    size = lax.axis_size(axis)
    return exchange(jnp.broadcast_to(field[None], (size,) + field.shape), axis)


def sum_low(pieces):
    return jnp.sum(pieces.astype(FULL), axis=0).astype(LOW)


def split_rows(field, axis):
    size = lax.axis_size(axis)
    return field.reshape(
        field.shape[:-2] + (size, field.shape[-2] // size, field.shape[-1])
    )


def scatter_plane(half_grad):
    return sum_low(exchange(split_rows(half_grad, "im"), "im"))


def scatter_steps(pieces):
    size = pieces.shape[0]
    if size > 4:
        return sum_low(exchange(pieces, "im"))
    mine = lax.axis_index("im")
    total = lax.dynamic_index_in_dim(pieces, mine, 0, False).astype(FULL)
    for step in range(1, size):
        give = lax.dynamic_index_in_dim(pieces, mine ^ step, 0, False)
        got = lax.ppermute(give, "im", [(at, at ^ step) for at in range(size)])
        total = total + got.astype(FULL)
    return total.astype(LOW)


def gather_halves(part):
    return lax.all_gather(part, ("half", "im"), axis=0, tiled=True)


def scatter_row(parts):
    pieces = jnp.stack([split_rows(part, "row") for part in parts], axis=1)
    return sum_low(exchange(pieces, "row"))


def assemble(part, other, at):
    first = lax.axis_index("half") == 0
    top, bottom = (jnp.where(first, part, other), jnp.where(first, other, part))
    width = part.shape[-1]
    return jnp.concatenate(
        [top[:, :, at].reshape(-1, width), bottom[:, :, at].reshape(-1, width)], axis=0
    ).astype(FULL)


def shards(
    x_in,
    pre_reduce,
    pre_conv,
    pre_expand,
    pre_mid_gain,
    pre_mid_shift,
    pre_out_gain,
    pre_out_shift,
    post_reduce,
    post_conv,
    post_expand,
    post_mid_gain,
    post_mid_shift,
    post_out_gain,
    post_out_shift,
    read_weight,
    read_bias,
    cotangent,
):
    count, strip, side, width = x_in.shape
    strips = lax.axis_size("row")
    tokens = count * strip * side
    cols = side // 2
    rows = strip // 2
    slabs = count * rows
    padded = slabs * SLAB
    small = slabs * cols
    features = read_weight.shape[1]
    cost = 2 * tokens * width * width
    post_cost = 2 * padded * width * width
    x_low = x_in.reshape(tokens, width)
    pre_taps = pre_conv.reshape(9, width).astype(FULL)
    post_taps = post_conv.reshape(9, width).astype(FULL)
    pre_out_g, pre_out_s = (pre_out_gain[None], pre_out_shift[None])
    post_out_g, post_out_s = (post_out_gain[None], post_out_shift[None])
    cot = cotangent.reshape(count, strips, rows, cols, features)
    cot = jnp.moveaxis(cot, 1, 0).reshape(strips * small, features)

    first, top, bottom, normed_a, factor_a = call(
        pre_reduce_kernel,
        [
            like(tokens, width, dtype=LOW),
            like(count, side, width, dtype=LOW),
            like(count, side, width, dtype=LOW),
            like(tokens, width),
            like(tokens, 1),
        ],
        [(tokens, width)],
        cost,
        x_low,
        pre_reduce,
        pre_mid_gain,
        pre_mid_shift,
    )
    before, after = edges(top, bottom)
    x_pair = pair_columns(x_low)
    before, after, x_pair = tie(before, after, x_pair)
    (
        second,
        normed_b,
        factor_b,
        normed_c,
        factor_c,
        summed,
        pooled,
        pooled_low,
        post_first,
        post_top,
        post_bottom,
        post_normed_a,
        post_factor_a,
    ) = call(
        pre_rest_kernel,
        [
            like(tokens, width, dtype=LOW),
            like(tokens, width),
            like(tokens, 1),
            like(tokens, width),
            like(tokens, 1),
            like(tokens, width),
            like(padded, width),
            like(padded, width, dtype=LOW),
            like(padded, width, dtype=LOW),
            like(count, SLAB, width, dtype=LOW),
            like(count, SLAB, width, dtype=LOW),
            like(padded, width),
            like(padded, 1),
        ],
        [
            (count, strip + 2, side, width),
            (tokens, width),
            (side * width // LANES, LANES),
            (padded, width),
        ],
        cost + post_cost,
        x_low,
        first,
        before,
        after,
        pre_taps,
        pre_expand,
        pre_mid_gain,
        pre_mid_shift,
        pre_out_g,
        pre_out_s,
        post_reduce,
        post_mid_gain,
        post_mid_shift,
    )
    post_before, post_after = edges(post_top, post_bottom)
    second_pair = pair_columns(second)
    post_before, post_after, second_pair = tie(post_before, post_after, second_pair)
    (
        block_two,
        post_second,
        post_normed_b,
        post_factor_b,
        post_normed_c,
        post_factor_c,
        post_summed,
    ) = call(
        functools.partial(post_rest_kernel, cols=cols),
        [
            like(small, width, dtype=LOW),
            like(padded, width, dtype=LOW),
            like(padded, width),
            like(padded, 1),
            like(padded, width),
            like(padded, 1),
            like(padded, width),
        ],
        [
            (count, rows + 2, SLAB, width),
            (padded, width),
            (small, width),
        ],
        post_cost,
        pooled,
        post_first,
        post_before,
        post_after,
        post_taps,
        post_expand,
        post_mid_gain,
        post_mid_shift,
        post_out_g,
        post_out_s,
    )
    whole = lax.all_gather(block_two, "row", axis=0, tiled=True)
    post_in_pair = pair_columns(pooled_low)
    post_second_pair = pair_columns(post_second)
    readout, grad_pre, terms, d_read_b = call(
        readout_kernel,
        [
            like(strips * small, features, dtype=LOW),
            like(strips * small, features, dtype=LOW),
            like(strips * small, width, dtype=LOW),
            like(1, features),
        ],
        [],
        2 * cost,
        whole,
        read_weight,
        read_bias[None],
        cot,
    )
    terms = exchange(terms.reshape(strips, small, width), "row")
    read_half = outer(pair_columns(whole), pair_rows(grad_pre))
    read_part = scatter_steps(split_rows(read_half, "im"))
    (
        post_gs,
        post_ge,
        post_gc,
        post_top,
        post_bottom,
        post_small_b,
    ) = call(
        functools.partial(post_back_kernel, cols=cols),
        [
            like(padded, width),
            like(padded, width, dtype=LOW),
            like(padded, width, dtype=LOW),
            like(count, SLAB, width, dtype=LOW),
            like(count, SLAB, width, dtype=LOW),
            like(4, width),
        ],
        [
            (small, width),
            (padded, width),
            (padded, width),
        ],
        post_cost,
        terms,
        post_expand,
        post_mid_gain,
        post_mid_shift,
        post_out_g,
        post_normed_b,
        post_factor_b,
        post_normed_c,
        post_factor_c,
        post_summed,
    )
    back_before, back_after = edges(post_top, post_bottom)
    back_before, back_after, read_part, post_in_pair, post_second_pair = tie(
        back_before, back_after, read_part, post_in_pair, post_second_pair
    )
    read_total = gather_halves(read_part)
    (
        post_gr,
        pre_gs,
        pre_ge,
        pre_gc,
        pre_top,
        pre_bottom,
        post_small_a,
        pre_small_b,
    ) = call(
        functools.partial(middle_back_kernel, cols=cols),
        [
            like(padded, width, dtype=LOW),
            like(tokens, width),
            like(tokens, width, dtype=LOW),
            like(tokens, width, dtype=LOW),
            like(count, side, width, dtype=LOW),
            like(count, side, width, dtype=LOW),
            like(11, width),
            like(4, width),
        ],
        [
            (count, rows + 2, SLAB, width),
            (count, rows + 2, SLAB, width),
            (9, 8, width),
            (padded, width),
            (side * width // LANES, LANES),
            (tokens, width),
            (2, 8, width),
        ],
        cost + post_cost,
        post_gc,
        back_before,
        back_after,
        post_first,
        post_before,
        post_after,
        post_taps,
        post_reduce,
        post_mid_gain,
        post_mid_shift,
        post_normed_a,
        post_factor_a,
        post_gs,
        pre_expand,
        pre_mid_gain,
        pre_mid_shift,
        pre_out_g,
        normed_b,
        factor_b,
        normed_c,
        factor_c,
        summed,
    )
    back_before, back_after = edges(pre_top, pre_bottom)
    post_pair = pair_rows(jnp.stack([post_gr, post_ge], axis=1))
    ge_pair = pair_rows(pre_ge)
    back_before, back_after, post_pair, ge_pair = tie(back_before, back_after, post_pair, ge_pair)
    pre_gr, pre_small_a = call(
        pre_back_kernel,
        [like(tokens, width, dtype=LOW), like(11, width)],
        [
            (count, strip + 2, side, width),
            (count, strip + 2, side, width),
            (9, 8, width),
            (2, 8, width),
        ],
        0,
        pre_gc,
        back_before,
        back_after,
        first,
        before,
        after,
        pre_taps,
        pre_mid_gain,
        pre_mid_shift,
        normed_a,
        factor_a,
    )
    post_half = jnp.concatenate(
        [
            split_rows(outer(post_in_pair, post_pair[:, 0]), "im"),
            split_rows(outer(post_second_pair, post_pair[:, 1]), "im"),
        ],
        axis=1,
    )
    post_part = scatter_steps(post_half)
    post_part = lax.psum_scatter(
        jnp.moveaxis(post_part.reshape(2, strips, -1, width), 1, 0).reshape(-1, width),
        "row",
        scatter_dimension=0,
        tiled=True,
    )
    post_total = gather_halves(lax.all_gather(post_part, "row", axis=0, tiled=True))
    expand_part = scatter_plane(outer(second_pair, ge_pair))
    gr_pair, expand_part = tie(pair_rows(pre_gr), expand_part)
    reduce_part = scatter_plane(outer(x_pair, gr_pair))
    part = spread(scatter_row([expand_part, reduce_part]), "row")
    part = spread(part, "im")
    other = swap(part)
    pre_expand_g = assemble(part, other, 0)
    pre_reduce_g = assemble(part, other, 1)
    post_total = post_total.reshape(2, -1, strips, 2, post_part.shape[0] // 2, width)
    post_reduce_g = post_total[:, :, :, 0].reshape(-1, width).astype(FULL)
    post_expand_g = post_total[:, :, :, 1].reshape(-1, width).astype(FULL)
    grad_in = pre_gs + jnp.einsum("tm,cm->tc", pre_gr, pre_reduce, preferred_element_type=FULL)

    sums = jnp.concatenate([pre_small_a, pre_small_b, post_small_a, post_small_b]).astype(LOW)
    sums = lax.all_gather(sums, "row", axis=0, tiled=False)
    sums = jnp.concatenate([sum_low(sums), d_read_b.astype(LOW)])
    sums = lax.all_gather(sums, IMG, axis=0, tiled=False)
    sums = jnp.sum(sums.astype(FULL), axis=0)

    def small_grads(part):
        return (
            part[:9].reshape(3, 3, width),
            jnp.stack([part[9], part[11]]),
            jnp.stack([part[10], part[12]]),
            part[13],
            part[14],
        )

    pre_conv_g, pre_gain_g, pre_shift_g, pre_og_g, pre_os_g = small_grads(sums[:15])
    post_conv_g, post_gain_g, post_shift_g, post_og_g, post_os_g = small_grads(sums[15:30])
    readout = readout.reshape(strips, count, rows, cols, features)
    readout = jnp.moveaxis(readout, 0, 1).reshape(cotangent.shape)
    return (
        readout,
        grad_in.astype(LOW).reshape(x_in.shape),
        pre_reduce_g,
        pre_conv_g,
        pre_expand_g,
        pre_gain_g,
        pre_shift_g,
        pre_og_g,
        pre_os_g,
        post_reduce_g,
        post_conv_g,
        post_expand_g,
        post_gain_g,
        post_shift_g,
        post_og_g,
        post_os_g,
        read_total.astype(FULL),
        sums[30],
    )


def solution(mesh):
    images, strips = mesh.devices.shape
    split = jax.sharding.Mesh(
        mesh.devices.reshape(images // 2, 2, strips), ("im", "half", "row")
    )
    return jax.shard_map(
        shards,
        mesh=split,
        in_specs=(P(IMG, "row", None, None),)
        + (P(),) * 14
        + (P(None, "row"), P("row"), P(IMG, None, None, "row")),
        out_specs=(P(IMG, None, None, "row"), P(IMG, "row", None, None))
        + (P(),) * 14
        + (P(None, "row"), P("row")),
        check_vma=False,
    )
```

```python
import functools

import jax
import jax.numpy as jnp
from jax import lax
from jax.experimental import pallas as pl
from jax.experimental.pallas import tpu as pltpu
from jax.sharding import PartitionSpec as P

EPSILON = 1e-06
SQRT_HALF = 0.7071067811865476
INV_SQRT_TWO_PI = 0.3989422804014327
LOW = jnp.bfloat16
FULL = jnp.float32
IMG = ("im", "half")
TILE = 256
SLAB = 16
LANES = 128
VMEM_BYTES = 60 * 1024 * 1024


def tie(*values):
    return lax.optimization_barrier(values)


def norm(value):
    centred = value - jnp.mean(value, axis=-1, keepdims=True)
    factor = lax.rsqrt(jnp.mean(centred * centred, axis=-1, keepdims=True) + EPSILON)
    return (centred * factor, factor)


def norm_back(grad, normed, factor, gain):
    scaled = grad * gain
    return factor * (
        scaled
        - jnp.mean(scaled, axis=-1, keepdims=True)
        - normed * jnp.mean(scaled * normed, axis=-1, keepdims=True)
    )


def gate(value):
    return 0.5 * jnp.tanh(0.5 * value) + 0.5


def silu(value):
    return value * gate(value)


def silu_back(grad, value):
    sigma = gate(value)
    return grad * sigma * (1.0 + value * (1.0 - sigma))


def wide(factor):
    return jnp.broadcast_to(factor, (factor.shape[0], LANES))


def fold(value):
    return jnp.sum(value.reshape(-1, 8, value.shape[-1]), axis=0)


def live(rows, cols):
    at = lax.broadcasted_iota(jnp.int32, (rows, 1), 0)
    return lax.rem(at, SLAB) < cols


def from_left(value):
    at = lax.broadcasted_iota(jnp.int32, (value.shape[0], 1), 0)
    return jnp.where(at == 0, 0.0, pltpu.roll(value, 1, 0))


def from_right(value):
    last = value.shape[0] - 1
    at = lax.broadcasted_iota(jnp.int32, (value.shape[0], 1), 0)
    return jnp.where(at == last, 0.0, pltpu.roll(value, last, 0))


def matmul(left_ref, right_ref, out_ref):
    @pl.loop(0, right_ref.shape[1] // TILE)
    def _(at):
        cols = pl.ds(pl.multiple_of(at * TILE, TILE), TILE)
        out_ref[:, cols] = jnp.dot(
            left_ref[...], right_ref[:, cols], preferred_element_type=FULL
        )


def matmul_back(left_ref, right_ref, out_ref):
    @pl.loop(0, right_ref.shape[0] // TILE)
    def _(at):
        cols = pl.ds(pl.multiple_of(at * TILE, TILE), TILE)
        out_ref[:, cols] = lax.dot_general(
            left_ref[...],
            right_ref[cols, :],
            (((1,), (1,)), ((), ())),
            preferred_element_type=FULL,
        ).astype(out_ref.dtype)


def rows_of(at, size):
    return pl.ds(pl.multiple_of(at * size, SLAB), size)


def fill_halo(pad_ref, low_ref, before_ref, after_ref):
    count, rows, cols, width = pad_ref.shape
    rows = rows - 2
    for image in range(count):
        pad_ref[image, 0] = before_ref[image].astype(FULL)
        pad_ref[image, rows + 1] = after_ref[image].astype(FULL)

    size = cols if cols % SLAB == 0 else 2 * cols
    per = size // cols
    each = rows // per

    @pl.loop(0, count * each)
    def _(at):
        part = low_ref[rows_of(at, size), :].astype(FULL).reshape(per, cols, width)
        pad_ref[at // each, pl.ds(1 + per * lax.rem(at, each), per)] = part


def conv_row(pad_ref, taps, image, row):
    lines = [pad_ref[image, row + top] for top in range(3)]
    sums = [
        lines[0] * taps[left] + lines[1] * taps[3 + left] + lines[2] * taps[6 + left]
        for left in range(3)
    ]
    return from_left(sums[0]) + sums[1] + from_right(sums[2])


def conv_back_row(pad_ref, grad_ref, taps, taps_ref, image, row):
    lines = [grad_ref[image, row + top] for top in range(3)]
    sums = [
        lines[2] * taps[left] + lines[1] * taps[3 + left] + lines[0] * taps[6 + left]
        for left in range(3)
    ]
    shifted = [from_right(lines[1]), lines[1], from_left(lines[1])]
    for top in range(3):
        source = pad_ref[image, row + top]
        for left in range(3):
            taps_ref[3 * top + left] += fold(source * shifted[left])
    return from_right(sums[0]) + sums[1] + from_left(sums[2])


def narrow(pair, value):
    side = value.shape[0]
    parts = []
    for at in range(value.shape[1] // LANES):
        pair[pl.ds(at * side, side), :] = value[:, at * LANES : (at + 1) * LANES]
        parts.append(
            pair[pl.ds(at * side, side // 2, stride=2), :]
            + pair[pl.ds(at * side + 1, side // 2, stride=2), :]
        )
    return jnp.concatenate(parts, axis=1)


def widen(pair, value):
    cols = value.shape[0]
    parts = []
    for at in range(value.shape[1] // LANES):
        part = value[:, at * LANES : (at + 1) * LANES]
        pair[pl.ds(2 * cols * at, cols, stride=2), :] = part
        pair[pl.ds(2 * cols * at + 1, cols, stride=2), :] = part
        parts.append(pair[pl.ds(2 * cols * at, 2 * cols), :])
    return jnp.concatenate(parts, axis=1)


def tap_rows(conv_ref):
    return [conv_ref[pl.ds(at, 1), :] for at in range(9)]


def finish(small_ref, sums_ref, at, place):
    small_ref[pl.ds(place, 1), :] = jnp.sum(sums_ref[at], axis=0, keepdims=True)


def pre_reduce_kernel(
    need, send, x_ref, w_ref, gain_ref, shift_ref, first_ref, top_ref, bottom_ref, normed_ref, factor_ref, red
):
    count, side, width = top_ref.shape
    size = 2 * side
    steps = x_ref.shape[0] // size
    need(x_ref, w_ref)
    matmul(x_ref, w_ref, red)
    need(gain_ref, shift_ref)
    gain, shift = (gain_ref[pl.ds(0, 1), :], shift_ref[pl.ds(0, 1), :])

    @pl.loop(0, steps)
    def _(at):
        rows = rows_of(at, size)
        normed, factor = norm(red[rows, :])
        normed_ref[rows, :] = normed
        factor_ref[rows, :] = wide(factor)
        first_ref[rows, :] = silu(normed * gain + shift).astype(LOW)

    each = steps // count
    for image in range(count):
        head = first_ref[pl.ds(image * each * size, size), :].astype(FULL)
        tail = first_ref[pl.ds((image * each + each - 1) * size, size), :].astype(FULL)
        top_ref[image] = head[:side].astype(LOW)
        bottom_ref[image] = tail[side:].astype(LOW)


def pre_rest_kernel(
    need, send, x_ref,
    first_ref,
    before_ref,
    after_ref,
    conv_ref,
    expand_ref,
    gain_ref,
    shift_ref,
    out_gain_ref,
    out_shift_ref,
    reduce_ref,
    post_gain_ref,
    post_shift_ref,
    second_ref,
    normed_b_ref,
    factor_b_ref,
    normed_c_ref,
    factor_c_ref,
    summed_ref,
    pooled_ref,
    pooled_low_ref,
    post_first_ref,
    post_top_ref,
    post_bottom_ref,
    post_normed_ref,
    post_factor_ref,
    pad,
    exp,
    pair,
    red,
):
    count, strip, side, width = pad.shape
    strip = strip - 2
    size = 2 * side
    each = strip // 2
    need(first_ref, before_ref, after_ref)
    fill_halo(pad, first_ref, before_ref, after_ref)
    need(conv_ref, gain_ref, shift_ref)
    taps = tap_rows(conv_ref)
    gain, shift = (gain_ref[pl.ds(1, 1), :], shift_ref[pl.ds(1, 1), :])

    @pl.loop(0, count * each)
    def _(at):
        rows = rows_of(at, size)
        image, row = (at // each, 2 * lax.rem(at, each))
        conv = jnp.concatenate(
            [conv_row(pad, taps, image, row), conv_row(pad, taps, image, row + 1)], axis=0
        )
        normed, factor = norm(conv)
        normed_b_ref[rows, :] = normed
        factor_b_ref[rows, :] = wide(factor)
        second_ref[rows, :] = silu(normed * gain + shift).astype(LOW)

    send(second_ref, normed_b_ref, factor_b_ref)
    need(expand_ref)
    matmul(second_ref, expand_ref, exp)
    need(x_ref, out_gain_ref, out_shift_ref)
    out_gain, out_shift = (out_gain_ref[...], out_shift_ref[...])
    cols = side // 2
    for at in range(count * each):
        rows = pl.ds(at * size, size)
        normed, factor = norm(exp[rows, :])
        normed_c_ref[rows, :] = normed
        factor_c_ref[rows, :] = wide(factor)
        summed = x_ref[rows, :].astype(FULL) + normed * out_gain + out_shift
        summed_ref[rows, :] = summed
        block = silu(summed)
        half = narrow(pair, block[:side] + block[side:])
        pooled_ref[pl.ds(at * SLAB, cols), :] = 0.25 * half
        pooled_ref[pl.ds(at * SLAB + cols, SLAB - cols), :] = jnp.zeros(
            (SLAB - cols, width), FULL
        )
    pooled_low_ref[...] = pooled_ref[...].astype(LOW)
    send(normed_c_ref, factor_c_ref, summed_ref, pooled_ref, pooled_low_ref)
    need(reduce_ref, post_gain_ref, post_shift_ref)
    matmul(pooled_low_ref, reduce_ref, red)
    normed, factor = norm(red[...])
    post_normed_ref[...] = normed
    post_factor_ref[...] = wide(factor)
    first = silu(normed * post_gain_ref[pl.ds(0, 1), :] + post_shift_ref[pl.ds(0, 1), :])
    post_first_ref[...] = jnp.where(live(red.shape[0], cols), first, 0.0).astype(LOW)
    for image in range(count):
        post_top_ref[image] = post_first_ref[pl.ds(image * each * SLAB, SLAB), :]
        post_bottom_ref[image] = post_first_ref[pl.ds((image * each + each - 1) * SLAB, SLAB), :]


def post_rest_kernel(
    need, send, pooled_ref,
    first_ref,
    before_ref,
    after_ref,
    conv_ref,
    expand_ref,
    gain_ref,
    shift_ref,
    out_gain_ref,
    out_shift_ref,
    block_ref,
    second_ref,
    normed_b_ref,
    factor_b_ref,
    normed_c_ref,
    factor_c_ref,
    summed_ref,
    pad,
    exp,
    compact,
    *,
    cols
):
    count, rows, _, width = pad.shape
    rows = rows - 2
    need(first_ref, before_ref, after_ref, conv_ref, gain_ref, shift_ref)
    fill_halo(pad, first_ref, before_ref, after_ref)
    taps = tap_rows(conv_ref)
    gain, shift = (gain_ref[pl.ds(1, 1), :], shift_ref[pl.ds(1, 1), :])

    @pl.loop(0, count * rows)
    def _(at):
        place = rows_of(at, SLAB)
        normed, factor = norm(conv_row(pad, taps, at // rows, lax.rem(at, rows)))
        normed_b_ref[place, :] = normed
        factor_b_ref[place, :] = wide(factor)
        second_ref[place, :] = silu(normed * gain + shift).astype(LOW)

    send(second_ref, normed_b_ref, factor_b_ref)
    need(expand_ref)
    matmul(second_ref, expand_ref, exp)
    need(pooled_ref, out_gain_ref, out_shift_ref)
    normed, factor = norm(exp[...])
    normed_c_ref[...] = normed
    factor_c_ref[...] = wide(factor)
    summed = pooled_ref[...] + normed * out_gain_ref[...] + out_shift_ref[...]
    summed_ref[...] = summed
    exp[...] = silu(summed)
    for at in range(count * rows):
        compact[pl.ds(at * cols, cols), :] = exp[pl.ds(at * SLAB, cols), :]
    block_ref[...] = compact[...].astype(LOW)


def readout_kernel(
    need, send,
    whole_ref,
    w_ref,
    bias_ref,
    cot_ref,
    out_ref,
    grad_ref,
    terms_ref,
    bias_grad_ref,
    cot,
    out,
    *,
    strips
):
    images, lines, cols, _ = cot_ref.shape
    rows = lines // strips
    need(cot_ref)
    for at in range(images * lines):
        strip, image, row = (at // (images * rows), at // rows % images, at % rows)
        cot[pl.ds(at * cols, cols), :] = cot_ref[image, strip * rows + row].astype(FULL)
    need(whole_ref, w_ref, bias_ref)

    @pl.loop(0, w_ref.shape[1] // TILE)
    def _(at):
        lanes = pl.ds(pl.multiple_of(at * TILE, TILE), TILE)
        act = jnp.dot(whole_ref[...], w_ref[:, lanes], preferred_element_type=FULL)
        act = act + bias_ref[:, lanes]
        cdf = 0.5 * (1.0 + lax.erf(act * SQRT_HALF))
        density = jnp.exp(-0.5 * act * act) * INV_SQRT_TWO_PI
        out[:, lanes] = act * cdf
        grad = (cot[:, lanes] * (cdf + act * density)).astype(LOW)
        grad_ref[:, lanes] = grad
        bias_grad_ref[:, lanes] = jnp.sum(grad.astype(FULL), axis=0, keepdims=True)

    send(grad_ref, bias_grad_ref)
    matmul_back(grad_ref, w_ref, terms_ref)
    send(terms_ref)
    for at in range(images * lines):
        strip, image, row = (at // (images * rows), at // rows % images, at % rows)
        out_ref[image, strip * rows + row] = out[pl.ds(at * cols, cols), :].astype(LOW)


def post_back_kernel(
    need, send, pieces_ref,
    expand_ref,
    gain_ref,
    shift_ref,
    out_gain_ref,
    normed_b_ref,
    factor_b_ref,
    normed_c_ref,
    factor_c_ref,
    summed_ref,
    grad_sum_ref,
    grad_exp_ref,
    grad_conv_ref,
    top_ref,
    bottom_ref,
    small_ref,
    compact,
    spread_out,
    sec,
    *,
    cols
):
    count = top_ref.shape[0]
    tokens, width = grad_sum_ref.shape
    each = tokens // SLAB // count
    need(pieces_ref)
    total = pieces_ref[0].astype(FULL)
    for at in range(1, pieces_ref.shape[0]):
        total = total + pieces_ref[at].astype(FULL)
    compact[...] = total
    spread_out[...] = jnp.zeros((tokens, width), FULL)
    for at in range(tokens // SLAB):
        spread_out[pl.ds(at * SLAB, cols), :] = compact[pl.ds(at * cols, cols), :]
    need(summed_ref, normed_c_ref, factor_c_ref, out_gain_ref)
    grad_sum = silu_back(spread_out[...], summed_ref[...])
    grad_sum_ref[...] = grad_sum
    normed = normed_c_ref[...]
    grad_exp_ref[...] = norm_back(grad_sum, normed, factor_c_ref[:, :1], out_gain_ref[...]).astype(
        LOW
    )
    small_ref[pl.ds(2, 1), :] = jnp.sum(grad_sum * normed, axis=0, keepdims=True)
    small_ref[pl.ds(3, 1), :] = jnp.sum(grad_sum, axis=0, keepdims=True)
    send(grad_sum_ref, grad_exp_ref)
    need(expand_ref)
    matmul_back(grad_exp_ref, expand_ref, sec)
    need(gain_ref, shift_ref, normed_b_ref, factor_b_ref)
    gain, shift = (gain_ref[pl.ds(1, 1), :], shift_ref[pl.ds(1, 1), :])
    normed = normed_b_ref[...]
    grad = silu_back(sec[...], normed * gain + shift)
    grad_conv_ref[...] = norm_back(grad, normed, factor_b_ref[:, :1], gain).astype(LOW)
    small_ref[pl.ds(0, 1), :] = jnp.sum(grad * normed, axis=0, keepdims=True)
    small_ref[pl.ds(1, 1), :] = jnp.sum(grad, axis=0, keepdims=True)
    for image in range(count):
        top_ref[image] = grad_conv_ref[pl.ds(image * each * SLAB, SLAB), :]
        bottom_ref[image] = grad_conv_ref[pl.ds((image * each + each - 1) * SLAB, SLAB), :]


def middle_back_kernel(
    need, send, grad_conv_ref,
    before_ref,
    after_ref,
    first_ref,
    first_before_ref,
    first_after_ref,
    post_conv_ref,
    post_reduce_ref,
    post_gain_ref,
    post_shift_ref,
    post_normed_ref,
    post_factor_ref,
    post_grad_sum_ref,
    expand_ref,
    gain_ref,
    shift_ref,
    out_gain_ref,
    normed_b_ref,
    factor_b_ref,
    normed_c_ref,
    factor_c_ref,
    summed_ref,
    post_grad_red_ref,
    grad_sum_ref,
    grad_exp_ref,
    pre_grad_conv_ref,
    top_ref,
    bottom_ref,
    post_small_ref,
    small_ref,
    pad,
    grad_pad,
    taps_sum,
    grad_in,
    pair,
    sec,
    sums,
    *,
    cols
):
    count, side, width = top_ref.shape
    need(grad_conv_ref, before_ref, after_ref)
    fill_halo(grad_pad, grad_conv_ref, before_ref, after_ref)
    need(first_ref, first_before_ref, first_after_ref, post_conv_ref)
    fill_halo(pad, first_ref, first_before_ref, first_after_ref)
    need(post_gain_ref, post_shift_ref, post_normed_ref, post_factor_ref)
    taps = tap_rows(post_conv_ref)
    taps_sum[...] = jnp.zeros_like(taps_sum)
    sums[...] = jnp.zeros_like(sums)
    gain, shift = (post_gain_ref[pl.ds(0, 1), :], post_shift_ref[pl.ds(0, 1), :])
    each = post_grad_sum_ref.shape[0] // SLAB // count

    @pl.loop(0, count * each)
    def _(at):
        place = rows_of(at, SLAB)
        grad = conv_back_row(pad, grad_pad, taps, taps_sum, at // each, lax.rem(at, each))
        normed = post_normed_ref[place, :]
        grad = jnp.where(live(SLAB, cols), silu_back(grad, normed * gain + shift), 0.0)
        sums[0] += fold(grad * normed)
        sums[1] += fold(grad)
        post_grad_red_ref[place, :] = norm_back(
            grad, normed, post_factor_ref[place, :1], gain
        ).astype(LOW)

    for at in range(9):
        finish(post_small_ref, taps_sum, at, at)
    finish(post_small_ref, sums, 0, 9)
    finish(post_small_ref, sums, 1, 10)
    send(post_grad_red_ref, post_small_ref)
    need(post_reduce_ref)
    matmul_back(post_grad_red_ref, post_reduce_ref, grad_in)
    sums[...] = jnp.zeros_like(sums)
    size = 2 * side
    need(out_gain_ref, post_grad_sum_ref, summed_ref, normed_c_ref, factor_c_ref)
    out_gain = out_gain_ref[...]
    for at in range(count * each):
        rows = pl.ds(at * size, size)
        place = pl.ds(at * SLAB, cols)
        grad = 0.25 * (post_grad_sum_ref[place, :] + grad_in[place, :])
        grad = widen(pair, grad)
        grad = jnp.concatenate([grad, grad], axis=0)
        grad_sum = silu_back(grad, summed_ref[rows, :])
        grad_sum_ref[rows, :] = grad_sum
        normed = normed_c_ref[rows, :]
        sums[0] += fold(grad_sum * normed)
        sums[1] += fold(grad_sum)
        grad_exp_ref[rows, :] = norm_back(
            grad_sum, normed, factor_c_ref[rows, :1], out_gain
        ).astype(LOW)
    finish(small_ref, sums, 0, 2)
    finish(small_ref, sums, 1, 3)
    send(grad_sum_ref, grad_exp_ref)
    need(expand_ref)
    matmul_back(grad_exp_ref, expand_ref, sec)
    need(gain_ref, shift_ref, normed_b_ref, factor_b_ref)
    sums[...] = jnp.zeros_like(sums)
    gain_b, shift_b = (gain_ref[pl.ds(1, 1), :], shift_ref[pl.ds(1, 1), :])

    @pl.loop(0, count * each)
    def _(at):
        rows = rows_of(at, size)
        normed = normed_b_ref[rows, :]
        grad = silu_back(sec[rows, :], normed * gain_b + shift_b)
        sums[0] += fold(grad * normed)
        sums[1] += fold(grad)
        pre_grad_conv_ref[rows, :] = norm_back(
            grad, normed, factor_b_ref[rows, :1], gain_b
        ).astype(LOW)

    finish(small_ref, sums, 0, 0)
    finish(small_ref, sums, 1, 1)
    for image in range(count):
        head = pre_grad_conv_ref[pl.ds(image * each * size, size), :].astype(FULL)
        tail = pre_grad_conv_ref[pl.ds((image * each + each - 1) * size, size), :].astype(FULL)
        top_ref[image] = head[:side].astype(LOW)
        bottom_ref[image] = tail[side:].astype(LOW)


def pre_back_kernel(
    need, send, grad_conv_ref,
    before_ref,
    after_ref,
    first_ref,
    first_before_ref,
    first_after_ref,
    conv_ref,
    gain_ref,
    shift_ref,
    normed_ref,
    factor_ref,
    grad_red_ref,
    small_ref,
    pad,
    grad_pad,
    taps_sum,
    sums,
):
    count, strip, side, width = pad.shape
    strip = strip - 2
    size = 2 * side
    each = strip // 2
    need(grad_conv_ref, before_ref, after_ref)
    fill_halo(grad_pad, grad_conv_ref, before_ref, after_ref)
    need(first_ref, first_before_ref, first_after_ref, conv_ref)
    fill_halo(pad, first_ref, first_before_ref, first_after_ref)
    need(gain_ref, shift_ref, normed_ref, factor_ref)
    taps = tap_rows(conv_ref)
    taps_sum[...] = jnp.zeros_like(taps_sum)
    sums[...] = jnp.zeros_like(sums)
    gain, shift = (gain_ref[pl.ds(0, 1), :], shift_ref[pl.ds(0, 1), :])

    @pl.loop(0, count * each)
    def _(at):
        rows = rows_of(at, size)
        image, row = (at // each, 2 * lax.rem(at, each))
        grad = jnp.concatenate(
            [
                conv_back_row(pad, grad_pad, taps, taps_sum, image, row),
                conv_back_row(pad, grad_pad, taps, taps_sum, image, row + 1),
            ],
            axis=0,
        )
        normed = normed_ref[rows, :]
        grad = silu_back(grad, normed * gain + shift)
        sums[0] += fold(grad * normed)
        sums[1] += fold(grad)
        grad_red_ref[rows, :] = norm_back(grad, normed, factor_ref[rows, :1], gain).astype(LOW)

    for at in range(9):
        finish(small_ref, taps_sum, at, at)
    finish(small_ref, sums, 0, 9)
    finish(small_ref, sums, 1, 10)


def pair_outer_kernel(need, send, at_ref, *refs, pairs, parts):
    takes = 4 * pairs
    outs = refs[takes:]
    half, plane = (at_ref[0], at_ref[1])
    rows = outs[0].shape[0] // pairs
    for pair in range(pairs):
        left, left_far, right, right_far = refs[4 * pair : 4 * pair + 4]
        need(left, left_far, right, right_far)
        for step in range(parts):
            begin = half * (rows * parts) + jnp.bitwise_xor(plane, step) * rows
            lanes = pl.ds(pl.multiple_of(begin, LANES), rows)
            total = lax.dot_general(
                left[:, lanes], right[...], (((0,), (0,)), ((), ())), preferred_element_type=FULL
            ) + lax.dot_general(
                left_far[:, lanes],
                right_far[...],
                (((0,), (0,)), ((), ())),
                preferred_element_type=FULL,
            )
            outs[step][pl.ds(pair * rows, rows), :] = total.astype(LOW)
    send(*outs)


def sum_split_kernel(need, send, at_ref, *refs, pairs, parts, pieces):
    takes, outs = (refs[:pieces], refs[pieces : pieces + parts])
    total = refs[-1]
    need(*takes)
    value = takes[0][...].astype(FULL)
    for at in range(1, pieces):
        value = value + takes[at][...].astype(FULL)
    total[...] = value
    rows = total.shape[0] // pairs // parts
    for step in range(parts):
        begin = jnp.bitwise_xor(at_ref[2], step) * rows
        for pair in range(pairs):
            place = pl.ds(pl.multiple_of(pair * rows * parts + begin, SLAB), rows)
            outs[step][pl.ds(pair * rows, rows), :] = total[place, :].astype(LOW)
    send(*outs)


def assemble_body(at_ref, *refs, pairs, planes, strips):
    takes = 2 * planes
    parts, outs = (refs[:takes], refs[takes : takes + pairs])
    near = refs[takes + pairs : 2 * takes + pairs]
    full = refs[2 * takes + pairs : 2 * takes + 2 * pairs]
    in_sem, out_sem = refs[-2:]
    reads = [pltpu.make_async_copy(parts[at], near[at], in_sem.at[at]) for at in range(takes)]
    for read in reads:
        read.start()
    half, plane, row = (at_ref[0], at_ref[1], at_ref[2])
    rows = near[0].shape[0] // pairs // strips
    block = rows * strips
    writes = []
    for at in range(takes):
        reads[at].wait()
        side = jnp.bitwise_xor(half, at // planes)
        begin = side * (planes * block) + jnp.bitwise_xor(plane, at % planes) * block
        for pair in range(pairs):
            for step in range(strips):
                place = begin + jnp.bitwise_xor(row, step) * rows
                full[pair][pl.ds(pl.multiple_of(place, SLAB), rows), :] = near[at][
                    pl.ds((step * pairs + pair) * rows, rows), :
                ].astype(FULL)
            span = pl.ds(pl.multiple_of(begin, SLAB), block)
            write = pltpu.make_async_copy(
                full[pair].at[span, :], outs[pair].at[span, :], out_sem.at[len(writes)]
            )
            write.start()
            writes.append(write)
    for write in writes:
        write.wait()


def assemble(index, parts, pairs, planes, strips):
    takes = len(parts)
    width = parts[0].shape[1]
    out = like(2 * planes * parts[0].shape[0] // pairs, width)
    far = pl.BlockSpec(memory_space=pltpu.HBM)
    return pl.pallas_call(
        functools.partial(assemble_body, pairs=pairs, planes=planes, strips=strips),
        out_shape=[out] * pairs,
        in_specs=[pl.BlockSpec(memory_space=pltpu.SMEM)] + [far] * takes,
        out_specs=[far] * pairs,
        scratch_shapes=[pltpu.VMEM(part.shape, part.dtype) for part in parts]
        + [pltpu.VMEM(out.shape, FULL)] * pairs
        + [pltpu.SemaphoreType.DMA((takes,)), pltpu.SemaphoreType.DMA((takes * pairs,))],
        compiler_params=pltpu.CompilerParams(vmem_limit_bytes=VMEM_BYTES),
        cost_estimate=pl.CostEstimate(
            flops=0, bytes_accessed=pairs * out.size * 6, transcendentals=0
        ),
    )(index, *parts)


def like(*shape, dtype=FULL):
    return jax.ShapeDtypeStruct(shape, dtype)


def call(kernel, outs, scratch, flops, *args, index=None):
    takes, gives = (len(args), len(outs))
    lead = 0 if index is None else 1

    def body(*refs):
        given, refs = (refs[:lead], refs[lead:])
        far_in, far_out = (refs[:takes], refs[takes : takes + gives])
        near = refs[takes + gives :]
        near_in, near_out = (near[:takes], near[takes : takes + gives])
        rest, (in_sem, out_sem) = (near[takes + gives : -2], near[-2:])
        reads = [
            pltpu.make_async_copy(far_in[at], near_in[at], in_sem.at[at]) for at in range(takes)
        ]
        writes = [
            pltpu.make_async_copy(near_out[at], far_out[at], out_sem.at[at])
            for at in range(gives)
        ]
        read_left, write_left = (list(range(takes)), list(range(gives)))
        for read in reads:
            read.start()

        def need(*wanted):
            for at in list(read_left):
                if any(near_in[at] is ref for ref in wanted):
                    reads[at].wait()
                    read_left.remove(at)

        def send(*ready):
            for at in list(write_left):
                if any(near_out[at] is ref for ref in ready):
                    writes[at].start()
                    write_left.remove(at)

        kernel(need, send, *given, *near_in, *near_out, *rest)
        need(*near_in)
        send(*near_out)
        for write in writes:
            write.wait()

    moved = sum(arg.size * arg.dtype.itemsize for arg in args)
    moved += sum(out.size * out.dtype.itemsize for out in outs)
    far = pl.BlockSpec(memory_space=pltpu.HBM)
    head = [] if index is None else [pl.BlockSpec(memory_space=pltpu.SMEM)]
    lead_args = [] if index is None else [index]
    return pl.pallas_call(
        body,
        out_shape=outs,
        in_specs=head + [far] * takes,
        out_specs=[far] * gives,
        scratch_shapes=[pltpu.VMEM(arg.shape, arg.dtype) for arg in args]
        + [pltpu.VMEM(out.shape, out.dtype) for out in outs]
        + [pltpu.VMEM(shape, FULL) for shape in scratch]
        + [pltpu.SemaphoreType.DMA((takes,)), pltpu.SemaphoreType.DMA((gives,))],
        compiler_params=pltpu.CompilerParams(vmem_limit_bytes=VMEM_BYTES),
        cost_estimate=pl.CostEstimate(flops=flops, bytes_accessed=moved, transcendentals=0),
    )(*lead_args, *args)


def edges(top, bottom):
    size = lax.axis_size("row")
    up = [(at, at + 1) for at in range(size - 1)]
    down = [(at + 1, at) for at in range(size - 1)]
    return (lax.ppermute(bottom, "row", up), lax.ppermute(top, "row", down))


def swap(field):
    return lax.ppermute(field, "half", [(0, 1), (1, 0)])


def exchange(pieces, axis):
    return lax.all_to_all(pieces, axis, 0, 0, tiled=True)


def steps_of(value, axis, step):
    size = lax.axis_size(axis)
    return lax.ppermute(value, axis, [(at, at ^ step) for at in range(size)])


def share(parts, axis):
    return [parts[0]] + [steps_of(parts[at], axis, at) for at in range(1, len(parts))]


def share_same(part, axis):
    size = lax.axis_size(axis)
    return [part] + [steps_of(part, axis, at) for at in range(1, size)]


def call_list(*args, **named):
    return list(call(*args, **named))


def pair_outer(index, pairs):
    size = lax.axis_size("im")
    rows = pairs[0][0].shape[1] // 2 // size * len(pairs)
    width = pairs[0][2].shape[1]
    flops = sum(2 * pair[0].shape[0] * rows * size * width for pair in pairs)
    return call_list(
        functools.partial(pair_outer_kernel, pairs=len(pairs), parts=size),
        [like(rows, width, dtype=LOW)] * size,
        [],
        2 * flops,
        *[ref for pair in pairs for ref in pair],
        index=index,
    )


def sum_split(index, pieces, pairs):
    size = lax.axis_size("row")
    rows, width = pieces[0].shape
    return call_list(
        functools.partial(
            sum_split_kernel, pairs=pairs, parts=size, pieces=len(pieces)
        ),
        [like(rows // size, width, dtype=LOW)] * size,
        [(rows, width)],
        0,
        *pieces,
        index=index,
    )


def add_low(pieces):
    total = pieces[0].astype(FULL)
    for piece in pieces[1:]:
        total = total + piece.astype(FULL)
    return total.astype(LOW)


def total_small(value, kept):
    value = value + swap(value)
    step = 1
    while step < lax.axis_size("im"):
        value = value + steps_of(value, "im", step)
        step *= 2
    alone, value = (value[kept:], value[:kept])
    step = 1
    while step < lax.axis_size("row"):
        value = value + steps_of(value, "row", step)
        step *= 2
    return (value, alone)


def sum_far(left, right, axes):
    part = jnp.einsum("tm,tc->mc", left, right, preferred_element_type=FULL)
    return lax.psum(part, axes)


def shards(
    x_in,
    pre_reduce,
    pre_conv,
    pre_expand,
    pre_mid_gain,
    pre_mid_shift,
    pre_out_gain,
    pre_out_shift,
    post_reduce,
    post_conv,
    post_expand,
    post_mid_gain,
    post_mid_shift,
    post_out_gain,
    post_out_shift,
    read_weight,
    read_bias,
    cotangent,
):
    count, strip, side, width = x_in.shape
    strips = lax.axis_size("row")
    tokens = count * strip * side
    cols = side // 2
    rows = strip // 2
    slabs = count * rows
    padded = slabs * SLAB
    small = slabs * cols
    features = read_weight.shape[1]
    cost = 2 * tokens * width * width
    post_cost = 2 * padded * width * width
    x_low = x_in.reshape(tokens, width)
    pre_taps = pre_conv.reshape(9, width).astype(FULL)
    post_taps = post_conv.reshape(9, width).astype(FULL)
    pre_out_g, pre_out_s = (pre_out_gain[None], pre_out_shift[None])
    post_out_g, post_out_s = (post_out_gain[None], post_out_shift[None])
    index = jnp.stack([lax.axis_index("half"), lax.axis_index("im"), lax.axis_index("row")])
    quick = lax.axis_size("im") == 4 and strips == 4
    if quick:
        x_far = swap(x_low)

    first, top, bottom, normed_a, factor_a = call(
        pre_reduce_kernel,
        [
            like(tokens, width, dtype=LOW),
            like(count, side, width, dtype=LOW),
            like(count, side, width, dtype=LOW),
            like(tokens, width),
            like(tokens, LANES),
        ],
        [(tokens, width)],
        cost,
        x_low,
        pre_reduce,
        pre_mid_gain,
        pre_mid_shift,
    )
    before, after = edges(top, bottom)
    if quick:
        before, after, x_far = tie(before, after, x_far)
    (
        second,
        normed_b,
        factor_b,
        normed_c,
        factor_c,
        summed,
        pooled,
        pooled_low,
        post_first,
        post_top,
        post_bottom,
        post_normed_a,
        post_factor_a,
    ) = call(
        pre_rest_kernel,
        [
            like(tokens, width, dtype=LOW),
            like(tokens, width),
            like(tokens, LANES),
            like(tokens, width),
            like(tokens, LANES),
            like(tokens, width),
            like(padded, width),
            like(padded, width, dtype=LOW),
            like(padded, width, dtype=LOW),
            like(count, SLAB, width, dtype=LOW),
            like(count, SLAB, width, dtype=LOW),
            like(padded, width),
            like(padded, LANES),
        ],
        [
            (count, strip + 2, side, width),
            (tokens, width),
            (side * width // LANES, LANES),
            (padded, width),
        ],
        cost + post_cost,
        x_low,
        first,
        before,
        after,
        pre_taps,
        pre_expand,
        pre_mid_gain,
        pre_mid_shift,
        pre_out_g,
        pre_out_s,
        post_reduce,
        post_mid_gain,
        post_mid_shift,
    )
    post_before, post_after = edges(post_top, post_bottom)
    if quick:
        second_far = swap(second)
        post_before, post_after, second_far = tie(post_before, post_after, second_far)
    (
        block_two,
        post_second,
        post_normed_b,
        post_factor_b,
        post_normed_c,
        post_factor_c,
        post_summed,
    ) = call(
        functools.partial(post_rest_kernel, cols=cols),
        [
            like(small, width, dtype=LOW),
            like(padded, width, dtype=LOW),
            like(padded, width),
            like(padded, LANES),
            like(padded, width),
            like(padded, LANES),
            like(padded, width),
        ],
        [
            (count, rows + 2, SLAB, width),
            (padded, width),
            (small, width),
        ],
        post_cost,
        pooled,
        post_first,
        post_before,
        post_after,
        post_taps,
        post_expand,
        post_mid_gain,
        post_mid_shift,
        post_out_g,
        post_out_s,
    )
    whole = lax.all_gather(block_two, "row", axis=0, tiled=True)
    if quick:
        post_in_far = swap(pooled_low)
        post_second_far = swap(post_second)
        whole, post_in_far, post_second_far = tie(whole, post_in_far, post_second_far)
        whole_far = swap(whole)
    readout, grad_pre, terms, d_read_b = call(
        functools.partial(readout_kernel, strips=strips),
        [
            like(*cotangent.shape, dtype=LOW),
            like(strips * small, features, dtype=LOW),
            like(strips * small, width, dtype=LOW),
            like(1, features),
        ],
        [(strips * small, features), (strips * small, features)],
        2 * cost,
        whole,
        read_weight,
        read_bias[None],
        cotangent,
    )
    terms = exchange(terms.reshape(strips, small, width), "row")
    if quick:
        read_parts = pair_outer(index, [(whole, whole_far, grad_pre, swap(grad_pre))])
        terms, read_parts[0] = tie(terms, read_parts[0])
        read_part = add_low(share(read_parts, "im"))
    (
        post_gs,
        post_ge,
        post_gc,
        post_top,
        post_bottom,
        post_small_b,
    ) = call(
        functools.partial(post_back_kernel, cols=cols),
        [
            like(padded, width),
            like(padded, width, dtype=LOW),
            like(padded, width, dtype=LOW),
            like(count, SLAB, width, dtype=LOW),
            like(count, SLAB, width, dtype=LOW),
            like(4, width),
        ],
        [
            (small, width),
            (padded, width),
            (padded, width),
        ],
        post_cost,
        terms,
        post_expand,
        post_mid_gain,
        post_mid_shift,
        post_out_g,
        post_normed_b,
        post_factor_b,
        post_normed_c,
        post_factor_c,
        post_summed,
    )
    back_before, back_after = edges(post_top, post_bottom)
    if quick:
        post_ge_far = swap(post_ge)
        back_before, back_after, read_part, post_ge_far = tie(
            back_before, back_after, read_part, post_ge_far
        )
        read_total = lax.all_gather(read_part, ("half", "im"), axis=0, tiled=True)
    (
        post_gr,
        pre_gs,
        pre_ge,
        pre_gc,
        pre_top,
        pre_bottom,
        post_small_a,
        pre_small_b,
    ) = call(
        functools.partial(middle_back_kernel, cols=cols),
        [
            like(padded, width, dtype=LOW),
            like(tokens, width),
            like(tokens, width, dtype=LOW),
            like(tokens, width, dtype=LOW),
            like(count, side, width, dtype=LOW),
            like(count, side, width, dtype=LOW),
            like(11, width),
            like(4, width),
        ],
        [
            (count, rows + 2, SLAB, width),
            (count, rows + 2, SLAB, width),
            (9, 8, width),
            (padded, width),
            (side * width // LANES, LANES),
            (tokens, width),
            (2, 8, width),
        ],
        cost + post_cost,
        post_gc,
        back_before,
        back_after,
        post_first,
        post_before,
        post_after,
        post_taps,
        post_reduce,
        post_mid_gain,
        post_mid_shift,
        post_normed_a,
        post_factor_a,
        post_gs,
        pre_expand,
        pre_mid_gain,
        pre_mid_shift,
        pre_out_g,
        normed_b,
        factor_b,
        normed_c,
        factor_c,
        summed,
    )
    back_before, back_after = edges(pre_top, pre_bottom)
    if quick:
        post_parts = pair_outer(
            index,
            [
                (pooled_low, post_in_far, post_gr, swap(post_gr)),
                (post_second, post_second_far, post_ge, post_ge_far),
            ],
        )
        expand_parts = pair_outer(index, [(second, second_far, pre_ge, swap(pre_ge))])
        back_before, back_after, post_parts[0], expand_parts[0] = tie(
            back_before, back_after, post_parts[0], expand_parts[0]
        )
    pre_gr, pre_small_a = call(
        pre_back_kernel,
        [like(tokens, width, dtype=LOW), like(11, width)],
        [
            (count, strip + 2, side, width),
            (count, strip + 2, side, width),
            (9, 8, width),
            (2, 8, width),
        ],
        0,
        pre_gc,
        back_before,
        back_after,
        first,
        before,
        after,
        pre_taps,
        pre_mid_gain,
        pre_mid_shift,
        normed_a,
        factor_a,
    )
    if quick:
        reduce_parts = pair_outer(index, [(x_low, x_far, pre_gr, swap(pre_gr))])
        post_parts = sum_split(index, share(post_parts, "im"), 2)
        expand_parts = sum_split(index, share(expand_parts, "im"), 1)
        reduce_parts = sum_split(index, share(reduce_parts, "im"), 1)
        streams = []
        for pairs, parts in ((2, post_parts), (1, expand_parts), (1, reduce_parts)):
            part = add_low(share(parts, "row"))
            part = jnp.concatenate(share_same(part, "row"), axis=0)
            parts = share_same(part, "im")
            parts = parts + [swap(part) for part in parts]
            streams.append(assemble(index, parts, pairs, 4, strips))
        (post_reduce_g, post_expand_g), (pre_expand_g,), (pre_reduce_g,) = streams
        read_total = read_total.astype(FULL)
    else:
        axes = IMG + ("row",)
        post_reduce_g = sum_far(pooled_low, post_gr, axes)
        post_expand_g = sum_far(post_second, post_ge, axes)
        pre_expand_g = sum_far(second, pre_ge, axes)
        pre_reduce_g = sum_far(x_low, pre_gr, axes)
        read_total = sum_far(whole, grad_pre, IMG)
    grad_in = pre_gs + jnp.einsum("tm,cm->tc", pre_gr, pre_reduce, preferred_element_type=FULL)

    sums = jnp.concatenate([pre_small_a, pre_small_b, post_small_a, post_small_b, d_read_b])
    sums, read_bias_g = total_small(sums, 30)

    def small_grads(part):
        return (
            part[:9].reshape(3, 3, width),
            jnp.stack([part[9], part[11]]),
            jnp.stack([part[10], part[12]]),
            part[13],
            part[14],
        )

    pre_conv_g, pre_gain_g, pre_shift_g, pre_og_g, pre_os_g = small_grads(sums[:15])
    post_conv_g, post_gain_g, post_shift_g, post_og_g, post_os_g = small_grads(sums[15:30])
    return (
        readout,
        grad_in.astype(LOW).reshape(x_in.shape),
        pre_reduce_g,
        pre_conv_g,
        pre_expand_g,
        pre_gain_g,
        pre_shift_g,
        pre_og_g,
        pre_os_g,
        post_reduce_g,
        post_conv_g,
        post_expand_g,
        post_gain_g,
        post_shift_g,
        post_og_g,
        post_os_g,
        read_total,
        read_bias_g[0],
    )


def solution(mesh):
    images, strips = mesh.devices.shape
    split = jax.sharding.Mesh(
        mesh.devices.reshape(images // 2, 2, strips), ("im", "half", "row")
    )
    return jax.shard_map(
        shards,
        mesh=split,
        in_specs=(P(IMG, "row", None, None),)
        + (P(),) * 14
        + (P(None, "row"), P("row"), P(IMG, None, None, "row")),
        out_specs=(P(IMG, None, None, "row"), P(IMG, "row", None, None))
        + (P(),) * 14
        + (P(None, "row"), P("row")),
        check_vma=False,
    )
```

```python
import functools

import jax
import jax.numpy as jnp
from jax import lax
from jax.experimental import pallas as pl
from jax.experimental.pallas import tpu as pltpu
from jax.sharding import PartitionSpec as P

EPSILON = 1e-06
SQRT_HALF = 0.7071067811865476
INV_SQRT_TWO_PI = 0.3989422804014327
LOW = jnp.bfloat16
FULL = jnp.float32
IMG = ("im", "half")
TILE = 256
SLAB = 16
LANES = 128
VMEM_BYTES = 20 * 1024 * 1024


def tie(*values):
    return lax.optimization_barrier(values)


def norm(value):
    centred = value - jnp.mean(value, axis=-1, keepdims=True)
    factor = lax.rsqrt(jnp.mean(centred * centred, axis=-1, keepdims=True) + EPSILON)
    return (centred * factor, factor)


def norm_back(grad, normed, factor, gain):
    scaled = grad * gain
    return factor * (
        scaled
        - jnp.mean(scaled, axis=-1, keepdims=True)
        - normed * jnp.mean(scaled * normed, axis=-1, keepdims=True)
    )


def gate(value):
    return 0.5 * jnp.tanh(0.5 * value) + 0.5


def silu(value):
    return value * gate(value)


def silu_back(grad, value):
    sigma = gate(value)
    return grad * sigma * (1.0 + value * (1.0 - sigma))


def wide(factor):
    return jnp.broadcast_to(factor, (factor.shape[0], LANES))


def fold(value):
    return jnp.sum(value.reshape(-1, 8, value.shape[-1]), axis=0)


def live(rows, cols):
    at = lax.broadcasted_iota(jnp.int32, (rows, 1), 0)
    return lax.rem(at, SLAB) < cols


def from_left(value):
    at = lax.broadcasted_iota(jnp.int32, (value.shape[0], 1), 0)
    return jnp.where(at == 0, 0.0, pltpu.roll(value, 1, 0))


def from_right(value):
    last = value.shape[0] - 1
    at = lax.broadcasted_iota(jnp.int32, (value.shape[0], 1), 0)
    return jnp.where(at == last, 0.0, pltpu.roll(value, last, 0))


def matmul(left_ref, right_ref, out_ref):
    @pl.loop(0, right_ref.shape[1] // TILE)
    def _(at):
        cols = pl.ds(pl.multiple_of(at * TILE, TILE), TILE)
        out_ref[:, cols] = jnp.dot(
            left_ref[...], right_ref[:, cols], preferred_element_type=FULL
        )


def matmul_back(left_ref, right_ref, out_ref):
    @pl.loop(0, right_ref.shape[0] // TILE)
    def _(at):
        cols = pl.ds(pl.multiple_of(at * TILE, TILE), TILE)
        out_ref[:, cols] = lax.dot_general(
            left_ref[...],
            right_ref[cols, :],
            (((1,), (1,)), ((), ())),
            preferred_element_type=FULL,
        ).astype(out_ref.dtype)


def rows_of(at, size):
    return pl.ds(pl.multiple_of(at * size, SLAB), size)


def fill_halo(at_ref, pad_ref, low_ref, got_a_ref, got_b_ref):
    count, rows, cols, width = pad_ref.shape
    rows = rows - 2
    even = lax.rem(at_ref[2], 2) == 0
    for image in range(count):
        got_a, got_b = (got_a_ref[image].astype(FULL), got_b_ref[image].astype(FULL))
        pad_ref[image, 0] = jnp.where(even, got_b, got_a)
        pad_ref[image, rows + 1] = jnp.where(even, got_a, got_b)

    size = cols if cols % SLAB == 0 else 2 * cols
    per = size // cols
    each = rows // per

    @pl.loop(0, count * each)
    def _(at):
        part = low_ref[rows_of(at, size), :].astype(FULL).reshape(per, cols, width)
        pad_ref[at // each, pl.ds(1 + per * lax.rem(at, each), per)] = part


def set_edges(at_ref, edge_a_ref, edge_b_ref, image, head, tail):
    even = lax.rem(at_ref[2], 2) == 0
    edge_a_ref[image] = jnp.where(even, tail, head).astype(LOW)
    edge_b_ref[image] = jnp.where(even, head, tail).astype(LOW)


def conv_row(pad_ref, taps, image, row):
    lines = [pad_ref[image, row + top] for top in range(3)]
    sums = [
        lines[0] * taps[left] + lines[1] * taps[3 + left] + lines[2] * taps[6 + left]
        for left in range(3)
    ]
    return from_left(sums[0]) + sums[1] + from_right(sums[2])


def conv_back_row(pad_ref, grad_ref, taps, taps_ref, image, row):
    lines = [grad_ref[image, row + top] for top in range(3)]
    sums = [
        lines[2] * taps[left] + lines[1] * taps[3 + left] + lines[0] * taps[6 + left]
        for left in range(3)
    ]
    shifted = [from_right(lines[1]), lines[1], from_left(lines[1])]
    for top in range(3):
        source = pad_ref[image, row + top]
        for left in range(3):
            taps_ref[3 * top + left] += fold(source * shifted[left])
    return from_right(sums[0]) + sums[1] + from_left(sums[2])


def narrow(pair, value):
    side = value.shape[0]
    parts = []
    for at in range(value.shape[1] // LANES):
        pair[pl.ds(at * side, side), :] = value[:, at * LANES : (at + 1) * LANES]
        parts.append(
            pair[pl.ds(at * side, side // 2, stride=2), :]
            + pair[pl.ds(at * side + 1, side // 2, stride=2), :]
        )
    return jnp.concatenate(parts, axis=1)


def widen(pair, value):
    cols = value.shape[0]
    parts = []
    for at in range(value.shape[1] // LANES):
        part = value[:, at * LANES : (at + 1) * LANES]
        pair[pl.ds(2 * cols * at, cols, stride=2), :] = part
        pair[pl.ds(2 * cols * at + 1, cols, stride=2), :] = part
        parts.append(pair[pl.ds(2 * cols * at, 2 * cols), :])
    return jnp.concatenate(parts, axis=1)


def tap_rows(conv_ref):
    lines = [conv_ref[top].astype(FULL) for top in range(3)]
    return [lines[at // 3][at % 3 : at % 3 + 1] for at in range(9)]


def finish(small_ref, sums_ref, at, place):
    small_ref[pl.ds(place, 1), :] = jnp.sum(sums_ref[at], axis=0, keepdims=True)


def pre_reduce_kernel(
    at_ref,
    x_ref, w_ref, gain_ref, shift_ref, first_ref, edge_a_ref, edge_b_ref, normed_ref, factor_ref, red
):
    count, side, width = edge_a_ref.shape
    size = 2 * side
    steps = x_ref.shape[0] // size
    matmul(x_ref, w_ref, red)
    gain, shift = (gain_ref[pl.ds(0, 1), :], shift_ref[pl.ds(0, 1), :])

    @pl.loop(0, steps)
    def _(at):
        rows = rows_of(at, size)
        normed, factor = norm(red[rows, :])
        normed_ref[rows, :] = normed
        factor_ref[rows, :] = wide(factor)
        first_ref[rows, :] = silu(normed * gain + shift).astype(LOW)

    each = steps // count
    for image in range(count):
        head = first_ref[pl.ds(image * each * size, size), :].astype(FULL)
        tail = first_ref[pl.ds((image * each + each - 1) * size, size), :].astype(FULL)
        set_edges(at_ref, edge_a_ref, edge_b_ref, image, head[:side], tail[side:])


def pre_rest_kernel(
    at_ref,
    x_ref,
    first_ref,
    before_ref,
    after_ref,
    conv_ref,
    expand_ref,
    gain_ref,
    shift_ref,
    out_gain_ref,
    out_shift_ref,
    reduce_ref,
    post_gain_ref,
    post_shift_ref,
    second_ref,
    normed_b_ref,
    factor_b_ref,
    normed_c_ref,
    factor_c_ref,
    summed_ref,
    pooled_ref,
    pooled_low_ref,
    post_first_ref,
    edge_a_ref,
    edge_b_ref,
    post_normed_ref,
    post_factor_ref,
    pad,
    exp,
    pair,
    red,
):
    count, strip, side, width = pad.shape
    strip = strip - 2
    size = 2 * side
    each = strip // 2
    fill_halo(at_ref, pad, first_ref, before_ref, after_ref)
    taps = tap_rows(conv_ref)
    gain, shift = (gain_ref[pl.ds(1, 1), :], shift_ref[pl.ds(1, 1), :])

    @pl.loop(0, count * each)
    def _(at):
        rows = rows_of(at, size)
        image, row = (at // each, 2 * lax.rem(at, each))
        conv = jnp.concatenate(
            [conv_row(pad, taps, image, row), conv_row(pad, taps, image, row + 1)], axis=0
        )
        normed, factor = norm(conv)
        normed_b_ref[rows, :] = normed
        factor_b_ref[rows, :] = wide(factor)
        second_ref[rows, :] = silu(normed * gain + shift).astype(LOW)

    matmul(second_ref, expand_ref, exp)
    out_gain, out_shift = (out_gain_ref[...], out_shift_ref[...])
    cols = side // 2
    for at in range(count * each):
        rows = pl.ds(at * size, size)
        normed, factor = norm(exp[rows, :])
        normed_c_ref[rows, :] = normed
        factor_c_ref[rows, :] = wide(factor)
        summed = x_ref[rows, :].astype(FULL) + normed * out_gain + out_shift
        summed_ref[rows, :] = summed
        block = silu(summed)
        half = narrow(pair, block[:side] + block[side:])
        pooled_ref[pl.ds(at * SLAB, cols), :] = 0.25 * half
        pooled_ref[pl.ds(at * SLAB + cols, SLAB - cols), :] = jnp.zeros(
            (SLAB - cols, width), FULL
        )
    pooled_low_ref[...] = pooled_ref[...].astype(LOW)
    matmul(pooled_low_ref, reduce_ref, red)
    normed, factor = norm(red[...])
    post_normed_ref[...] = normed
    post_factor_ref[...] = wide(factor)
    first = silu(normed * post_gain_ref[pl.ds(0, 1), :] + post_shift_ref[pl.ds(0, 1), :])
    post_first_ref[...] = jnp.where(live(red.shape[0], cols), first, 0.0).astype(LOW)
    for image in range(count):
        head = post_first_ref[pl.ds(image * each * SLAB, SLAB), :].astype(FULL)
        tail = post_first_ref[pl.ds((image * each + each - 1) * SLAB, SLAB), :].astype(FULL)
        set_edges(at_ref, edge_a_ref, edge_b_ref, image, head, tail)


def post_rest_kernel(
    at_ref,
    pooled_ref,
    first_ref,
    before_ref,
    after_ref,
    conv_ref,
    expand_ref,
    gain_ref,
    shift_ref,
    out_gain_ref,
    out_shift_ref,
    block_ref,
    second_ref,
    normed_b_ref,
    factor_b_ref,
    normed_c_ref,
    factor_c_ref,
    summed_ref,
    pad,
    exp,
    compact,
    *,
    cols
):
    count, rows, _, width = pad.shape
    rows = rows - 2
    fill_halo(at_ref, pad, first_ref, before_ref, after_ref)
    taps = tap_rows(conv_ref)
    gain, shift = (gain_ref[pl.ds(1, 1), :], shift_ref[pl.ds(1, 1), :])

    @pl.loop(0, count * rows)
    def _(at):
        place = rows_of(at, SLAB)
        normed, factor = norm(conv_row(pad, taps, at // rows, lax.rem(at, rows)))
        normed_b_ref[place, :] = normed
        factor_b_ref[place, :] = wide(factor)
        second_ref[place, :] = silu(normed * gain + shift).astype(LOW)

    matmul(second_ref, expand_ref, exp)
    normed, factor = norm(exp[...])
    normed_c_ref[...] = normed
    factor_c_ref[...] = wide(factor)
    summed = pooled_ref[...] + normed * out_gain_ref[...] + out_shift_ref[...]
    summed_ref[...] = summed
    exp[...] = silu(summed)
    for at in range(count * rows):
        compact[pl.ds(at * cols, cols), :] = exp[pl.ds(at * SLAB, cols), :]
    block_ref[...] = compact[...].astype(LOW)


def readout_kernel(
    whole_ref,
    w_ref,
    bias_ref,
    cot_ref,
    out_ref,
    grad_ref,
    terms_ref,
    bias_grad_ref,
    cot,
    out,
    *,
    strips
):
    images, lines, cols, _ = cot_ref.shape
    rows = lines // strips
    for at in range(images * lines):
        strip, image, row = (at // (images * rows), at // rows % images, at % rows)
        cot[pl.ds(at * cols, cols), :] = cot_ref[image, strip * rows + row].astype(FULL)

    @pl.loop(0, w_ref.shape[1] // TILE)
    def _(at):
        lanes = pl.ds(pl.multiple_of(at * TILE, TILE), TILE)
        act = jnp.dot(whole_ref[...], w_ref[:, lanes], preferred_element_type=FULL)
        act = act + bias_ref[:, lanes]
        cdf = 0.5 * (1.0 + lax.erf(act * SQRT_HALF))
        density = jnp.exp(-0.5 * act * act) * INV_SQRT_TWO_PI
        out[:, lanes] = act * cdf
        grad = (cot[:, lanes] * (cdf + act * density)).astype(LOW)
        grad_ref[:, lanes] = grad
        bias_grad_ref[:, lanes] = jnp.sum(grad.astype(FULL), axis=0, keepdims=True)

    matmul_back(grad_ref, w_ref, terms_ref)
    for at in range(images * lines):
        strip, image, row = (at // (images * rows), at // rows % images, at % rows)
        out_ref[image, strip * rows + row] = out[pl.ds(at * cols, cols), :].astype(LOW)


def post_back_kernel(
    at_ref,
    pieces_ref,
    expand_ref,
    gain_ref,
    shift_ref,
    out_gain_ref,
    normed_b_ref,
    factor_b_ref,
    normed_c_ref,
    factor_c_ref,
    summed_ref,
    grad_sum_ref,
    grad_exp_ref,
    grad_conv_ref,
    edge_a_ref,
    edge_b_ref,
    small_ref,
    compact,
    spread_out,
    sec,
    *,
    cols
):
    count = edge_a_ref.shape[0]
    tokens, width = grad_sum_ref.shape
    each = tokens // SLAB // count
    total = pieces_ref[0].astype(FULL)
    for at in range(1, pieces_ref.shape[0]):
        total = total + pieces_ref[at].astype(FULL)
    compact[...] = total
    spread_out[...] = jnp.zeros((tokens, width), FULL)
    for at in range(tokens // SLAB):
        spread_out[pl.ds(at * SLAB, cols), :] = compact[pl.ds(at * cols, cols), :]
    grad_sum = silu_back(spread_out[...], summed_ref[...])
    grad_sum_ref[...] = grad_sum
    normed = normed_c_ref[...]
    grad_exp_ref[...] = norm_back(grad_sum, normed, factor_c_ref[:, :1], out_gain_ref[...]).astype(
        LOW
    )
    small_ref[pl.ds(2, 1), :] = jnp.sum(grad_sum * normed, axis=0, keepdims=True)
    small_ref[pl.ds(3, 1), :] = jnp.sum(grad_sum, axis=0, keepdims=True)
    matmul_back(grad_exp_ref, expand_ref, sec)
    gain, shift = (gain_ref[pl.ds(1, 1), :], shift_ref[pl.ds(1, 1), :])
    normed = normed_b_ref[...]
    grad = silu_back(sec[...], normed * gain + shift)
    grad_conv_ref[...] = norm_back(grad, normed, factor_b_ref[:, :1], gain).astype(LOW)
    small_ref[pl.ds(0, 1), :] = jnp.sum(grad * normed, axis=0, keepdims=True)
    small_ref[pl.ds(1, 1), :] = jnp.sum(grad, axis=0, keepdims=True)
    for image in range(count):
        head = grad_conv_ref[pl.ds(image * each * SLAB, SLAB), :].astype(FULL)
        tail = grad_conv_ref[pl.ds((image * each + each - 1) * SLAB, SLAB), :].astype(FULL)
        set_edges(at_ref, edge_a_ref, edge_b_ref, image, head, tail)


def middle_back_kernel(
    at_ref,
    grad_conv_ref,
    before_ref,
    after_ref,
    first_ref,
    first_before_ref,
    first_after_ref,
    post_conv_ref,
    post_reduce_ref,
    post_gain_ref,
    post_shift_ref,
    post_normed_ref,
    post_factor_ref,
    post_grad_sum_ref,
    expand_ref,
    gain_ref,
    shift_ref,
    out_gain_ref,
    normed_b_ref,
    factor_b_ref,
    normed_c_ref,
    factor_c_ref,
    summed_ref,
    post_grad_red_ref,
    grad_sum_ref,
    grad_exp_ref,
    pre_grad_conv_ref,
    edge_a_ref,
    edge_b_ref,
    post_small_ref,
    small_ref,
    pad,
    grad_pad,
    taps_sum,
    grad_in,
    pair,
    sec,
    sums,
    *,
    cols
):
    count, side, width = edge_a_ref.shape
    fill_halo(at_ref, grad_pad, grad_conv_ref, before_ref, after_ref)
    fill_halo(at_ref, pad, first_ref, first_before_ref, first_after_ref)
    taps = tap_rows(post_conv_ref)
    taps_sum[...] = jnp.zeros_like(taps_sum)
    sums[...] = jnp.zeros_like(sums)
    gain, shift = (post_gain_ref[pl.ds(0, 1), :], post_shift_ref[pl.ds(0, 1), :])
    each = post_grad_sum_ref.shape[0] // SLAB // count

    @pl.loop(0, count * each)
    def _(at):
        place = rows_of(at, SLAB)
        grad = conv_back_row(pad, grad_pad, taps, taps_sum, at // each, lax.rem(at, each))
        normed = post_normed_ref[place, :]
        grad = jnp.where(live(SLAB, cols), silu_back(grad, normed * gain + shift), 0.0)
        sums[0] += fold(grad * normed)
        sums[1] += fold(grad)
        post_grad_red_ref[place, :] = norm_back(
            grad, normed, post_factor_ref[place, :1], gain
        ).astype(LOW)

    for at in range(9):
        finish(post_small_ref, taps_sum, at, at)
    finish(post_small_ref, sums, 0, 9)
    finish(post_small_ref, sums, 1, 10)
    matmul_back(post_grad_red_ref, post_reduce_ref, grad_in)
    sums[...] = jnp.zeros_like(sums)
    size = 2 * side
    out_gain = out_gain_ref[...]
    for at in range(count * each):
        rows = pl.ds(at * size, size)
        place = pl.ds(at * SLAB, cols)
        grad = 0.25 * (post_grad_sum_ref[place, :] + grad_in[place, :])
        grad = widen(pair, grad)
        grad = jnp.concatenate([grad, grad], axis=0)
        grad_sum = silu_back(grad, summed_ref[rows, :])
        grad_sum_ref[rows, :] = grad_sum
        normed = normed_c_ref[rows, :]
        sums[0] += fold(grad_sum * normed)
        sums[1] += fold(grad_sum)
        grad_exp_ref[rows, :] = norm_back(
            grad_sum, normed, factor_c_ref[rows, :1], out_gain
        ).astype(LOW)
    finish(small_ref, sums, 0, 2)
    finish(small_ref, sums, 1, 3)
    matmul_back(grad_exp_ref, expand_ref, sec)
    sums[...] = jnp.zeros_like(sums)
    gain_b, shift_b = (gain_ref[pl.ds(1, 1), :], shift_ref[pl.ds(1, 1), :])

    @pl.loop(0, count * each)
    def _(at):
        rows = rows_of(at, size)
        normed = normed_b_ref[rows, :]
        grad = silu_back(sec[rows, :], normed * gain_b + shift_b)
        sums[0] += fold(grad * normed)
        sums[1] += fold(grad)
        pre_grad_conv_ref[rows, :] = norm_back(
            grad, normed, factor_b_ref[rows, :1], gain_b
        ).astype(LOW)

    finish(small_ref, sums, 0, 0)
    finish(small_ref, sums, 1, 1)
    for image in range(count):
        head = pre_grad_conv_ref[pl.ds(image * each * size, size), :].astype(FULL)
        tail = pre_grad_conv_ref[pl.ds((image * each + each - 1) * size, size), :].astype(FULL)
        set_edges(at_ref, edge_a_ref, edge_b_ref, image, head[:side], tail[side:])


def pre_back_kernel(
    at_ref,
    grad_conv_ref,
    before_ref,
    after_ref,
    first_ref,
    first_before_ref,
    first_after_ref,
    conv_ref,
    gain_ref,
    shift_ref,
    normed_ref,
    factor_ref,
    grad_red_ref,
    small_ref,
    pad,
    grad_pad,
    taps_sum,
    sums,
):
    count, strip, side, width = pad.shape
    strip = strip - 2
    size = 2 * side
    each = strip // 2
    fill_halo(at_ref, grad_pad, grad_conv_ref, before_ref, after_ref)
    fill_halo(at_ref, pad, first_ref, first_before_ref, first_after_ref)
    taps = tap_rows(conv_ref)
    taps_sum[...] = jnp.zeros_like(taps_sum)
    sums[...] = jnp.zeros_like(sums)
    gain, shift = (gain_ref[pl.ds(0, 1), :], shift_ref[pl.ds(0, 1), :])

    @pl.loop(0, count * each)
    def _(at):
        rows = rows_of(at, size)
        image, row = (at // each, 2 * lax.rem(at, each))
        grad = jnp.concatenate(
            [
                conv_back_row(pad, grad_pad, taps, taps_sum, image, row),
                conv_back_row(pad, grad_pad, taps, taps_sum, image, row + 1),
            ],
            axis=0,
        )
        normed = normed_ref[rows, :]
        grad = silu_back(grad, normed * gain + shift)
        sums[0] += fold(grad * normed)
        sums[1] += fold(grad)
        grad_red_ref[rows, :] = norm_back(grad, normed, factor_ref[rows, :1], gain).astype(LOW)

    for at in range(9):
        finish(small_ref, taps_sum, at, at)
    finish(small_ref, sums, 0, 9)
    finish(small_ref, sums, 1, 10)


def pair_outer_kernel(at_ref, *refs, pairs, parts):
    takes = 4 * pairs
    outs = refs[takes:]
    half, plane = (at_ref[0], at_ref[1])
    rows = outs[0].shape[0] // pairs
    for pair in range(pairs):
        left, left_far, right, right_far = refs[4 * pair : 4 * pair + 4]
        for step in range(parts):
            begin = half * (rows * parts) + jnp.bitwise_xor(plane, step) * rows
            lanes = pl.ds(pl.multiple_of(begin, LANES), rows)
            total = lax.dot_general(
                left[:, lanes], right[...], (((0,), (0,)), ((), ())), preferred_element_type=FULL
            ) + lax.dot_general(
                left_far[:, lanes],
                right_far[...],
                (((0,), (0,)), ((), ())),
                preferred_element_type=FULL,
            )
            outs[step][pl.ds(pair * rows, rows), :] = total.astype(LOW)


def sum_split_kernel(at_ref, *refs, pairs, parts, pieces):
    takes, outs = (refs[:pieces], refs[pieces : pieces + parts])
    total = refs[-1]
    value = takes[0][...].astype(FULL)
    for at in range(1, pieces):
        value = value + takes[at][...].astype(FULL)
    total[...] = value
    rows = total.shape[0] // pairs // parts
    for step in range(parts):
        begin = jnp.bitwise_xor(at_ref[2], step) * rows
        for pair in range(pairs):
            place = pl.ds(pl.multiple_of(pair * rows * parts + begin, SLAB), rows)
            outs[step][pl.ds(pair * rows, rows), :] = total[place, :].astype(LOW)


def assemble_kernel(at_ref, *refs, pairs, planes, strips):
    takes = 2 * planes
    parts, outs = (refs[:takes], refs[takes : takes + pairs])
    half, plane, row = (at_ref[0], at_ref[1], at_ref[2])
    rows = parts[0].shape[0] // pairs // strips
    block = rows * strips
    for at in range(takes):
        side = jnp.bitwise_xor(half, at // planes)
        begin = side * (planes * block) + jnp.bitwise_xor(plane, at % planes) * block
        for pair in range(pairs):
            for step in range(strips):
                place = begin + jnp.bitwise_xor(row, step) * rows
                outs[pair][pl.ds(pl.multiple_of(place, SLAB), rows), :] = parts[at][
                    pl.ds((step * pairs + pair) * rows, rows), :
                ].astype(FULL)


def assemble(index, parts, pairs, planes, strips):
    width = parts[0].shape[1]
    out = like(2 * planes * parts[0].shape[0] // pairs, width)
    return call(
        functools.partial(assemble_kernel, pairs=pairs, planes=planes, strips=strips),
        [out] * pairs,
        [],
        0,
        *parts,
        index=index,
    )


def like(*shape, dtype=FULL):
    return jax.ShapeDtypeStruct(shape, dtype)


def call(kernel, outs, scratch, flops, *args, index=None):
    moved = sum(arg.size * arg.dtype.itemsize for arg in args)
    moved += sum(out.size * out.dtype.itemsize for out in outs)
    near = pl.BlockSpec(memory_space=pltpu.VMEM)
    head = [] if index is None else [pl.BlockSpec(memory_space=pltpu.SMEM)]
    lead_args = [] if index is None else [index]
    return pl.pallas_call(
        kernel,
        out_shape=outs,
        in_specs=head + [near] * len(args),
        out_specs=[near] * len(outs),
        scratch_shapes=[pltpu.VMEM(shape, FULL) for shape in scratch],
        compiler_params=pltpu.CompilerParams(vmem_limit_bytes=VMEM_BYTES),
        cost_estimate=pl.CostEstimate(flops=flops, bytes_accessed=moved, transcendentals=0),
    )(*lead_args, *args)


def edges(parity_edges):
    size = lax.axis_size("row")
    inner = [(at, at ^ 1) for at in range(size)]
    outer = [(at, at + 1) for at in range(1, size - 1, 2)]
    outer = outer + [(to, at) for at, to in outer]
    return (
        lax.ppermute(parity_edges[0], "row", inner),
        lax.ppermute(parity_edges[1], "row", outer),
    )


def swap(field):
    return lax.ppermute(field, "half", [(0, 1), (1, 0)])


def exchange(pieces, axis):
    return lax.all_to_all(pieces, axis, 0, 0, tiled=True)


def steps_of(value, axis, step):
    size = lax.axis_size(axis)
    return lax.ppermute(value, axis, [(at, at ^ step) for at in range(size)])


def share(parts, axis):
    return [parts[0]] + [steps_of(parts[at], axis, at) for at in range(1, len(parts))]


def share_same(part, axis):
    size = lax.axis_size(axis)
    return [part] + [steps_of(part, axis, at) for at in range(1, size)]


def call_list(*args, **named):
    return list(call(*args, **named))


def pair_outer(index, pairs):
    size = lax.axis_size("im")
    rows = pairs[0][0].shape[1] // 2 // size * len(pairs)
    width = pairs[0][2].shape[1]
    flops = sum(2 * pair[0].shape[0] * rows * size * width for pair in pairs)
    return call_list(
        functools.partial(pair_outer_kernel, pairs=len(pairs), parts=size),
        [like(rows, width, dtype=LOW)] * size,
        [],
        2 * flops,
        *[ref for pair in pairs for ref in pair],
        index=index,
    )


def sum_split(index, pieces, pairs):
    size = lax.axis_size("row")
    rows, width = pieces[0].shape
    return call_list(
        functools.partial(
            sum_split_kernel, pairs=pairs, parts=size, pieces=len(pieces)
        ),
        [like(rows // size, width, dtype=LOW)] * size,
        [(rows, width)],
        0,
        *pieces,
        index=index,
    )


def add_low(pieces):
    total = pieces[0].astype(FULL)
    for piece in pieces[1:]:
        total = total + piece.astype(FULL)
    return total.astype(LOW)


def sum_far(left, right, axes):
    part = jnp.einsum("tm,tc->mc", left, right, preferred_element_type=FULL)
    return lax.psum(part, axes)


def shards(
    x_in,
    pre_reduce,
    pre_conv,
    pre_expand,
    pre_mid_gain,
    pre_mid_shift,
    pre_out_gain,
    pre_out_shift,
    post_reduce,
    post_conv,
    post_expand,
    post_mid_gain,
    post_mid_shift,
    post_out_gain,
    post_out_shift,
    read_weight,
    read_bias,
    cotangent,
):
    count, strip, side, width = x_in.shape
    strips = lax.axis_size("row")
    tokens = count * strip * side
    cols = side // 2
    rows = strip // 2
    slabs = count * rows
    padded = slabs * SLAB
    small = slabs * cols
    features = read_weight.shape[1]
    cost = 2 * tokens * width * width
    post_cost = 2 * padded * width * width
    x_low = x_in.reshape(tokens, width)
    pre_out_g, pre_out_s = (pre_out_gain[None], pre_out_shift[None])
    post_out_g, post_out_s = (post_out_gain[None], post_out_shift[None])
    index = jnp.stack([lax.axis_index("half"), lax.axis_index("im"), lax.axis_index("row")])
    quick = lax.axis_size("im") == 4 and strips == 4
    if quick:
        x_far = swap(x_low)

    first, top, bottom, normed_a, factor_a = call(
        pre_reduce_kernel,
        [
            like(tokens, width, dtype=LOW),
            like(count, side, width, dtype=LOW),
            like(count, side, width, dtype=LOW),
            like(tokens, width),
            like(tokens, LANES),
        ],
        [(tokens, width)],
        cost,
        x_low,
        pre_reduce,
        pre_mid_gain,
        pre_mid_shift,
        index=index,
    )
    before, after = edges((top, bottom))
    if quick:
        before, after, x_far = tie(before, after, x_far)
    (
        second,
        normed_b,
        factor_b,
        normed_c,
        factor_c,
        summed,
        pooled,
        pooled_low,
        post_first,
        post_top,
        post_bottom,
        post_normed_a,
        post_factor_a,
    ) = call(
        pre_rest_kernel,
        [
            like(tokens, width, dtype=LOW),
            like(tokens, width),
            like(tokens, LANES),
            like(tokens, width),
            like(tokens, LANES),
            like(tokens, width),
            like(padded, width),
            like(padded, width, dtype=LOW),
            like(padded, width, dtype=LOW),
            like(count, SLAB, width, dtype=LOW),
            like(count, SLAB, width, dtype=LOW),
            like(padded, width),
            like(padded, LANES),
        ],
        [
            (count, strip + 2, side, width),
            (tokens, width),
            (side * width // LANES, LANES),
            (padded, width),
        ],
        cost + post_cost,
        x_low,
        first,
        before,
        after,
        pre_conv,
        pre_expand,
        pre_mid_gain,
        pre_mid_shift,
        pre_out_g,
        pre_out_s,
        post_reduce,
        post_mid_gain,
        post_mid_shift,
        index=index,
    )
    post_before, post_after = edges((post_top, post_bottom))
    if quick:
        second_far = swap(second)
        post_before, post_after, second_far = tie(post_before, post_after, second_far)
    (
        block_two,
        post_second,
        post_normed_b,
        post_factor_b,
        post_normed_c,
        post_factor_c,
        post_summed,
    ) = call(
        functools.partial(post_rest_kernel, cols=cols),
        [
            like(small, width, dtype=LOW),
            like(padded, width, dtype=LOW),
            like(padded, width),
            like(padded, LANES),
            like(padded, width),
            like(padded, LANES),
            like(padded, width),
        ],
        [
            (count, rows + 2, SLAB, width),
            (padded, width),
            (small, width),
        ],
        post_cost,
        pooled,
        post_first,
        post_before,
        post_after,
        post_conv,
        post_expand,
        post_mid_gain,
        post_mid_shift,
        post_out_g,
        post_out_s,
        index=index,
    )
    whole = lax.all_gather(block_two, "row", axis=0, tiled=True)
    if quick:
        post_in_far = swap(pooled_low)
        post_second_far = swap(post_second)
        whole, post_in_far, post_second_far = tie(whole, post_in_far, post_second_far)
        whole_far = swap(whole)
    readout, grad_pre, terms, d_read_b = call(
        functools.partial(readout_kernel, strips=strips),
        [
            like(*cotangent.shape, dtype=LOW),
            like(strips * small, features, dtype=LOW),
            like(strips * small, width, dtype=LOW),
            like(1, features),
        ],
        [(strips * small, features), (strips * small, features)],
        2 * cost,
        whole,
        read_weight,
        read_bias[None],
        cotangent,
    )
    terms = exchange(terms.reshape(strips, small, width), "row")
    if quick:
        read_parts = pair_outer(index, [(whole, whole_far, grad_pre, swap(grad_pre))])
        terms, read_parts[0] = tie(terms, read_parts[0])
        read_part = add_low(share(read_parts, "im"))
    (
        post_gs,
        post_ge,
        post_gc,
        post_top,
        post_bottom,
        post_small_b,
    ) = call(
        functools.partial(post_back_kernel, cols=cols),
        [
            like(padded, width),
            like(padded, width, dtype=LOW),
            like(padded, width, dtype=LOW),
            like(count, SLAB, width, dtype=LOW),
            like(count, SLAB, width, dtype=LOW),
            like(4, width),
        ],
        [
            (small, width),
            (padded, width),
            (padded, width),
        ],
        post_cost,
        terms,
        post_expand,
        post_mid_gain,
        post_mid_shift,
        post_out_g,
        post_normed_b,
        post_factor_b,
        post_normed_c,
        post_factor_c,
        post_summed,
        index=index,
    )
    back_before, back_after = edges((post_top, post_bottom))
    if quick:
        post_ge_far = swap(post_ge)
        back_before, back_after, read_part, post_ge_far = tie(
            back_before, back_after, read_part, post_ge_far
        )
        read_total = lax.all_gather(read_part, ("half", "im"), axis=0, tiled=True)
    (
        post_gr,
        pre_gs,
        pre_ge,
        pre_gc,
        pre_top,
        pre_bottom,
        post_small_a,
        pre_small_b,
    ) = call(
        functools.partial(middle_back_kernel, cols=cols),
        [
            like(padded, width, dtype=LOW),
            like(tokens, width),
            like(tokens, width, dtype=LOW),
            like(tokens, width, dtype=LOW),
            like(count, side, width, dtype=LOW),
            like(count, side, width, dtype=LOW),
            like(11, width),
            like(4, width),
        ],
        [
            (count, rows + 2, SLAB, width),
            (count, rows + 2, SLAB, width),
            (9, 8, width),
            (padded, width),
            (side * width // LANES, LANES),
            (tokens, width),
            (2, 8, width),
        ],
        cost + post_cost,
        post_gc,
        back_before,
        back_after,
        post_first,
        post_before,
        post_after,
        post_conv,
        post_reduce,
        post_mid_gain,
        post_mid_shift,
        post_normed_a,
        post_factor_a,
        post_gs,
        pre_expand,
        pre_mid_gain,
        pre_mid_shift,
        pre_out_g,
        normed_b,
        factor_b,
        normed_c,
        factor_c,
        summed,
        index=index,
    )
    back_before, back_after = edges((pre_top, pre_bottom))
    if quick:
        post_parts = pair_outer(
            index,
            [
                (pooled_low, post_in_far, post_gr, swap(post_gr)),
                (post_second, post_second_far, post_ge, post_ge_far),
            ],
        )
        expand_parts = pair_outer(index, [(second, second_far, pre_ge, swap(pre_ge))])
        back_before, back_after, post_parts[0], expand_parts[0] = tie(
            back_before, back_after, post_parts[0], expand_parts[0]
        )
    pre_gr, pre_small_a = call(
        pre_back_kernel,
        [like(tokens, width, dtype=LOW), like(11, width)],
        [
            (count, strip + 2, side, width),
            (count, strip + 2, side, width),
            (9, 8, width),
            (2, 8, width),
        ],
        0,
        pre_gc,
        back_before,
        back_after,
        first,
        before,
        after,
        pre_conv,
        pre_mid_gain,
        pre_mid_shift,
        normed_a,
        factor_a,
        index=index,
    )
    sums = jnp.concatenate([pre_small_a, pre_small_b, post_small_a, post_small_b, d_read_b])
    if quick:
        far = swap(pre_gr)
        sums = sums + swap(sums)
        far, sums = tie(far, sums)
        reduce_parts = pair_outer(index, [(x_low, x_far, pre_gr, far)])
        post_parts = share(post_parts, "im")
        expand_parts = share(expand_parts, "im")
        reduce_parts[0], post_parts[0], expand_parts[0] = tie(
            reduce_parts[0], post_parts[0], expand_parts[0]
        )
        post_parts = sum_split(index, post_parts, 2)
        expand_parts = sum_split(index, expand_parts, 1)
        reduce_parts = share(reduce_parts, "im")
        sums = sums + steps_of(sums, "im", 1)
        sums, reduce_parts[0] = tie(sums, reduce_parts[0])
        reduce_parts = sum_split(index, reduce_parts, 1)
        sums = sums + steps_of(sums, "im", 2)
        reduce_parts = share(reduce_parts, "row")
        sums, reduce_parts[0] = tie(sums, reduce_parts[0])
        read_bias_g = sums[30]
        sums = sums + steps_of(sums, "row", 1)
        reduce_part = share_same(add_low(reduce_parts), "row")
        sums, reduce_part[0] = tie(sums, reduce_part[0])
        sums = sums + steps_of(sums, "row", 2)
        streams = []
        for pairs, part in (
            (2, share_same(add_low(share(post_parts, "row")), "row")),
            (1, share_same(add_low(share(expand_parts, "row")), "row")),
            (1, reduce_part),
        ):
            parts = share_same(jnp.concatenate(part, axis=0), "im")
            parts = parts + [swap(part) for part in parts]
            streams.append(assemble(index, parts, pairs, 4, strips))
        (post_reduce_g, post_expand_g), (pre_expand_g,), (pre_reduce_g,) = streams
        read_total = read_total.astype(FULL)
    else:
        axes = IMG + ("row",)
        post_reduce_g = sum_far(pooled_low, post_gr, axes)
        post_expand_g = sum_far(post_second, post_ge, axes)
        pre_expand_g = sum_far(second, pre_ge, axes)
        pre_reduce_g = sum_far(x_low, pre_gr, axes)
        read_total = sum_far(whole, grad_pre, IMG)
        read_bias_g = lax.psum(sums[30], IMG)
        sums = lax.psum(sums, axes)
    grad_in = pre_gs + jnp.einsum("tm,cm->tc", pre_gr, pre_reduce, preferred_element_type=FULL)

    def small_grads(part):
        return (
            part[:9].reshape(3, 3, width),
            jnp.stack([part[9], part[11]]),
            jnp.stack([part[10], part[12]]),
            part[13],
            part[14],
        )

    pre_conv_g, pre_gain_g, pre_shift_g, pre_og_g, pre_os_g = small_grads(sums[:15])
    post_conv_g, post_gain_g, post_shift_g, post_og_g, post_os_g = small_grads(sums[15:30])
    return (
        readout,
        grad_in.astype(LOW).reshape(x_in.shape),
        pre_reduce_g,
        pre_conv_g,
        pre_expand_g,
        pre_gain_g,
        pre_shift_g,
        pre_og_g,
        pre_os_g,
        post_reduce_g,
        post_conv_g,
        post_expand_g,
        post_gain_g,
        post_shift_g,
        post_og_g,
        post_os_g,
        read_total,
        read_bias_g,
    )


def solution(mesh):
    images, strips = mesh.devices.shape
    split = jax.sharding.Mesh(
        mesh.devices.reshape(images // 2, 2, strips), ("im", "half", "row")
    )
    return jax.shard_map(
        shards,
        mesh=split,
        in_specs=(P(IMG, "row", None, None),)
        + (P(),) * 14
        + (P(None, "row"), P("row"), P(IMG, None, None, "row")),
        out_specs=(P(IMG, None, None, "row"), P(IMG, "row", None, None))
        + (P(),) * 14
        + (P(None, "row"), P("row")),
        check_vma=False,
    )
```

```python
import functools

import jax
import jax.numpy as jnp
from jax import lax
from jax.experimental import pallas as pl
from jax.experimental.pallas import tpu as pltpu
from jax.sharding import PartitionSpec as P

EPSILON = 1e-06
SQRT_HALF = 0.7071067811865476
INV_SQRT_TWO_PI = 0.3989422804014327
LOW = jnp.bfloat16
FULL = jnp.float32
IMG = ("im", "half")
TILE = 256
SLAB = 16
LANES = 128
VMEM_BYTES = 40 * 1024 * 1024


def tie(*values):
    return lax.optimization_barrier(values)


def norm(value):
    centred = value - jnp.mean(value, axis=-1, keepdims=True)
    factor = lax.rsqrt(jnp.mean(centred * centred, axis=-1, keepdims=True) + EPSILON)
    return (centred * factor, factor)


def norm_back(grad, normed, factor, gain):
    scaled = grad * gain
    return factor * (
        scaled
        - jnp.mean(scaled, axis=-1, keepdims=True)
        - normed * jnp.mean(scaled * normed, axis=-1, keepdims=True)
    )


def gate(value):
    return 0.5 * jnp.tanh(0.5 * value) + 0.5


def silu(value):
    return value * gate(value)


def silu_back(grad, value):
    sigma = gate(value)
    return grad * sigma * (1.0 + value * (1.0 - sigma))


def wide(factor):
    return jnp.broadcast_to(factor, (factor.shape[0], LANES))


def fold(value):
    return jnp.sum(value.reshape(-1, 8, value.shape[-1]), axis=0)


def live(rows, cols):
    at = lax.broadcasted_iota(jnp.int32, (rows, 1), 0)
    return lax.rem(at, SLAB) < cols


def from_left(value):
    at = lax.broadcasted_iota(jnp.int32, (value.shape[0], 1), 0)
    return jnp.where(at == 0, 0.0, pltpu.roll(value, 1, 0))


def from_right(value):
    last = value.shape[0] - 1
    at = lax.broadcasted_iota(jnp.int32, (value.shape[0], 1), 0)
    return jnp.where(at == last, 0.0, pltpu.roll(value, last, 0))


def matmul(left_ref, right_ref, out_ref):
    @pl.loop(0, right_ref.shape[1] // TILE)
    def _(at):
        cols = pl.ds(pl.multiple_of(at * TILE, TILE), TILE)
        out_ref[:, cols] = jnp.dot(
            left_ref[...].astype(LOW), right_ref[:, cols], preferred_element_type=FULL
        )


def matmul_back(left_ref, right_ref, out_ref):
    @pl.loop(0, right_ref.shape[0] // TILE)
    def _(at):
        cols = pl.ds(pl.multiple_of(at * TILE, TILE), TILE)
        out_ref[:, cols] = lax.dot_general(
            left_ref[...].astype(LOW),
            right_ref[cols, :],
            (((1,), (1,)), ((), ())),
            preferred_element_type=FULL,
        ).astype(out_ref.dtype)


def rows_of(at, size):
    return pl.ds(pl.multiple_of(at * size, SLAB), size)


def fill_halo(at_ref, pad_ref, low_ref, got_a_ref, got_b_ref):
    count, rows, cols, width = pad_ref.shape
    rows = rows - 2
    even = lax.rem(at_ref[2], 2) == 0
    for image in range(count):
        got_a, got_b = (got_a_ref[image].astype(FULL), got_b_ref[image].astype(FULL))
        pad_ref[image, 0] = jnp.where(even, got_b, got_a)
        pad_ref[image, rows + 1] = jnp.where(even, got_a, got_b)

    size = cols if cols % SLAB == 0 else 2 * cols
    per = size // cols
    each = rows // per

    @pl.loop(0, count * each)
    def _(at):
        part = low_ref[rows_of(at, size), :].astype(FULL).reshape(per, cols, width)
        pad_ref[at // each, pl.ds(1 + per * lax.rem(at, each), per)] = part


def set_edges(at_ref, edge_a_ref, edge_b_ref, image, head, tail):
    even = lax.rem(at_ref[2], 2) == 0
    edge_a_ref[image] = jnp.where(even, tail, head).astype(LOW)
    edge_b_ref[image] = jnp.where(even, head, tail).astype(LOW)


def conv_row(pad_ref, taps, image, row):
    lines = [pad_ref[image, row + top] for top in range(3)]
    sums = [
        lines[0] * taps[left] + lines[1] * taps[3 + left] + lines[2] * taps[6 + left]
        for left in range(3)
    ]
    return from_left(sums[0]) + sums[1] + from_right(sums[2])


def conv_back_row(pad_ref, grad_ref, taps, taps_ref, image, row):
    lines = [grad_ref[image, row + top] for top in range(3)]
    sums = [
        lines[2] * taps[left] + lines[1] * taps[3 + left] + lines[0] * taps[6 + left]
        for left in range(3)
    ]
    shifted = [from_right(lines[1]), lines[1], from_left(lines[1])]
    for top in range(3):
        source = pad_ref[image, row + top]
        for left in range(3):
            taps_ref[3 * top + left] += fold(source * shifted[left])
    return from_right(sums[0]) + sums[1] + from_left(sums[2])


def pack(compact, source, out_ref, cols):
    compact[...] = jnp.zeros(compact.shape, FULL)
    for at in range(source.shape[0] // SLAB):
        compact[pl.ds(at * cols, cols), :] = source[pl.ds(at * SLAB, cols), :]
    out_ref[...] = compact[...].astype(LOW)


def narrow(pair, value):
    side = value.shape[0]
    parts = []
    for at in range(value.shape[1] // LANES):
        pair[pl.ds(at * side, side), :] = value[:, at * LANES : (at + 1) * LANES]
        parts.append(
            pair[pl.ds(at * side, side // 2, stride=2), :]
            + pair[pl.ds(at * side + 1, side // 2, stride=2), :]
        )
    return jnp.concatenate(parts, axis=1)


def widen(pair, value):
    cols = value.shape[0]
    parts = []
    for at in range(value.shape[1] // LANES):
        part = value[:, at * LANES : (at + 1) * LANES]
        pair[pl.ds(2 * cols * at, cols, stride=2), :] = part
        pair[pl.ds(2 * cols * at + 1, cols, stride=2), :] = part
        parts.append(pair[pl.ds(2 * cols * at, 2 * cols), :])
    return jnp.concatenate(parts, axis=1)


def tap_rows(conv_ref):
    lines = [conv_ref[top].astype(FULL) for top in range(3)]
    return [lines[at // 3][at % 3 : at % 3 + 1] for at in range(9)]


def finish(small_ref, sums_ref, at, place):
    small_ref[pl.ds(place, 1), :] = jnp.sum(sums_ref[at], axis=0, keepdims=True)


def pre_reduce_kernel(
    need,
    send,
    at_ref,
    x_ref, w_ref, gain_ref, shift_ref, first_ref, edge_a_ref, edge_b_ref, normed_ref, factor_ref, red
):
    count, side, width = edge_a_ref.shape
    size = 2 * side
    steps = x_ref.shape[0] // size
    need(x_ref, w_ref)
    matmul(x_ref, w_ref, red)
    need(gain_ref, shift_ref)
    gain, shift = (gain_ref[pl.ds(0, 1), :], shift_ref[pl.ds(0, 1), :])

    @pl.loop(0, steps)
    def _(at):
        rows = rows_of(at, size)
        normed, factor = norm(red[rows, :])
        normed_ref[rows, :] = normed
        factor_ref[rows, :] = wide(factor)
        first_ref[rows, :] = silu(normed * gain + shift).astype(LOW)

    each = steps // count
    for image in range(count):
        head = first_ref[pl.ds(image * each * size, size), :].astype(FULL)
        tail = first_ref[pl.ds((image * each + each - 1) * size, size), :].astype(FULL)
        set_edges(at_ref, edge_a_ref, edge_b_ref, image, head[:side], tail[side:])


def pre_rest_kernel(
    need,
    send,
    at_ref,
    x_ref,
    first_ref,
    got_a_ref,
    got_b_ref,
    conv_ref,
    expand_ref,
    gain_ref,
    shift_ref,
    out_gain_ref,
    out_shift_ref,
    reduce_ref,
    post_gain_ref,
    post_shift_ref,
    second_ref,
    normed_b_ref,
    factor_b_ref,
    normed_c_ref,
    factor_c_ref,
    summed_ref,
    pooled_ref,
    post_first_ref,
    edge_a_ref,
    edge_b_ref,
    post_normed_ref,
    post_factor_ref,
    pad,
    exp,
    pair,
    red,
):
    count, strip, side, width = pad.shape
    strip = strip - 2
    size = 2 * side
    each = strip // 2
    need(first_ref, got_a_ref, got_b_ref)
    fill_halo(at_ref, pad, first_ref, got_a_ref, got_b_ref)
    need(conv_ref, gain_ref, shift_ref)
    send(pad)
    taps = tap_rows(conv_ref)
    gain, shift = (gain_ref[pl.ds(1, 1), :], shift_ref[pl.ds(1, 1), :])

    @pl.loop(0, count * each)
    def _(at):
        rows = rows_of(at, size)
        image, row = (at // each, 2 * lax.rem(at, each))
        conv = jnp.concatenate(
            [conv_row(pad, taps, image, row), conv_row(pad, taps, image, row + 1)], axis=0
        )
        normed, factor = norm(conv)
        normed_b_ref[rows, :] = normed
        factor_b_ref[rows, :] = wide(factor)
        second_ref[rows, :] = silu(normed * gain + shift).astype(LOW)

    send(second_ref, normed_b_ref, factor_b_ref)
    need(expand_ref)
    matmul(second_ref, expand_ref, exp)
    need(x_ref, out_gain_ref, out_shift_ref)
    out_gain, out_shift = (out_gain_ref[...], out_shift_ref[...])
    cols = side // 2
    for at in range(count * each):
        rows = pl.ds(at * size, size)
        normed, factor = norm(exp[rows, :])
        normed_c_ref[rows, :] = normed
        factor_c_ref[rows, :] = wide(factor)
        summed = x_ref[rows, :].astype(FULL) + normed * out_gain + out_shift
        summed_ref[rows, :] = summed
        block = silu(summed)
        half = narrow(pair, block[:side] + block[side:])
        pooled_ref[pl.ds(at * SLAB, cols), :] = 0.25 * half
        pooled_ref[pl.ds(at * SLAB + cols, SLAB - cols), :] = jnp.zeros(
            (SLAB - cols, width), FULL
        )
    send(normed_c_ref, factor_c_ref, summed_ref)
    need(reduce_ref, post_gain_ref, post_shift_ref)
    matmul(pooled_ref, reduce_ref, red)
    normed, factor = norm(red[...])
    post_normed_ref[...] = normed
    post_factor_ref[...] = wide(factor)
    first = silu(normed * post_gain_ref[pl.ds(0, 1), :] + post_shift_ref[pl.ds(0, 1), :])
    post_first_ref[...] = jnp.where(live(red.shape[0], cols), first, 0.0).astype(LOW)
    for image in range(count):
        head = post_first_ref[pl.ds(image * each * SLAB, SLAB), :].astype(FULL)
        tail = post_first_ref[pl.ds((image * each + each - 1) * SLAB, SLAB), :].astype(FULL)
        set_edges(at_ref, edge_a_ref, edge_b_ref, image, head, tail)


def post_rest_kernel(
    need,
    send,
    at_ref,
    pooled_ref,
    first_ref,
    got_a_ref,
    got_b_ref,
    conv_ref,
    expand_ref,
    gain_ref,
    shift_ref,
    out_gain_ref,
    out_shift_ref,
    block_ref,
    lefts_ref,
    *refs,
    cols,
    strips
):
    slots, refs = (refs[:strips], refs[strips:])
    (
        normed_b_ref,
        factor_b_ref,
        normed_c_ref,
        factor_c_ref,
        summed_ref,
        pad,
        second,
        exp,
        compact,
    ) = refs
    count, rows, _, width = pad.shape
    rows = rows - 2
    small = block_ref.shape[0]
    need(first_ref, got_a_ref, got_b_ref)
    fill_halo(at_ref, pad, first_ref, got_a_ref, got_b_ref)
    send(pad)
    need(conv_ref, gain_ref, shift_ref, pooled_ref)
    taps = tap_rows(conv_ref)
    gain, shift = (gain_ref[pl.ds(1, 1), :], shift_ref[pl.ds(1, 1), :])

    @pl.loop(0, count * rows)
    def _(at):
        place = rows_of(at, SLAB)
        normed, factor = norm(conv_row(pad, taps, at // rows, lax.rem(at, rows)))
        normed_b_ref[place, :] = normed
        factor_b_ref[place, :] = wide(factor)
        second[place, :] = silu(normed * gain + shift)

    send(normed_b_ref, factor_b_ref)
    need(expand_ref)
    matmul(second, expand_ref, exp)
    need(out_gain_ref, out_shift_ref)
    normed, factor = norm(exp[...])
    normed_c_ref[...] = normed
    factor_c_ref[...] = wide(factor)
    summed = pooled_ref[...] + normed * out_gain_ref[...] + out_shift_ref[...]
    summed_ref[...] = summed
    exp[...] = silu(summed)
    compact[...] = jnp.zeros(compact.shape, FULL)
    for at in range(count * rows):
        compact[pl.ds(at * cols, cols), :] = exp[pl.ds(at * SLAB, cols), :]
    block_ref[...] = compact[pl.ds(0, small), :].astype(LOW)
    send(block_ref, normed_c_ref, factor_c_ref, summed_ref)
    half = compact.shape[0]
    for place, source in enumerate((pooled_ref, second)):
        for at in range(count * rows):
            compact[pl.ds(at * cols, cols), :] = source[pl.ds(at * SLAB, cols), :]
        lefts_ref[pl.ds(place * half, half), :] = compact[...].astype(LOW)
    each = width // strips
    for step in range(strips):
        begin = jnp.bitwise_xor(at_ref[2], step) * each
        slots[step][...] = lefts_ref[:, pl.ds(pl.multiple_of(begin, LANES), each)]


def readout_kernel(
    need,
    send,
    at_ref,
    whole_ref,
    w_ref,
    bias_ref,
    cot_ref,
    out_ref,
    grad_ref,
    terms_ref,
    bias_grad_ref,
    cot,
    out,
    *,
    strips
):
    images, lines, cols, _ = cot_ref.shape
    rows = lines // strips
    need(cot_ref)
    for at in range(images * lines):
        strip, image, row = (at // (images * rows), at // rows % images, at % rows)
        cot[pl.ds(at * cols, cols), :] = cot_ref[image, strip * rows + row].astype(FULL)
    need(whole_ref, w_ref, bias_ref)

    @pl.loop(0, w_ref.shape[1] // TILE)
    def _(at):
        lanes = pl.ds(pl.multiple_of(at * TILE, TILE), TILE)
        act = jnp.dot(whole_ref[...], w_ref[:, lanes], preferred_element_type=FULL)
        act = act + bias_ref[:, lanes]
        cdf = 0.5 * (1.0 + lax.erf(act * SQRT_HALF))
        density = jnp.exp(-0.5 * act * act) * INV_SQRT_TWO_PI
        out[:, lanes] = act * cdf
        grad = (cot[:, lanes] * (cdf + act * density)).astype(LOW)
        grad_ref[:, lanes] = grad
        bias_grad_ref[:, lanes] = jnp.sum(grad.astype(FULL), axis=0, keepdims=True)

    send(grad_ref, bias_grad_ref)
    matmul_back(grad_ref, w_ref, terms_ref)
    send(terms_ref)
    for at in range(images * lines):
        strip, image, row = (at // (images * rows), at // rows % images, at % rows)
        out_ref[image, strip * rows + row] = out[pl.ds(at * cols, cols), :].astype(LOW)


def post_back_kernel(
    need,
    send,
    at_ref,
    pieces_ref,
    expand_ref,
    gain_ref,
    shift_ref,
    out_gain_ref,
    normed_b_ref,
    factor_b_ref,
    normed_c_ref,
    factor_c_ref,
    summed_ref,
    grad_sum_ref,
    grad_exp_ref,
    grad_conv_ref,
    edge_a_ref,
    edge_b_ref,
    small_ref,
    compact,
    spread_out,
    exp,
    sec,
    *,
    cols
):
    count = edge_a_ref.shape[0]
    tokens, width = grad_sum_ref.shape
    each = tokens // SLAB // count
    need(pieces_ref)
    total = pieces_ref[0].astype(FULL)
    for at in range(1, pieces_ref.shape[0]):
        total = total + pieces_ref[at].astype(FULL)
    compact[...] = jnp.zeros(compact.shape, FULL)
    compact[pl.ds(0, total.shape[0]), :] = total
    spread_out[...] = jnp.zeros((tokens, width), FULL)
    for at in range(tokens // SLAB):
        spread_out[pl.ds(at * SLAB, cols), :] = compact[pl.ds(at * cols, cols), :]
    need(summed_ref, normed_c_ref, factor_c_ref, out_gain_ref)
    grad_sum = silu_back(spread_out[...], summed_ref[...])
    grad_sum_ref[...] = grad_sum
    normed = normed_c_ref[...]
    exp[...] = norm_back(grad_sum, normed, factor_c_ref[:, :1], out_gain_ref[...])
    small_ref[pl.ds(2, 1), :] = jnp.sum(grad_sum * normed, axis=0, keepdims=True)
    small_ref[pl.ds(3, 1), :] = jnp.sum(grad_sum, axis=0, keepdims=True)
    pack(compact, exp, grad_exp_ref, cols)
    send(grad_sum_ref, grad_exp_ref)
    need(expand_ref)
    matmul_back(exp, expand_ref, sec)
    need(gain_ref, shift_ref, normed_b_ref, factor_b_ref)
    gain, shift = (gain_ref[pl.ds(1, 1), :], shift_ref[pl.ds(1, 1), :])
    normed = normed_b_ref[...]
    grad = silu_back(sec[...], normed * gain + shift)
    grad_conv_ref[...] = norm_back(grad, normed, factor_b_ref[:, :1], gain).astype(LOW)
    small_ref[pl.ds(0, 1), :] = jnp.sum(grad * normed, axis=0, keepdims=True)
    small_ref[pl.ds(1, 1), :] = jnp.sum(grad, axis=0, keepdims=True)
    for image in range(count):
        head = grad_conv_ref[pl.ds(image * each * SLAB, SLAB), :].astype(FULL)
        tail = grad_conv_ref[pl.ds((image * each + each - 1) * SLAB, SLAB), :].astype(FULL)
        set_edges(at_ref, edge_a_ref, edge_b_ref, image, head, tail)


def middle_back_kernel(
    need,
    send,
    at_ref,
    grad_conv_ref,
    got_a_ref,
    got_b_ref,
    pad,
    post_conv_ref,
    post_reduce_ref,
    post_gain_ref,
    post_shift_ref,
    post_normed_ref,
    post_factor_ref,
    post_grad_sum_ref,
    expand_ref,
    gain_ref,
    shift_ref,
    out_gain_ref,
    normed_b_ref,
    factor_b_ref,
    normed_c_ref,
    factor_c_ref,
    summed_ref,
    post_grad_red_ref,
    grad_sum_ref,
    grad_exp_ref,
    pre_grad_conv_ref,
    edge_a_ref,
    edge_b_ref,
    post_small_ref,
    small_ref,
    grad_pad,
    taps_sum,
    grad_in,
    pair,
    sec,
    sums,
    post_red,
    compact,
    *,
    cols
):
    count, side, width = edge_a_ref.shape
    need(grad_conv_ref, got_a_ref, got_b_ref)
    fill_halo(at_ref, grad_pad, grad_conv_ref, got_a_ref, got_b_ref)
    need(pad, post_conv_ref)
    need(post_gain_ref, post_shift_ref, post_normed_ref, post_factor_ref)
    taps = tap_rows(post_conv_ref)
    taps_sum[...] = jnp.zeros_like(taps_sum)
    sums[...] = jnp.zeros_like(sums)
    gain, shift = (post_gain_ref[pl.ds(0, 1), :], post_shift_ref[pl.ds(0, 1), :])
    each = post_grad_sum_ref.shape[0] // SLAB // count

    @pl.loop(0, count * each)
    def _(at):
        place = rows_of(at, SLAB)
        grad = conv_back_row(pad, grad_pad, taps, taps_sum, at // each, lax.rem(at, each))
        normed = post_normed_ref[place, :]
        grad = jnp.where(live(SLAB, cols), silu_back(grad, normed * gain + shift), 0.0)
        sums[0] += fold(grad * normed)
        sums[1] += fold(grad)
        post_red[place, :] = norm_back(grad, normed, post_factor_ref[place, :1], gain)

    for at in range(9):
        finish(post_small_ref, taps_sum, at, at)
    finish(post_small_ref, sums, 0, 9)
    finish(post_small_ref, sums, 1, 10)
    pack(compact, post_red, post_grad_red_ref, cols)
    send(post_grad_red_ref, post_small_ref)
    need(post_reduce_ref)
    matmul_back(post_red, post_reduce_ref, grad_in)
    sums[...] = jnp.zeros_like(sums)
    size = 2 * side
    need(out_gain_ref, post_grad_sum_ref, summed_ref, normed_c_ref, factor_c_ref)
    out_gain = out_gain_ref[...]
    for at in range(count * each):
        rows = pl.ds(at * size, size)
        place = pl.ds(at * SLAB, cols)
        grad = 0.25 * (post_grad_sum_ref[place, :] + grad_in[place, :])
        grad = widen(pair, grad)
        grad = jnp.concatenate([grad, grad], axis=0)
        grad_sum = silu_back(grad, summed_ref[rows, :])
        grad_sum_ref[rows, :] = grad_sum
        normed = normed_c_ref[rows, :]
        sums[0] += fold(grad_sum * normed)
        sums[1] += fold(grad_sum)
        grad_exp_ref[rows, :] = norm_back(
            grad_sum, normed, factor_c_ref[rows, :1], out_gain
        ).astype(LOW)
    finish(small_ref, sums, 0, 2)
    finish(small_ref, sums, 1, 3)
    send(grad_sum_ref, grad_exp_ref)
    need(expand_ref)
    matmul_back(grad_exp_ref, expand_ref, sec)
    need(gain_ref, shift_ref, normed_b_ref, factor_b_ref)
    sums[...] = jnp.zeros_like(sums)
    gain_b, shift_b = (gain_ref[pl.ds(1, 1), :], shift_ref[pl.ds(1, 1), :])

    @pl.loop(0, count * each)
    def _(at):
        rows = rows_of(at, size)
        normed = normed_b_ref[rows, :]
        grad = silu_back(sec[rows, :], normed * gain_b + shift_b)
        sums[0] += fold(grad * normed)
        sums[1] += fold(grad)
        pre_grad_conv_ref[rows, :] = norm_back(
            grad, normed, factor_b_ref[rows, :1], gain_b
        ).astype(LOW)

    finish(small_ref, sums, 0, 0)
    finish(small_ref, sums, 1, 1)
    for image in range(count):
        head = pre_grad_conv_ref[pl.ds(image * each * size, size), :].astype(FULL)
        tail = pre_grad_conv_ref[pl.ds((image * each + each - 1) * size, size), :].astype(FULL)
        set_edges(at_ref, edge_a_ref, edge_b_ref, image, head[:side], tail[side:])


def pre_back_kernel(
    need,
    send,
    at_ref,
    grad_conv_ref,
    got_a_ref,
    got_b_ref,
    pad,
    conv_ref,
    gain_ref,
    shift_ref,
    normed_ref,
    factor_ref,
    grad_red_ref,
    small_ref,
    grad_pad,
    taps_sum,
    sums,
):
    count, strip, side, width = pad.shape
    strip = strip - 2
    size = 2 * side
    each = strip // 2
    need(grad_conv_ref, got_a_ref, got_b_ref)
    fill_halo(at_ref, grad_pad, grad_conv_ref, got_a_ref, got_b_ref)
    need(pad, conv_ref)
    need(gain_ref, shift_ref, normed_ref, factor_ref)
    taps = tap_rows(conv_ref)
    taps_sum[...] = jnp.zeros_like(taps_sum)
    sums[...] = jnp.zeros_like(sums)
    gain, shift = (gain_ref[pl.ds(0, 1), :], shift_ref[pl.ds(0, 1), :])

    @pl.loop(0, count * each)
    def _(at):
        rows = rows_of(at, size)
        image, row = (at // each, 2 * lax.rem(at, each))
        grad = jnp.concatenate(
            [
                conv_back_row(pad, grad_pad, taps, taps_sum, image, row),
                conv_back_row(pad, grad_pad, taps, taps_sum, image, row + 1),
            ],
            axis=0,
        )
        normed = normed_ref[rows, :]
        grad = silu_back(grad, normed * gain + shift)
        sums[0] += fold(grad * normed)
        sums[1] += fold(grad)
        grad_red_ref[rows, :] = norm_back(grad, normed, factor_ref[rows, :1], gain).astype(LOW)

    for at in range(9):
        finish(small_ref, taps_sum, at, at)
    finish(small_ref, sums, 0, 9)
    finish(small_ref, sums, 1, 10)


def pair_outer_kernel(need, send, at_ref, *refs, pairs, parts):
    takes = 4 * pairs
    outs = refs[takes:]
    half, plane = (at_ref[0], at_ref[1])
    rows = outs[0].shape[0] // pairs
    for pair in range(pairs):
        left, left_far, right, right_far = refs[4 * pair : 4 * pair + 4]
        need(left, left_far, right, right_far)
        for step in range(parts):
            begin = half * (rows * parts) + jnp.bitwise_xor(plane, step) * rows
            lanes = pl.ds(pl.multiple_of(begin, LANES), rows)
            total = lax.dot_general(
                left[:, lanes], right[...], (((0,), (0,)), ((), ())), preferred_element_type=FULL
            ) + lax.dot_general(
                left_far[:, lanes],
                right_far[...],
                (((0,), (0,)), ((), ())),
                preferred_element_type=FULL,
            )
            outs[step][pl.ds(pair * rows, rows), :] = total.astype(LOW)
    send(*outs)


def sum_split_kernel(need, send, at_ref, *refs, pairs, parts, pieces, along):
    takes, outs = (refs[:pieces], refs[pieces : pieces + parts])
    total = refs[-1]
    need(*takes)
    value = takes[0][...].astype(FULL)
    for at in range(1, pieces):
        value = value + takes[at][...].astype(FULL)
    total[...] = value
    rows = total.shape[0] // pairs // parts
    for step in range(parts):
        begin = jnp.bitwise_xor(at_ref[along], step) * rows
        for pair in range(pairs):
            place = pl.ds(pl.multiple_of(pair * rows * parts + begin, SLAB), rows)
            outs[step][pl.ds(pair * rows, rows), :] = total[place, :].astype(LOW)
    send(*outs)


def post_outer_kernel(need, send, at_ref, *refs, strips):
    lefts, rights = (refs[:strips], (refs[strips : 2 * strips], refs[2 * strips : 3 * strips]))
    keep_ref, give_ref, total = refs[3 * strips :]
    rows = total.shape[0] // 2
    tokens = rights[0][0].shape[0]
    need(*refs[: 3 * strips])
    for place in range(2):
        value = jnp.zeros(total.shape, FULL)
        for step in range(strips):
            value = value + lax.dot_general(
                lefts[step][pl.ds(place * tokens, tokens), :],
                rights[place][step][...],
                (((0,), (0,)), ((), ())),
                preferred_element_type=FULL,
            )
        total[...] = value
        for side, out_ref in ((at_ref[0], keep_ref), (1 - at_ref[0], give_ref)):
            source = pl.ds(pl.multiple_of(side * rows, SLAB), rows)
            out_ref[pl.ds(place * rows, rows), :] = total[source, :].astype(LOW)


def assemble_kernel(at_ref, *refs, pairs, planes, strips, by_strip):
    takes = 2 * planes
    parts, outs = (refs[:takes], refs[takes : takes + pairs])
    full, sem = (refs[takes + pairs : takes + 2 * pairs], refs[-1])
    half, plane, row = (at_ref[0], at_ref[1], at_ref[2])
    rows = parts[0].shape[0] // pairs // strips
    writes = []

    def put(at, step, place):
        for pair in range(pairs):
            full[pair][pl.ds(pl.multiple_of(place, SLAB), rows), :] = parts[at][
                pl.ds((step * pairs + pair) * rows, rows), :
            ].astype(FULL)

    def write_out(begin, size):
        span = pl.ds(pl.multiple_of(begin, SLAB), size)
        for pair in range(pairs):
            write = pltpu.make_async_copy(
                full[pair].at[span, :], outs[pair].at[span, :], sem.at[len(writes)]
            )
            write.start()
            writes.append(write)

    sides = [
        (jnp.bitwise_xor(half, at // planes), jnp.bitwise_xor(plane, at % planes))
        for at in range(takes)
    ]
    if by_strip:
        for step in range(strips):
            begin = jnp.bitwise_xor(row, step) * (takes * rows)
            for at, (side, spot) in enumerate(sides):
                put(at, step, begin + side * (planes * rows) + spot * rows)
            write_out(begin, takes * rows)
    else:
        for at, (side, spot) in enumerate(sides):
            begin = side * (planes * strips * rows) + spot * (strips * rows)
            for step in range(strips):
                put(at, step, begin + jnp.bitwise_xor(row, step) * rows)
            write_out(begin, strips * rows)
    for write in writes:
        write.wait()


def assemble(index, parts, pairs, planes, strips, by_strip):
    takes = len(parts)
    out = like(2 * planes * parts[0].shape[0] // pairs, parts[0].shape[1])
    blocks = strips if by_strip else takes
    return pl.pallas_call(
        functools.partial(
            assemble_kernel, pairs=pairs, planes=planes, strips=strips, by_strip=by_strip
        ),
        out_shape=[out] * pairs,
        in_specs=[pl.BlockSpec(memory_space=pltpu.SMEM)]
        + [pl.BlockSpec(memory_space=pltpu.VMEM)] * takes,
        out_specs=[pl.BlockSpec(memory_space=pltpu.HBM)] * pairs,
        scratch_shapes=[pltpu.VMEM(out.shape, FULL)] * pairs
        + [pltpu.SemaphoreType.DMA((blocks * pairs,))],
        compiler_params=pltpu.CompilerParams(vmem_limit_bytes=VMEM_BYTES),
        cost_estimate=pl.CostEstimate(
            flops=0, bytes_accessed=pairs * out.size * 6, transcendentals=0
        ),
    )(index, *parts)


class Near:
    def __init__(self, value):
        self.value = value


def like(*shape, dtype=FULL):
    return jax.ShapeDtypeStruct(shape, dtype)


def low(*shape):
    return like(*shape, dtype=LOW)


def call(kernel, outs, scratch, flops, index, *args):
    near_in = [isinstance(arg, Near) for arg in args]
    near_out = [isinstance(out, Near) for out in outs]
    args = [arg.value if isinstance(arg, Near) else arg for arg in args]
    outs = [out.value if isinstance(out, Near) else out for out in outs]
    takes, gives = (len(args), len(outs))
    far_in = [at for at in range(takes) if not near_in[at]]
    far_out = [at for at in range(gives) if not near_out[at]]

    def body(at_ref, *refs):
        given, refs = (list(refs[:takes]), refs[takes:])
        made, refs = (list(refs[:gives]), refs[gives:])
        rest = refs[len(far_in) + len(far_out) :]
        reads, writes = ({}, {})
        if far_in:
            in_sem = rest[-1]
            rest = rest[:-1]
        if far_out:
            out_sem = rest[-1]
            rest = rest[:-1]
        for place, at in enumerate(far_in):
            reads[at] = pltpu.make_async_copy(given[at], refs[place], in_sem.at[place])
            given[at] = refs[place]
        for place, at in enumerate(far_out):
            mirror = refs[len(far_in) + place]
            writes[at] = pltpu.make_async_copy(mirror, made[at], out_sem.at[place])
            made[at] = mirror
        for read in reads.values():
            read.start()
        started = []

        def need(*wanted):
            for at in list(reads):
                if any(given[at] is ref for ref in wanted):
                    reads.pop(at).wait()

        def send(*ready):
            for at in list(writes):
                if any(made[at] is ref for ref in ready):
                    started.append(writes.pop(at))
                    started[-1].start()

        kernel(need, send, at_ref, *given, *made, *rest)
        need(*given)
        send(*made)
        for write in started:
            write.wait()

    moved = sum(arg.size * arg.dtype.itemsize for arg in args)
    moved += sum(out.size * out.dtype.itemsize for out in outs)
    spaces = {True: pltpu.VMEM, False: pltpu.HBM}
    return pl.pallas_call(
        body,
        out_shape=outs,
        in_specs=[pl.BlockSpec(memory_space=pltpu.SMEM)]
        + [pl.BlockSpec(memory_space=spaces[near]) for near in near_in],
        out_specs=[pl.BlockSpec(memory_space=spaces[near]) for near in near_out],
        scratch_shapes=[pltpu.VMEM(args[at].shape, args[at].dtype) for at in far_in]
        + [pltpu.VMEM(outs[at].shape, outs[at].dtype) for at in far_out]
        + [pltpu.VMEM(shape, FULL) for shape in scratch]
        + [pltpu.SemaphoreType.DMA((len(far_out),))] * bool(far_out)
        + [pltpu.SemaphoreType.DMA((len(far_in),))] * bool(far_in),
        compiler_params=pltpu.CompilerParams(vmem_limit_bytes=VMEM_BYTES),
        cost_estimate=pl.CostEstimate(flops=flops, bytes_accessed=moved, transcendentals=0),
    )(index, *args)


def edges(parity_edges):
    size = lax.axis_size("row")
    inner = [(at, at ^ 1) for at in range(size)]
    outer = [(at, at + 1) for at in range(1, size - 1, 2)]
    outer = outer + [(to, at) for at, to in outer]
    return (
        lax.ppermute(parity_edges[0], "row", inner),
        lax.ppermute(parity_edges[1], "row", outer),
    )


def exchange(pieces, axis):
    return lax.all_to_all(pieces, axis, 0, 0, tiled=True)


def swap(field):
    return lax.ppermute(field, "half", [(0, 1), (1, 0)])


def steps_of(value, axis, step):
    size = lax.axis_size(axis)
    return lax.ppermute(value, axis, [(at, at ^ step) for at in range(size)])


def share(parts, axis):
    return [parts[0]] + [steps_of(parts[at], axis, at) for at in range(1, len(parts))]


def share_same(part, axis):
    size = lax.axis_size(axis)
    return [part] + [steps_of(part, axis, at) for at in range(1, size)]


def pair_outer(index, left, left_far, right, right_far):
    size = lax.axis_size("im")
    values = [arg.value if isinstance(arg, Near) else arg for arg in (left, right)]
    rows = values[0].shape[1] // 2 // size
    width = values[1].shape[1]
    return list(
        call(
            functools.partial(pair_outer_kernel, pairs=1, parts=size),
            [Near(low(rows, width))] * size,
            [],
            4 * values[0].shape[0] * rows * size * width,
            index,
            left,
            left_far,
            right,
            right_far,
        )
    )


def sum_split(index, pieces, pairs, axis):
    size = lax.axis_size(axis)
    rows, width = pieces[0].shape
    return list(
        call(
            functools.partial(
                sum_split_kernel,
                pairs=pairs,
                parts=size,
                pieces=len(pieces),
                along={"im": 1, "row": 2}[axis],
            ),
            [Near(low(rows // size, width))] * size,
            [(rows, width)],
            0,
            index,
            *[Near(piece) for piece in pieces],
        )
    )


def add_low(pieces):
    total = pieces[0].astype(FULL)
    for piece in pieces[1:]:
        total = total + piece.astype(FULL)
    return total.astype(LOW)


def sum_far(left, right, axes):
    part = jnp.einsum("tm,tc->mc", left, right, preferred_element_type=FULL)
    return lax.psum(part, axes)


def shards(
    x_in,
    pre_reduce,
    pre_conv,
    pre_expand,
    pre_mid_gain,
    pre_mid_shift,
    pre_out_gain,
    pre_out_shift,
    post_reduce,
    post_conv,
    post_expand,
    post_mid_gain,
    post_mid_shift,
    post_out_gain,
    post_out_shift,
    read_weight,
    read_bias,
    cotangent,
):
    count, strip, side, width = x_in.shape
    strips = lax.axis_size("row")
    tokens = count * strip * side
    cols = side // 2
    rows = strip // 2
    slabs = count * rows
    padded = slabs * SLAB
    small = slabs * cols
    block = -(-small // SLAB) * SLAB
    features = read_weight.shape[1]
    cost = 2 * tokens * width * width
    post_cost = 2 * padded * width * width
    x_low = x_in.reshape(tokens, width)
    pre_out_g, pre_out_s = (pre_out_gain[None], pre_out_shift[None])
    post_out_g, post_out_s = (post_out_gain[None], post_out_shift[None])
    pre_edge = Near(low(count, side, width))
    post_edge = Near(low(count, SLAB, width))
    index = jnp.stack([lax.axis_index("half"), lax.axis_index("im"), lax.axis_index("row")])
    quick = lax.axis_size("im") == 4 and strips == 4
    if quick:
        x_far = swap(x_low)

    first, edge_a, edge_b, normed_a, factor_a = call(
        pre_reduce_kernel,
        [Near(low(tokens, width)), pre_edge, pre_edge, like(tokens, width), like(tokens, LANES)],
        [(tokens, width)],
        cost,
        index,
        x_low,
        pre_reduce,
        pre_mid_gain,
        pre_mid_shift,
    )
    got_a, got_b = edges((edge_a, edge_b))
    if quick:
        got_a, got_b, x_far = tie(got_a, got_b, x_far)
    (
        second,
        normed_b,
        factor_b,
        normed_c,
        factor_c,
        summed,
        pooled,
        post_first,
        edge_a,
        edge_b,
        post_normed_a,
        post_factor_a,
        pad,
    ) = call(
        pre_rest_kernel,
        [
            low(tokens, width),
            like(tokens, width),
            like(tokens, LANES),
            like(tokens, width),
            like(tokens, LANES),
            like(tokens, width),
            Near(like(padded, width)),
            Near(low(padded, width)),
            post_edge,
            post_edge,
            like(padded, width),
            like(padded, LANES),
            like(count, strip + 2, side, width),
        ],
        [(tokens, width), (side * width // LANES, LANES), (padded, width)],
        cost + post_cost,
        index,
        x_low,
        Near(first),
        Near(got_a),
        Near(got_b),
        pre_conv,
        pre_expand,
        pre_mid_gain,
        pre_mid_shift,
        pre_out_g,
        pre_out_s,
        post_reduce,
        post_mid_gain,
        post_mid_shift,
    )
    got_a, got_b = edges((edge_a, edge_b))
    if quick:
        second_far = swap(second)
        got_a, got_b, second_far = tie(got_a, got_b, second_far)
    made = call(
        functools.partial(post_rest_kernel, cols=cols, strips=strips),
        [Near(low(small, width)), low(2 * block, width)]
        + [low(2 * block, width // strips)] * strips
        + [
            like(padded, width),
            like(padded, LANES),
            like(padded, width),
            like(padded, LANES),
            like(padded, width),
            like(count, rows + 2, SLAB, width),
        ],
        [(padded, width), (padded, width), (block, width)],
        post_cost,
        index,
        Near(pooled),
        Near(post_first),
        Near(got_a),
        Near(got_b),
        post_conv,
        post_expand,
        post_mid_gain,
        post_mid_shift,
        post_out_g,
        post_out_s,
    )
    block_two, lefts = made[:2]
    slots, made = (list(made[2 : 2 + strips]), made[2 + strips :])
    post_normed_b, post_factor_b, post_normed_c, post_factor_c, post_summed, post_pad = made
    whole = lax.all_gather(block_two, "row", axis=0, tiled=True)
    if quick:
        whole_far = swap(whole)
    readout, grad_pre, terms, d_read_b = call(
        functools.partial(readout_kernel, strips=strips),
        [
            like(*cotangent.shape, dtype=LOW),
            Near(low(strips * small, features)),
            Near(low(strips * small, width)),
            like(1, features),
        ],
        [(strips * small, features), (strips * small, features)],
        2 * cost,
        index,
        Near(whole),
        read_weight,
        read_bias[None],
        cotangent,
    )
    terms = exchange(terms.reshape(strips, small, width), "row")
    if quick:
        parts = pair_outer(index, Near(whole), Near(whole_far), Near(grad_pre), Near(swap(grad_pre)))
        terms, parts[0], *slots = tie(terms, parts[0], *slots)
        slots = share(slots, "row")
        read_parts = share(parts, "im")
    post_gs, post_ge, post_gc, edge_a, edge_b, post_small_b = call(
        functools.partial(post_back_kernel, cols=cols),
        [
            Near(like(padded, width)),
            Near(low(block, width)),
            Near(low(padded, width)),
            post_edge,
            post_edge,
            like(4, width),
        ],
        [(block, width), (padded, width), (padded, width), (padded, width)],
        post_cost,
        index,
        Near(terms),
        post_expand,
        post_mid_gain,
        post_mid_shift,
        post_out_g,
        post_normed_b,
        post_factor_b,
        post_normed_c,
        post_factor_c,
        post_summed,
    )
    got_a, got_b = edges((edge_a, edge_b))
    if quick:
        got_a, got_b, *read_parts = tie(got_a, got_b, *read_parts)
        read_part = add_low(read_parts)
        ge_slots = share_same(post_ge, "row")
    (
        post_gr,
        pre_gs,
        pre_ge,
        pre_gc,
        edge_a,
        edge_b,
        post_small_a,
        pre_small_b,
    ) = call(
        functools.partial(middle_back_kernel, cols=cols),
        [
            Near(low(block, width)),
            like(tokens, width),
            Near(low(tokens, width)),
            Near(low(tokens, width)),
            pre_edge,
            pre_edge,
            like(11, width),
            like(4, width),
        ],
        [
            (count, rows + 2, SLAB, width),
            (9, 8, width),
            (padded, width),
            (side * width // LANES, LANES),
            (tokens, width),
            (2, 8, width),
            (padded, width),
            (block, width),
        ],
        cost + post_cost,
        index,
        Near(post_gc),
        Near(got_a),
        Near(got_b),
        post_pad,
        post_conv,
        post_reduce,
        post_mid_gain,
        post_mid_shift,
        post_normed_a,
        post_factor_a,
        Near(post_gs),
        pre_expand,
        pre_mid_gain,
        pre_mid_shift,
        pre_out_g,
        normed_b,
        factor_b,
        normed_c,
        factor_c,
        summed,
    )
    got_a, got_b = edges((edge_a, edge_b))
    if quick:
        read_total = lax.all_gather(read_part, ("half", "im"), axis=0, tiled=True)
        expand_parts = pair_outer(index, second, second_far, Near(pre_ge), Near(swap(pre_ge)))
        got_a, got_b, expand_parts[0], read_total, *rest = tie(
            got_a, got_b, expand_parts[0], read_total, *ge_slots, *slots
        )
        ge_slots, slots = (rest[:strips], rest[strips:])
        expand_parts = share(expand_parts, "im")
        gr_slots = share_same(post_gr, "row")
    pre_gr, pre_small_a = call(
        pre_back_kernel,
        [Near(low(tokens, width)), like(11, width)],
        [
            (count, strip + 2, side, width),
            (9, 8, width),
            (2, 8, width),
        ],
        0,
        index,
        Near(pre_gc),
        Near(got_a),
        Near(got_b),
        pad,
        pre_conv,
        pre_mid_gain,
        pre_mid_shift,
        normed_a,
        factor_a,
    )
    sums = jnp.concatenate([pre_small_a, pre_small_b, post_small_a, post_small_b, d_read_b])
    if quick:
        far = swap(pre_gr)
        sums = sums + swap(sums)
        far, sums, *gr_slots = tie(far, sums, *gr_slots)
        reduce_parts = pair_outer(index, x_low, x_far, Near(pre_gr), Near(far))
        reduce_parts[0], *expand_parts = tie(reduce_parts[0], *expand_parts)
        keep, give = call(
            functools.partial(post_outer_kernel, strips=strips),
            [Near(low(width // 4, width))] * 2,
            [(width // 4, width)],
            4 * strips * block * width * width // strips,
            index,
            *[Near(slot) for slot in slots + gr_slots + ge_slots],
        )
        post_parts = sum_split(index, [keep, swap(give)], 2, "im")
        reduce_parts = share(reduce_parts, "im")
        post_parts = share(post_parts, "im")
        expand_parts = sum_split(index, expand_parts, 1, "row")
        post_part = add_low(post_parts)
        sums = sums + steps_of(sums, "im", 1)
        sums, reduce_parts[0] = tie(sums, reduce_parts[0])
        reduce_parts = sum_split(index, reduce_parts, 1, "row")
        sums = sums + steps_of(sums, "im", 2)
        reduce_parts = share(reduce_parts, "row")
        sums, reduce_parts[0] = tie(sums, reduce_parts[0])
        read_bias_g = sums[30]
        sums = sums + steps_of(sums, "row", 1)
        reduce_part = share_same(add_low(reduce_parts), "row")
        sums, reduce_part[0] = tie(sums, reduce_part[0])
        sums = sums + steps_of(sums, "row", 2)
        streams = []
        for pairs, part in (
            (2, share_same(post_part, "row")),
            (1, share_same(add_low(share(expand_parts, "row")), "row")),
            (1, reduce_part),
        ):
            parts = share_same(jnp.concatenate(part, axis=0), "im")
            parts = parts + [swap(part) for part in parts]
            streams.append(assemble(index, parts, pairs, 4, strips, pairs == 2))
        (post_reduce_g, post_expand_g), (pre_expand_g,), (pre_reduce_g,) = streams
        read_total = read_total.astype(FULL)
    else:
        axes = IMG + ("row",)
        post_reduce_g = sum_far(lefts[:block], post_gr, axes)
        post_expand_g = sum_far(lefts[block:], post_ge, axes)
        pre_expand_g = sum_far(second, pre_ge, axes)
        pre_reduce_g = sum_far(x_low, pre_gr, axes)
        read_total = sum_far(whole, grad_pre, IMG)
        read_bias_g = lax.psum(sums[30], IMG)
        sums = lax.psum(sums, axes)
    grad_in = pre_gs + jnp.einsum("tm,cm->tc", pre_gr, pre_reduce, preferred_element_type=FULL)

    def small_grads(part):
        return (
            part[:9].reshape(3, 3, width),
            jnp.stack([part[9], part[11]]),
            jnp.stack([part[10], part[12]]),
            part[13],
            part[14],
        )

    pre_conv_g, pre_gain_g, pre_shift_g, pre_og_g, pre_os_g = small_grads(sums[:15])
    post_conv_g, post_gain_g, post_shift_g, post_og_g, post_os_g = small_grads(sums[15:30])
    return (
        readout,
        grad_in.astype(LOW).reshape(x_in.shape),
        pre_reduce_g,
        pre_conv_g,
        pre_expand_g,
        pre_gain_g,
        pre_shift_g,
        pre_og_g,
        pre_os_g,
        post_reduce_g,
        post_conv_g,
        post_expand_g,
        post_gain_g,
        post_shift_g,
        post_og_g,
        post_os_g,
        read_total,
        read_bias_g,
    )


def solution(mesh):
    images, strips = mesh.devices.shape
    split = jax.sharding.Mesh(
        mesh.devices.reshape(images // 2, 2, strips), ("im", "half", "row")
    )
    return jax.shard_map(
        shards,
        mesh=split,
        in_specs=(P(IMG, "row", None, None),)
        + (P(),) * 14
        + (P(None, "row"), P("row"), P(IMG, None, None, "row")),
        out_specs=(P(IMG, None, None, "row"), P(IMG, "row", None, None))
        + (P(),) * 14
        + (P(None, "row"), P("row")),
        check_vma=False,
    )
```

```python
import functools

import jax
import jax.numpy as jnp
from jax import lax
from jax.experimental import pallas as pl
from jax.experimental.pallas import tpu as pltpu
from jax.sharding import PartitionSpec as P

EPSILON = 1e-06
SQRT_HALF = 0.7071067811865476
INV_SQRT_TWO_PI = 0.3989422804014327
LOW = jnp.bfloat16
FULL = jnp.float32
IMG = ("im", "half")
TILE = 256
SLAB = 16
LANES = 128
VMEM_BYTES = 60 * 1024 * 1024


def tie(*values):
    return lax.optimization_barrier(values)


def norm(value):
    centred = value - jnp.mean(value, axis=-1, keepdims=True)
    factor = lax.rsqrt(jnp.mean(centred * centred, axis=-1, keepdims=True) + EPSILON)
    return (centred * factor, factor)


def norm_back(grad, normed, factor, gain):
    scaled = grad * gain
    return factor * (
        scaled
        - jnp.mean(scaled, axis=-1, keepdims=True)
        - normed * jnp.mean(scaled * normed, axis=-1, keepdims=True)
    )


def gate(value):
    return 0.5 * jnp.tanh(0.5 * value) + 0.5


def silu(value):
    return value * gate(value)


def silu_back(grad, value):
    sigma = gate(value)
    return grad * sigma * (1.0 + value * (1.0 - sigma))


def wide(factor):
    return jnp.broadcast_to(factor, (factor.shape[0], LANES))


def fold(value):
    return jnp.sum(value.reshape(-1, 8, value.shape[-1]), axis=0)


def live(rows, cols):
    at = lax.broadcasted_iota(jnp.int32, (rows, 1), 0)
    return lax.rem(at, SLAB) < cols


def from_left(value):
    at = lax.broadcasted_iota(jnp.int32, (value.shape[0], 1), 0)
    return jnp.where(at == 0, 0.0, pltpu.roll(value, 1, 0))


def from_right(value):
    last = value.shape[0] - 1
    at = lax.broadcasted_iota(jnp.int32, (value.shape[0], 1), 0)
    return jnp.where(at == last, 0.0, pltpu.roll(value, last, 0))


def matmul(left_ref, right_ref, out_ref):
    @pl.loop(0, right_ref.shape[1] // TILE)
    def _(at):
        cols = pl.ds(pl.multiple_of(at * TILE, TILE), TILE)
        out_ref[:, cols] = jnp.dot(
            left_ref[...].astype(LOW), right_ref[:, cols], preferred_element_type=FULL
        )


def matmul_back(left_ref, right_ref, out_ref):
    @pl.loop(0, right_ref.shape[0] // TILE)
    def _(at):
        cols = pl.ds(pl.multiple_of(at * TILE, TILE), TILE)
        out_ref[:, cols] = lax.dot_general(
            left_ref[...].astype(LOW),
            right_ref[cols, :],
            (((1,), (1,)), ((), ())),
            preferred_element_type=FULL,
        ).astype(out_ref.dtype)


def rows_of(at, size):
    return pl.ds(pl.multiple_of(at * size, SLAB), size)


def fill_halo(at_ref, pad_ref, low_ref, got_a_ref, got_b_ref):
    count, rows, cols, width = pad_ref.shape
    rows = rows - 2
    even = lax.rem(at_ref[2], 2) == 0
    for image in range(count):
        got_a, got_b = (got_a_ref[image].astype(FULL), got_b_ref[image].astype(FULL))
        pad_ref[image, 0] = jnp.where(even, got_b, got_a)
        pad_ref[image, rows + 1] = jnp.where(even, got_a, got_b)

    size = cols if cols % SLAB == 0 else 2 * cols
    per = size // cols
    each = rows // per

    @pl.loop(0, count * each)
    def _(at):
        part = low_ref[rows_of(at, size), :].astype(FULL).reshape(per, cols, width)
        pad_ref[at // each, pl.ds(1 + per * lax.rem(at, each), per)] = part


def set_edges(at_ref, edge_a_ref, edge_b_ref, image, head, tail):
    even = lax.rem(at_ref[2], 2) == 0
    edge_a_ref[image] = jnp.where(even, tail, head).astype(LOW)
    edge_b_ref[image] = jnp.where(even, head, tail).astype(LOW)


def conv_row(pad_ref, taps, image, row):
    lines = [pad_ref[image, row + top] for top in range(3)]
    sums = [
        lines[0] * taps[left] + lines[1] * taps[3 + left] + lines[2] * taps[6 + left]
        for left in range(3)
    ]
    return from_left(sums[0]) + sums[1] + from_right(sums[2])


def conv_back_row(pad_ref, grad_ref, taps, taps_ref, image, row):
    lines = [grad_ref[image, row + top] for top in range(3)]
    sums = [
        lines[2] * taps[left] + lines[1] * taps[3 + left] + lines[0] * taps[6 + left]
        for left in range(3)
    ]
    shifted = [from_right(lines[1]), lines[1], from_left(lines[1])]
    for top in range(3):
        source = pad_ref[image, row + top]
        for left in range(3):
            taps_ref[3 * top + left] += fold(source * shifted[left])
    return from_right(sums[0]) + sums[1] + from_left(sums[2])


def pack(compact, source, out_ref, cols):
    compact[...] = jnp.zeros(compact.shape, FULL)
    for at in range(source.shape[0] // SLAB):
        compact[pl.ds(at * cols, cols), :] = source[pl.ds(at * SLAB, cols), :]
    out_ref[...] = compact[...].astype(LOW)


def narrow(pair, value):
    side = value.shape[0]
    parts = []
    for at in range(value.shape[1] // LANES):
        pair[pl.ds(at * side, side), :] = value[:, at * LANES : (at + 1) * LANES]
        parts.append(
            pair[pl.ds(at * side, side // 2, stride=2), :]
            + pair[pl.ds(at * side + 1, side // 2, stride=2), :]
        )
    return jnp.concatenate(parts, axis=1)


def widen(pair, value):
    cols = value.shape[0]
    parts = []
    for at in range(value.shape[1] // LANES):
        part = value[:, at * LANES : (at + 1) * LANES]
        pair[pl.ds(2 * cols * at, cols, stride=2), :] = part
        pair[pl.ds(2 * cols * at + 1, cols, stride=2), :] = part
        parts.append(pair[pl.ds(2 * cols * at, 2 * cols), :])
    return jnp.concatenate(parts, axis=1)


def tap_rows(conv_ref):
    lines = [conv_ref[top].astype(FULL) for top in range(3)]
    return [lines[at // 3][at % 3 : at % 3 + 1] for at in range(9)]


def finish(small_ref, sums_ref, at, place):
    small_ref[pl.ds(place, 1), :] = jnp.sum(sums_ref[at], axis=0, keepdims=True)


def pre_reduce_kernel(
    need,
    send,
    at_ref,
    x_ref, w_ref, gain_ref, shift_ref, first_ref, edge_a_ref, edge_b_ref, normed_ref, factor_ref, red
):
    count, side, width = edge_a_ref.shape
    size = 2 * side
    steps = x_ref.shape[0] // size
    need(x_ref, w_ref)
    matmul(x_ref, w_ref, red)
    need(gain_ref, shift_ref)
    gain, shift = (gain_ref[pl.ds(0, 1), :], shift_ref[pl.ds(0, 1), :])

    @pl.loop(0, steps)
    def _(at):
        rows = rows_of(at, size)
        normed, factor = norm(red[rows, :])
        normed_ref[rows, :] = normed
        factor_ref[rows, :] = wide(factor)
        first_ref[rows, :] = silu(normed * gain + shift).astype(LOW)

    each = steps // count
    for image in range(count):
        head = first_ref[pl.ds(image * each * size, size), :].astype(FULL)
        tail = first_ref[pl.ds((image * each + each - 1) * size, size), :].astype(FULL)
        set_edges(at_ref, edge_a_ref, edge_b_ref, image, head[:side], tail[side:])


def pre_rest_kernel(
    need,
    send,
    at_ref,
    x_ref,
    first_ref,
    got_a_ref,
    got_b_ref,
    conv_ref,
    expand_ref,
    gain_ref,
    shift_ref,
    out_gain_ref,
    out_shift_ref,
    reduce_ref,
    post_gain_ref,
    post_shift_ref,
    second_ref,
    normed_b_ref,
    factor_b_ref,
    normed_c_ref,
    factor_c_ref,
    summed_ref,
    pooled_ref,
    post_first_ref,
    edge_a_ref,
    edge_b_ref,
    post_normed_ref,
    post_factor_ref,
    pad,
    exp,
    pair,
    red,
):
    count, strip, side, width = pad.shape
    strip = strip - 2
    size = 2 * side
    each = strip // 2
    need(first_ref, got_a_ref, got_b_ref)
    fill_halo(at_ref, pad, first_ref, got_a_ref, got_b_ref)
    need(conv_ref, gain_ref, shift_ref)
    send(pad)
    taps = tap_rows(conv_ref)
    gain, shift = (gain_ref[pl.ds(1, 1), :], shift_ref[pl.ds(1, 1), :])

    @pl.loop(0, count * each)
    def _(at):
        rows = rows_of(at, size)
        image, row = (at // each, 2 * lax.rem(at, each))
        conv = jnp.concatenate(
            [conv_row(pad, taps, image, row), conv_row(pad, taps, image, row + 1)], axis=0
        )
        normed, factor = norm(conv)
        normed_b_ref[rows, :] = normed
        factor_b_ref[rows, :] = wide(factor)
        second_ref[rows, :] = silu(normed * gain + shift).astype(LOW)

    send(second_ref, normed_b_ref, factor_b_ref)
    need(expand_ref)
    matmul(second_ref, expand_ref, exp)
    need(x_ref, out_gain_ref, out_shift_ref)
    out_gain, out_shift = (out_gain_ref[...], out_shift_ref[...])
    cols = side // 2
    for at in range(count * each):
        rows = pl.ds(at * size, size)
        normed, factor = norm(exp[rows, :])
        normed_c_ref[rows, :] = normed
        factor_c_ref[rows, :] = wide(factor)
        summed = x_ref[rows, :].astype(FULL) + normed * out_gain + out_shift
        summed_ref[rows, :] = summed
        block = silu(summed)
        half = narrow(pair, block[:side] + block[side:])
        pooled_ref[pl.ds(at * SLAB, cols), :] = 0.25 * half
        pooled_ref[pl.ds(at * SLAB + cols, SLAB - cols), :] = jnp.zeros(
            (SLAB - cols, width), FULL
        )
    send(normed_c_ref, factor_c_ref, summed_ref)
    need(reduce_ref, post_gain_ref, post_shift_ref)
    matmul(pooled_ref, reduce_ref, red)
    normed, factor = norm(red[...])
    post_normed_ref[...] = normed
    post_factor_ref[...] = wide(factor)
    first = silu(normed * post_gain_ref[pl.ds(0, 1), :] + post_shift_ref[pl.ds(0, 1), :])
    post_first_ref[...] = jnp.where(live(red.shape[0], cols), first, 0.0).astype(LOW)
    for image in range(count):
        head = post_first_ref[pl.ds(image * each * SLAB, SLAB), :].astype(FULL)
        tail = post_first_ref[pl.ds((image * each + each - 1) * SLAB, SLAB), :].astype(FULL)
        set_edges(at_ref, edge_a_ref, edge_b_ref, image, head, tail)


def post_rest_kernel(
    need,
    send,
    at_ref,
    pooled_ref,
    first_ref,
    got_a_ref,
    got_b_ref,
    conv_ref,
    expand_ref,
    gain_ref,
    shift_ref,
    out_gain_ref,
    out_shift_ref,
    block_ref,
    left_in_ref,
    left_second_ref,
    normed_b_ref,
    factor_b_ref,
    normed_c_ref,
    factor_c_ref,
    summed_ref,
    pad,
    second,
    exp,
    compact,
    *,
    cols
):
    count, rows, _, width = pad.shape
    rows = rows - 2
    small = block_ref.shape[0]
    need(first_ref, got_a_ref, got_b_ref)
    fill_halo(at_ref, pad, first_ref, got_a_ref, got_b_ref)
    send(pad)
    need(conv_ref, gain_ref, shift_ref, pooled_ref)
    taps = tap_rows(conv_ref)
    gain, shift = (gain_ref[pl.ds(1, 1), :], shift_ref[pl.ds(1, 1), :])

    @pl.loop(0, count * rows)
    def _(at):
        place = rows_of(at, SLAB)
        normed, factor = norm(conv_row(pad, taps, at // rows, lax.rem(at, rows)))
        normed_b_ref[place, :] = normed
        factor_b_ref[place, :] = wide(factor)
        second[place, :] = silu(normed * gain + shift)

    send(normed_b_ref, factor_b_ref)
    need(expand_ref)
    matmul(second, expand_ref, exp)
    need(out_gain_ref, out_shift_ref)
    normed, factor = norm(exp[...])
    normed_c_ref[...] = normed
    factor_c_ref[...] = wide(factor)
    summed = pooled_ref[...] + normed * out_gain_ref[...] + out_shift_ref[...]
    summed_ref[...] = summed
    exp[...] = silu(summed)
    compact[...] = jnp.zeros(compact.shape, FULL)
    for at in range(count * rows):
        compact[pl.ds(at * cols, cols), :] = exp[pl.ds(at * SLAB, cols), :]
    block_ref[...] = compact[pl.ds(0, small), :].astype(LOW)
    send(block_ref, normed_c_ref, factor_c_ref, summed_ref)
    pack(compact, pooled_ref, left_in_ref, cols)
    pack(compact, second, left_second_ref, cols)


def readout_kernel(
    need,
    send,
    at_ref,
    whole_ref,
    w_ref,
    bias_ref,
    cot_ref,
    out_ref,
    grad_ref,
    terms_ref,
    bias_grad_ref,
    cot,
    out,
    *,
    strips
):
    images, lines, cols, _ = cot_ref.shape
    rows = lines // strips
    need(cot_ref)
    for at in range(images * lines):
        strip, image, row = (at // (images * rows), at // rows % images, at % rows)
        cot[pl.ds(at * cols, cols), :] = cot_ref[image, strip * rows + row].astype(FULL)
    need(whole_ref, w_ref, bias_ref)

    @pl.loop(0, w_ref.shape[1] // TILE)
    def _(at):
        lanes = pl.ds(pl.multiple_of(at * TILE, TILE), TILE)
        act = jnp.dot(whole_ref[...], w_ref[:, lanes], preferred_element_type=FULL)
        act = act + bias_ref[:, lanes]
        cdf = 0.5 * (1.0 + lax.erf(act * SQRT_HALF))
        density = jnp.exp(-0.5 * act * act) * INV_SQRT_TWO_PI
        out[:, lanes] = act * cdf
        grad = (cot[:, lanes] * (cdf + act * density)).astype(LOW)
        grad_ref[:, lanes] = grad
        bias_grad_ref[:, lanes] = jnp.sum(grad.astype(FULL), axis=0, keepdims=True)

    send(grad_ref, bias_grad_ref)
    matmul_back(grad_ref, w_ref, terms_ref)
    send(terms_ref)
    for at in range(images * lines):
        strip, image, row = (at // (images * rows), at // rows % images, at % rows)
        out_ref[image, strip * rows + row] = out[pl.ds(at * cols, cols), :].astype(LOW)


def post_back_kernel(
    need,
    send,
    at_ref,
    pieces_ref,
    expand_ref,
    gain_ref,
    shift_ref,
    out_gain_ref,
    normed_b_ref,
    factor_b_ref,
    normed_c_ref,
    factor_c_ref,
    summed_ref,
    grad_sum_ref,
    grad_exp_ref,
    grad_conv_ref,
    edge_a_ref,
    edge_b_ref,
    small_ref,
    compact,
    spread_out,
    exp,
    sec,
    *,
    cols
):
    count = edge_a_ref.shape[0]
    tokens, width = grad_sum_ref.shape
    each = tokens // SLAB // count
    need(pieces_ref)
    total = pieces_ref[0].astype(FULL)
    for at in range(1, pieces_ref.shape[0]):
        total = total + pieces_ref[at].astype(FULL)
    compact[...] = jnp.zeros(compact.shape, FULL)
    compact[pl.ds(0, total.shape[0]), :] = total
    spread_out[...] = jnp.zeros((tokens, width), FULL)
    for at in range(tokens // SLAB):
        spread_out[pl.ds(at * SLAB, cols), :] = compact[pl.ds(at * cols, cols), :]
    need(summed_ref, normed_c_ref, factor_c_ref, out_gain_ref)
    grad_sum = silu_back(spread_out[...], summed_ref[...])
    grad_sum_ref[...] = grad_sum
    normed = normed_c_ref[...]
    exp[...] = norm_back(grad_sum, normed, factor_c_ref[:, :1], out_gain_ref[...])
    small_ref[pl.ds(2, 1), :] = jnp.sum(grad_sum * normed, axis=0, keepdims=True)
    small_ref[pl.ds(3, 1), :] = jnp.sum(grad_sum, axis=0, keepdims=True)
    pack(compact, exp, grad_exp_ref, cols)
    send(grad_sum_ref, grad_exp_ref)
    need(expand_ref)
    matmul_back(exp, expand_ref, sec)
    need(gain_ref, shift_ref, normed_b_ref, factor_b_ref)
    gain, shift = (gain_ref[pl.ds(1, 1), :], shift_ref[pl.ds(1, 1), :])
    normed = normed_b_ref[...]
    grad = silu_back(sec[...], normed * gain + shift)
    grad_conv_ref[...] = norm_back(grad, normed, factor_b_ref[:, :1], gain).astype(LOW)
    small_ref[pl.ds(0, 1), :] = jnp.sum(grad * normed, axis=0, keepdims=True)
    small_ref[pl.ds(1, 1), :] = jnp.sum(grad, axis=0, keepdims=True)
    for image in range(count):
        head = grad_conv_ref[pl.ds(image * each * SLAB, SLAB), :].astype(FULL)
        tail = grad_conv_ref[pl.ds((image * each + each - 1) * SLAB, SLAB), :].astype(FULL)
        set_edges(at_ref, edge_a_ref, edge_b_ref, image, head, tail)


def middle_back_kernel(
    need,
    send,
    at_ref,
    grad_conv_ref,
    got_a_ref,
    got_b_ref,
    pad,
    post_conv_ref,
    post_reduce_ref,
    post_gain_ref,
    post_shift_ref,
    post_normed_ref,
    post_factor_ref,
    post_grad_sum_ref,
    expand_ref,
    gain_ref,
    shift_ref,
    out_gain_ref,
    normed_b_ref,
    factor_b_ref,
    normed_c_ref,
    factor_c_ref,
    summed_ref,
    post_grad_red_ref,
    grad_sum_ref,
    grad_exp_ref,
    pre_grad_conv_ref,
    edge_a_ref,
    edge_b_ref,
    post_small_ref,
    small_ref,
    grad_pad,
    taps_sum,
    grad_in,
    pair,
    sec,
    sums,
    post_red,
    compact,
    *,
    cols
):
    count, side, width = edge_a_ref.shape
    need(grad_conv_ref, got_a_ref, got_b_ref)
    fill_halo(at_ref, grad_pad, grad_conv_ref, got_a_ref, got_b_ref)
    need(pad, post_conv_ref)
    need(post_gain_ref, post_shift_ref, post_normed_ref, post_factor_ref)
    taps = tap_rows(post_conv_ref)
    taps_sum[...] = jnp.zeros_like(taps_sum)
    sums[...] = jnp.zeros_like(sums)
    gain, shift = (post_gain_ref[pl.ds(0, 1), :], post_shift_ref[pl.ds(0, 1), :])
    each = post_grad_sum_ref.shape[0] // SLAB // count

    @pl.loop(0, count * each)
    def _(at):
        place = rows_of(at, SLAB)
        grad = conv_back_row(pad, grad_pad, taps, taps_sum, at // each, lax.rem(at, each))
        normed = post_normed_ref[place, :]
        grad = jnp.where(live(SLAB, cols), silu_back(grad, normed * gain + shift), 0.0)
        sums[0] += fold(grad * normed)
        sums[1] += fold(grad)
        post_red[place, :] = norm_back(grad, normed, post_factor_ref[place, :1], gain)

    for at in range(9):
        finish(post_small_ref, taps_sum, at, at)
    finish(post_small_ref, sums, 0, 9)
    finish(post_small_ref, sums, 1, 10)
    pack(compact, post_red, post_grad_red_ref, cols)
    send(post_grad_red_ref, post_small_ref)
    need(post_reduce_ref)
    matmul_back(post_red, post_reduce_ref, grad_in)
    sums[...] = jnp.zeros_like(sums)
    size = 2 * side
    need(out_gain_ref, post_grad_sum_ref, summed_ref, normed_c_ref, factor_c_ref)
    out_gain = out_gain_ref[...]
    for at in range(count * each):
        rows = pl.ds(at * size, size)
        place = pl.ds(at * SLAB, cols)
        grad = 0.25 * (post_grad_sum_ref[place, :] + grad_in[place, :])
        grad = widen(pair, grad)
        grad = jnp.concatenate([grad, grad], axis=0)
        grad_sum = silu_back(grad, summed_ref[rows, :])
        grad_sum_ref[rows, :] = grad_sum
        normed = normed_c_ref[rows, :]
        sums[0] += fold(grad_sum * normed)
        sums[1] += fold(grad_sum)
        grad_exp_ref[rows, :] = norm_back(
            grad_sum, normed, factor_c_ref[rows, :1], out_gain
        ).astype(LOW)
    finish(small_ref, sums, 0, 2)
    finish(small_ref, sums, 1, 3)
    send(grad_sum_ref, grad_exp_ref)
    need(expand_ref)
    matmul_back(grad_exp_ref, expand_ref, sec)
    need(gain_ref, shift_ref, normed_b_ref, factor_b_ref)
    sums[...] = jnp.zeros_like(sums)
    gain_b, shift_b = (gain_ref[pl.ds(1, 1), :], shift_ref[pl.ds(1, 1), :])

    @pl.loop(0, count * each)
    def _(at):
        rows = rows_of(at, size)
        normed = normed_b_ref[rows, :]
        grad = silu_back(sec[rows, :], normed * gain_b + shift_b)
        sums[0] += fold(grad * normed)
        sums[1] += fold(grad)
        pre_grad_conv_ref[rows, :] = norm_back(
            grad, normed, factor_b_ref[rows, :1], gain_b
        ).astype(LOW)

    finish(small_ref, sums, 0, 0)
    finish(small_ref, sums, 1, 1)
    for image in range(count):
        head = pre_grad_conv_ref[pl.ds(image * each * size, size), :].astype(FULL)
        tail = pre_grad_conv_ref[pl.ds((image * each + each - 1) * size, size), :].astype(FULL)
        set_edges(at_ref, edge_a_ref, edge_b_ref, image, head[:side], tail[side:])


def pre_back_kernel(
    need,
    send,
    at_ref,
    grad_conv_ref,
    got_a_ref,
    got_b_ref,
    pad,
    conv_ref,
    gain_ref,
    shift_ref,
    normed_ref,
    factor_ref,
    grad_red_ref,
    small_ref,
    grad_pad,
    taps_sum,
    sums,
):
    count, strip, side, width = pad.shape
    strip = strip - 2
    size = 2 * side
    each = strip // 2
    need(grad_conv_ref, got_a_ref, got_b_ref)
    fill_halo(at_ref, grad_pad, grad_conv_ref, got_a_ref, got_b_ref)
    need(pad, conv_ref)
    need(gain_ref, shift_ref, normed_ref, factor_ref)
    taps = tap_rows(conv_ref)
    taps_sum[...] = jnp.zeros_like(taps_sum)
    sums[...] = jnp.zeros_like(sums)
    gain, shift = (gain_ref[pl.ds(0, 1), :], shift_ref[pl.ds(0, 1), :])

    @pl.loop(0, count * each)
    def _(at):
        rows = rows_of(at, size)
        image, row = (at // each, 2 * lax.rem(at, each))
        grad = jnp.concatenate(
            [
                conv_back_row(pad, grad_pad, taps, taps_sum, image, row),
                conv_back_row(pad, grad_pad, taps, taps_sum, image, row + 1),
            ],
            axis=0,
        )
        normed = normed_ref[rows, :]
        grad = silu_back(grad, normed * gain + shift)
        sums[0] += fold(grad * normed)
        sums[1] += fold(grad)
        grad_red_ref[rows, :] = norm_back(grad, normed, factor_ref[rows, :1], gain).astype(LOW)

    for at in range(9):
        finish(small_ref, taps_sum, at, at)
    finish(small_ref, sums, 0, 9)
    finish(small_ref, sums, 1, 10)


def pair_outer_kernel(need, send, at_ref, *refs, pairs, parts):
    takes = 4 * pairs
    outs = refs[takes:]
    half, plane = (at_ref[0], at_ref[1])
    rows = outs[0].shape[0] // pairs
    for pair in range(pairs):
        left, left_far, right, right_far = refs[4 * pair : 4 * pair + 4]
        need(left, left_far, right, right_far)
        for step in range(parts):
            begin = half * (rows * parts) + jnp.bitwise_xor(plane, step) * rows
            lanes = pl.ds(pl.multiple_of(begin, LANES), rows)
            total = lax.dot_general(
                left[:, lanes], right[...], (((0,), (0,)), ((), ())), preferred_element_type=FULL
            ) + lax.dot_general(
                left_far[:, lanes],
                right_far[...],
                (((0,), (0,)), ((), ())),
                preferred_element_type=FULL,
            )
            outs[step][pl.ds(pair * rows, rows), :] = total.astype(LOW)
    send(*outs)


def sum_split_kernel(need, send, at_ref, *refs, pairs, parts, pieces, along=2):
    takes, outs = (refs[:pieces], refs[pieces : pieces + parts])
    total = refs[-1]
    need(*takes)
    value = takes[0][...].astype(FULL)
    for at in range(1, pieces):
        value = value + takes[at][...].astype(FULL)
    total[...] = value
    rows = total.shape[0] // pairs // parts
    for step in range(parts):
        begin = jnp.bitwise_xor(at_ref[along], step) * rows
        for pair in range(pairs):
            place = pl.ds(pl.multiple_of(pair * rows * parts + begin, SLAB), rows)
            outs[step][pl.ds(pair * rows, rows), :] = total[place, :].astype(LOW)
    send(*outs)


def assemble_kernel(at_ref, *refs, pairs, planes, strips):
    takes = 2 * planes
    parts, outs = (refs[:takes], refs[takes : takes + pairs])
    full, sem = (refs[takes + pairs : takes + 2 * pairs], refs[-1])
    half, plane, row = (at_ref[0], at_ref[1], at_ref[2])
    rows = parts[0].shape[0] // pairs // strips
    writes = []

    def put(at, step, place):
        for pair in range(pairs):
            full[pair][pl.ds(pl.multiple_of(place, SLAB), rows), :] = parts[at][
                pl.ds((step * pairs + pair) * rows, rows), :
            ].astype(FULL)

    def write_out(begin, size):
        span = pl.ds(pl.multiple_of(begin, SLAB), size)
        for pair in range(pairs):
            write = pltpu.make_async_copy(
                full[pair].at[span, :], outs[pair].at[span, :], sem.at[len(writes)]
            )
            write.start()
            writes.append(write)

    sides = [
        (jnp.bitwise_xor(half, at // planes), jnp.bitwise_xor(plane, at % planes))
        for at in range(takes)
    ]
    for at, (side, spot) in enumerate(sides):
        begin = side * (planes * strips * rows) + spot * (strips * rows)
        for step in range(strips):
            put(at, step, begin + jnp.bitwise_xor(row, step) * rows)
        write_out(begin, strips * rows)
    for write in writes:
        write.wait()


def assemble(index, parts, pairs, planes, strips):
    takes = len(parts)
    out = like(2 * planes * parts[0].shape[0] // pairs, parts[0].shape[1])
    return pl.pallas_call(
        functools.partial(assemble_kernel, pairs=pairs, planes=planes, strips=strips),
        out_shape=[out] * pairs,
        in_specs=[pl.BlockSpec(memory_space=pltpu.SMEM)]
        + [pl.BlockSpec(memory_space=pltpu.VMEM)] * takes,
        out_specs=[pl.BlockSpec(memory_space=pltpu.HBM)] * pairs,
        scratch_shapes=[pltpu.VMEM(out.shape, FULL)] * pairs
        + [pltpu.SemaphoreType.DMA((takes * pairs,))],
        compiler_params=pltpu.CompilerParams(vmem_limit_bytes=VMEM_BYTES),
        cost_estimate=pl.CostEstimate(
            flops=0, bytes_accessed=pairs * out.size * 6, transcendentals=0
        ),
    )(index, *parts)


class Near:
    def __init__(self, value):
        self.value = value


def like(*shape, dtype=FULL):
    return jax.ShapeDtypeStruct(shape, dtype)


def low(*shape):
    return like(*shape, dtype=LOW)


def call(kernel, outs, scratch, span, index, *args):
    near_in = [isinstance(arg, Near) for arg in args]
    near_out = [isinstance(out, Near) for out in outs]
    args = [arg.value if isinstance(arg, Near) else arg for arg in args]
    outs = [out.value if isinstance(out, Near) else out for out in outs]
    takes, gives = (len(args), len(outs))
    far_in = [at for at in range(takes) if not near_in[at]]
    far_out = [at for at in range(gives) if not near_out[at]]

    def body(at_ref, *refs):
        given, refs = (list(refs[:takes]), refs[takes:])
        made, refs = (list(refs[:gives]), refs[gives:])
        rest = refs[len(far_in) + len(far_out) :]
        reads, writes = ({}, {})
        if far_in:
            in_sem = rest[-1]
            rest = rest[:-1]
        if far_out:
            out_sem = rest[-1]
            rest = rest[:-1]
        for place, at in enumerate(far_in):
            reads[at] = pltpu.make_async_copy(given[at], refs[place], in_sem.at[place])
            given[at] = refs[place]
        for place, at in enumerate(far_out):
            mirror = refs[len(far_in) + place]
            writes[at] = pltpu.make_async_copy(mirror, made[at], out_sem.at[place])
            made[at] = mirror
        for read in reads.values():
            read.start()
        started = []

        def need(*wanted):
            for at in list(reads):
                if any(given[at] is ref for ref in wanted):
                    reads.pop(at).wait()

        def send(*ready):
            for at in list(writes):
                if any(made[at] is ref for ref in ready):
                    started.append(writes.pop(at))
                    started[-1].start()

        kernel(need, send, at_ref, *given, *made, *rest)
        need(*given)
        send(*made)
        for write in started:
            write.wait()

    moved = sum(arg.size * arg.dtype.itemsize for arg in args)
    moved += sum(out.size * out.dtype.itemsize for out in outs)
    spaces = {True: pltpu.VMEM, False: pltpu.HBM}
    return pl.pallas_call(
        body,
        out_shape=outs,
        in_specs=[pl.BlockSpec(memory_space=pltpu.SMEM)]
        + [pl.BlockSpec(memory_space=spaces[near]) for near in near_in],
        out_specs=[pl.BlockSpec(memory_space=spaces[near]) for near in near_out],
        scratch_shapes=[pltpu.VMEM(args[at].shape, args[at].dtype) for at in far_in]
        + [pltpu.VMEM(outs[at].shape, outs[at].dtype) for at in far_out]
        + [pltpu.VMEM(shape, FULL) for shape in scratch]
        + [pltpu.SemaphoreType.DMA((len(far_out),))] * bool(far_out)
        + [pltpu.SemaphoreType.DMA((len(far_in),))] * bool(far_in),
        compiler_params=pltpu.CompilerParams(vmem_limit_bytes=VMEM_BYTES),
        cost_estimate=pl.CostEstimate(
            flops=int(span * 1e9), bytes_accessed=moved, transcendentals=0
        ),
    )(index, *args)


def edges(parity_edges):
    size = lax.axis_size("row")
    inner = [(at, at ^ 1) for at in range(size)]
    outer = [(at, at + 1) for at in range(1, size - 1, 2)]
    outer = outer + [(to, at) for at, to in outer]
    return (
        lax.ppermute(parity_edges[0], "row", inner),
        lax.ppermute(parity_edges[1], "row", outer),
    )


def exchange(pieces, axis):
    return lax.all_to_all(pieces, axis, 0, 0, tiled=True)


def swap(field):
    return lax.ppermute(field, "half", [(0, 1), (1, 0)])


def steps_of(value, axis, step):
    size = lax.axis_size(axis)
    return lax.ppermute(value, axis, [(at, at ^ step) for at in range(size)])


def share(parts, axis):
    return [parts[0]] + [steps_of(parts[at], axis, at) for at in range(1, len(parts))]


def share_same(part, axis):
    size = lax.axis_size(axis)
    return [part] + [steps_of(part, axis, at) for at in range(1, size)]


def pair_outer(index, *pairs):
    size = lax.axis_size("im")
    first = pairs[0][0].value if isinstance(pairs[0][0], Near) else pairs[0][0]
    width = first.shape[1]
    rows = width // 2 // size * len(pairs)
    return list(
        call(
            functools.partial(pair_outer_kernel, pairs=len(pairs), parts=size),
            [Near(low(rows, width))] * size,
            [],
            1.0 + 1.5 * len(pairs),
            index,
            *[ref for pair in pairs for ref in pair],
        )
    )


def sum_split(index, pieces, pairs):
    size = lax.axis_size("row")
    rows, width = pieces[0].shape
    return list(
        call(
            functools.partial(
                sum_split_kernel,
                pairs=pairs,
                parts=size,
                pieces=len(pieces),
            ),
            [Near(low(rows // size, width))] * size,
            [(rows, width)],
            1.0,
            index,
            *[Near(piece) for piece in pieces],
        )
    )


def add_low(pieces):
    total = pieces[0].astype(FULL)
    for piece in pieces[1:]:
        total = total + piece.astype(FULL)
    return total.astype(LOW)


def sum_far(left, right, axes):
    part = jnp.einsum("tm,tc->mc", left, right, preferred_element_type=FULL)
    return lax.psum(part, axes)


def shards(
    x_in,
    pre_reduce,
    pre_conv,
    pre_expand,
    pre_mid_gain,
    pre_mid_shift,
    pre_out_gain,
    pre_out_shift,
    post_reduce,
    post_conv,
    post_expand,
    post_mid_gain,
    post_mid_shift,
    post_out_gain,
    post_out_shift,
    read_weight,
    read_bias,
    cotangent,
):
    count, strip, side, width = x_in.shape
    strips = lax.axis_size("row")
    tokens = count * strip * side
    cols = side // 2
    rows = strip // 2
    slabs = count * rows
    padded = slabs * SLAB
    small = slabs * cols
    block = -(-small // SLAB) * SLAB
    features = read_weight.shape[1]
    x_low = x_in.reshape(tokens, width)
    pre_out_g, pre_out_s = (pre_out_gain[None], pre_out_shift[None])
    post_out_g, post_out_s = (post_out_gain[None], post_out_shift[None])
    pre_edge = Near(low(count, side, width))
    post_edge = Near(low(count, SLAB, width))
    index = jnp.stack([lax.axis_index("half"), lax.axis_index("im"), lax.axis_index("row")])
    quick = lax.axis_size("im") == 4 and strips == 4
    if quick:
        x_far = swap(x_low)

    first, edge_a, edge_b, normed_a, factor_a = call(
        pre_reduce_kernel,
        [Near(low(tokens, width)), pre_edge, pre_edge, like(tokens, width), like(tokens, LANES)],
        [(tokens, width)],
        6.0,
        index,
        x_low,
        pre_reduce,
        pre_mid_gain,
        pre_mid_shift,
    )
    got_a, got_b = edges((edge_a, edge_b))
    if quick:
        got_a, got_b, x_far = tie(got_a, got_b, x_far)
    (
        second,
        normed_b,
        factor_b,
        normed_c,
        factor_c,
        summed,
        pooled,
        post_first,
        edge_a,
        edge_b,
        post_normed_a,
        post_factor_a,
        pad,
    ) = call(
        pre_rest_kernel,
        [
            low(tokens, width),
            like(tokens, width),
            like(tokens, LANES),
            like(tokens, width),
            like(tokens, LANES),
            like(tokens, width),
            Near(like(padded, width)),
            Near(low(padded, width)),
            post_edge,
            post_edge,
            like(padded, width),
            like(padded, LANES),
            like(count, strip + 2, side, width),
        ],
        [(tokens, width), (side * width // LANES, LANES), (padded, width)],
        9.0,
        index,
        x_low,
        Near(first),
        Near(got_a),
        Near(got_b),
        pre_conv,
        pre_expand,
        pre_mid_gain,
        pre_mid_shift,
        pre_out_g,
        pre_out_s,
        post_reduce,
        post_mid_gain,
        post_mid_shift,
    )
    got_a, got_b = edges((edge_a, edge_b))
    if quick:
        second_far = swap(second)
        got_a, got_b, second_far = tie(got_a, got_b, second_far)
    (
        block_two,
        left_in,
        left_second,
        post_normed_b,
        post_factor_b,
        post_normed_c,
        post_factor_c,
        post_summed,
        post_pad,
    ) = call(
        functools.partial(post_rest_kernel, cols=cols),
        [
            Near(low(small, width)),
            low(block, width),
            low(block, width),
            like(padded, width),
            like(padded, LANES),
            like(padded, width),
            like(padded, LANES),
            like(padded, width),
            like(count, rows + 2, SLAB, width),
        ],
        [(padded, width), (padded, width), (block, width)],
        6.0,
        index,
        Near(pooled),
        Near(post_first),
        Near(got_a),
        Near(got_b),
        post_conv,
        post_expand,
        post_mid_gain,
        post_mid_shift,
        post_out_g,
        post_out_s,
    )
    whole = lax.all_gather(block_two, "row", axis=0, tiled=True)
    readout, grad_pre, terms, d_read_b = call(
        functools.partial(readout_kernel, strips=strips),
        [
            like(*cotangent.shape, dtype=LOW),
            Near(low(strips * small, features)),
            Near(low(strips * small, width)),
            like(1, features),
        ],
        [(strips * small, features), (strips * small, features)],
        6.0,
        index,
        Near(whole),
        read_weight,
        read_bias[None],
        cotangent,
    )
    terms = exchange(terms.reshape(strips, small, width), "row")
    if quick:
        parts = pair_outer(
            index, (Near(whole), Near(swap(whole)), Near(grad_pre), Near(swap(grad_pre)))
        )
        terms, parts[0] = tie(terms, parts[0])
        read_parts = share(parts, "im")
    post_gs, post_ge, post_gc, edge_a, edge_b, post_small_b = call(
        functools.partial(post_back_kernel, cols=cols),
        [
            Near(like(padded, width)),
            Near(low(block, width)),
            Near(low(padded, width)),
            post_edge,
            post_edge,
            like(4, width),
        ],
        [(block, width), (padded, width), (padded, width), (padded, width)],
        5.0,
        index,
        Near(terms),
        post_expand,
        post_mid_gain,
        post_mid_shift,
        post_out_g,
        post_normed_b,
        post_factor_b,
        post_normed_c,
        post_factor_c,
        post_summed,
    )
    got_a, got_b = edges((edge_a, edge_b))
    if quick:
        left_in_far, left_second_far, ge_far = (swap(left_in), swap(left_second), swap(post_ge))
        got_a, got_b, left_in_far, left_second_far, ge_far, *read_parts = tie(
            got_a, got_b, left_in_far, left_second_far, ge_far, *read_parts
        )
        read_part = add_low(read_parts)
    (
        post_gr,
        pre_gs,
        pre_ge,
        pre_gc,
        edge_a,
        edge_b,
        post_small_a,
        pre_small_b,
    ) = call(
        functools.partial(middle_back_kernel, cols=cols),
        [
            Near(low(block, width)),
            like(tokens, width),
            Near(low(tokens, width)),
            Near(low(tokens, width)),
            pre_edge,
            pre_edge,
            like(11, width),
            like(4, width),
        ],
        [
            (count, rows + 2, SLAB, width),
            (9, 8, width),
            (padded, width),
            (side * width // LANES, LANES),
            (tokens, width),
            (2, 8, width),
            (padded, width),
            (block, width),
        ],
        10.0,
        index,
        Near(post_gc),
        Near(got_a),
        Near(got_b),
        post_pad,
        post_conv,
        post_reduce,
        post_mid_gain,
        post_mid_shift,
        post_normed_a,
        post_factor_a,
        Near(post_gs),
        pre_expand,
        pre_mid_gain,
        pre_mid_shift,
        pre_out_g,
        normed_b,
        factor_b,
        normed_c,
        factor_c,
        summed,
    )
    got_a, got_b = edges((edge_a, edge_b))
    if quick:
        read_total = lax.all_gather(read_part, ("half", "im"), axis=0, tiled=True)
        pre_ge_far = swap(pre_ge)
        post_parts = pair_outer(
            index,
            (left_in, left_in_far, Near(post_gr), Near(swap(post_gr))),
            (left_second, left_second_far, Near(post_ge), Near(ge_far)),
        )
        got_a, got_b, pre_ge_far, post_parts[0], read_total = tie(
            got_a, got_b, pre_ge_far, post_parts[0], read_total
        )
        post_parts = share(post_parts, "im")
    pre_gr, pre_small_a = call(
        pre_back_kernel,
        [Near(low(tokens, width)), like(11, width)],
        [
            (count, strip + 2, side, width),
            (9, 8, width),
            (2, 8, width),
        ],
        6.0,
        index,
        Near(pre_gc),
        Near(got_a),
        Near(got_b),
        pad,
        pre_conv,
        pre_mid_gain,
        pre_mid_shift,
        normed_a,
        factor_a,
    )
    sums = jnp.concatenate([pre_small_a, pre_small_b, post_small_a, post_small_b, d_read_b])
    if quick:
        far = swap(pre_gr)
        sums = sums + swap(sums)
        far, sums = tie(far, sums)
        parts = pair_outer(
            index,
            (second, second_far, Near(pre_ge), Near(pre_ge_far)),
            (x_low, x_far, Near(pre_gr), Near(far)),
        )
        parts[0], *post_parts = tie(parts[0], *post_parts)
        parts = share(parts, "im")
        post_parts = share(sum_split(index, post_parts, 2), "row")
        sums = sums + steps_of(sums, "im", 1)
        grad_in = pre_gs + jnp.einsum("tm,cm->tc", pre_gr, pre_reduce, preferred_element_type=FULL)
        grad_in = grad_in.astype(LOW)
        sums, grad_in, read_total, *rest = tie(
            sums, grad_in, read_total.astype(FULL), *parts, *post_parts
        )
        parts, post_parts = (rest[:4], rest[4:])
        sums = sums + steps_of(sums, "im", 2)
        parts = share(sum_split(index, parts, 2), "row")
        post_parts = share_same(add_low(post_parts), "row")
        sums, *rest = tie(sums, *parts, *post_parts)
        parts, post_parts = (rest[:4], rest[4:])
        read_bias_g = sums[30]
        sums = sums + steps_of(sums, "row", 1)
        post_parts = share_same(jnp.concatenate(post_parts, axis=0), "im")
        parts = share_same(add_low(parts), "row")
        sums, *rest = tie(sums, *parts, *post_parts)
        parts, post_parts = (rest[:4], rest[4:])
        sums = sums + steps_of(sums, "row", 2)
        parts = share_same(jnp.concatenate(parts, axis=0), "im")
        post_parts = post_parts + [swap(part) for part in post_parts]
        post_reduce_g, post_expand_g = assemble(index, post_parts, 2, 4, strips)
        parts = parts + [swap(part) for part in parts]
        pre_expand_g, pre_reduce_g = assemble(index, parts, 2, 4, strips)
    else:
        axes = IMG + ("row",)
        post_reduce_g = sum_far(left_in, post_gr, axes)
        post_expand_g = sum_far(left_second, post_ge, axes)
        pre_expand_g = sum_far(second, pre_ge, axes)
        pre_reduce_g = sum_far(x_low, pre_gr, axes)
        read_total = sum_far(whole, grad_pre, IMG)
        read_bias_g = lax.psum(sums[30], IMG)
        sums = lax.psum(sums, axes)
        grad_in = pre_gs + jnp.einsum("tm,cm->tc", pre_gr, pre_reduce, preferred_element_type=FULL)
        grad_in = grad_in.astype(LOW)

    def small_grads(part):
        return (
            part[:9].reshape(3, 3, width),
            jnp.stack([part[9], part[11]]),
            jnp.stack([part[10], part[12]]),
            part[13],
            part[14],
        )

    pre_conv_g, pre_gain_g, pre_shift_g, pre_og_g, pre_os_g = small_grads(sums[:15])
    post_conv_g, post_gain_g, post_shift_g, post_og_g, post_os_g = small_grads(sums[15:30])
    return (
        readout,
        grad_in.reshape(x_in.shape),
        pre_reduce_g,
        pre_conv_g,
        pre_expand_g,
        pre_gain_g,
        pre_shift_g,
        pre_og_g,
        pre_os_g,
        post_reduce_g,
        post_conv_g,
        post_expand_g,
        post_gain_g,
        post_shift_g,
        post_og_g,
        post_os_g,
        read_total,
        read_bias_g,
    )


def solution(mesh):
    images, strips = mesh.devices.shape
    split = jax.sharding.Mesh(
        mesh.devices.reshape(images // 2, 2, strips), ("im", "half", "row")
    )
    return jax.shard_map(
        shards,
        mesh=split,
        in_specs=(P(IMG, "row", None, None),)
        + (P(),) * 14
        + (P(None, "row"), P("row"), P(IMG, None, None, "row")),
        out_specs=(P(IMG, None, None, "row"), P(IMG, "row", None, None))
        + (P(),) * 14
        + (P(None, "row"), P("row")),
        check_vma=False,
    )
```

```python
import functools

import jax
import jax.numpy as jnp
from jax import lax
from jax.experimental import pallas as pl
from jax.experimental.pallas import tpu as pltpu
from jax.sharding import PartitionSpec as P

EPSILON = 1e-06
SQRT_HALF = 0.7071067811865476
INV_SQRT_TWO_PI = 0.3989422804014327
LOW = jnp.bfloat16
FULL = jnp.float32
IMG = ("im", "half")
TILE = 256
SLAB = 16
LANES = 128
VMEM_BYTES = 60 * 1024 * 1024


def tie(*values):
    return lax.optimization_barrier(values)


def norm(value):
    centred = value - jnp.mean(value, axis=-1, keepdims=True)
    factor = lax.rsqrt(jnp.mean(centred * centred, axis=-1, keepdims=True) + EPSILON)
    return (centred * factor, factor)


def norm_back(grad, normed, factor, gain):
    scaled = grad * gain
    return factor * (
        scaled
        - jnp.mean(scaled, axis=-1, keepdims=True)
        - normed * jnp.mean(scaled * normed, axis=-1, keepdims=True)
    )


def gate(value):
    return 0.5 * jnp.tanh(0.5 * value) + 0.5


def silu(value):
    return value * gate(value)


def silu_back(grad, value):
    sigma = gate(value)
    return grad * sigma * (1.0 + value * (1.0 - sigma))


def flip(place, step):
    bit = 1
    while bit <= step:
        if step & bit:
            place = place + bit - 2 * bit * ((place // bit) % 2)
        bit *= 2
    return place


def wide(factor):
    return jnp.broadcast_to(factor, (factor.shape[0], LANES))


def fold(value):
    return jnp.sum(value.reshape(-1, 8, value.shape[-1]), axis=0)


def live(rows, cols):
    at = lax.broadcasted_iota(jnp.int32, (rows, 1), 0)
    return lax.rem(at, SLAB) < cols


def from_left(value):
    at = lax.broadcasted_iota(jnp.int32, (value.shape[0], 1), 0)
    return jnp.where(at == 0, 0.0, pltpu.roll(value, 1, 0))


def from_right(value):
    last = value.shape[0] - 1
    at = lax.broadcasted_iota(jnp.int32, (value.shape[0], 1), 0)
    return jnp.where(at == last, 0.0, pltpu.roll(value, last, 0))


def matmul(left_ref, right_ref, out_ref):
    @pl.loop(0, right_ref.shape[1] // TILE)
    def _(at):
        cols = pl.ds(pl.multiple_of(at * TILE, TILE), TILE)
        out_ref[:, cols] = jnp.dot(
            left_ref[...].astype(LOW), right_ref[:, cols], preferred_element_type=FULL
        )


def matmul_back(left_ref, right_ref, out_ref):
    @pl.loop(0, right_ref.shape[0] // TILE)
    def _(at):
        cols = pl.ds(pl.multiple_of(at * TILE, TILE), TILE)
        out_ref[:, cols] = lax.dot_general(
            left_ref[...].astype(LOW),
            right_ref[cols, :],
            (((1,), (1,)), ((), ())),
            preferred_element_type=FULL,
        ).astype(out_ref.dtype)


def rows_of(at, size):
    return pl.ds(pl.multiple_of(at * size, SLAB), size)


def fill_halo(at_ref, pad_ref, low_ref, got_a_ref, got_b_ref):
    count, rows, cols, width = pad_ref.shape
    rows = rows - 2
    even = lax.rem(at_ref[2], 2) == 0
    for image in range(count):
        got_a, got_b = (got_a_ref[image].astype(FULL), got_b_ref[image].astype(FULL))
        pad_ref[image, 0] = jnp.where(even, got_b, got_a)
        pad_ref[image, rows + 1] = jnp.where(even, got_a, got_b)

    size = cols if cols % SLAB == 0 else 2 * cols
    per = size // cols
    each = rows // per

    @pl.loop(0, count * each)
    def _(at):
        part = low_ref[rows_of(at, size), :].astype(FULL).reshape(per, cols, width)
        pad_ref[at // each, pl.ds(1 + per * lax.rem(at, each), per)] = part


def set_edges(at_ref, edge_a_ref, edge_b_ref, image, head, tail):
    even = lax.rem(at_ref[2], 2) == 0
    edge_a_ref[image] = jnp.where(even, tail, head).astype(LOW)
    edge_b_ref[image] = jnp.where(even, head, tail).astype(LOW)


def conv_row(pad_ref, taps, image, row):
    lines = [pad_ref[image, row + top] for top in range(3)]
    sums = [
        lines[0] * taps[left] + lines[1] * taps[3 + left] + lines[2] * taps[6 + left]
        for left in range(3)
    ]
    return from_left(sums[0]) + sums[1] + from_right(sums[2])


def conv_back_row(pad_ref, grad_ref, taps, taps_ref, image, row):
    lines = [grad_ref[image, row + top] for top in range(3)]
    sums = [
        lines[2] * taps[left] + lines[1] * taps[3 + left] + lines[0] * taps[6 + left]
        for left in range(3)
    ]
    shifted = [from_right(lines[1]), lines[1], from_left(lines[1])]
    for top in range(3):
        source = pad_ref[image, row + top]
        for left in range(3):
            taps_ref[3 * top + left] += fold(source * shifted[left])
    return from_right(sums[0]) + sums[1] + from_left(sums[2])


def pack(compact, source, out_ref, cols):
    compact[...] = jnp.zeros(compact.shape, FULL)
    for at in range(source.shape[0] // SLAB):
        compact[pl.ds(at * cols, cols), :] = source[pl.ds(at * SLAB, cols), :]
    out_ref[...] = compact[...].astype(LOW)


def narrow(pair, value):
    side = value.shape[0]
    parts = []
    for at in range(value.shape[1] // LANES):
        pair[pl.ds(at * side, side), :] = value[:, at * LANES : (at + 1) * LANES]
        parts.append(
            pair[pl.ds(at * side, side // 2, stride=2), :]
            + pair[pl.ds(at * side + 1, side // 2, stride=2), :]
        )
    return jnp.concatenate(parts, axis=1)


def widen(pair, value):
    cols = value.shape[0]
    parts = []
    for at in range(value.shape[1] // LANES):
        part = value[:, at * LANES : (at + 1) * LANES]
        pair[pl.ds(2 * cols * at, cols, stride=2), :] = part
        pair[pl.ds(2 * cols * at + 1, cols, stride=2), :] = part
        parts.append(pair[pl.ds(2 * cols * at, 2 * cols), :])
    return jnp.concatenate(parts, axis=1)


def tap_rows(conv_ref):
    lines = [conv_ref[top].astype(FULL) for top in range(3)]
    return [lines[at // 3][at % 3 : at % 3 + 1] for at in range(9)]


def finish(small_ref, sums_ref, at, place):
    small_ref[pl.ds(place, 1), :] = jnp.sum(sums_ref[at], axis=0, keepdims=True)


def pre_reduce_kernel(
    need,
    send,
    at_ref,
    x_ref, w_ref, gain_ref, shift_ref, first_ref, edge_a_ref, edge_b_ref, normed_ref, factor_ref, red
):
    count, side, width = edge_a_ref.shape
    size = 2 * side
    steps = x_ref.shape[0] // size
    need(x_ref, w_ref)
    matmul(x_ref, w_ref, red)
    need(gain_ref, shift_ref)
    gain, shift = (gain_ref[pl.ds(0, 1), :], shift_ref[pl.ds(0, 1), :])

    @pl.loop(0, steps)
    def _(at):
        rows = rows_of(at, size)
        normed, factor = norm(red[rows, :])
        normed_ref[rows, :] = normed
        factor_ref[rows, :] = wide(factor)
        first_ref[rows, :] = silu(normed * gain + shift).astype(LOW)

    each = steps // count
    for image in range(count):
        head = first_ref[pl.ds(image * each * size, size), :].astype(FULL)
        tail = first_ref[pl.ds((image * each + each - 1) * size, size), :].astype(FULL)
        set_edges(at_ref, edge_a_ref, edge_b_ref, image, head[:side], tail[side:])


def pre_rest_kernel(
    need,
    send,
    at_ref,
    x_ref,
    first_ref,
    got_a_ref,
    got_b_ref,
    conv_ref,
    expand_ref,
    gain_ref,
    shift_ref,
    out_gain_ref,
    out_shift_ref,
    reduce_ref,
    post_gain_ref,
    post_shift_ref,
    second_ref,
    normed_b_ref,
    factor_b_ref,
    normed_c_ref,
    factor_c_ref,
    summed_ref,
    pooled_ref,
    post_first_ref,
    edge_a_ref,
    edge_b_ref,
    post_normed_ref,
    post_factor_ref,
    pad,
    exp,
    pair,
    red,
):
    count, strip, side, width = pad.shape
    strip = strip - 2
    size = 2 * side
    each = strip // 2
    need(first_ref, got_a_ref, got_b_ref)
    fill_halo(at_ref, pad, first_ref, got_a_ref, got_b_ref)
    need(conv_ref, gain_ref, shift_ref)
    send(pad)
    taps = tap_rows(conv_ref)
    gain, shift = (gain_ref[pl.ds(1, 1), :], shift_ref[pl.ds(1, 1), :])

    @pl.loop(0, count * each)
    def _(at):
        rows = rows_of(at, size)
        image, row = (at // each, 2 * lax.rem(at, each))
        conv = jnp.concatenate(
            [conv_row(pad, taps, image, row), conv_row(pad, taps, image, row + 1)], axis=0
        )
        normed, factor = norm(conv)
        normed_b_ref[rows, :] = normed
        factor_b_ref[rows, :] = wide(factor)
        second_ref[rows, :] = silu(normed * gain + shift).astype(LOW)

    send(second_ref, normed_b_ref, factor_b_ref)
    need(expand_ref)
    matmul(second_ref, expand_ref, exp)
    need(x_ref, out_gain_ref, out_shift_ref)
    out_gain, out_shift = (out_gain_ref[...], out_shift_ref[...])
    cols = side // 2
    for at in range(count * each):
        rows = pl.ds(at * size, size)
        normed, factor = norm(exp[rows, :])
        normed_c_ref[rows, :] = normed
        factor_c_ref[rows, :] = wide(factor)
        summed = x_ref[rows, :].astype(FULL) + normed * out_gain + out_shift
        summed_ref[rows, :] = summed
        block = silu(summed)
        half = narrow(pair, block[:side] + block[side:])
        pooled_ref[pl.ds(at * SLAB, cols), :] = 0.25 * half
        pooled_ref[pl.ds(at * SLAB + cols, SLAB - cols), :] = jnp.zeros(
            (SLAB - cols, width), FULL
        )
    send(normed_c_ref, factor_c_ref, summed_ref)
    need(reduce_ref, post_gain_ref, post_shift_ref)
    matmul(pooled_ref, reduce_ref, red)
    normed, factor = norm(red[...])
    post_normed_ref[...] = normed
    post_factor_ref[...] = wide(factor)
    first = silu(normed * post_gain_ref[pl.ds(0, 1), :] + post_shift_ref[pl.ds(0, 1), :])
    post_first_ref[...] = jnp.where(live(red.shape[0], cols), first, 0.0).astype(LOW)
    for image in range(count):
        head = post_first_ref[pl.ds(image * each * SLAB, SLAB), :].astype(FULL)
        tail = post_first_ref[pl.ds((image * each + each - 1) * SLAB, SLAB), :].astype(FULL)
        set_edges(at_ref, edge_a_ref, edge_b_ref, image, head, tail)


def post_rest_kernel(
    need,
    send,
    at_ref,
    pooled_ref,
    first_ref,
    got_a_ref,
    got_b_ref,
    conv_ref,
    expand_ref,
    gain_ref,
    shift_ref,
    out_gain_ref,
    out_shift_ref,
    block_ref,
    left_in_ref,
    left_second_ref,
    normed_b_ref,
    factor_b_ref,
    normed_c_ref,
    factor_c_ref,
    summed_ref,
    pad,
    second,
    exp,
    compact,
    *,
    cols
):
    count, rows, _, width = pad.shape
    rows = rows - 2
    small = block_ref.shape[0]
    need(first_ref, got_a_ref, got_b_ref)
    fill_halo(at_ref, pad, first_ref, got_a_ref, got_b_ref)
    send(pad)
    need(conv_ref, gain_ref, shift_ref, pooled_ref)
    taps = tap_rows(conv_ref)
    gain, shift = (gain_ref[pl.ds(1, 1), :], shift_ref[pl.ds(1, 1), :])

    @pl.loop(0, count * rows)
    def _(at):
        place = rows_of(at, SLAB)
        normed, factor = norm(conv_row(pad, taps, at // rows, lax.rem(at, rows)))
        normed_b_ref[place, :] = normed
        factor_b_ref[place, :] = wide(factor)
        second[place, :] = silu(normed * gain + shift)

    send(normed_b_ref, factor_b_ref)
    need(expand_ref)
    matmul(second, expand_ref, exp)
    need(out_gain_ref, out_shift_ref)
    normed, factor = norm(exp[...])
    normed_c_ref[...] = normed
    factor_c_ref[...] = wide(factor)
    summed = pooled_ref[...] + normed * out_gain_ref[...] + out_shift_ref[...]
    summed_ref[...] = summed
    exp[...] = silu(summed)
    compact[...] = jnp.zeros(compact.shape, FULL)
    for at in range(count * rows):
        compact[pl.ds(at * cols, cols), :] = exp[pl.ds(at * SLAB, cols), :]
    block_ref[...] = compact[pl.ds(0, small), :].astype(LOW)
    send(block_ref, normed_c_ref, factor_c_ref, summed_ref)
    pack(compact, pooled_ref, left_in_ref, cols)
    pack(compact, second, left_second_ref, cols)


def readout_kernel(
    need,
    send,
    at_ref,
    whole_ref,
    w_ref,
    bias_ref,
    cot_ref,
    out_ref,
    grad_ref,
    *refs,
    strips
):
    slots, (bias_grad_ref, cot, out, terms_ref) = (refs[:strips], refs[strips:])
    images, lines, cols, _ = cot_ref.shape
    rows = lines // strips
    need(cot_ref)
    for at in range(images * lines):
        strip, image, row = (at // (images * rows), at // rows % images, at % rows)
        cot[pl.ds(at * cols, cols), :] = cot_ref[image, strip * rows + row].astype(FULL)
    need(whole_ref, w_ref, bias_ref)

    @pl.loop(0, w_ref.shape[1] // TILE)
    def _(at):
        lanes = pl.ds(pl.multiple_of(at * TILE, TILE), TILE)
        act = jnp.dot(whole_ref[...], w_ref[:, lanes], preferred_element_type=FULL)
        act = act + bias_ref[:, lanes]
        cdf = 0.5 * (1.0 + lax.erf(act * SQRT_HALF))
        density = jnp.exp(-0.5 * act * act) * INV_SQRT_TWO_PI
        out[:, lanes] = act * cdf
        grad = (cot[:, lanes] * (cdf + act * density)).astype(LOW)
        grad_ref[:, lanes] = grad
        bias_grad_ref[:, lanes] = jnp.sum(grad.astype(FULL), axis=0, keepdims=True)

    send(grad_ref, bias_grad_ref)
    matmul_back(grad_ref, w_ref, terms_ref)
    small = slots[0].shape[0]
    for step in range(strips):
        begin = pl.multiple_of(flip(at_ref[2], step) * small, 8)
        slots[step][...] = terms_ref[pl.ds(begin, small), :].astype(LOW)
    for at in range(images * lines):
        strip, image, row = (at // (images * rows), at // rows % images, at % rows)
        out_ref[image, strip * rows + row] = out[pl.ds(at * cols, cols), :].astype(LOW)


def post_back_kernel(
    need,
    send,
    at_ref,
    *refs,
    cols,
    strips
):
    pieces, refs = (refs[:strips], refs[strips:])
    (
    expand_ref,
    gain_ref,
    shift_ref,
    out_gain_ref,
    normed_b_ref,
    factor_b_ref,
    normed_c_ref,
    factor_c_ref,
    summed_ref,
    grad_sum_ref,
    grad_exp_ref,
    grad_conv_ref,
    edge_a_ref,
    edge_b_ref,
    small_ref,
    compact,
    spread_out,
    exp,
    sec,
    ) = refs
    count = edge_a_ref.shape[0]
    tokens, width = grad_sum_ref.shape
    each = tokens // SLAB // count
    need(*pieces)
    total = pieces[0][...].astype(FULL)
    for piece in pieces[1:]:
        total = total + piece[...].astype(FULL)
    compact[...] = jnp.zeros(compact.shape, FULL)
    compact[pl.ds(0, total.shape[0]), :] = total
    spread_out[...] = jnp.zeros((tokens, width), FULL)
    for at in range(tokens // SLAB):
        spread_out[pl.ds(at * SLAB, cols), :] = compact[pl.ds(at * cols, cols), :]
    need(summed_ref, normed_c_ref, factor_c_ref, out_gain_ref)
    grad_sum = silu_back(spread_out[...], summed_ref[...])
    grad_sum_ref[...] = grad_sum
    normed = normed_c_ref[...]
    exp[...] = norm_back(grad_sum, normed, factor_c_ref[:, :1], out_gain_ref[...])
    small_ref[pl.ds(2, 1), :] = jnp.sum(grad_sum * normed, axis=0, keepdims=True)
    small_ref[pl.ds(3, 1), :] = jnp.sum(grad_sum, axis=0, keepdims=True)
    pack(compact, exp, grad_exp_ref, cols)
    send(grad_sum_ref, grad_exp_ref)
    need(expand_ref)
    matmul_back(exp, expand_ref, sec)
    need(gain_ref, shift_ref, normed_b_ref, factor_b_ref)
    gain, shift = (gain_ref[pl.ds(1, 1), :], shift_ref[pl.ds(1, 1), :])
    normed = normed_b_ref[...]
    grad = silu_back(sec[...], normed * gain + shift)
    grad_conv_ref[...] = norm_back(grad, normed, factor_b_ref[:, :1], gain).astype(LOW)
    small_ref[pl.ds(0, 1), :] = jnp.sum(grad * normed, axis=0, keepdims=True)
    small_ref[pl.ds(1, 1), :] = jnp.sum(grad, axis=0, keepdims=True)
    for image in range(count):
        head = grad_conv_ref[pl.ds(image * each * SLAB, SLAB), :].astype(FULL)
        tail = grad_conv_ref[pl.ds((image * each + each - 1) * SLAB, SLAB), :].astype(FULL)
        set_edges(at_ref, edge_a_ref, edge_b_ref, image, head, tail)


def middle_back_kernel(
    need,
    send,
    at_ref,
    grad_conv_ref,
    got_a_ref,
    got_b_ref,
    pad,
    post_conv_ref,
    post_reduce_ref,
    post_gain_ref,
    post_shift_ref,
    post_normed_ref,
    post_factor_ref,
    post_grad_sum_ref,
    expand_ref,
    gain_ref,
    shift_ref,
    out_gain_ref,
    normed_b_ref,
    factor_b_ref,
    normed_c_ref,
    factor_c_ref,
    summed_ref,
    post_grad_red_ref,
    grad_sum_ref,
    grad_exp_ref,
    pre_grad_conv_ref,
    edge_a_ref,
    edge_b_ref,
    post_small_ref,
    small_ref,
    grad_pad,
    taps_sum,
    grad_in,
    pair,
    sec,
    sums,
    post_red,
    compact,
    *,
    cols
):
    count, side, width = edge_a_ref.shape
    need(grad_conv_ref, got_a_ref, got_b_ref)
    fill_halo(at_ref, grad_pad, grad_conv_ref, got_a_ref, got_b_ref)
    need(pad, post_conv_ref)
    need(post_gain_ref, post_shift_ref, post_normed_ref, post_factor_ref)
    taps = tap_rows(post_conv_ref)
    taps_sum[...] = jnp.zeros_like(taps_sum)
    sums[...] = jnp.zeros_like(sums)
    gain, shift = (post_gain_ref[pl.ds(0, 1), :], post_shift_ref[pl.ds(0, 1), :])
    each = post_grad_sum_ref.shape[0] // SLAB // count

    @pl.loop(0, count * each)
    def _(at):
        place = rows_of(at, SLAB)
        grad = conv_back_row(pad, grad_pad, taps, taps_sum, at // each, lax.rem(at, each))
        normed = post_normed_ref[place, :]
        grad = jnp.where(live(SLAB, cols), silu_back(grad, normed * gain + shift), 0.0)
        sums[0] += fold(grad * normed)
        sums[1] += fold(grad)
        post_red[place, :] = norm_back(grad, normed, post_factor_ref[place, :1], gain)

    for at in range(9):
        finish(post_small_ref, taps_sum, at, at)
    finish(post_small_ref, sums, 0, 9)
    finish(post_small_ref, sums, 1, 10)
    pack(compact, post_red, post_grad_red_ref, cols)
    send(post_grad_red_ref, post_small_ref)
    need(post_reduce_ref)
    matmul_back(post_red, post_reduce_ref, grad_in)
    sums[...] = jnp.zeros_like(sums)
    size = 2 * side
    need(out_gain_ref, post_grad_sum_ref, summed_ref, normed_c_ref, factor_c_ref)
    out_gain = out_gain_ref[...]
    for at in range(count * each):
        rows = pl.ds(at * size, size)
        place = pl.ds(at * SLAB, cols)
        grad = 0.25 * (post_grad_sum_ref[place, :] + grad_in[place, :])
        grad = widen(pair, grad)
        grad = jnp.concatenate([grad, grad], axis=0)
        grad_sum = silu_back(grad, summed_ref[rows, :])
        grad_sum_ref[rows, :] = grad_sum
        normed = normed_c_ref[rows, :]
        sums[0] += fold(grad_sum * normed)
        sums[1] += fold(grad_sum)
        grad_exp_ref[rows, :] = norm_back(
            grad_sum, normed, factor_c_ref[rows, :1], out_gain
        ).astype(LOW)
    finish(small_ref, sums, 0, 2)
    finish(small_ref, sums, 1, 3)
    send(grad_sum_ref, grad_exp_ref)
    need(expand_ref)
    matmul_back(grad_exp_ref, expand_ref, sec)
    need(gain_ref, shift_ref, normed_b_ref, factor_b_ref)
    sums[...] = jnp.zeros_like(sums)
    gain_b, shift_b = (gain_ref[pl.ds(1, 1), :], shift_ref[pl.ds(1, 1), :])

    @pl.loop(0, count * each)
    def _(at):
        rows = rows_of(at, size)
        normed = normed_b_ref[rows, :]
        grad = silu_back(sec[rows, :], normed * gain_b + shift_b)
        sums[0] += fold(grad * normed)
        sums[1] += fold(grad)
        pre_grad_conv_ref[rows, :] = norm_back(
            grad, normed, factor_b_ref[rows, :1], gain_b
        ).astype(LOW)

    finish(small_ref, sums, 0, 0)
    finish(small_ref, sums, 1, 1)
    for image in range(count):
        head = pre_grad_conv_ref[pl.ds(image * each * size, size), :].astype(FULL)
        tail = pre_grad_conv_ref[pl.ds((image * each + each - 1) * size, size), :].astype(FULL)
        set_edges(at_ref, edge_a_ref, edge_b_ref, image, head[:side], tail[side:])


def pre_back_kernel(
    need,
    send,
    at_ref,
    grad_conv_ref,
    got_a_ref,
    got_b_ref,
    pad,
    conv_ref,
    gain_ref,
    shift_ref,
    normed_ref,
    factor_ref,
    grad_red_ref,
    small_ref,
    grad_pad,
    taps_sum,
    sums,
):
    count, strip, side, width = pad.shape
    strip = strip - 2
    size = 2 * side
    each = strip // 2
    need(grad_conv_ref, got_a_ref, got_b_ref)
    fill_halo(at_ref, grad_pad, grad_conv_ref, got_a_ref, got_b_ref)
    need(pad, conv_ref)
    need(gain_ref, shift_ref, normed_ref, factor_ref)
    taps = tap_rows(conv_ref)
    taps_sum[...] = jnp.zeros_like(taps_sum)
    sums[...] = jnp.zeros_like(sums)
    gain, shift = (gain_ref[pl.ds(0, 1), :], shift_ref[pl.ds(0, 1), :])

    @pl.loop(0, count * each)
    def _(at):
        rows = rows_of(at, size)
        image, row = (at // each, 2 * lax.rem(at, each))
        grad = jnp.concatenate(
            [
                conv_back_row(pad, grad_pad, taps, taps_sum, image, row),
                conv_back_row(pad, grad_pad, taps, taps_sum, image, row + 1),
            ],
            axis=0,
        )
        normed = normed_ref[rows, :]
        grad = silu_back(grad, normed * gain + shift)
        sums[0] += fold(grad * normed)
        sums[1] += fold(grad)
        grad_red_ref[rows, :] = norm_back(grad, normed, factor_ref[rows, :1], gain).astype(LOW)

    for at in range(9):
        finish(small_ref, taps_sum, at, at)
    finish(small_ref, sums, 0, 9)
    finish(small_ref, sums, 1, 10)


def pair_outer_kernel(need, send, at_ref, *refs, pairs, parts):
    takes = 4 * pairs
    outs = refs[takes:]
    half, plane = (at_ref[0], at_ref[1])
    rows = outs[0].shape[0] // pairs
    for pair in range(pairs):
        left, left_far, right, right_far = refs[4 * pair : 4 * pair + 4]
        need(left, left_far, right, right_far)
        for step in range(parts):
            begin = half * (rows * parts) + flip(plane, step) * rows
            lanes = pl.ds(pl.multiple_of(begin, LANES), rows)
            total = lax.dot_general(
                left[:, lanes], right[...], (((0,), (0,)), ((), ())), preferred_element_type=FULL
            ) + lax.dot_general(
                left_far[:, lanes],
                right_far[...],
                (((0,), (0,)), ((), ())),
                preferred_element_type=FULL,
            )
            outs[step][pl.ds(pair * rows, rows), :] = total.astype(LOW)
    send(*outs)


def sum_split_kernel(need, send, at_ref, *refs, pairs, parts, pieces, along=2):
    takes, outs = (refs[:pieces], refs[pieces : pieces + parts])
    total = refs[-1]
    need(*takes)
    value = takes[0][...].astype(FULL)
    for at in range(1, pieces):
        value = value + takes[at][...].astype(FULL)
    total[...] = value
    rows = total.shape[0] // pairs // parts
    for step in range(parts):
        begin = flip(at_ref[along], step) * rows
        for pair in range(pairs):
            place = pl.ds(pl.multiple_of(pair * rows * parts + begin, SLAB), rows)
            outs[step][pl.ds(pair * rows, rows), :] = total[place, :].astype(LOW)
    send(*outs)


def assemble_kernel(*refs, pairs, planes, strips):
    takes = 2 * planes
    parts, outs = (refs[:takes], refs[takes : takes + pairs])
    full, sem = (refs[takes + pairs : takes + 2 * pairs], refs[-1])
    half, plane, row = places()
    rows = parts[0].shape[0] // pairs // strips
    block = strips * rows
    writes = []
    for pair in range(pairs):
        for at in range(takes):
            side, spot = (flip(half, at // planes), flip(plane, at % planes))
            for step in range(strips):
                place = side * (planes * block) + spot * block
                if strips > 1:
                    place = place + flip(row, step) * rows
                full[pair][pl.ds(pl.multiple_of(place, SLAB), rows), :] = parts[at][
                    pl.ds((step * pairs + pair) * rows, rows), :
                ].astype(FULL)
        writes.append(pltpu.make_async_copy(full[pair], outs[pair], sem.at[pair]))
        writes[-1].start()
    for write in writes:
        write.wait()


def assemble(parts, pairs, planes, strips):
    takes = len(parts)
    out = like(2 * planes * parts[0].shape[0] // pairs, parts[0].shape[1])
    return pl.pallas_call(
        functools.partial(assemble_kernel, pairs=pairs, planes=planes, strips=strips),
        out_shape=[out] * pairs,
        in_specs=[pl.BlockSpec(memory_space=pltpu.VMEM)] * takes,
        out_specs=[pl.BlockSpec(memory_space=pltpu.HBM)] * pairs,
        scratch_shapes=[pltpu.VMEM(out.shape, FULL)] * pairs
        + [pltpu.SemaphoreType.DMA((pairs,))],
        compiler_params=pltpu.CompilerParams(vmem_limit_bytes=VMEM_BYTES),
        cost_estimate=pl.CostEstimate(flops=0, bytes_accessed=0, transcendentals=0),
    )(*parts)


class Near:
    def __init__(self, value):
        self.value = value


def like(*shape, dtype=FULL):
    return jax.ShapeDtypeStruct(shape, dtype)


def low(*shape):
    return like(*shape, dtype=LOW)


def places():
    return [lax.axis_index(axis) for axis in ("half", "im", "row")]


def call(kernel, outs, scratch, *args):
    near_in = [isinstance(arg, Near) for arg in args]
    near_out = [isinstance(out, Near) for out in outs]
    args = [arg.value if isinstance(arg, Near) else arg for arg in args]
    outs = [out.value if isinstance(out, Near) else out for out in outs]
    takes, gives = (len(args), len(outs))
    far_in = [at for at in range(takes) if not near_in[at]]
    far_out = [at for at in range(gives) if not near_out[at]]

    def body(*refs):
        given, refs = (list(refs[:takes]), refs[takes:])
        made, refs = (list(refs[:gives]), refs[gives:])
        rest = refs[len(far_in) + len(far_out) :]
        reads, writes = ({}, {})
        if far_in:
            in_sem = rest[-1]
            rest = rest[:-1]
        if far_out:
            out_sem = rest[-1]
            rest = rest[:-1]
        for place, at in enumerate(far_in):
            reads[at] = pltpu.make_async_copy(given[at], refs[place], in_sem.at[place])
            given[at] = refs[place]
        for place, at in enumerate(far_out):
            mirror = refs[len(far_in) + place]
            writes[at] = pltpu.make_async_copy(mirror, made[at], out_sem.at[place])
            made[at] = mirror
        for at in sorted(reads, key=lambda at: args[at].size):
            reads[at].start()
        started = []

        def need(*wanted):
            for at in list(reads):
                if any(given[at] is ref for ref in wanted):
                    reads.pop(at).wait()

        def send(*ready):
            for at in list(writes):
                if any(made[at] is ref for ref in ready):
                    started.append(writes.pop(at))
                    started[-1].start()

        kernel(need, send, places(), *given, *made, *rest)
        need(*given)
        send(*made)
        for write in started:
            write.wait()

    spaces = {True: pltpu.VMEM, False: pltpu.HBM}
    return pl.pallas_call(
        body,
        out_shape=outs,
        in_specs=[pl.BlockSpec(memory_space=spaces[near]) for near in near_in],
        out_specs=[pl.BlockSpec(memory_space=spaces[near]) for near in near_out],
        scratch_shapes=[pltpu.VMEM(args[at].shape, args[at].dtype) for at in far_in]
        + [pltpu.VMEM(outs[at].shape, outs[at].dtype) for at in far_out]
        + [pltpu.VMEM(shape, FULL) for shape in scratch]
        + [pltpu.SemaphoreType.DMA((len(far_out),))] * bool(far_out)
        + [pltpu.SemaphoreType.DMA((len(far_in),))] * bool(far_in),
        compiler_params=pltpu.CompilerParams(vmem_limit_bytes=VMEM_BYTES),
        cost_estimate=pl.CostEstimate(flops=0, bytes_accessed=0, transcendentals=0),
    )(*args)


def edges(parity_edges):
    size = lax.axis_size("row")
    inner = [(at, at ^ 1) for at in range(size)]
    outer = [(at, at + 1) for at in range(1, size - 1, 2)]
    outer = outer + [(to, at) for at, to in outer]
    return (
        lax.ppermute(parity_edges[0], "row", inner),
        lax.ppermute(parity_edges[1], "row", outer),
    )


def swap(field):
    return lax.ppermute(field, "half", [(0, 1), (1, 0)])


def steps_of(value, axis, step):
    size = lax.axis_size(axis)
    return lax.ppermute(value, axis, [(at, at ^ step) for at in range(size)])


def share(parts, axis):
    return [parts[0]] + [steps_of(parts[at], axis, at) for at in range(1, len(parts))]


def share_same(part, axis):
    size = lax.axis_size(axis)
    return [part] + [steps_of(part, axis, at) for at in range(1, size)]


def pair_outer(*pairs):
    size = lax.axis_size("im")
    first = pairs[0][0].value if isinstance(pairs[0][0], Near) else pairs[0][0]
    width = first.shape[1]
    rows = width // 2 // size * len(pairs)
    return list(
        call(
            functools.partial(pair_outer_kernel, pairs=len(pairs), parts=size),
            [Near(low(rows, width))] * size,
            [],
            *[ref for pair in pairs for ref in pair],
        )
    )


def sum_split(pieces, pairs):
    size = lax.axis_size("row")
    rows, width = pieces[0].shape
    return list(
        call(
            functools.partial(
                sum_split_kernel,
                pairs=pairs,
                parts=size,
                pieces=len(pieces),
            ),
            [Near(low(rows // size, width))] * size,
            [(rows, width)],
            *[Near(piece) for piece in pieces],
        )
    )


def add_low(pieces):
    total = pieces[0].astype(FULL)
    for piece in pieces[1:]:
        total = total + piece.astype(FULL)
    return total.astype(LOW)


def sum_far(left, right, axes):
    part = jnp.einsum("tm,tc->mc", left, right, preferred_element_type=FULL)
    return lax.psum(part, axes)


def shards(
    x_in,
    pre_reduce,
    pre_conv,
    pre_expand,
    pre_mid_gain,
    pre_mid_shift,
    pre_out_gain,
    pre_out_shift,
    post_reduce,
    post_conv,
    post_expand,
    post_mid_gain,
    post_mid_shift,
    post_out_gain,
    post_out_shift,
    read_weight,
    read_bias,
    cotangent,
):
    count, strip, side, width = x_in.shape
    strips = lax.axis_size("row")
    tokens = count * strip * side
    cols = side // 2
    rows = strip // 2
    slabs = count * rows
    padded = slabs * SLAB
    small = slabs * cols
    block = -(-small // SLAB) * SLAB
    features = read_weight.shape[1]
    x_low = x_in.reshape(tokens, width)
    pre_out_g, pre_out_s = (pre_out_gain[None], pre_out_shift[None])
    post_out_g, post_out_s = (post_out_gain[None], post_out_shift[None])
    pre_edge = Near(low(count, side, width))
    post_edge = Near(low(count, SLAB, width))
    quick = lax.axis_size("im") == 4 and strips == 4
    if quick:
        x_far = swap(x_low)

    first, edge_a, edge_b, normed_a, factor_a = call(
        pre_reduce_kernel,
        [Near(low(tokens, width)), pre_edge, pre_edge, like(tokens, width), like(tokens, LANES)],
        [(tokens, width)],
        x_low,
        pre_reduce,
        pre_mid_gain,
        pre_mid_shift,
    )
    got_a, got_b = edges((edge_a, edge_b))
    if quick:
        got_a, got_b, x_far = tie(got_a, got_b, x_far)
    (
        second,
        normed_b,
        factor_b,
        normed_c,
        factor_c,
        summed,
        pooled,
        post_first,
        edge_a,
        edge_b,
        post_normed_a,
        post_factor_a,
        pad,
    ) = call(
        pre_rest_kernel,
        [
            low(tokens, width),
            like(tokens, width),
            like(tokens, LANES),
            like(tokens, width),
            like(tokens, LANES),
            like(tokens, width),
            Near(like(padded, width)),
            Near(low(padded, width)),
            post_edge,
            post_edge,
            like(padded, width),
            like(padded, LANES),
            like(count, strip + 2, side, width),
        ],
        [(tokens, width), (side * width // LANES, LANES), (padded, width)],
        x_low,
        Near(first),
        Near(got_a),
        Near(got_b),
        pre_conv,
        pre_expand,
        pre_mid_gain,
        pre_mid_shift,
        pre_out_g,
        pre_out_s,
        post_reduce,
        post_mid_gain,
        post_mid_shift,
    )
    got_a, got_b = edges((edge_a, edge_b))
    if quick:
        second_far = swap(second)
        got_a, got_b, second_far = tie(got_a, got_b, second_far)
    (
        block_two,
        left_in,
        left_second,
        post_normed_b,
        post_factor_b,
        post_normed_c,
        post_factor_c,
        post_summed,
        post_pad,
    ) = call(
        functools.partial(post_rest_kernel, cols=cols),
        [
            Near(low(small, width)),
            low(block, width),
            low(block, width),
            like(padded, width),
            like(padded, LANES),
            like(padded, width),
            like(padded, LANES),
            like(padded, width),
            like(count, rows + 2, SLAB, width),
        ],
        [(padded, width), (padded, width), (block, width)],
        Near(pooled),
        Near(post_first),
        Near(got_a),
        Near(got_b),
        post_conv,
        post_expand,
        post_mid_gain,
        post_mid_shift,
        post_out_g,
        post_out_s,
    )
    whole = lax.all_gather(block_two, "row", axis=0, tiled=True)
    readout, grad_pre, *terms, d_read_b = call(
        functools.partial(readout_kernel, strips=strips),
        [
            like(*cotangent.shape, dtype=LOW),
            Near(low(strips * small, features)),
        ]
        + [Near(low(small, width))] * strips
        + [like(1, features)],
        [
            (strips * small, features),
            (strips * small, features),
            (strips * small, width),
        ],
        Near(whole),
        read_weight,
        read_bias[None],
        cotangent,
    )
    terms = share(terms, "row")
    if quick:
        parts = pair_outer(
            (Near(whole), Near(swap(whole)), Near(grad_pre), Near(swap(grad_pre)))
        )
        parts[0], *terms = tie(parts[0], *terms)
        read_parts = share(parts, "im")
    post_gs, post_ge, post_gc, edge_a, edge_b, post_small_b = call(
        functools.partial(post_back_kernel, cols=cols, strips=strips),
        [
            Near(like(padded, width)),
            Near(low(block, width)),
            Near(low(padded, width)),
            post_edge,
            post_edge,
            like(4, width),
        ],
        [(block, width), (padded, width), (padded, width), (padded, width)],
        *[Near(term) for term in terms],
        post_expand,
        post_mid_gain,
        post_mid_shift,
        post_out_g,
        post_normed_b,
        post_factor_b,
        post_normed_c,
        post_factor_c,
        post_summed,
    )
    got_a, got_b = edges((edge_a, edge_b))
    if quick:
        left_in_far, left_second_far, ge_far = (swap(left_in), swap(left_second), swap(post_ge))
        got_a, got_b, left_in_far, left_second_far, ge_far, *read_parts = tie(
            got_a, got_b, left_in_far, left_second_far, ge_far, *read_parts
        )
        read_part = add_low(read_parts)
        read_parts = [read_part, steps_of(read_part, "im", 1), steps_of(read_part, "im", 2)]
        got_a, got_b, *read_parts = tie(got_a, got_b, *read_parts)
    (
        post_gr,
        pre_gs,
        pre_ge,
        pre_gc,
        edge_a,
        edge_b,
        post_small_a,
        pre_small_b,
    ) = call(
        functools.partial(middle_back_kernel, cols=cols),
        [
            Near(low(block, width)),
            like(tokens, width),
            Near(low(tokens, width)),
            Near(low(tokens, width)),
            pre_edge,
            pre_edge,
            like(11, width),
            like(4, width),
        ],
        [
            (count, rows + 2, SLAB, width),
            (9, 8, width),
            (padded, width),
            (side * width // LANES, LANES),
            (tokens, width),
            (2, 8, width),
            (padded, width),
            (block, width),
        ],
        Near(post_gc),
        Near(got_a),
        Near(got_b),
        post_pad,
        post_conv,
        post_reduce,
        post_mid_gain,
        post_mid_shift,
        post_normed_a,
        post_factor_a,
        Near(post_gs),
        pre_expand,
        pre_mid_gain,
        pre_mid_shift,
        pre_out_g,
        normed_b,
        factor_b,
        normed_c,
        factor_c,
        summed,
    )
    got_a, got_b = edges((edge_a, edge_b))
    if quick:
        pre_ge_far = swap(pre_ge)
        post_parts = pair_outer(
            (left_in, left_in_far, Near(post_gr), Near(swap(post_gr))),
            (left_second, left_second_far, Near(post_ge), Near(ge_far)),
        )
        read_parts.append(steps_of(read_parts[0], "im", 3))
        got_a, got_b, pre_ge_far, post_parts[0], *read_parts = tie(
            got_a, got_b, pre_ge_far, post_parts[0], *read_parts
        )
        post_parts = share(post_parts, "im")
    pre_gr, pre_small_a = call(
        pre_back_kernel,
        [Near(low(tokens, width)), like(11, width)],
        [
            (count, strip + 2, side, width),
            (9, 8, width),
            (2, 8, width),
        ],
        Near(pre_gc),
        Near(got_a),
        Near(got_b),
        pad,
        pre_conv,
        pre_mid_gain,
        pre_mid_shift,
        normed_a,
        factor_a,
    )
    sums = jnp.concatenate([pre_small_a, pre_small_b, post_small_a, post_small_b, d_read_b])
    if quick:
        far = swap(pre_gr)
        sums = sums + swap(sums)
        sums, far = tie(sums, far)
        parts = pair_outer(
            (second, second_far, Near(pre_ge), Near(pre_ge_far)),
            (x_low, x_far, Near(pre_gr), Near(far)),
        )
        parts[0], *post_parts = tie(parts[0], *post_parts)
        post_parts = share(sum_split(post_parts, 2), "row")
        near_parts = [steps_of(parts[at], "im", at) for at in (1, 2)]
        sums = sums + steps_of(sums, "im", 1)
        grad_in = pre_gs + jnp.einsum("tm,cm->tc", pre_gr, pre_reduce, preferred_element_type=FULL)
        grad_in = grad_in.astype(LOW)
        sums, grad_in, last, *rest = tie(sums, grad_in, parts[3], *post_parts, *near_parts)
        post_parts, near_parts = (rest[:4], rest[4:])
        sums = sums + steps_of(sums, "im", 2)
        post_parts = share_same(add_low(post_parts), "row")
        last = steps_of(last, "im", 3)
        (read_total,) = assemble(read_parts + [swap(part) for part in read_parts], 1, 4, 1)
        sums, read_total, last, *post_parts = tie(sums, read_total, last, *post_parts)
        parts = share(sum_split([parts[0]] + near_parts + [last], 2), "row")
        whole_part = jnp.concatenate(post_parts, axis=0)
        post_parts = [whole_part, steps_of(whole_part, "im", 1), steps_of(whole_part, "im", 2)]
        read_bias_g = sums[30]
        sums = sums + steps_of(sums, "row", 1)
        sums, *rest = tie(sums, *parts, *post_parts)
        parts, post_parts = (rest[:4], rest[4:])
        parts = share_same(add_low(parts), "row")
        post_parts.append(steps_of(post_parts[0], "im", 3))
        sums = sums + steps_of(sums, "row", 2)
        sums, *rest = tie(sums, *parts, *post_parts)
        parts, post_parts = (rest[:4], rest[4:])
        whole_part = jnp.concatenate(parts, axis=0)
        parts = [whole_part, steps_of(whole_part, "im", 1), steps_of(whole_part, "im", 2)]
        post_parts = post_parts + [swap(part) for part in post_parts]
        post_reduce_g, post_expand_g = assemble(post_parts, 2, 4, strips)
        post_reduce_g, *parts = tie(post_reduce_g, *parts)
        parts.append(steps_of(parts[0], "im", 3))
        parts = parts + [swap(part) for part in parts]
        pre_expand_g, pre_reduce_g = assemble(parts, 2, 4, strips)
    else:
        axes = IMG + ("row",)
        post_reduce_g = sum_far(left_in, post_gr, axes)
        post_expand_g = sum_far(left_second, post_ge, axes)
        pre_expand_g = sum_far(second, pre_ge, axes)
        pre_reduce_g = sum_far(x_low, pre_gr, axes)
        read_total = sum_far(whole, grad_pre, IMG)
        read_bias_g = lax.psum(sums[30], IMG)
        sums = lax.psum(sums, axes)
        grad_in = pre_gs + jnp.einsum("tm,cm->tc", pre_gr, pre_reduce, preferred_element_type=FULL)
        grad_in = grad_in.astype(LOW)

    def small_grads(part):
        return (
            part[:9].reshape(3, 3, width),
            jnp.stack([part[9], part[11]]),
            jnp.stack([part[10], part[12]]),
            part[13],
            part[14],
        )

    pre_conv_g, pre_gain_g, pre_shift_g, pre_og_g, pre_os_g = small_grads(sums[:15])
    post_conv_g, post_gain_g, post_shift_g, post_og_g, post_os_g = small_grads(sums[15:30])
    return (
        readout,
        grad_in.reshape(x_in.shape),
        pre_reduce_g,
        pre_conv_g,
        pre_expand_g,
        pre_gain_g,
        pre_shift_g,
        pre_og_g,
        pre_os_g,
        post_reduce_g,
        post_conv_g,
        post_expand_g,
        post_gain_g,
        post_shift_g,
        post_og_g,
        post_os_g,
        read_total,
        read_bias_g,
    )


def solution(mesh):
    images, strips = mesh.devices.shape
    split = jax.sharding.Mesh(
        mesh.devices.reshape(images // 2, 2, strips), ("im", "half", "row")
    )
    return jax.shard_map(
        shards,
        mesh=split,
        in_specs=(P(IMG, "row", None, None),)
        + (P(),) * 14
        + (P(None, "row"), P("row"), P(IMG, None, None, "row")),
        out_specs=(P(IMG, None, None, "row"), P(IMG, "row", None, None))
        + (P(),) * 14
        + (P(None, "row"), P("row")),
        check_vma=False,
    )
```

```python
import functools

import jax
import jax.numpy as jnp
from jax import lax
from jax.experimental import pallas as pl
from jax.experimental.pallas import tpu as pltpu
from jax.sharding import PartitionSpec as P

EPSILON = 1e-06
SQRT_HALF = 0.7071067811865476
INV_SQRT_TWO_PI = 0.3989422804014327
LOW = jnp.bfloat16
FULL = jnp.float32
IMG = ("im", "half")
TILE = 256
SLAB = 16
LANES = 128
VMEM_BYTES = 24 * 1024 * 1024


def tie(*values):
    return lax.optimization_barrier(values)


def norm(value):
    centred = value - jnp.mean(value, axis=-1, keepdims=True)
    factor = lax.rsqrt(jnp.mean(centred * centred, axis=-1, keepdims=True) + EPSILON)
    return (centred * factor, factor)


def norm_back(grad, normed, factor, gain):
    scaled = grad * gain
    return factor * (
        scaled
        - jnp.mean(scaled, axis=-1, keepdims=True)
        - normed * jnp.mean(scaled * normed, axis=-1, keepdims=True)
    )


def gate(value):
    return 0.5 * jnp.tanh(0.5 * value) + 0.5


def silu(value):
    return value * gate(value)


def silu_back(grad, value):
    sigma = gate(value)
    return grad * sigma * (1.0 + value * (1.0 - sigma))


def flip(place, step):
    bit = 1
    while bit <= step:
        if step & bit:
            place = place + bit - 2 * bit * ((place // bit) % 2)
        bit *= 2
    return place


def wide(factor):
    return jnp.broadcast_to(factor, (factor.shape[0], LANES))


def fold(value):
    return jnp.sum(value.reshape(-1, 8, value.shape[-1]), axis=0)


def live(rows, cols):
    at = lax.broadcasted_iota(jnp.int32, (rows, 1), 0)
    return lax.rem(at, SLAB) < cols


def from_left(value):
    at = lax.broadcasted_iota(jnp.int32, (value.shape[0], 1), 0)
    return jnp.where(at == 0, 0.0, pltpu.roll(value, 1, 0))


def from_right(value):
    last = value.shape[0] - 1
    at = lax.broadcasted_iota(jnp.int32, (value.shape[0], 1), 0)
    return jnp.where(at == last, 0.0, pltpu.roll(value, last, 0))


def matmul(left_ref, right_ref, out_ref):
    @pl.loop(0, right_ref.shape[1] // TILE)
    def _(at):
        cols = pl.ds(pl.multiple_of(at * TILE, TILE), TILE)
        out_ref[:, cols] = jnp.dot(
            left_ref[...].astype(LOW), right_ref[:, cols], preferred_element_type=FULL
        )


def matmul_back(left_ref, right_ref, out_ref):
    @pl.loop(0, right_ref.shape[0] // TILE)
    def _(at):
        cols = pl.ds(pl.multiple_of(at * TILE, TILE), TILE)
        out_ref[:, cols] = lax.dot_general(
            left_ref[...].astype(LOW),
            right_ref[cols, :],
            (((1,), (1,)), ((), ())),
            preferred_element_type=FULL,
        ).astype(out_ref.dtype)


def rows_of(at, size):
    return pl.ds(pl.multiple_of(at * size, SLAB), size)


def fill_halo(at_ref, pad_ref, low_ref, got_a_ref, got_b_ref):
    count, rows, cols, width = pad_ref.shape
    rows = rows - 2
    even = lax.rem(at_ref[2], 2) == 0
    for image in range(count):
        got_a, got_b = (got_a_ref[image].astype(FULL), got_b_ref[image].astype(FULL))
        pad_ref[image, 0] = jnp.where(even, got_b, got_a)
        pad_ref[image, rows + 1] = jnp.where(even, got_a, got_b)

    size = cols if cols % SLAB == 0 else 2 * cols
    per = size // cols
    each = rows // per

    @pl.loop(0, count * each)
    def _(at):
        part = low_ref[rows_of(at, size), :].astype(FULL).reshape(per, cols, width)
        pad_ref[at // each, pl.ds(1 + per * lax.rem(at, each), per)] = part


def set_edges(at_ref, edge_a_ref, edge_b_ref, image, head, tail):
    even = lax.rem(at_ref[2], 2) == 0
    edge_a_ref[image] = jnp.where(even, tail, head).astype(LOW)
    edge_b_ref[image] = jnp.where(even, head, tail).astype(LOW)


def conv_row(pad_ref, taps, image, row):
    lines = [pad_ref[image, row + top] for top in range(3)]
    sums = [
        lines[0] * taps[left] + lines[1] * taps[3 + left] + lines[2] * taps[6 + left]
        for left in range(3)
    ]
    return from_left(sums[0]) + sums[1] + from_right(sums[2])


def conv_back_row(pad_ref, grad_ref, taps, taps_ref, image, row):
    lines = [grad_ref[image, row + top] for top in range(3)]
    sums = [
        lines[2] * taps[left] + lines[1] * taps[3 + left] + lines[0] * taps[6 + left]
        for left in range(3)
    ]
    shifted = [from_right(lines[1]), lines[1], from_left(lines[1])]
    for top in range(3):
        source = pad_ref[image, row + top]
        for left in range(3):
            taps_ref[3 * top + left] += fold(source * shifted[left])
    return from_right(sums[0]) + sums[1] + from_left(sums[2])


def pack(compact, source, out_ref, cols):
    compact[...] = jnp.zeros(compact.shape, FULL)
    for at in range(source.shape[0] // SLAB):
        compact[pl.ds(at * cols, cols), :] = source[pl.ds(at * SLAB, cols), :]
    out_ref[...] = compact[...].astype(LOW)


def narrow(pair, value):
    side = value.shape[0]
    parts = []
    for at in range(value.shape[1] // LANES):
        pair[pl.ds(at * side, side), :] = value[:, at * LANES : (at + 1) * LANES]
        parts.append(
            pair[pl.ds(at * side, side // 2, stride=2), :]
            + pair[pl.ds(at * side + 1, side // 2, stride=2), :]
        )
    return jnp.concatenate(parts, axis=1)


def widen(pair, value):
    cols = value.shape[0]
    parts = []
    for at in range(value.shape[1] // LANES):
        part = value[:, at * LANES : (at + 1) * LANES]
        pair[pl.ds(2 * cols * at, cols, stride=2), :] = part
        pair[pl.ds(2 * cols * at + 1, cols, stride=2), :] = part
        parts.append(pair[pl.ds(2 * cols * at, 2 * cols), :])
    return jnp.concatenate(parts, axis=1)


def tap_rows(conv_ref):
    lines = [conv_ref[top].astype(FULL) for top in range(3)]
    return [lines[at // 3][at % 3 : at % 3 + 1] for at in range(9)]


def finish(small_ref, sums_ref, at, place):
    small_ref[pl.ds(place, 1), :] = jnp.sum(sums_ref[at], axis=0, keepdims=True)


def pre_reduce_kernel(
    need,
    send,
    at_ref,
    x_ref, w_ref, gain_ref, shift_ref, first_ref, edge_a_ref, edge_b_ref, normed_ref, factor_ref, red
):
    count, side, width = edge_a_ref.shape
    size = 2 * side
    steps = x_ref.shape[0] // size
    need(x_ref, w_ref)
    matmul(x_ref, w_ref, red)
    need(gain_ref, shift_ref)
    gain, shift = (gain_ref[pl.ds(0, 1), :], shift_ref[pl.ds(0, 1), :])

    @pl.loop(0, steps)
    def _(at):
        rows = rows_of(at, size)
        normed, factor = norm(red[rows, :])
        normed_ref[rows, :] = normed
        factor_ref[rows, :] = wide(factor)
        first_ref[rows, :] = silu(normed * gain + shift).astype(LOW)

    each = steps // count
    for image in range(count):
        head = first_ref[pl.ds(image * each * size, size), :].astype(FULL)
        tail = first_ref[pl.ds((image * each + each - 1) * size, size), :].astype(FULL)
        set_edges(at_ref, edge_a_ref, edge_b_ref, image, head[:side], tail[side:])


def pre_rest_kernel(
    need,
    send,
    at_ref,
    x_ref,
    first_ref,
    got_a_ref,
    got_b_ref,
    conv_ref,
    expand_ref,
    gain_ref,
    shift_ref,
    out_gain_ref,
    out_shift_ref,
    reduce_ref,
    post_gain_ref,
    post_shift_ref,
    second_ref,
    normed_b_ref,
    factor_b_ref,
    normed_c_ref,
    factor_c_ref,
    summed_ref,
    pooled_ref,
    post_first_ref,
    edge_a_ref,
    edge_b_ref,
    post_normed_ref,
    post_factor_ref,
    pad,
    exp,
    pair,
    red,
):
    count, strip, side, width = pad.shape
    strip = strip - 2
    size = 2 * side
    each = strip // 2
    need(first_ref, got_a_ref, got_b_ref)
    fill_halo(at_ref, pad, first_ref, got_a_ref, got_b_ref)
    need(conv_ref, gain_ref, shift_ref)
    send(pad)
    taps = tap_rows(conv_ref)
    gain, shift = (gain_ref[pl.ds(1, 1), :], shift_ref[pl.ds(1, 1), :])

    @pl.loop(0, count * each)
    def _(at):
        rows = rows_of(at, size)
        image, row = (at // each, 2 * lax.rem(at, each))
        conv = jnp.concatenate(
            [conv_row(pad, taps, image, row), conv_row(pad, taps, image, row + 1)], axis=0
        )
        normed, factor = norm(conv)
        normed_b_ref[rows, :] = normed
        factor_b_ref[rows, :] = wide(factor)
        second_ref[rows, :] = silu(normed * gain + shift).astype(LOW)

    send(second_ref, normed_b_ref, factor_b_ref)
    need(expand_ref)
    matmul(second_ref, expand_ref, exp)
    need(x_ref, out_gain_ref, out_shift_ref)
    out_gain, out_shift = (out_gain_ref[...], out_shift_ref[...])
    cols = side // 2
    for at in range(count * each):
        rows = pl.ds(at * size, size)
        normed, factor = norm(exp[rows, :])
        normed_c_ref[rows, :] = normed
        factor_c_ref[rows, :] = wide(factor)
        summed = x_ref[rows, :].astype(FULL) + normed * out_gain + out_shift
        summed_ref[rows, :] = summed
        block = silu(summed)
        half = narrow(pair, block[:side] + block[side:])
        pooled_ref[pl.ds(at * SLAB, cols), :] = 0.25 * half
        pooled_ref[pl.ds(at * SLAB + cols, SLAB - cols), :] = jnp.zeros(
            (SLAB - cols, width), FULL
        )
    send(normed_c_ref, factor_c_ref, summed_ref)
    need(reduce_ref, post_gain_ref, post_shift_ref)
    matmul(pooled_ref, reduce_ref, red)
    normed, factor = norm(red[...])
    post_normed_ref[...] = normed
    post_factor_ref[...] = wide(factor)
    first = silu(normed * post_gain_ref[pl.ds(0, 1), :] + post_shift_ref[pl.ds(0, 1), :])
    post_first_ref[...] = jnp.where(live(red.shape[0], cols), first, 0.0).astype(LOW)
    for image in range(count):
        head = post_first_ref[pl.ds(image * each * SLAB, SLAB), :].astype(FULL)
        tail = post_first_ref[pl.ds((image * each + each - 1) * SLAB, SLAB), :].astype(FULL)
        set_edges(at_ref, edge_a_ref, edge_b_ref, image, head, tail)


def post_rest_kernel(
    need,
    send,
    at_ref,
    pooled_ref,
    first_ref,
    got_a_ref,
    got_b_ref,
    conv_ref,
    expand_ref,
    gain_ref,
    shift_ref,
    out_gain_ref,
    out_shift_ref,
    block_ref,
    left_in_ref,
    left_second_ref,
    normed_b_ref,
    factor_b_ref,
    normed_c_ref,
    factor_c_ref,
    summed_ref,
    pad,
    second,
    exp,
    compact,
    *,
    cols
):
    count, rows, _, width = pad.shape
    rows = rows - 2
    small = block_ref.shape[0]
    need(first_ref, got_a_ref, got_b_ref)
    fill_halo(at_ref, pad, first_ref, got_a_ref, got_b_ref)
    send(pad)
    need(conv_ref, gain_ref, shift_ref, pooled_ref)
    taps = tap_rows(conv_ref)
    gain, shift = (gain_ref[pl.ds(1, 1), :], shift_ref[pl.ds(1, 1), :])

    @pl.loop(0, count * rows)
    def _(at):
        place = rows_of(at, SLAB)
        normed, factor = norm(conv_row(pad, taps, at // rows, lax.rem(at, rows)))
        normed_b_ref[place, :] = normed
        factor_b_ref[place, :] = wide(factor)
        second[place, :] = silu(normed * gain + shift)

    send(normed_b_ref, factor_b_ref)
    need(expand_ref)
    matmul(second, expand_ref, exp)
    need(out_gain_ref, out_shift_ref)
    normed, factor = norm(exp[...])
    normed_c_ref[...] = normed
    factor_c_ref[...] = wide(factor)
    summed = pooled_ref[...] + normed * out_gain_ref[...] + out_shift_ref[...]
    summed_ref[...] = summed
    exp[...] = silu(summed)
    compact[...] = jnp.zeros(compact.shape, FULL)
    for at in range(count * rows):
        compact[pl.ds(at * cols, cols), :] = exp[pl.ds(at * SLAB, cols), :]
    block_ref[...] = compact[pl.ds(0, small), :].astype(LOW)
    send(block_ref, normed_c_ref, factor_c_ref, summed_ref)
    pack(compact, pooled_ref, left_in_ref, cols)
    pack(compact, second, left_second_ref, cols)


def readout_kernel(
    need,
    send,
    at_ref,
    whole_ref,
    w_ref,
    bias_ref,
    cot_ref,
    out_ref,
    grad_ref,
    *refs,
    strips
):
    slots, (bias_grad_ref, cot, out, terms_ref) = (refs[:strips], refs[strips:])
    images, lines, cols, _ = cot_ref.shape
    rows = lines // strips
    need(cot_ref)
    for at in range(images * lines):
        strip, image, row = (at // (images * rows), at // rows % images, at % rows)
        cot[pl.ds(at * cols, cols), :] = cot_ref[image, strip * rows + row].astype(FULL)
    need(whole_ref, w_ref, bias_ref)

    @pl.loop(0, w_ref.shape[1] // TILE)
    def _(at):
        lanes = pl.ds(pl.multiple_of(at * TILE, TILE), TILE)
        act = jnp.dot(whole_ref[...], w_ref[:, lanes], preferred_element_type=FULL)
        act = act + bias_ref[:, lanes]
        cdf = 0.5 * (1.0 + lax.erf(act * SQRT_HALF))
        density = jnp.exp(-0.5 * act * act) * INV_SQRT_TWO_PI
        out[:, lanes] = act * cdf
        grad = (cot[:, lanes] * (cdf + act * density)).astype(LOW)
        grad_ref[:, lanes] = grad
        bias_grad_ref[:, lanes] = jnp.sum(grad.astype(FULL), axis=0, keepdims=True)

    send(grad_ref, bias_grad_ref)
    matmul_back(grad_ref, w_ref, terms_ref)
    small = slots[0].shape[0]
    for step in range(strips):
        begin = pl.multiple_of(flip(at_ref[2], step) * small, 8)
        slots[step][...] = terms_ref[pl.ds(begin, small), :].astype(LOW)
    for at in range(images * lines):
        strip, image, row = (at // (images * rows), at // rows % images, at % rows)
        out_ref[image, strip * rows + row] = out[pl.ds(at * cols, cols), :].astype(LOW)


def post_back_kernel(
    need,
    send,
    at_ref,
    *refs,
    cols,
    strips
):
    pieces, refs = (refs[:strips], refs[strips:])
    (
    expand_ref,
    gain_ref,
    shift_ref,
    out_gain_ref,
    normed_b_ref,
    factor_b_ref,
    normed_c_ref,
    factor_c_ref,
    summed_ref,
    grad_sum_ref,
    grad_exp_ref,
    grad_conv_ref,
    edge_a_ref,
    edge_b_ref,
    small_ref,
    compact,
    spread_out,
    exp,
    sec,
    ) = refs
    count = edge_a_ref.shape[0]
    tokens, width = grad_sum_ref.shape
    each = tokens // SLAB // count
    need(*pieces)
    total = pieces[0][...].astype(FULL)
    for piece in pieces[1:]:
        total = total + piece[...].astype(FULL)
    compact[...] = jnp.zeros(compact.shape, FULL)
    compact[pl.ds(0, total.shape[0]), :] = total
    spread_out[...] = jnp.zeros((tokens, width), FULL)
    for at in range(tokens // SLAB):
        spread_out[pl.ds(at * SLAB, cols), :] = compact[pl.ds(at * cols, cols), :]
    need(summed_ref, normed_c_ref, factor_c_ref, out_gain_ref)
    grad_sum = silu_back(spread_out[...], summed_ref[...])
    grad_sum_ref[...] = grad_sum
    normed = normed_c_ref[...]
    exp[...] = norm_back(grad_sum, normed, factor_c_ref[:, :1], out_gain_ref[...])
    small_ref[pl.ds(2, 1), :] = jnp.sum(grad_sum * normed, axis=0, keepdims=True)
    small_ref[pl.ds(3, 1), :] = jnp.sum(grad_sum, axis=0, keepdims=True)
    pack(compact, exp, grad_exp_ref, cols)
    send(grad_sum_ref, grad_exp_ref)
    need(expand_ref)
    matmul_back(exp, expand_ref, sec)
    need(gain_ref, shift_ref, normed_b_ref, factor_b_ref)
    gain, shift = (gain_ref[pl.ds(1, 1), :], shift_ref[pl.ds(1, 1), :])
    normed = normed_b_ref[...]
    grad = silu_back(sec[...], normed * gain + shift)
    grad_conv_ref[...] = norm_back(grad, normed, factor_b_ref[:, :1], gain).astype(LOW)
    small_ref[pl.ds(0, 1), :] = jnp.sum(grad * normed, axis=0, keepdims=True)
    small_ref[pl.ds(1, 1), :] = jnp.sum(grad, axis=0, keepdims=True)
    for image in range(count):
        head = grad_conv_ref[pl.ds(image * each * SLAB, SLAB), :].astype(FULL)
        tail = grad_conv_ref[pl.ds((image * each + each - 1) * SLAB, SLAB), :].astype(FULL)
        set_edges(at_ref, edge_a_ref, edge_b_ref, image, head, tail)


def middle_back_kernel(
    need,
    send,
    at_ref,
    grad_conv_ref,
    got_a_ref,
    got_b_ref,
    pad,
    post_conv_ref,
    post_reduce_ref,
    post_gain_ref,
    post_shift_ref,
    post_normed_ref,
    post_factor_ref,
    post_grad_sum_ref,
    expand_ref,
    gain_ref,
    shift_ref,
    out_gain_ref,
    normed_b_ref,
    factor_b_ref,
    normed_c_ref,
    factor_c_ref,
    summed_ref,
    post_grad_red_ref,
    grad_sum_ref,
    grad_exp_ref,
    pre_grad_conv_ref,
    edge_a_ref,
    edge_b_ref,
    post_small_ref,
    small_ref,
    grad_pad,
    taps_sum,
    grad_in,
    pair,
    sec,
    sums,
    post_red,
    compact,
    *,
    cols
):
    count, side, width = edge_a_ref.shape
    need(grad_conv_ref, got_a_ref, got_b_ref)
    fill_halo(at_ref, grad_pad, grad_conv_ref, got_a_ref, got_b_ref)
    need(pad, post_conv_ref)
    need(post_gain_ref, post_shift_ref, post_normed_ref, post_factor_ref)
    taps = tap_rows(post_conv_ref)
    taps_sum[...] = jnp.zeros_like(taps_sum)
    sums[...] = jnp.zeros_like(sums)
    gain, shift = (post_gain_ref[pl.ds(0, 1), :], post_shift_ref[pl.ds(0, 1), :])
    each = post_grad_sum_ref.shape[0] // SLAB // count

    @pl.loop(0, count * each)
    def _(at):
        place = rows_of(at, SLAB)
        grad = conv_back_row(pad, grad_pad, taps, taps_sum, at // each, lax.rem(at, each))
        normed = post_normed_ref[place, :]
        grad = jnp.where(live(SLAB, cols), silu_back(grad, normed * gain + shift), 0.0)
        sums[0] += fold(grad * normed)
        sums[1] += fold(grad)
        post_red[place, :] = norm_back(grad, normed, post_factor_ref[place, :1], gain)

    for at in range(9):
        finish(post_small_ref, taps_sum, at, at)
    finish(post_small_ref, sums, 0, 9)
    finish(post_small_ref, sums, 1, 10)
    pack(compact, post_red, post_grad_red_ref, cols)
    send(post_grad_red_ref, post_small_ref)
    need(post_reduce_ref)
    matmul_back(post_red, post_reduce_ref, grad_in)
    sums[...] = jnp.zeros_like(sums)
    size = 2 * side
    need(out_gain_ref, post_grad_sum_ref, summed_ref, normed_c_ref, factor_c_ref)
    out_gain = out_gain_ref[...]
    for at in range(count * each):
        rows = pl.ds(at * size, size)
        place = pl.ds(at * SLAB, cols)
        grad = 0.25 * (post_grad_sum_ref[place, :] + grad_in[place, :])
        grad = widen(pair, grad)
        grad = jnp.concatenate([grad, grad], axis=0)
        grad_sum = silu_back(grad, summed_ref[rows, :])
        grad_sum_ref[rows, :] = grad_sum
        normed = normed_c_ref[rows, :]
        sums[0] += fold(grad_sum * normed)
        sums[1] += fold(grad_sum)
        grad_exp_ref[rows, :] = norm_back(
            grad_sum, normed, factor_c_ref[rows, :1], out_gain
        ).astype(LOW)
    finish(small_ref, sums, 0, 2)
    finish(small_ref, sums, 1, 3)
    send(grad_sum_ref, grad_exp_ref)
    need(expand_ref)
    matmul_back(grad_exp_ref, expand_ref, sec)
    need(gain_ref, shift_ref, normed_b_ref, factor_b_ref)
    sums[...] = jnp.zeros_like(sums)
    gain_b, shift_b = (gain_ref[pl.ds(1, 1), :], shift_ref[pl.ds(1, 1), :])

    @pl.loop(0, count * each)
    def _(at):
        rows = rows_of(at, size)
        normed = normed_b_ref[rows, :]
        grad = silu_back(sec[rows, :], normed * gain_b + shift_b)
        sums[0] += fold(grad * normed)
        sums[1] += fold(grad)
        pre_grad_conv_ref[rows, :] = norm_back(
            grad, normed, factor_b_ref[rows, :1], gain_b
        ).astype(LOW)

    finish(small_ref, sums, 0, 0)
    finish(small_ref, sums, 1, 1)
    for image in range(count):
        head = pre_grad_conv_ref[pl.ds(image * each * size, size), :].astype(FULL)
        tail = pre_grad_conv_ref[pl.ds((image * each + each - 1) * size, size), :].astype(FULL)
        set_edges(at_ref, edge_a_ref, edge_b_ref, image, head[:side], tail[side:])


def pre_back_kernel(
    need,
    send,
    at_ref,
    grad_conv_ref,
    got_a_ref,
    got_b_ref,
    pad,
    conv_ref,
    gain_ref,
    shift_ref,
    normed_ref,
    factor_ref,
    grad_red_ref,
    small_ref,
    grad_pad,
    taps_sum,
    sums,
):
    count, strip, side, width = pad.shape
    strip = strip - 2
    size = 2 * side
    each = strip // 2
    need(grad_conv_ref, got_a_ref, got_b_ref)
    fill_halo(at_ref, grad_pad, grad_conv_ref, got_a_ref, got_b_ref)
    need(pad, conv_ref)
    need(gain_ref, shift_ref, normed_ref, factor_ref)
    taps = tap_rows(conv_ref)
    taps_sum[...] = jnp.zeros_like(taps_sum)
    sums[...] = jnp.zeros_like(sums)
    gain, shift = (gain_ref[pl.ds(0, 1), :], shift_ref[pl.ds(0, 1), :])

    @pl.loop(0, count * each)
    def _(at):
        rows = rows_of(at, size)
        image, row = (at // each, 2 * lax.rem(at, each))
        grad = jnp.concatenate(
            [
                conv_back_row(pad, grad_pad, taps, taps_sum, image, row),
                conv_back_row(pad, grad_pad, taps, taps_sum, image, row + 1),
            ],
            axis=0,
        )
        normed = normed_ref[rows, :]
        grad = silu_back(grad, normed * gain + shift)
        sums[0] += fold(grad * normed)
        sums[1] += fold(grad)
        grad_red_ref[rows, :] = norm_back(grad, normed, factor_ref[rows, :1], gain).astype(LOW)

    for at in range(9):
        finish(small_ref, taps_sum, at, at)
    finish(small_ref, sums, 0, 9)
    finish(small_ref, sums, 1, 10)


def pair_outer_kernel(need, send, at_ref, *refs, pairs, parts):
    takes = 4 * pairs
    outs = refs[takes:]
    half, plane = (at_ref[0], at_ref[1])
    rows = outs[0].shape[0] // pairs
    for pair in range(pairs):
        left, left_far, right, right_far = refs[4 * pair : 4 * pair + 4]
        need(left, left_far, right, right_far)
        for step in range(parts):
            begin = half * (rows * parts) + flip(plane, step) * rows
            lanes = pl.ds(pl.multiple_of(begin, LANES), rows)
            total = lax.dot_general(
                left[:, lanes], right[...], (((0,), (0,)), ((), ())), preferred_element_type=FULL
            ) + lax.dot_general(
                left_far[:, lanes],
                right_far[...],
                (((0,), (0,)), ((), ())),
                preferred_element_type=FULL,
            )
            outs[step][pl.ds(pair * rows, rows), :] = total.astype(LOW)
    send(*outs)


def sum_split_kernel(need, send, at_ref, *refs, pairs, parts, pieces, along=2):
    takes, outs = (refs[:pieces], refs[pieces : pieces + parts])
    total = refs[-1]
    need(*takes)
    value = takes[0][...].astype(FULL)
    for at in range(1, pieces):
        value = value + takes[at][...].astype(FULL)
    total[...] = value
    rows = total.shape[0] // pairs // parts
    for step in range(parts):
        begin = flip(at_ref[along], step) * rows
        for pair in range(pairs):
            place = pl.ds(pl.multiple_of(pair * rows * parts + begin, SLAB), rows)
            outs[step][pl.ds(pair * rows, rows), :] = total[place, :].astype(LOW)
    send(*outs)


def assemble_kernel(*refs, pairs, planes, strips):
    takes = 2 * planes
    parts, outs = (refs[:takes], refs[takes : takes + pairs])
    full, sem = (refs[takes + pairs : takes + 2 * pairs], refs[-1])
    half, plane, row = places()
    rows = parts[0].shape[0] // pairs // strips
    block = strips * rows
    writes = []
    for pair in range(pairs):
        for at in range(takes):
            side, spot = (flip(half, at // planes), flip(plane, at % planes))
            for step in range(strips):
                place = side * (planes * block) + spot * block
                if strips > 1:
                    place = place + flip(row, step) * rows
                full[pair][pl.ds(pl.multiple_of(place, SLAB), rows), :] = parts[at][
                    pl.ds((step * pairs + pair) * rows, rows), :
                ].astype(FULL)
        writes.append(pltpu.make_async_copy(full[pair], outs[pair], sem.at[pair]))
        writes[-1].start()
    for write in writes:
        write.wait()


def assemble(parts, pairs, planes, strips):
    takes = len(parts)
    out = like(2 * planes * parts[0].shape[0] // pairs, parts[0].shape[1])
    parts = [pltpu.with_memory_space_constraint(part, pltpu.VMEM) for part in parts]
    return pl.pallas_call(
        functools.partial(assemble_kernel, pairs=pairs, planes=planes, strips=strips),
        out_shape=[pltpu.HBM(out.shape, out.dtype)] * pairs,
        in_specs=[pl.BlockSpec(memory_space=pltpu.VMEM)] * takes,
        out_specs=[pl.BlockSpec(memory_space=pltpu.HBM)] * pairs,
        scratch_shapes=[pltpu.VMEM(out.shape, FULL)] * pairs
        + [pltpu.SemaphoreType.DMA((pairs,))],
        compiler_params=pltpu.CompilerParams(vmem_limit_bytes=VMEM_BYTES),
        cost_estimate=pl.CostEstimate(flops=0, bytes_accessed=0, transcendentals=0),
    )(*parts)


class Near:
    def __init__(self, value):
        self.value = value


def like(*shape, dtype=FULL):
    return jax.ShapeDtypeStruct(shape, dtype)


def low(*shape):
    return like(*shape, dtype=LOW)


def places():
    return [lax.axis_index(axis) for axis in ("half", "im", "row")]


def call(kernel, outs, scratch, *args):
    near_in = [isinstance(arg, Near) for arg in args]
    near_out = [isinstance(out, Near) for out in outs]
    args = [arg.value if isinstance(arg, Near) else arg for arg in args]
    outs = [out.value if isinstance(out, Near) else out for out in outs]
    takes, gives = (len(args), len(outs))
    far_in = [at for at in range(takes) if not near_in[at]]
    far_out = [at for at in range(gives) if not near_out[at]]

    def body(*refs):
        given, refs = (list(refs[:takes]), refs[takes:])
        made, refs = (list(refs[:gives]), refs[gives:])
        rest = refs[len(far_in) + len(far_out) :]
        reads, writes = ({}, {})
        if far_in:
            in_sem = rest[-1]
            rest = rest[:-1]
        if far_out:
            out_sem = rest[-1]
            rest = rest[:-1]
        for place, at in enumerate(far_in):
            reads[at] = pltpu.make_async_copy(given[at], refs[place], in_sem.at[place])
            given[at] = refs[place]
        for place, at in enumerate(far_out):
            mirror = refs[len(far_in) + place]
            writes[at] = pltpu.make_async_copy(mirror, made[at], out_sem.at[place])
            made[at] = mirror
        for at in sorted(reads, key=lambda at: args[at].size):
            reads[at].start()
        started = []

        def need(*wanted):
            for at in list(reads):
                if any(given[at] is ref for ref in wanted):
                    reads.pop(at).wait()

        def send(*ready):
            for at in list(writes):
                if any(made[at] is ref for ref in ready):
                    started.append(writes.pop(at))
                    started[-1].start()

        kernel(need, send, places(), *given, *made, *rest)
        need(*given)
        send(*made)
        for write in started:
            write.wait()

    spaces = {True: pltpu.VMEM, False: pltpu.HBM}
    args = [
        pltpu.with_memory_space_constraint(arg, spaces[near]) for arg, near in zip(args, near_in)
    ]
    return pl.pallas_call(
        body,
        out_shape=[spaces[near](out.shape, out.dtype) for out, near in zip(outs, near_out)],
        in_specs=[pl.BlockSpec(memory_space=spaces[near]) for near in near_in],
        out_specs=[pl.BlockSpec(memory_space=spaces[near]) for near in near_out],
        scratch_shapes=[pltpu.VMEM(args[at].shape, args[at].dtype) for at in far_in]
        + [pltpu.VMEM(outs[at].shape, outs[at].dtype) for at in far_out]
        + [pltpu.VMEM(shape, FULL) for shape in scratch]
        + [pltpu.SemaphoreType.DMA((len(far_out),))] * bool(far_out)
        + [pltpu.SemaphoreType.DMA((len(far_in),))] * bool(far_in),
        compiler_params=pltpu.CompilerParams(vmem_limit_bytes=VMEM_BYTES),
        cost_estimate=pl.CostEstimate(flops=0, bytes_accessed=0, transcendentals=0),
    )(*args)


def edges(parity_edges):
    size = lax.axis_size("row")
    inner = [(at, at ^ 1) for at in range(size)]
    outer = [(at, at + 1) for at in range(1, size - 1, 2)]
    outer = outer + [(to, at) for at, to in outer]
    return (
        lax.ppermute(parity_edges[0], "row", inner),
        lax.ppermute(parity_edges[1], "row", outer),
    )


def swap(field):
    return lax.ppermute(field, "half", [(0, 1), (1, 0)])


def steps_of(value, axis, step):
    size = lax.axis_size(axis)
    return lax.ppermute(value, axis, [(at, at ^ step) for at in range(size)])


def share(parts, axis):
    return [parts[0]] + [steps_of(parts[at], axis, at) for at in range(1, len(parts))]


def share_same(part, axis):
    size = lax.axis_size(axis)
    return [part] + [steps_of(part, axis, at) for at in range(1, size)]


def pair_outer(*pairs):
    size = lax.axis_size("im")
    first = pairs[0][0].value if isinstance(pairs[0][0], Near) else pairs[0][0]
    width = first.shape[1]
    rows = width // 2 // size * len(pairs)
    return list(
        call(
            functools.partial(pair_outer_kernel, pairs=len(pairs), parts=size),
            [Near(low(rows, width))] * size,
            [],
            *[ref for pair in pairs for ref in pair],
        )
    )


def sum_split(pieces, pairs):
    size = lax.axis_size("row")
    rows, width = pieces[0].shape
    return list(
        call(
            functools.partial(
                sum_split_kernel,
                pairs=pairs,
                parts=size,
                pieces=len(pieces),
            ),
            [Near(low(rows // size, width))] * size,
            [(rows, width)],
            *[Near(piece) for piece in pieces],
        )
    )


def add_low(pieces):
    total = pieces[0].astype(FULL)
    for piece in pieces[1:]:
        total = total + piece.astype(FULL)
    return total.astype(LOW)


def sum_far(left, right, axes):
    part = jnp.einsum("tm,tc->mc", left, right, preferred_element_type=FULL)
    return lax.psum(part, axes)


def shards(
    x_in,
    pre_reduce,
    pre_conv,
    pre_expand,
    pre_mid_gain,
    pre_mid_shift,
    pre_out_gain,
    pre_out_shift,
    post_reduce,
    post_conv,
    post_expand,
    post_mid_gain,
    post_mid_shift,
    post_out_gain,
    post_out_shift,
    read_weight,
    read_bias,
    cotangent,
):
    count, strip, side, width = x_in.shape
    strips = lax.axis_size("row")
    tokens = count * strip * side
    cols = side // 2
    rows = strip // 2
    slabs = count * rows
    padded = slabs * SLAB
    small = slabs * cols
    block = -(-small // SLAB) * SLAB
    features = read_weight.shape[1]
    x_low = x_in.reshape(tokens, width)
    pre_out_g, pre_out_s = (pre_out_gain[None], pre_out_shift[None])
    post_out_g, post_out_s = (post_out_gain[None], post_out_shift[None])
    pre_edge = Near(low(count, side, width))
    post_edge = Near(low(count, SLAB, width))
    quick = lax.axis_size("im") == 4 and strips == 4
    if quick:
        x_far = swap(x_low)

    first, edge_a, edge_b, normed_a, factor_a = call(
        pre_reduce_kernel,
        [Near(low(tokens, width)), pre_edge, pre_edge, like(tokens, width), like(tokens, LANES)],
        [(tokens, width)],
        x_low,
        pre_reduce,
        pre_mid_gain,
        pre_mid_shift,
    )
    got_a, got_b = edges((edge_a, edge_b))
    if quick:
        got_a, got_b, x_far = tie(got_a, got_b, x_far)
    (
        second,
        normed_b,
        factor_b,
        normed_c,
        factor_c,
        summed,
        pooled,
        post_first,
        edge_a,
        edge_b,
        post_normed_a,
        post_factor_a,
        pad,
    ) = call(
        pre_rest_kernel,
        [
            low(tokens, width),
            like(tokens, width),
            like(tokens, LANES),
            like(tokens, width),
            like(tokens, LANES),
            like(tokens, width),
            Near(like(padded, width)),
            Near(low(padded, width)),
            post_edge,
            post_edge,
            like(padded, width),
            like(padded, LANES),
            like(count, strip + 2, side, width),
        ],
        [(tokens, width), (side * width // LANES, LANES), (padded, width)],
        x_low,
        Near(first),
        Near(got_a),
        Near(got_b),
        pre_conv,
        pre_expand,
        pre_mid_gain,
        pre_mid_shift,
        pre_out_g,
        pre_out_s,
        post_reduce,
        post_mid_gain,
        post_mid_shift,
    )
    got_a, got_b = edges((edge_a, edge_b))
    if quick:
        second_far = swap(second)
        got_a, got_b, second_far = tie(got_a, got_b, second_far)
    (
        block_two,
        left_in,
        left_second,
        post_normed_b,
        post_factor_b,
        post_normed_c,
        post_factor_c,
        post_summed,
        post_pad,
    ) = call(
        functools.partial(post_rest_kernel, cols=cols),
        [
            Near(low(small, width)),
            low(block, width),
            low(block, width),
            like(padded, width),
            like(padded, LANES),
            like(padded, width),
            like(padded, LANES),
            like(padded, width),
            like(count, rows + 2, SLAB, width),
        ],
        [(padded, width), (padded, width), (block, width)],
        Near(pooled),
        Near(post_first),
        Near(got_a),
        Near(got_b),
        post_conv,
        post_expand,
        post_mid_gain,
        post_mid_shift,
        post_out_g,
        post_out_s,
    )
    whole = lax.all_gather(block_two, "row", axis=0, tiled=True)
    readout, grad_pre, *terms, d_read_b = call(
        functools.partial(readout_kernel, strips=strips),
        [
            like(*cotangent.shape, dtype=LOW),
            Near(low(strips * small, features)),
        ]
        + [Near(low(small, width))] * strips
        + [like(1, features)],
        [
            (strips * small, features),
            (strips * small, features),
            (strips * small, width),
        ],
        Near(whole),
        read_weight,
        read_bias[None],
        cotangent,
    )
    terms = share(terms, "row")
    if quick:
        parts = pair_outer(
            (Near(whole), Near(swap(whole)), Near(grad_pre), Near(swap(grad_pre)))
        )
        parts[0], *terms = tie(parts[0], *terms)
        read_parts = share(parts, "im")
    post_gs, post_ge, post_gc, edge_a, edge_b, post_small_b = call(
        functools.partial(post_back_kernel, cols=cols, strips=strips),
        [
            Near(like(padded, width)),
            Near(low(block, width)),
            Near(low(padded, width)),
            post_edge,
            post_edge,
            like(4, width),
        ],
        [(block, width), (padded, width), (padded, width), (padded, width)],
        *[Near(term) for term in terms],
        post_expand,
        post_mid_gain,
        post_mid_shift,
        post_out_g,
        post_normed_b,
        post_factor_b,
        post_normed_c,
        post_factor_c,
        post_summed,
    )
    got_a, got_b = edges((edge_a, edge_b))
    if quick:
        left_in_far, left_second_far, ge_far = (swap(left_in), swap(left_second), swap(post_ge))
        got_a, got_b, left_in_far, left_second_far, ge_far, *read_parts = tie(
            got_a, got_b, left_in_far, left_second_far, ge_far, *read_parts
        )
        read_part = add_low(read_parts)
        read_parts = [read_part, steps_of(read_part, "im", 1), steps_of(read_part, "im", 2)]
        got_a, got_b, *read_parts = tie(got_a, got_b, *read_parts)
    (
        post_gr,
        pre_gs,
        pre_ge,
        pre_gc,
        edge_a,
        edge_b,
        post_small_a,
        pre_small_b,
    ) = call(
        functools.partial(middle_back_kernel, cols=cols),
        [
            Near(low(block, width)),
            like(tokens, width),
            Near(low(tokens, width)),
            Near(low(tokens, width)),
            pre_edge,
            pre_edge,
            like(11, width),
            like(4, width),
        ],
        [
            (count, rows + 2, SLAB, width),
            (9, 8, width),
            (padded, width),
            (side * width // LANES, LANES),
            (tokens, width),
            (2, 8, width),
            (padded, width),
            (block, width),
        ],
        Near(post_gc),
        Near(got_a),
        Near(got_b),
        post_pad,
        post_conv,
        post_reduce,
        post_mid_gain,
        post_mid_shift,
        post_normed_a,
        post_factor_a,
        Near(post_gs),
        pre_expand,
        pre_mid_gain,
        pre_mid_shift,
        pre_out_g,
        normed_b,
        factor_b,
        normed_c,
        factor_c,
        summed,
    )
    got_a, got_b = edges((edge_a, edge_b))
    if quick:
        pre_ge_far = swap(pre_ge)
        post_parts = pair_outer(
            (left_in, left_in_far, Near(post_gr), Near(swap(post_gr))),
            (left_second, left_second_far, Near(post_ge), Near(ge_far)),
        )
        read_parts.append(steps_of(read_parts[0], "im", 3))
        got_a, got_b, pre_ge_far, post_parts[0], *read_parts = tie(
            got_a, got_b, pre_ge_far, post_parts[0], *read_parts
        )
        post_parts = share(post_parts, "im")
    pre_gr, pre_small_a = call(
        pre_back_kernel,
        [Near(low(tokens, width)), like(11, width)],
        [
            (count, strip + 2, side, width),
            (9, 8, width),
            (2, 8, width),
        ],
        Near(pre_gc),
        Near(got_a),
        Near(got_b),
        pad,
        pre_conv,
        pre_mid_gain,
        pre_mid_shift,
        normed_a,
        factor_a,
    )
    sums = jnp.concatenate([pre_small_a, pre_small_b, post_small_a, post_small_b, d_read_b])
    if quick:
        far = swap(pre_gr)
        sums = sums + swap(sums)
        sums, far = tie(sums, far)
        parts = pair_outer(
            (second, second_far, Near(pre_ge), Near(pre_ge_far)),
            (x_low, x_far, Near(pre_gr), Near(far)),
        )
        parts[0], *post_parts = tie(parts[0], *post_parts)
        post_parts = share(sum_split(post_parts, 2), "row")
        near_parts = [steps_of(parts[at], "im", at) for at in (1, 2)]
        sums = sums + steps_of(sums, "im", 1)
        grad_in = pre_gs + jnp.einsum("tm,cm->tc", pre_gr, pre_reduce, preferred_element_type=FULL)
        grad_in = grad_in.astype(LOW)
        sums, grad_in, last, *rest = tie(sums, grad_in, parts[3], *post_parts, *near_parts)
        post_parts, near_parts = (rest[:4], rest[4:])
        sums = sums + steps_of(sums, "im", 2)
        post_parts = share_same(add_low(post_parts), "row")
        last = steps_of(last, "im", 3)
        (read_total,) = assemble(read_parts + [swap(part) for part in read_parts], 1, 4, 1)
        sums, read_total, last, *post_parts = tie(sums, read_total, last, *post_parts)
        parts = share(sum_split([parts[0]] + near_parts + [last], 2), "row")
        whole_part = jnp.concatenate(post_parts, axis=0)
        post_parts = [whole_part, steps_of(whole_part, "im", 1), steps_of(whole_part, "im", 2)]
        read_bias_g = sums[30]
        sums = sums + steps_of(sums, "row", 1)
        sums, *rest = tie(sums, *parts, *post_parts)
        parts, post_parts = (rest[:4], rest[4:])
        parts = share_same(add_low(parts), "row")
        post_parts.append(steps_of(post_parts[0], "im", 3))
        sums = sums + steps_of(sums, "row", 2)
        sums, *rest = tie(sums, *parts, *post_parts)
        parts, post_parts = (rest[:4], rest[4:])
        whole_part = jnp.concatenate(parts, axis=0)
        parts = [whole_part, steps_of(whole_part, "im", 1), steps_of(whole_part, "im", 2)]
        post_parts = post_parts + [swap(part) for part in post_parts]
        post_reduce_g, post_expand_g = assemble(post_parts, 2, 4, strips)
        post_reduce_g, *parts = tie(post_reduce_g, *parts)
        parts.append(steps_of(parts[0], "im", 3))
        parts = parts + [swap(part) for part in parts]
        pre_expand_g, pre_reduce_g = assemble(parts, 2, 4, strips)
    else:
        axes = IMG + ("row",)
        post_reduce_g = sum_far(left_in, post_gr, axes)
        post_expand_g = sum_far(left_second, post_ge, axes)
        pre_expand_g = sum_far(second, pre_ge, axes)
        pre_reduce_g = sum_far(x_low, pre_gr, axes)
        read_total = sum_far(whole, grad_pre, IMG)
        read_bias_g = lax.psum(sums[30], IMG)
        sums = lax.psum(sums, axes)
        grad_in = pre_gs + jnp.einsum("tm,cm->tc", pre_gr, pre_reduce, preferred_element_type=FULL)
        grad_in = grad_in.astype(LOW)

    def small_grads(part):
        return (
            part[:9].reshape(3, 3, width),
            jnp.stack([part[9], part[11]]),
            jnp.stack([part[10], part[12]]),
            part[13],
            part[14],
        )

    pre_conv_g, pre_gain_g, pre_shift_g, pre_og_g, pre_os_g = small_grads(sums[:15])
    post_conv_g, post_gain_g, post_shift_g, post_og_g, post_os_g = small_grads(sums[15:30])
    return (
        readout,
        grad_in.reshape(x_in.shape),
        pre_reduce_g,
        pre_conv_g,
        pre_expand_g,
        pre_gain_g,
        pre_shift_g,
        pre_og_g,
        pre_os_g,
        post_reduce_g,
        post_conv_g,
        post_expand_g,
        post_gain_g,
        post_shift_g,
        post_og_g,
        post_os_g,
        read_total,
        read_bias_g,
    )


def solution(mesh):
    images, strips = mesh.devices.shape
    split = jax.sharding.Mesh(
        mesh.devices.reshape(images // 2, 2, strips), ("im", "half", "row")
    )
    return jax.shard_map(
        shards,
        mesh=split,
        in_specs=(P(IMG, "row", None, None),)
        + (P(),) * 14
        + (P(None, "row"), P("row"), P(IMG, None, None, "row")),
        out_specs=(P(IMG, None, None, "row"), P(IMG, "row", None, None))
        + (P(),) * 14
        + (P(None, "row"), P("row")),
        check_vma=False,
    )
```

```python
import functools

import jax
import jax.numpy as jnp
from jax import lax
from jax.experimental import pallas as pl
from jax.experimental.pallas import tpu as pltpu
from jax.sharding import PartitionSpec as P

EPSILON = 1e-06
SQRT_HALF = 0.7071067811865476
INV_SQRT_TWO_PI = 0.3989422804014327
LOW = jnp.bfloat16
FULL = jnp.float32
IMG = ("im", "half")
TILE = 256
SLAB = 16
LANES = 128
VMEM_BYTES = 24 * 1024 * 1024


def tie(*values):
    return lax.optimization_barrier(values)


def norm(value):
    centred = value - jnp.mean(value, axis=-1, keepdims=True)
    factor = lax.rsqrt(jnp.mean(centred * centred, axis=-1, keepdims=True) + EPSILON)
    return (centred * factor, factor)


def norm_back(grad, normed, factor, gain):
    scaled = grad * gain
    return factor * (
        scaled
        - jnp.mean(scaled, axis=-1, keepdims=True)
        - normed * jnp.mean(scaled * normed, axis=-1, keepdims=True)
    )


def gate(value):
    return 0.5 * jnp.tanh(0.5 * value) + 0.5


def silu(value):
    return value * gate(value)


def silu_back(grad, value):
    sigma = gate(value)
    return grad * sigma * (1.0 + value * (1.0 - sigma))


def flip(place, step):
    bit = 1
    while bit <= step:
        if step & bit:
            place = place + bit - 2 * bit * ((place // bit) % 2)
        bit *= 2
    return place


def wide(factor):
    return jnp.broadcast_to(factor, (factor.shape[0], LANES))


def fold(value):
    return jnp.sum(value.reshape(-1, 8, value.shape[-1]), axis=0)


def live(rows, cols):
    at = lax.broadcasted_iota(jnp.int32, (rows, 1), 0)
    return lax.rem(at, SLAB) < cols


def from_left(value):
    at = lax.broadcasted_iota(jnp.int32, (value.shape[0], 1), 0)
    return jnp.where(at == 0, 0.0, pltpu.roll(value, 1, 0))


def from_right(value):
    last = value.shape[0] - 1
    at = lax.broadcasted_iota(jnp.int32, (value.shape[0], 1), 0)
    return jnp.where(at == last, 0.0, pltpu.roll(value, last, 0))


def matmul(left_ref, right_ref, out_ref):
    @pl.loop(0, right_ref.shape[1] // TILE)
    def _(at):
        cols = pl.ds(pl.multiple_of(at * TILE, TILE), TILE)
        out_ref[:, cols] = jnp.dot(
            left_ref[...].astype(LOW), right_ref[:, cols], preferred_element_type=FULL
        )


def matmul_back(left_ref, right_ref, out_ref):
    @pl.loop(0, right_ref.shape[0] // TILE)
    def _(at):
        cols = pl.ds(pl.multiple_of(at * TILE, TILE), TILE)
        out_ref[:, cols] = lax.dot_general(
            left_ref[...].astype(LOW),
            right_ref[cols, :],
            (((1,), (1,)), ((), ())),
            preferred_element_type=FULL,
        ).astype(out_ref.dtype)


def rows_of(at, size):
    return pl.ds(pl.multiple_of(at * size, SLAB), size)


def fill_halo(at_ref, pad_ref, low_ref, got_a_ref, got_b_ref):
    count, rows, cols, width = pad_ref.shape
    rows = rows - 2
    even = lax.rem(at_ref[2], 2) == 0
    for image in range(count):
        got_a, got_b = (got_a_ref[image].astype(FULL), got_b_ref[image].astype(FULL))
        pad_ref[image, 0] = jnp.where(even, got_b, got_a)
        pad_ref[image, rows + 1] = jnp.where(even, got_a, got_b)

    size = cols if cols % SLAB == 0 else 2 * cols
    per = size // cols
    each = rows // per

    @pl.loop(0, count * each)
    def _(at):
        part = low_ref[rows_of(at, size), :].astype(FULL).reshape(per, cols, width)
        pad_ref[at // each, pl.ds(1 + per * lax.rem(at, each), per)] = part


def set_edges(at_ref, edge_a_ref, edge_b_ref, image, head, tail):
    even = lax.rem(at_ref[2], 2) == 0
    edge_a_ref[image] = jnp.where(even, tail, head).astype(LOW)
    edge_b_ref[image] = jnp.where(even, head, tail).astype(LOW)


def conv_row(pad_ref, taps, image, row):
    lines = [pad_ref[image, row + top] for top in range(3)]
    sums = [
        lines[0] * taps[left] + lines[1] * taps[3 + left] + lines[2] * taps[6 + left]
        for left in range(3)
    ]
    return from_left(sums[0]) + sums[1] + from_right(sums[2])


def conv_back_row(pad_ref, grad_ref, taps, taps_ref, image, row):
    lines = [grad_ref[image, row + top] for top in range(3)]
    sums = [
        lines[2] * taps[left] + lines[1] * taps[3 + left] + lines[0] * taps[6 + left]
        for left in range(3)
    ]
    shifted = [from_right(lines[1]), lines[1], from_left(lines[1])]
    for top in range(3):
        source = pad_ref[image, row + top]
        for left in range(3):
            taps_ref[3 * top + left] += fold(source * shifted[left])
    return from_right(sums[0]) + sums[1] + from_left(sums[2])


def pack(compact, source, out_ref, cols):
    compact[...] = jnp.zeros(compact.shape, FULL)
    for at in range(source.shape[0] // SLAB):
        compact[pl.ds(at * cols, cols), :] = source[pl.ds(at * SLAB, cols), :]
    out_ref[...] = compact[...].astype(LOW)


def narrow(pair, value):
    side = value.shape[0]
    parts = []
    for at in range(value.shape[1] // LANES):
        pair[pl.ds(at * side, side), :] = value[:, at * LANES : (at + 1) * LANES]
        parts.append(
            pair[pl.ds(at * side, side // 2, stride=2), :]
            + pair[pl.ds(at * side + 1, side // 2, stride=2), :]
        )
    return jnp.concatenate(parts, axis=1)


def widen(pair, value):
    cols = value.shape[0]
    parts = []
    for at in range(value.shape[1] // LANES):
        part = value[:, at * LANES : (at + 1) * LANES]
        pair[pl.ds(2 * cols * at, cols, stride=2), :] = part
        pair[pl.ds(2 * cols * at + 1, cols, stride=2), :] = part
        parts.append(pair[pl.ds(2 * cols * at, 2 * cols), :])
    return jnp.concatenate(parts, axis=1)


def tap_rows(conv_ref):
    lines = [conv_ref[top].astype(FULL) for top in range(3)]
    return [lines[at // 3][at % 3 : at % 3 + 1] for at in range(9)]


def finish(small_ref, sums_ref, at, place):
    small_ref[pl.ds(place, 1), :] = jnp.sum(sums_ref[at], axis=0, keepdims=True)


def pre_reduce_kernel(
    need,
    send,
    at_ref,
    x_ref, w_ref, gain_ref, shift_ref, first_ref, edge_a_ref, edge_b_ref, normed_ref, factor_ref, red
):
    count, side, width = edge_a_ref.shape
    size = 2 * side
    steps = x_ref.shape[0] // size
    need(x_ref, w_ref)
    matmul(x_ref, w_ref, red)
    need(gain_ref, shift_ref)
    gain, shift = (gain_ref[pl.ds(0, 1), :], shift_ref[pl.ds(0, 1), :])

    @pl.loop(0, steps)
    def _(at):
        rows = rows_of(at, size)
        normed, factor = norm(red[rows, :])
        normed_ref[rows, :] = normed
        factor_ref[rows, :] = wide(factor)
        first_ref[rows, :] = silu(normed * gain + shift).astype(LOW)

    each = steps // count
    for image in range(count):
        head = first_ref[pl.ds(image * each * size, size), :].astype(FULL)
        tail = first_ref[pl.ds((image * each + each - 1) * size, size), :].astype(FULL)
        set_edges(at_ref, edge_a_ref, edge_b_ref, image, head[:side], tail[side:])


def pre_rest_kernel(
    need,
    send,
    at_ref,
    x_ref,
    first_ref,
    got_a_ref,
    got_b_ref,
    conv_ref,
    expand_ref,
    gain_ref,
    shift_ref,
    out_gain_ref,
    out_shift_ref,
    reduce_ref,
    post_gain_ref,
    post_shift_ref,
    second_ref,
    normed_b_ref,
    factor_b_ref,
    normed_c_ref,
    factor_c_ref,
    summed_ref,
    pooled_ref,
    post_first_ref,
    edge_a_ref,
    edge_b_ref,
    post_normed_ref,
    post_factor_ref,
    pad,
    exp,
    pair,
    red,
):
    count, strip, side, width = pad.shape
    strip = strip - 2
    size = 2 * side
    each = strip // 2
    need(first_ref, got_a_ref, got_b_ref)
    fill_halo(at_ref, pad, first_ref, got_a_ref, got_b_ref)
    need(conv_ref, gain_ref, shift_ref)
    send(pad)
    taps = tap_rows(conv_ref)
    gain, shift = (gain_ref[pl.ds(1, 1), :], shift_ref[pl.ds(1, 1), :])

    @pl.loop(0, count * each)
    def _(at):
        rows = rows_of(at, size)
        image, row = (at // each, 2 * lax.rem(at, each))
        conv = jnp.concatenate(
            [conv_row(pad, taps, image, row), conv_row(pad, taps, image, row + 1)], axis=0
        )
        normed, factor = norm(conv)
        normed_b_ref[rows, :] = normed
        factor_b_ref[rows, :] = wide(factor)
        second_ref[rows, :] = silu(normed * gain + shift).astype(LOW)

    send(second_ref, normed_b_ref, factor_b_ref)
    need(expand_ref)
    matmul(second_ref, expand_ref, exp)
    need(x_ref, out_gain_ref, out_shift_ref)
    out_gain, out_shift = (out_gain_ref[...], out_shift_ref[...])
    cols = side // 2
    for at in range(count * each):
        rows = pl.ds(at * size, size)
        normed, factor = norm(exp[rows, :])
        normed_c_ref[rows, :] = normed
        factor_c_ref[rows, :] = wide(factor)
        summed = x_ref[rows, :].astype(FULL) + normed * out_gain + out_shift
        summed_ref[rows, :] = summed
        block = silu(summed)
        half = narrow(pair, block[:side] + block[side:])
        pooled_ref[pl.ds(at * SLAB, cols), :] = 0.25 * half
        pooled_ref[pl.ds(at * SLAB + cols, SLAB - cols), :] = jnp.zeros(
            (SLAB - cols, width), FULL
        )
    send(normed_c_ref, factor_c_ref, summed_ref)
    need(reduce_ref, post_gain_ref, post_shift_ref)
    matmul(pooled_ref, reduce_ref, red)
    normed, factor = norm(red[...])
    post_normed_ref[...] = normed
    post_factor_ref[...] = wide(factor)
    first = silu(normed * post_gain_ref[pl.ds(0, 1), :] + post_shift_ref[pl.ds(0, 1), :])
    post_first_ref[...] = jnp.where(live(red.shape[0], cols), first, 0.0).astype(LOW)
    for image in range(count):
        head = post_first_ref[pl.ds(image * each * SLAB, SLAB), :].astype(FULL)
        tail = post_first_ref[pl.ds((image * each + each - 1) * SLAB, SLAB), :].astype(FULL)
        set_edges(at_ref, edge_a_ref, edge_b_ref, image, head, tail)


def post_rest_kernel(
    need,
    send,
    at_ref,
    pooled_ref,
    first_ref,
    got_a_ref,
    got_b_ref,
    conv_ref,
    expand_ref,
    gain_ref,
    shift_ref,
    out_gain_ref,
    out_shift_ref,
    block_ref,
    left_in_ref,
    left_second_ref,
    normed_b_ref,
    factor_b_ref,
    normed_c_ref,
    factor_c_ref,
    summed_ref,
    pad,
    second,
    exp,
    compact,
    *,
    cols
):
    count, rows, _, width = pad.shape
    rows = rows - 2
    small = block_ref.shape[0]
    need(first_ref, got_a_ref, got_b_ref)
    fill_halo(at_ref, pad, first_ref, got_a_ref, got_b_ref)
    send(pad)
    need(conv_ref, gain_ref, shift_ref, pooled_ref)
    taps = tap_rows(conv_ref)
    gain, shift = (gain_ref[pl.ds(1, 1), :], shift_ref[pl.ds(1, 1), :])

    @pl.loop(0, count * rows)
    def _(at):
        place = rows_of(at, SLAB)
        normed, factor = norm(conv_row(pad, taps, at // rows, lax.rem(at, rows)))
        normed_b_ref[place, :] = normed
        factor_b_ref[place, :] = wide(factor)
        second[place, :] = silu(normed * gain + shift)

    send(normed_b_ref, factor_b_ref)
    need(expand_ref)
    matmul(second, expand_ref, exp)
    need(out_gain_ref, out_shift_ref)
    normed, factor = norm(exp[...])
    normed_c_ref[...] = normed
    factor_c_ref[...] = wide(factor)
    summed = pooled_ref[...] + normed * out_gain_ref[...] + out_shift_ref[...]
    summed_ref[...] = summed
    exp[...] = silu(summed)
    compact[...] = jnp.zeros(compact.shape, FULL)
    for at in range(count * rows):
        compact[pl.ds(at * cols, cols), :] = exp[pl.ds(at * SLAB, cols), :]
    block_ref[...] = compact[pl.ds(0, small), :].astype(LOW)
    send(block_ref, normed_c_ref, factor_c_ref, summed_ref)
    pack(compact, pooled_ref, left_in_ref, cols)
    pack(compact, second, left_second_ref, cols)


def readout_kernel(
    need,
    send,
    at_ref,
    whole_ref,
    w_ref,
    bias_ref,
    cot_ref,
    out_ref,
    grad_ref,
    *refs,
    strips
):
    slots, (bias_grad_ref, cot, out, terms_ref) = (refs[:strips], refs[strips:])
    images, lines, cols, _ = cot_ref.shape
    rows = lines // strips
    need(cot_ref)
    for at in range(images * lines):
        strip, image, row = (at // (images * rows), at // rows % images, at % rows)
        cot[pl.ds(at * cols, cols), :] = cot_ref[image, strip * rows + row].astype(FULL)
    need(whole_ref, w_ref, bias_ref)

    @pl.loop(0, w_ref.shape[1] // TILE)
    def _(at):
        lanes = pl.ds(pl.multiple_of(at * TILE, TILE), TILE)
        act = jnp.dot(whole_ref[...], w_ref[:, lanes], preferred_element_type=FULL)
        act = act + bias_ref[:, lanes]
        cdf = 0.5 * (1.0 + lax.erf(act * SQRT_HALF))
        density = jnp.exp(-0.5 * act * act) * INV_SQRT_TWO_PI
        out[:, lanes] = act * cdf
        grad = (cot[:, lanes] * (cdf + act * density)).astype(LOW)
        grad_ref[:, lanes] = grad
        bias_grad_ref[:, lanes] = jnp.sum(grad.astype(FULL), axis=0, keepdims=True)

    send(grad_ref, bias_grad_ref)
    matmul_back(grad_ref, w_ref, terms_ref)
    small = slots[0].shape[0]
    for step in range(strips):
        begin = pl.multiple_of(flip(at_ref[2], step) * small, 8)
        slots[step][...] = terms_ref[pl.ds(begin, small), :].astype(LOW)
    for at in range(images * lines):
        strip, image, row = (at // (images * rows), at // rows % images, at % rows)
        out_ref[image, strip * rows + row] = out[pl.ds(at * cols, cols), :].astype(LOW)


def post_back_kernel(
    need,
    send,
    at_ref,
    *refs,
    cols,
    strips
):
    pieces, refs = (refs[:strips], refs[strips:])
    (
    expand_ref,
    gain_ref,
    shift_ref,
    out_gain_ref,
    normed_b_ref,
    factor_b_ref,
    normed_c_ref,
    factor_c_ref,
    summed_ref,
    grad_sum_ref,
    grad_exp_ref,
    grad_conv_ref,
    edge_a_ref,
    edge_b_ref,
    small_ref,
    compact,
    spread_out,
    exp,
    sec,
    ) = refs
    count = edge_a_ref.shape[0]
    tokens, width = grad_sum_ref.shape
    each = tokens // SLAB // count
    need(*pieces)
    total = pieces[0][...].astype(FULL)
    for piece in pieces[1:]:
        total = total + piece[...].astype(FULL)
    compact[...] = jnp.zeros(compact.shape, FULL)
    compact[pl.ds(0, total.shape[0]), :] = total
    spread_out[...] = jnp.zeros((tokens, width), FULL)
    for at in range(tokens // SLAB):
        spread_out[pl.ds(at * SLAB, cols), :] = compact[pl.ds(at * cols, cols), :]
    need(summed_ref, normed_c_ref, factor_c_ref, out_gain_ref)
    grad_sum = silu_back(spread_out[...], summed_ref[...])
    grad_sum_ref[...] = grad_sum
    normed = normed_c_ref[...]
    exp[...] = norm_back(grad_sum, normed, factor_c_ref[:, :1], out_gain_ref[...])
    small_ref[pl.ds(2, 1), :] = jnp.sum(grad_sum * normed, axis=0, keepdims=True)
    small_ref[pl.ds(3, 1), :] = jnp.sum(grad_sum, axis=0, keepdims=True)
    pack(compact, exp, grad_exp_ref, cols)
    send(grad_sum_ref, grad_exp_ref)
    need(expand_ref)
    matmul_back(exp, expand_ref, sec)
    need(gain_ref, shift_ref, normed_b_ref, factor_b_ref)
    gain, shift = (gain_ref[pl.ds(1, 1), :], shift_ref[pl.ds(1, 1), :])
    normed = normed_b_ref[...]
    grad = silu_back(sec[...], normed * gain + shift)
    grad_conv_ref[...] = norm_back(grad, normed, factor_b_ref[:, :1], gain).astype(LOW)
    small_ref[pl.ds(0, 1), :] = jnp.sum(grad * normed, axis=0, keepdims=True)
    small_ref[pl.ds(1, 1), :] = jnp.sum(grad, axis=0, keepdims=True)
    for image in range(count):
        head = grad_conv_ref[pl.ds(image * each * SLAB, SLAB), :].astype(FULL)
        tail = grad_conv_ref[pl.ds((image * each + each - 1) * SLAB, SLAB), :].astype(FULL)
        set_edges(at_ref, edge_a_ref, edge_b_ref, image, head, tail)


def middle_back_kernel(
    need,
    send,
    at_ref,
    grad_conv_ref,
    got_a_ref,
    got_b_ref,
    pad,
    post_conv_ref,
    post_reduce_ref,
    post_gain_ref,
    post_shift_ref,
    post_normed_ref,
    post_factor_ref,
    post_grad_sum_ref,
    expand_ref,
    gain_ref,
    shift_ref,
    out_gain_ref,
    normed_b_ref,
    factor_b_ref,
    normed_c_ref,
    factor_c_ref,
    summed_ref,
    post_grad_red_ref,
    grad_sum_ref,
    grad_exp_ref,
    pre_grad_conv_ref,
    edge_a_ref,
    edge_b_ref,
    post_small_ref,
    small_ref,
    grad_pad,
    taps_sum,
    grad_in,
    pair,
    sec,
    sums,
    post_red,
    compact,
    *,
    cols
):
    count, side, width = edge_a_ref.shape
    need(grad_conv_ref, got_a_ref, got_b_ref)
    fill_halo(at_ref, grad_pad, grad_conv_ref, got_a_ref, got_b_ref)
    need(pad, post_conv_ref)
    need(post_gain_ref, post_shift_ref, post_normed_ref, post_factor_ref)
    taps = tap_rows(post_conv_ref)
    taps_sum[...] = jnp.zeros_like(taps_sum)
    sums[...] = jnp.zeros_like(sums)
    gain, shift = (post_gain_ref[pl.ds(0, 1), :], post_shift_ref[pl.ds(0, 1), :])
    each = post_grad_sum_ref.shape[0] // SLAB // count

    @pl.loop(0, count * each)
    def _(at):
        place = rows_of(at, SLAB)
        grad = conv_back_row(pad, grad_pad, taps, taps_sum, at // each, lax.rem(at, each))
        normed = post_normed_ref[place, :]
        grad = jnp.where(live(SLAB, cols), silu_back(grad, normed * gain + shift), 0.0)
        sums[0] += fold(grad * normed)
        sums[1] += fold(grad)
        post_red[place, :] = norm_back(grad, normed, post_factor_ref[place, :1], gain)

    for at in range(9):
        finish(post_small_ref, taps_sum, at, at)
    finish(post_small_ref, sums, 0, 9)
    finish(post_small_ref, sums, 1, 10)
    pack(compact, post_red, post_grad_red_ref, cols)
    send(post_grad_red_ref, post_small_ref)
    need(post_reduce_ref)
    matmul_back(post_red, post_reduce_ref, grad_in)
    sums[...] = jnp.zeros_like(sums)
    size = 2 * side
    need(out_gain_ref, post_grad_sum_ref, summed_ref, normed_c_ref, factor_c_ref)
    out_gain = out_gain_ref[...]
    for at in range(count * each):
        rows = pl.ds(at * size, size)
        place = pl.ds(at * SLAB, cols)
        grad = 0.25 * (post_grad_sum_ref[place, :] + grad_in[place, :])
        grad = widen(pair, grad)
        grad = jnp.concatenate([grad, grad], axis=0)
        grad_sum = silu_back(grad, summed_ref[rows, :])
        grad_sum_ref[rows, :] = grad_sum
        normed = normed_c_ref[rows, :]
        sums[0] += fold(grad_sum * normed)
        sums[1] += fold(grad_sum)
        grad_exp_ref[rows, :] = norm_back(
            grad_sum, normed, factor_c_ref[rows, :1], out_gain
        ).astype(LOW)
    finish(small_ref, sums, 0, 2)
    finish(small_ref, sums, 1, 3)
    send(grad_sum_ref, grad_exp_ref)
    need(expand_ref)
    matmul_back(grad_exp_ref, expand_ref, sec)
    need(gain_ref, shift_ref, normed_b_ref, factor_b_ref)
    sums[...] = jnp.zeros_like(sums)
    gain_b, shift_b = (gain_ref[pl.ds(1, 1), :], shift_ref[pl.ds(1, 1), :])

    @pl.loop(0, count * each)
    def _(at):
        rows = rows_of(at, size)
        normed = normed_b_ref[rows, :]
        grad = silu_back(sec[rows, :], normed * gain_b + shift_b)
        sums[0] += fold(grad * normed)
        sums[1] += fold(grad)
        pre_grad_conv_ref[rows, :] = norm_back(
            grad, normed, factor_b_ref[rows, :1], gain_b
        ).astype(LOW)

    finish(small_ref, sums, 0, 0)
    finish(small_ref, sums, 1, 1)
    for image in range(count):
        head = pre_grad_conv_ref[pl.ds(image * each * size, size), :].astype(FULL)
        tail = pre_grad_conv_ref[pl.ds((image * each + each - 1) * size, size), :].astype(FULL)
        set_edges(at_ref, edge_a_ref, edge_b_ref, image, head[:side], tail[side:])


def pre_back_kernel(
    need,
    send,
    at_ref,
    grad_conv_ref,
    got_a_ref,
    got_b_ref,
    pad,
    conv_ref,
    gain_ref,
    shift_ref,
    normed_ref,
    factor_ref,
    grad_red_ref,
    small_ref,
    grad_pad,
    taps_sum,
    sums,
):
    count, strip, side, width = pad.shape
    strip = strip - 2
    size = 2 * side
    each = strip // 2
    need(grad_conv_ref, got_a_ref, got_b_ref)
    fill_halo(at_ref, grad_pad, grad_conv_ref, got_a_ref, got_b_ref)
    need(pad, conv_ref)
    need(gain_ref, shift_ref, normed_ref, factor_ref)
    taps = tap_rows(conv_ref)
    taps_sum[...] = jnp.zeros_like(taps_sum)
    sums[...] = jnp.zeros_like(sums)
    gain, shift = (gain_ref[pl.ds(0, 1), :], shift_ref[pl.ds(0, 1), :])

    @pl.loop(0, count * each)
    def _(at):
        rows = rows_of(at, size)
        image, row = (at // each, 2 * lax.rem(at, each))
        grad = jnp.concatenate(
            [
                conv_back_row(pad, grad_pad, taps, taps_sum, image, row),
                conv_back_row(pad, grad_pad, taps, taps_sum, image, row + 1),
            ],
            axis=0,
        )
        normed = normed_ref[rows, :]
        grad = silu_back(grad, normed * gain + shift)
        sums[0] += fold(grad * normed)
        sums[1] += fold(grad)
        grad_red_ref[rows, :] = norm_back(grad, normed, factor_ref[rows, :1], gain).astype(LOW)

    for at in range(9):
        finish(small_ref, taps_sum, at, at)
    finish(small_ref, sums, 0, 9)
    finish(small_ref, sums, 1, 10)


def pair_outer_kernel(need, send, at_ref, *refs, pairs, parts):
    takes = 4 * pairs
    outs = refs[takes:]
    half, plane = (at_ref[0], at_ref[1])
    rows = outs[0].shape[0] // pairs
    for pair in range(pairs):
        left, left_far, right, right_far = refs[4 * pair : 4 * pair + 4]
        need(left, left_far, right, right_far)
        for step in range(parts):
            begin = half * (rows * parts) + flip(plane, step) * rows
            lanes = pl.ds(pl.multiple_of(begin, LANES), rows)
            total = lax.dot_general(
                left[:, lanes], right[...], (((0,), (0,)), ((), ())), preferred_element_type=FULL
            ) + lax.dot_general(
                left_far[:, lanes],
                right_far[...],
                (((0,), (0,)), ((), ())),
                preferred_element_type=FULL,
            )
            outs[step][pl.ds(pair * rows, rows), :] = total.astype(LOW)
    send(*outs)


def sum_split_kernel(need, send, at_ref, *refs, pairs, parts, pieces, along=2):
    takes, outs = (refs[:pieces], refs[pieces : pieces + parts])
    total = refs[-1]
    need(*takes)
    value = takes[0][...].astype(FULL)
    for at in range(1, pieces):
        value = value + takes[at][...].astype(FULL)
    total[...] = value
    rows = total.shape[0] // pairs // parts
    for step in range(parts):
        begin = flip(at_ref[along], step) * rows
        for pair in range(pairs):
            place = pl.ds(pl.multiple_of(pair * rows * parts + begin, SLAB), rows)
            outs[step][pl.ds(pair * rows, rows), :] = total[place, :].astype(LOW)
    send(*outs)


def assemble_kernel(*refs, pairs, planes, strips, cut):
    takes = 2 * (planes + cut)
    parts, outs = (refs[:takes], refs[takes : takes + pairs])
    full, sem = (refs[takes + pairs : takes + 2 * pairs], refs[-1])
    half, plane, row = places()
    rows = parts[0].shape[0] // pairs // strips
    block = strips * rows
    writes = []
    for pair in range(pairs):
        for at in range(2 * planes):
            side, spot = (flip(half, at // planes), flip(plane, at % planes))
            for step in range(strips):
                place = side * (planes * block) + spot * block
                if strips > 1:
                    place = place + flip(row, step) * rows
                source, begin = (at % planes, step)
                if cut and source == planes - 1 and 2 * step >= strips:
                    source, begin = (planes, step - strips // 2)
                part = parts[at // planes * (planes + cut) + source]
                full[pair][pl.ds(pl.multiple_of(place, SLAB), rows), :] = part[
                    pl.ds((begin * pairs + pair) * rows, rows), :
                ].astype(FULL)
        writes.append(pltpu.make_async_copy(full[pair], outs[pair], sem.at[pair]))
        writes[-1].start()
    for write in writes:
        write.wait()


def assemble(parts, pairs, planes, strips):
    takes = len(parts)
    out = like(2 * planes * parts[0].shape[0] // pairs, parts[0].shape[1])
    parts = [pltpu.with_memory_space_constraint(part, pltpu.VMEM) for part in parts]
    return pl.pallas_call(
        functools.partial(
            assemble_kernel, pairs=pairs, planes=planes, strips=strips, cut=takes // 2 - planes
        ),
        out_shape=[pltpu.HBM(out.shape, out.dtype)] * pairs,
        in_specs=[pl.BlockSpec(memory_space=pltpu.VMEM)] * takes,
        out_specs=[pl.BlockSpec(memory_space=pltpu.HBM)] * pairs,
        scratch_shapes=[pltpu.VMEM(out.shape, FULL)] * pairs + [pltpu.SemaphoreType.DMA((pairs,))],
        compiler_params=pltpu.CompilerParams(vmem_limit_bytes=VMEM_BYTES),
        cost_estimate=pl.CostEstimate(flops=0, bytes_accessed=0, transcendentals=0),
    )(*parts)


class Near:
    def __init__(self, value):
        self.value = value


def like(*shape, dtype=FULL):
    return jax.ShapeDtypeStruct(shape, dtype)


def low(*shape):
    return like(*shape, dtype=LOW)


def places():
    return [lax.axis_index(axis) for axis in ("half", "im", "row")]


def call(kernel, outs, scratch, *args):
    near_in = [isinstance(arg, Near) for arg in args]
    near_out = [isinstance(out, Near) for out in outs]
    args = [arg.value if isinstance(arg, Near) else arg for arg in args]
    outs = [out.value if isinstance(out, Near) else out for out in outs]
    takes, gives = (len(args), len(outs))
    far_in = [at for at in range(takes) if not near_in[at]]
    far_out = [at for at in range(gives) if not near_out[at]]

    def body(*refs):
        given, refs = (list(refs[:takes]), refs[takes:])
        made, refs = (list(refs[:gives]), refs[gives:])
        rest = refs[len(far_in) + len(far_out) :]
        reads, writes = ({}, {})
        if far_in:
            in_sem = rest[-1]
            rest = rest[:-1]
        if far_out:
            out_sem = rest[-1]
            rest = rest[:-1]
        for place, at in enumerate(far_in):
            reads[at] = pltpu.make_async_copy(given[at], refs[place], in_sem.at[place])
            given[at] = refs[place]
        for place, at in enumerate(far_out):
            mirror = refs[len(far_in) + place]
            writes[at] = pltpu.make_async_copy(mirror, made[at], out_sem.at[place])
            made[at] = mirror
        for at in sorted(reads, key=lambda at: args[at].size):
            reads[at].start()
        started = []

        def need(*wanted):
            for at in list(reads):
                if any(given[at] is ref for ref in wanted):
                    reads.pop(at).wait()

        def send(*ready):
            for at in list(writes):
                if any(made[at] is ref for ref in ready):
                    started.append(writes.pop(at))
                    started[-1].start()

        kernel(need, send, places(), *given, *made, *rest)
        need(*given)
        send(*made)
        for write in started:
            write.wait()

    spaces = {True: pltpu.VMEM, False: pltpu.HBM}
    args = [
        pltpu.with_memory_space_constraint(arg, spaces[near]) for arg, near in zip(args, near_in)
    ]
    return pl.pallas_call(
        body,
        out_shape=[spaces[near](out.shape, out.dtype) for out, near in zip(outs, near_out)],
        in_specs=[pl.BlockSpec(memory_space=spaces[near]) for near in near_in],
        out_specs=[pl.BlockSpec(memory_space=spaces[near]) for near in near_out],
        scratch_shapes=[pltpu.VMEM(args[at].shape, args[at].dtype) for at in far_in]
        + [pltpu.VMEM(outs[at].shape, outs[at].dtype) for at in far_out]
        + [pltpu.VMEM(shape, FULL) for shape in scratch]
        + [pltpu.SemaphoreType.DMA((len(far_out),))] * bool(far_out)
        + [pltpu.SemaphoreType.DMA((len(far_in),))] * bool(far_in),
        compiler_params=pltpu.CompilerParams(vmem_limit_bytes=VMEM_BYTES),
        cost_estimate=pl.CostEstimate(flops=0, bytes_accessed=0, transcendentals=0),
    )(*args)


def edges(parity_edges):
    size = lax.axis_size("row")
    inner = [(at, at ^ 1) for at in range(size)]
    outer = [(at, at + 1) for at in range(1, size - 1, 2)]
    outer = outer + [(to, at) for at, to in outer]
    return (
        lax.ppermute(parity_edges[0], "row", inner),
        lax.ppermute(parity_edges[1], "row", outer),
    )


def swap(field):
    return lax.ppermute(field, "half", [(0, 1), (1, 0)])


def steps_of(value, axis, step):
    size = lax.axis_size(axis)
    return lax.ppermute(value, axis, [(at, at ^ step) for at in range(size)])


def share(parts, axis):
    return [parts[0]] + [steps_of(parts[at], axis, at) for at in range(1, len(parts))]


def share_same(part, axis):
    size = lax.axis_size(axis)
    return [part] + [steps_of(part, axis, at) for at in range(1, size)]


def gather_near(part):
    return [part, steps_of(part, "im", 1), steps_of(part, "im", 2)]


def gather_rest(parts):
    half = parts[0].shape[0] // 2
    return [steps_of(parts[1][:half], "im", 2), steps_of(parts[2][half:], "im", 1)]


def small_outputs(part, width):
    return [
        part[:9].reshape(3, 3, width),
        jnp.stack([part[9], part[11]]),
        jnp.stack([part[10], part[12]]),
        part[13],
        part[14],
    ]


def pair_outer(*pairs):
    size = lax.axis_size("im")
    first = pairs[0][0].value if isinstance(pairs[0][0], Near) else pairs[0][0]
    width = first.shape[1]
    rows = width // 2 // size * len(pairs)
    return list(
        call(
            functools.partial(pair_outer_kernel, pairs=len(pairs), parts=size),
            [Near(low(rows, width))] * size,
            [],
            *[ref for pair in pairs for ref in pair],
        )
    )


def sum_split(pieces, pairs):
    size = lax.axis_size("row")
    rows, width = pieces[0].shape
    return list(
        call(
            functools.partial(
                sum_split_kernel,
                pairs=pairs,
                parts=size,
                pieces=len(pieces),
            ),
            [Near(low(rows // size, width))] * size,
            [(rows, width)],
            *[Near(piece) for piece in pieces],
        )
    )


def add_low(pieces):
    total = pieces[0].astype(FULL)
    for piece in pieces[1:]:
        total = total + piece.astype(FULL)
    return total.astype(LOW)


def sum_far(left, right, axes):
    part = jnp.einsum("tm,tc->mc", left, right, preferred_element_type=FULL)
    return lax.psum(part, axes)


def shards(
    x_in,
    pre_reduce,
    pre_conv,
    pre_expand,
    pre_mid_gain,
    pre_mid_shift,
    pre_out_gain,
    pre_out_shift,
    post_reduce,
    post_conv,
    post_expand,
    post_mid_gain,
    post_mid_shift,
    post_out_gain,
    post_out_shift,
    read_weight,
    read_bias,
    cotangent,
):
    count, strip, side, width = x_in.shape
    strips = lax.axis_size("row")
    tokens = count * strip * side
    cols = side // 2
    rows = strip // 2
    slabs = count * rows
    padded = slabs * SLAB
    small = slabs * cols
    block = -(-small // SLAB) * SLAB
    features = read_weight.shape[1]
    x_low = x_in.reshape(tokens, width)
    pre_out_g, pre_out_s = (pre_out_gain[None], pre_out_shift[None])
    post_out_g, post_out_s = (post_out_gain[None], post_out_shift[None])
    pre_edge = Near(low(count, side, width))
    post_edge = Near(low(count, SLAB, width))
    quick = lax.axis_size("im") == 4 and strips == 4

    first, edge_a, edge_b, normed_a, factor_a = call(
        pre_reduce_kernel,
        [Near(low(tokens, width)), pre_edge, pre_edge, like(tokens, width), like(tokens, LANES)],
        [(tokens, width)],
        x_low,
        pre_reduce,
        pre_mid_gain,
        pre_mid_shift,
    )
    got_a, got_b = edges((edge_a, edge_b))
    (
        second,
        normed_b,
        factor_b,
        normed_c,
        factor_c,
        summed,
        pooled,
        post_first,
        edge_a,
        edge_b,
        post_normed_a,
        post_factor_a,
        pad,
    ) = call(
        pre_rest_kernel,
        [
            low(tokens, width),
            like(tokens, width),
            like(tokens, LANES),
            like(tokens, width),
            like(tokens, LANES),
            like(tokens, width),
            Near(like(padded, width)),
            Near(low(padded, width)),
            post_edge,
            post_edge,
            like(padded, width),
            like(padded, LANES),
            like(count, strip + 2, side, width),
        ],
        [(tokens, width), (side * width // LANES, LANES), (padded, width)],
        x_low,
        Near(first),
        Near(got_a),
        Near(got_b),
        pre_conv,
        pre_expand,
        pre_mid_gain,
        pre_mid_shift,
        pre_out_g,
        pre_out_s,
        post_reduce,
        post_mid_gain,
        post_mid_shift,
    )
    got_a, got_b = edges((edge_a, edge_b))
    (
        block_two,
        left_in,
        left_second,
        post_normed_b,
        post_factor_b,
        post_normed_c,
        post_factor_c,
        post_summed,
        post_pad,
    ) = call(
        functools.partial(post_rest_kernel, cols=cols),
        [
            Near(low(small, width)),
            low(block, width),
            low(block, width),
            like(padded, width),
            like(padded, LANES),
            like(padded, width),
            like(padded, LANES),
            like(padded, width),
            like(count, rows + 2, SLAB, width),
        ],
        [(padded, width), (padded, width), (block, width)],
        Near(pooled),
        Near(post_first),
        Near(got_a),
        Near(got_b),
        post_conv,
        post_expand,
        post_mid_gain,
        post_mid_shift,
        post_out_g,
        post_out_s,
    )
    whole = lax.all_gather(block_two, "row", axis=0, tiled=True)
    readout, grad_pre, *terms, d_read_b = call(
        functools.partial(readout_kernel, strips=strips),
        [
            like(*cotangent.shape, dtype=LOW),
            Near(low(strips * small, features)),
        ]
        + [Near(low(small, width))] * strips
        + [like(1, features)],
        [
            (strips * small, features),
            (strips * small, features),
            (strips * small, width),
        ],
        Near(whole),
        read_weight,
        read_bias[None],
        cotangent,
    )
    terms = share(terms, "row")
    if quick:
        whole, grad_pre = tie(whole, grad_pre)
        parts = pair_outer(
            (Near(whole), Near(swap(whole)), Near(grad_pre), Near(swap(grad_pre)))
        )
        parts[0], *terms = tie(parts[0], *terms)
        read_parts = share(parts, "im")
    post_gs, post_ge, post_gc, edge_a, edge_b, post_small_b = call(
        functools.partial(post_back_kernel, cols=cols, strips=strips),
        [
            Near(like(padded, width)),
            Near(low(block, width)),
            Near(low(padded, width)),
            post_edge,
            post_edge,
            like(4, width),
        ],
        [(block, width), (padded, width), (padded, width), (padded, width)],
        *[Near(term) for term in terms],
        post_expand,
        post_mid_gain,
        post_mid_shift,
        post_out_g,
        post_normed_b,
        post_factor_b,
        post_normed_c,
        post_factor_c,
        post_summed,
    )
    got_a, got_b = edges((edge_a, edge_b))
    if quick:
        left_in_far, left_second_far, ge_far = (swap(left_in), swap(left_second), swap(post_ge))
        got_a, got_b, left_in_far, left_second_far, ge_far, *read_parts = tie(
            got_a, got_b, left_in_far, left_second_far, ge_far, *read_parts
        )
    (
        post_gr,
        pre_gs,
        pre_ge,
        pre_gc,
        edge_a,
        edge_b,
        post_small_a,
        pre_small_b,
    ) = call(
        functools.partial(middle_back_kernel, cols=cols),
        [
            Near(low(block, width)),
            like(tokens, width),
            Near(low(tokens, width)),
            Near(low(tokens, width)),
            pre_edge,
            pre_edge,
            like(11, width),
            like(4, width),
        ],
        [
            (count, rows + 2, SLAB, width),
            (9, 8, width),
            (padded, width),
            (side * width // LANES, LANES),
            (tokens, width),
            (2, 8, width),
            (padded, width),
            (block, width),
        ],
        Near(post_gc),
        Near(got_a),
        Near(got_b),
        post_pad,
        post_conv,
        post_reduce,
        post_mid_gain,
        post_mid_shift,
        post_normed_a,
        post_factor_a,
        Near(post_gs),
        pre_expand,
        pre_mid_gain,
        pre_mid_shift,
        pre_out_g,
        normed_b,
        factor_b,
        normed_c,
        factor_c,
        summed,
    )
    got_a, got_b = edges((edge_a, edge_b))
    if quick:
        pre_ge_far = swap(pre_ge)
        post_parts = pair_outer(
            (left_in, left_in_far, Near(post_gr), Near(swap(post_gr))),
            (left_second, left_second_far, Near(post_ge), Near(ge_far)),
        )
        post_parts = pair_outer(
            (left_in, left_in_far, Near(post_gr), Near(swap(post_gr))),
            (left_second, left_second_far, Near(post_ge), Near(ge_far)),
        )
        post_sums = [steps_of(post_parts[at], "im", at) for at in (1, 2)]
        read_parts = gather_near(add_low(read_parts))
        got_a, got_b, *rest = tie(got_a, got_b, *post_sums, *read_parts)
        post_sums, read_parts = (rest[:2], rest[2:])
    pre_gr, pre_small_a = call(
        pre_back_kernel,
        [Near(low(tokens, width)), like(11, width)],
        [
            (count, strip + 2, side, width),
            (9, 8, width),
            (2, 8, width),
        ],
        Near(pre_gc),
        Near(got_a),
        Near(got_b),
        pad,
        pre_conv,
        pre_mid_gain,
        pre_mid_shift,
        normed_a,
        factor_a,
    )
    sums = jnp.concatenate([pre_small_a, pre_small_b, post_small_a, post_small_b, d_read_b])
    if quick:
        post_sums = post_sums + [steps_of(post_parts[3], "im", 3)]
        parts = pair_outer(
            (second, swap(second), Near(pre_ge), Near(swap(pre_ge))),
            (x_low, swap(x_low), Near(pre_gr), Near(swap(pre_gr))),
        )
        sums = sums + swap(sums)
        sums, parts[0], *post_sums = tie(sums, parts[0], *post_sums)
        post_parts = share(sum_split(post_parts[:1] + post_sums, 2), "row")
        near_parts = [steps_of(parts[at], "im", at) for at in (1, 2)]
        sums = sums + steps_of(sums, "im", 1)
        grad_in = pre_gs + jnp.einsum("tm,cm->tc", pre_gr, pre_reduce, preferred_element_type=FULL)
        grad_in = grad_in.astype(LOW)
        sums, grad_in, last, *rest = tie(sums, grad_in, parts[3], *post_parts, *near_parts)
        post_parts, near_parts = (rest[:4], rest[4:])
        sums = sums + steps_of(sums, "im", 2)
        post_parts = share_same(add_low(post_parts), "row")
        last = steps_of(last, "im", 3)
        sums, last, *post_parts = tie(sums, last, *post_parts)
        parts = share(sum_split([parts[0]] + near_parts + [last], 2), "row")
        post_parts = gather_near(jnp.concatenate(post_parts, axis=0))
        read_bias_g = sums[30]
        sums = sums + steps_of(sums, "row", 1)
        read_last = steps_of(read_parts[0], "im", 3)
        sums, read_last, *rest = tie(sums, read_last, *parts, *post_parts)
        parts, post_parts = (rest[:4], rest[4:])
        read_parts = read_parts + [read_last]
        parts = share_same(add_low(parts), "row")
        post_far = [swap(part) for part in post_parts]
        post_parts = post_parts + gather_rest(post_parts)
        sums = sums + steps_of(sums, "row", 2)
        (read_total,) = assemble(read_parts + [swap(part) for part in read_parts], 1, 4, 1)
        sums, read_total, *rest = tie(sums, read_total, *parts, *post_parts, *post_far)
        parts, post_parts, post_far = (rest[:4], rest[4:9], rest[9:])
        parts = gather_near(jnp.concatenate(parts, axis=0))
        post_far = post_far + [swap(part) for part in post_parts[3:]]
        post_reduce_g, post_expand_g = assemble(post_parts + post_far, 2, 4, strips)
        small_out = small_outputs(sums[:15], width) + small_outputs(sums[15:30], width)
        post_reduce_g, *rest = tie(post_reduce_g, *parts, *small_out)
        parts, small_out = (rest[:3], rest[3:])
        far = [swap(part) for part in parts]
        parts = parts + gather_rest(parts)
        far = far + [swap(part) for part in parts[3:]]
        pre_expand_g, pre_reduce_g = assemble(parts + far, 2, 4, strips)
    else:
        axes = IMG + ("row",)
        post_reduce_g = sum_far(left_in, post_gr, axes)
        post_expand_g = sum_far(left_second, post_ge, axes)
        pre_expand_g = sum_far(second, pre_ge, axes)
        pre_reduce_g = sum_far(x_low, pre_gr, axes)
        read_total = sum_far(whole, grad_pre, IMG)
        read_bias_g = lax.psum(sums[30], IMG)
        sums = lax.psum(sums, axes)
        small_out = small_outputs(sums[:15], width) + small_outputs(sums[15:30], width)
        grad_in = pre_gs + jnp.einsum("tm,cm->tc", pre_gr, pre_reduce, preferred_element_type=FULL)
        grad_in = grad_in.astype(LOW)

    pre_conv_g, pre_gain_g, pre_shift_g, pre_og_g, pre_os_g = small_out[:5]
    post_conv_g, post_gain_g, post_shift_g, post_og_g, post_os_g = small_out[5:]
    return (
        readout,
        grad_in.reshape(x_in.shape),
        pre_reduce_g,
        pre_conv_g,
        pre_expand_g,
        pre_gain_g,
        pre_shift_g,
        pre_og_g,
        pre_os_g,
        post_reduce_g,
        post_conv_g,
        post_expand_g,
        post_gain_g,
        post_shift_g,
        post_og_g,
        post_os_g,
        read_total,
        read_bias_g,
    )


def solution(mesh):
    images, strips = mesh.devices.shape
    split = jax.sharding.Mesh(
        mesh.devices.reshape(images // 2, 2, strips), ("im", "half", "row")
    )
    return jax.shard_map(
        shards,
        mesh=split,
        in_specs=(P(IMG, "row", None, None),)
        + (P(),) * 14
        + (P(None, "row"), P("row"), P(IMG, None, None, "row")),
        out_specs=(P(IMG, None, None, "row"), P(IMG, "row", None, None))
        + (P(),) * 14
        + (P(None, "row"), P("row")),
        check_vma=False,
    )
```

```python
import functools

import jax
import jax.numpy as jnp
from jax import lax
from jax.experimental import pallas as pl
from jax.experimental.pallas import tpu as pltpu
from jax.sharding import PartitionSpec as P

EPSILON = 1e-06
SQRT_HALF = 0.7071067811865476
INV_SQRT_TWO_PI = 0.3989422804014327
LOW = jnp.bfloat16
FULL = jnp.float32
IMG = ("im", "half")
TILE = 256
SLAB = 16
LANES = 128
VMEM_BYTES = 24 * 1024 * 1024


def tie(*values):
    return lax.optimization_barrier(values)


def tie_later(first, second):
    first = list(tie(*first))
    out = list(tie(*first, *second))
    return (out[: len(first)], out[len(first) :])


def norm(value):
    centred = value - jnp.mean(value, axis=-1, keepdims=True)
    factor = lax.rsqrt(jnp.mean(centred * centred, axis=-1, keepdims=True) + EPSILON)
    return (centred * factor, factor)


def norm_back(grad, normed, factor, gain):
    scaled = grad * gain
    return factor * (
        scaled
        - jnp.mean(scaled, axis=-1, keepdims=True)
        - normed * jnp.mean(scaled * normed, axis=-1, keepdims=True)
    )


def gate(value):
    return 0.5 * jnp.tanh(0.5 * value) + 0.5


def silu(value):
    return value * gate(value)


def silu_back(grad, value):
    sigma = gate(value)
    return grad * sigma * (1.0 + value * (1.0 - sigma))


def flip(place, step):
    bit = 1
    while bit <= step:
        if step & bit:
            place = place + bit - 2 * bit * ((place // bit) % 2)
        bit *= 2
    return place


def wide(factor):
    return jnp.broadcast_to(factor, (factor.shape[0], LANES))


def fold(value):
    return jnp.sum(value.reshape(-1, 8, value.shape[-1]), axis=0)


def live(rows, cols):
    at = lax.broadcasted_iota(jnp.int32, (rows, 1), 0)
    return lax.rem(at, SLAB) < cols


def from_left(value):
    at = lax.broadcasted_iota(jnp.int32, (value.shape[0], 1), 0)
    return jnp.where(at == 0, 0.0, pltpu.roll(value, 1, 0))


def from_right(value):
    last = value.shape[0] - 1
    at = lax.broadcasted_iota(jnp.int32, (value.shape[0], 1), 0)
    return jnp.where(at == last, 0.0, pltpu.roll(value, last, 0))


def matmul(left_ref, right_ref, out_ref):
    @pl.loop(0, right_ref.shape[1] // TILE)
    def _(at):
        cols = pl.ds(pl.multiple_of(at * TILE, TILE), TILE)
        out_ref[:, cols] = jnp.dot(
            left_ref[...].astype(LOW), right_ref[:, cols], preferred_element_type=FULL
        )


def matmul_back(left_ref, right_ref, out_ref):
    @pl.loop(0, right_ref.shape[0] // TILE)
    def _(at):
        cols = pl.ds(pl.multiple_of(at * TILE, TILE), TILE)
        out_ref[:, cols] = lax.dot_general(
            left_ref[...].astype(LOW),
            right_ref[cols, :],
            (((1,), (1,)), ((), ())),
            preferred_element_type=FULL,
        ).astype(out_ref.dtype)


def rows_of(at, size):
    return pl.ds(pl.multiple_of(at * size, SLAB), size)


def fill_halo(at_ref, pad_ref, low_ref, got_a_ref, got_b_ref):
    count, rows, cols, width = pad_ref.shape
    rows = rows - 2
    even = lax.rem(at_ref[2], 2) == 0
    for image in range(count):
        got_a, got_b = (got_a_ref[image].astype(FULL), got_b_ref[image].astype(FULL))
        pad_ref[image, 0] = jnp.where(even, got_b, got_a)
        pad_ref[image, rows + 1] = jnp.where(even, got_a, got_b)

    size = cols if cols % SLAB == 0 else 2 * cols
    per = size // cols
    each = rows // per

    @pl.loop(0, count * each)
    def _(at):
        part = low_ref[rows_of(at, size), :].astype(FULL).reshape(per, cols, width)
        pad_ref[at // each, pl.ds(1 + per * lax.rem(at, each), per)] = part


def set_edges(at_ref, edge_a_ref, edge_b_ref, image, head, tail):
    even = lax.rem(at_ref[2], 2) == 0
    edge_a_ref[image] = jnp.where(even, tail, head).astype(LOW)
    edge_b_ref[image] = jnp.where(even, head, tail).astype(LOW)


def conv_row(pad_ref, taps, image, row):
    lines = [pad_ref[image, row + top] for top in range(3)]
    sums = [
        lines[0] * taps[left] + lines[1] * taps[3 + left] + lines[2] * taps[6 + left]
        for left in range(3)
    ]
    return from_left(sums[0]) + sums[1] + from_right(sums[2])


def conv_back_row(pad_ref, grad_ref, taps, taps_ref, image, row):
    lines = [grad_ref[image, row + top] for top in range(3)]
    sums = [
        lines[2] * taps[left] + lines[1] * taps[3 + left] + lines[0] * taps[6 + left]
        for left in range(3)
    ]
    shifted = [from_right(lines[1]), lines[1], from_left(lines[1])]
    for top in range(3):
        source = pad_ref[image, row + top]
        for left in range(3):
            taps_ref[3 * top + left] += fold(source * shifted[left])
    return from_right(sums[0]) + sums[1] + from_left(sums[2])


def pack(compact, source, out_ref, cols):
    compact[...] = jnp.zeros(compact.shape, FULL)
    for at in range(source.shape[0] // SLAB):
        compact[pl.ds(at * cols, cols), :] = source[pl.ds(at * SLAB, cols), :]
    out_ref[...] = compact[...].astype(LOW)


def narrow(pair, value):
    side = value.shape[0]
    parts = []
    for at in range(value.shape[1] // LANES):
        pair[pl.ds(at * side, side), :] = value[:, at * LANES : (at + 1) * LANES]
        parts.append(
            pair[pl.ds(at * side, side // 2, stride=2), :]
            + pair[pl.ds(at * side + 1, side // 2, stride=2), :]
        )
    return jnp.concatenate(parts, axis=1)


def widen(pair, value):
    cols = value.shape[0]
    parts = []
    for at in range(value.shape[1] // LANES):
        part = value[:, at * LANES : (at + 1) * LANES]
        pair[pl.ds(2 * cols * at, cols, stride=2), :] = part
        pair[pl.ds(2 * cols * at + 1, cols, stride=2), :] = part
        parts.append(pair[pl.ds(2 * cols * at, 2 * cols), :])
    return jnp.concatenate(parts, axis=1)


def tap_rows(conv_ref):
    lines = [conv_ref[top].astype(FULL) for top in range(3)]
    return [lines[at // 3][at % 3 : at % 3 + 1] for at in range(9)]


def finish(small_ref, sums_ref, at, place):
    small_ref[pl.ds(place, 1), :] = jnp.sum(sums_ref[at], axis=0, keepdims=True)


def pre_reduce_kernel(
    need,
    send,
    at_ref,
    x_ref, w_ref, gain_ref, shift_ref, first_ref, edge_a_ref, edge_b_ref, normed_ref, factor_ref, red
):
    count, side, width = edge_a_ref.shape
    size = 2 * side
    steps = x_ref.shape[0] // size
    need(x_ref, w_ref)
    matmul(x_ref, w_ref, red)
    need(gain_ref, shift_ref)
    gain, shift = (gain_ref[pl.ds(0, 1), :], shift_ref[pl.ds(0, 1), :])

    @pl.loop(0, steps)
    def _(at):
        rows = rows_of(at, size)
        normed, factor = norm(red[rows, :])
        normed_ref[rows, :] = normed
        factor_ref[rows, :] = wide(factor)
        first_ref[rows, :] = silu(normed * gain + shift).astype(LOW)

    each = steps // count
    for image in range(count):
        head = first_ref[pl.ds(image * each * size, size), :].astype(FULL)
        tail = first_ref[pl.ds((image * each + each - 1) * size, size), :].astype(FULL)
        set_edges(at_ref, edge_a_ref, edge_b_ref, image, head[:side], tail[side:])


def pre_rest_kernel(
    need,
    send,
    at_ref,
    x_ref,
    first_ref,
    got_a_ref,
    got_b_ref,
    conv_ref,
    expand_ref,
    gain_ref,
    shift_ref,
    out_gain_ref,
    out_shift_ref,
    reduce_ref,
    post_gain_ref,
    post_shift_ref,
    second_ref,
    normed_b_ref,
    factor_b_ref,
    normed_c_ref,
    factor_c_ref,
    summed_ref,
    pooled_ref,
    post_first_ref,
    edge_a_ref,
    edge_b_ref,
    post_normed_ref,
    post_factor_ref,
    pad,
    exp,
    pair,
    red,
):
    count, strip, side, width = pad.shape
    strip = strip - 2
    size = 2 * side
    each = strip // 2
    need(first_ref, got_a_ref, got_b_ref)
    fill_halo(at_ref, pad, first_ref, got_a_ref, got_b_ref)
    need(conv_ref, gain_ref, shift_ref)
    send(pad)
    taps = tap_rows(conv_ref)
    gain, shift = (gain_ref[pl.ds(1, 1), :], shift_ref[pl.ds(1, 1), :])

    @pl.loop(0, count * each)
    def _(at):
        rows = rows_of(at, size)
        image, row = (at // each, 2 * lax.rem(at, each))
        conv = jnp.concatenate(
            [conv_row(pad, taps, image, row), conv_row(pad, taps, image, row + 1)], axis=0
        )
        normed, factor = norm(conv)
        normed_b_ref[rows, :] = normed
        factor_b_ref[rows, :] = wide(factor)
        second_ref[rows, :] = silu(normed * gain + shift).astype(LOW)

    send(second_ref, normed_b_ref, factor_b_ref)
    need(expand_ref)
    matmul(second_ref, expand_ref, exp)
    need(x_ref, out_gain_ref, out_shift_ref)
    out_gain, out_shift = (out_gain_ref[...], out_shift_ref[...])
    cols = side // 2
    for at in range(count * each):
        rows = pl.ds(at * size, size)
        normed, factor = norm(exp[rows, :])
        normed_c_ref[rows, :] = normed
        factor_c_ref[rows, :] = wide(factor)
        summed = x_ref[rows, :].astype(FULL) + normed * out_gain + out_shift
        summed_ref[rows, :] = summed
        block = silu(summed)
        half = narrow(pair, block[:side] + block[side:])
        pooled_ref[pl.ds(at * SLAB, cols), :] = 0.25 * half
        pooled_ref[pl.ds(at * SLAB + cols, SLAB - cols), :] = jnp.zeros(
            (SLAB - cols, width), FULL
        )
    send(normed_c_ref, factor_c_ref, summed_ref)
    need(reduce_ref, post_gain_ref, post_shift_ref)
    matmul(pooled_ref, reduce_ref, red)
    normed, factor = norm(red[...])
    post_normed_ref[...] = normed
    post_factor_ref[...] = wide(factor)
    first = silu(normed * post_gain_ref[pl.ds(0, 1), :] + post_shift_ref[pl.ds(0, 1), :])
    post_first_ref[...] = jnp.where(live(red.shape[0], cols), first, 0.0).astype(LOW)
    for image in range(count):
        head = post_first_ref[pl.ds(image * each * SLAB, SLAB), :].astype(FULL)
        tail = post_first_ref[pl.ds((image * each + each - 1) * SLAB, SLAB), :].astype(FULL)
        set_edges(at_ref, edge_a_ref, edge_b_ref, image, head, tail)


def post_rest_kernel(
    need,
    send,
    at_ref,
    pooled_ref,
    first_ref,
    got_a_ref,
    got_b_ref,
    conv_ref,
    expand_ref,
    gain_ref,
    shift_ref,
    out_gain_ref,
    out_shift_ref,
    block_ref,
    left_in_ref,
    left_second_ref,
    normed_b_ref,
    factor_b_ref,
    normed_c_ref,
    factor_c_ref,
    summed_ref,
    pad,
    second,
    exp,
    compact,
    *,
    cols
):
    count, rows, _, width = pad.shape
    rows = rows - 2
    small = block_ref.shape[0]
    need(first_ref, got_a_ref, got_b_ref)
    fill_halo(at_ref, pad, first_ref, got_a_ref, got_b_ref)
    send(pad)
    need(conv_ref, gain_ref, shift_ref, pooled_ref)
    taps = tap_rows(conv_ref)
    gain, shift = (gain_ref[pl.ds(1, 1), :], shift_ref[pl.ds(1, 1), :])

    @pl.loop(0, count * rows)
    def _(at):
        place = rows_of(at, SLAB)
        normed, factor = norm(conv_row(pad, taps, at // rows, lax.rem(at, rows)))
        normed_b_ref[place, :] = normed
        factor_b_ref[place, :] = wide(factor)
        second[place, :] = silu(normed * gain + shift)

    send(normed_b_ref, factor_b_ref)
    need(expand_ref)
    matmul(second, expand_ref, exp)
    need(out_gain_ref, out_shift_ref)
    normed, factor = norm(exp[...])
    normed_c_ref[...] = normed
    factor_c_ref[...] = wide(factor)
    summed = pooled_ref[...] + normed * out_gain_ref[...] + out_shift_ref[...]
    summed_ref[...] = summed
    exp[...] = silu(summed)
    compact[...] = jnp.zeros(compact.shape, FULL)
    for at in range(count * rows):
        compact[pl.ds(at * cols, cols), :] = exp[pl.ds(at * SLAB, cols), :]
    block_ref[...] = compact[pl.ds(0, small), :].astype(LOW)
    send(block_ref, normed_c_ref, factor_c_ref, summed_ref)
    pack(compact, pooled_ref, left_in_ref, cols)
    pack(compact, second, left_second_ref, cols)


def readout_kernel(
    need,
    send,
    at_ref,
    whole_ref,
    w_ref,
    bias_ref,
    cot_ref,
    out_ref,
    grad_ref,
    *refs,
    strips
):
    slots, (bias_grad_ref, cot, out, terms_ref) = (refs[:strips], refs[strips:])
    images, lines, cols, _ = cot_ref.shape
    rows = lines // strips
    need(cot_ref)
    for at in range(images * lines):
        strip, image, row = (at // (images * rows), at // rows % images, at % rows)
        cot[pl.ds(at * cols, cols), :] = cot_ref[image, strip * rows + row].astype(FULL)
    need(whole_ref, w_ref, bias_ref)

    @pl.loop(0, w_ref.shape[1] // TILE)
    def _(at):
        lanes = pl.ds(pl.multiple_of(at * TILE, TILE), TILE)
        act = jnp.dot(whole_ref[...], w_ref[:, lanes], preferred_element_type=FULL)
        act = act + bias_ref[:, lanes]
        cdf = 0.5 * (1.0 + lax.erf(act * SQRT_HALF))
        density = jnp.exp(-0.5 * act * act) * INV_SQRT_TWO_PI
        out[:, lanes] = act * cdf
        grad = (cot[:, lanes] * (cdf + act * density)).astype(LOW)
        grad_ref[:, lanes] = grad
        bias_grad_ref[:, lanes] = jnp.sum(grad.astype(FULL), axis=0, keepdims=True)

    send(grad_ref, bias_grad_ref)
    matmul_back(grad_ref, w_ref, terms_ref)
    small = slots[0].shape[0]
    for step in range(strips):
        begin = pl.multiple_of(flip(at_ref[2], step) * small, 8)
        slots[step][...] = terms_ref[pl.ds(begin, small), :].astype(LOW)
    for at in range(images * lines):
        strip, image, row = (at // (images * rows), at // rows % images, at % rows)
        out_ref[image, strip * rows + row] = out[pl.ds(at * cols, cols), :].astype(LOW)


def post_back_kernel(
    need,
    send,
    at_ref,
    *refs,
    cols,
    strips
):
    pieces, refs = (refs[:strips], refs[strips:])
    (
    expand_ref,
    gain_ref,
    shift_ref,
    out_gain_ref,
    normed_b_ref,
    factor_b_ref,
    normed_c_ref,
    factor_c_ref,
    summed_ref,
    grad_sum_ref,
    grad_exp_ref,
    grad_conv_ref,
    edge_a_ref,
    edge_b_ref,
    small_ref,
    compact,
    spread_out,
    exp,
    sec,
    ) = refs
    count = edge_a_ref.shape[0]
    tokens, width = grad_sum_ref.shape
    each = tokens // SLAB // count
    need(*pieces)
    total = pieces[0][...].astype(FULL)
    for piece in pieces[1:]:
        total = total + piece[...].astype(FULL)
    compact[...] = jnp.zeros(compact.shape, FULL)
    compact[pl.ds(0, total.shape[0]), :] = total
    spread_out[...] = jnp.zeros((tokens, width), FULL)
    for at in range(tokens // SLAB):
        spread_out[pl.ds(at * SLAB, cols), :] = compact[pl.ds(at * cols, cols), :]
    need(summed_ref, normed_c_ref, factor_c_ref, out_gain_ref)
    grad_sum = silu_back(spread_out[...], summed_ref[...])
    grad_sum_ref[...] = grad_sum
    normed = normed_c_ref[...]
    exp[...] = norm_back(grad_sum, normed, factor_c_ref[:, :1], out_gain_ref[...])
    small_ref[pl.ds(2, 1), :] = jnp.sum(grad_sum * normed, axis=0, keepdims=True)
    small_ref[pl.ds(3, 1), :] = jnp.sum(grad_sum, axis=0, keepdims=True)
    pack(compact, exp, grad_exp_ref, cols)
    send(grad_sum_ref, grad_exp_ref)
    need(expand_ref)
    matmul_back(exp, expand_ref, sec)
    need(gain_ref, shift_ref, normed_b_ref, factor_b_ref)
    gain, shift = (gain_ref[pl.ds(1, 1), :], shift_ref[pl.ds(1, 1), :])
    normed = normed_b_ref[...]
    grad = silu_back(sec[...], normed * gain + shift)
    grad_conv_ref[...] = norm_back(grad, normed, factor_b_ref[:, :1], gain).astype(LOW)
    small_ref[pl.ds(0, 1), :] = jnp.sum(grad * normed, axis=0, keepdims=True)
    small_ref[pl.ds(1, 1), :] = jnp.sum(grad, axis=0, keepdims=True)
    for image in range(count):
        head = grad_conv_ref[pl.ds(image * each * SLAB, SLAB), :].astype(FULL)
        tail = grad_conv_ref[pl.ds((image * each + each - 1) * SLAB, SLAB), :].astype(FULL)
        set_edges(at_ref, edge_a_ref, edge_b_ref, image, head, tail)


def middle_back_kernel(
    need,
    send,
    at_ref,
    grad_conv_ref,
    got_a_ref,
    got_b_ref,
    pad,
    post_conv_ref,
    post_reduce_ref,
    post_gain_ref,
    post_shift_ref,
    post_normed_ref,
    post_factor_ref,
    post_grad_sum_ref,
    expand_ref,
    gain_ref,
    shift_ref,
    out_gain_ref,
    normed_b_ref,
    factor_b_ref,
    normed_c_ref,
    factor_c_ref,
    summed_ref,
    post_grad_red_ref,
    grad_sum_ref,
    grad_exp_ref,
    pre_grad_conv_ref,
    edge_a_ref,
    edge_b_ref,
    post_small_ref,
    small_ref,
    grad_pad,
    taps_sum,
    grad_in,
    pair,
    sec,
    sums,
    post_red,
    compact,
    *,
    cols
):
    count, side, width = edge_a_ref.shape
    need(grad_conv_ref, got_a_ref, got_b_ref)
    fill_halo(at_ref, grad_pad, grad_conv_ref, got_a_ref, got_b_ref)
    need(pad, post_conv_ref)
    need(post_gain_ref, post_shift_ref, post_normed_ref, post_factor_ref)
    taps = tap_rows(post_conv_ref)
    taps_sum[...] = jnp.zeros_like(taps_sum)
    sums[...] = jnp.zeros_like(sums)
    gain, shift = (post_gain_ref[pl.ds(0, 1), :], post_shift_ref[pl.ds(0, 1), :])
    each = post_grad_sum_ref.shape[0] // SLAB // count

    @pl.loop(0, count * each)
    def _(at):
        place = rows_of(at, SLAB)
        grad = conv_back_row(pad, grad_pad, taps, taps_sum, at // each, lax.rem(at, each))
        normed = post_normed_ref[place, :]
        grad = jnp.where(live(SLAB, cols), silu_back(grad, normed * gain + shift), 0.0)
        sums[0] += fold(grad * normed)
        sums[1] += fold(grad)
        post_red[place, :] = norm_back(grad, normed, post_factor_ref[place, :1], gain)

    for at in range(9):
        finish(post_small_ref, taps_sum, at, at)
    finish(post_small_ref, sums, 0, 9)
    finish(post_small_ref, sums, 1, 10)
    pack(compact, post_red, post_grad_red_ref, cols)
    send(post_grad_red_ref, post_small_ref)
    need(post_reduce_ref)
    matmul_back(post_red, post_reduce_ref, grad_in)
    sums[...] = jnp.zeros_like(sums)
    size = 2 * side
    need(out_gain_ref, post_grad_sum_ref, summed_ref, normed_c_ref, factor_c_ref)
    out_gain = out_gain_ref[...]
    for at in range(count * each):
        rows = pl.ds(at * size, size)
        place = pl.ds(at * SLAB, cols)
        grad = 0.25 * (post_grad_sum_ref[place, :] + grad_in[place, :])
        grad = widen(pair, grad)
        grad = jnp.concatenate([grad, grad], axis=0)
        grad_sum = silu_back(grad, summed_ref[rows, :])
        grad_sum_ref[rows, :] = grad_sum
        normed = normed_c_ref[rows, :]
        sums[0] += fold(grad_sum * normed)
        sums[1] += fold(grad_sum)
        grad_exp_ref[rows, :] = norm_back(
            grad_sum, normed, factor_c_ref[rows, :1], out_gain
        ).astype(LOW)
    finish(small_ref, sums, 0, 2)
    finish(small_ref, sums, 1, 3)
    send(grad_sum_ref, grad_exp_ref)
    need(expand_ref)
    matmul_back(grad_exp_ref, expand_ref, sec)
    need(gain_ref, shift_ref, normed_b_ref, factor_b_ref)
    sums[...] = jnp.zeros_like(sums)
    gain_b, shift_b = (gain_ref[pl.ds(1, 1), :], shift_ref[pl.ds(1, 1), :])

    @pl.loop(0, count * each)
    def _(at):
        rows = rows_of(at, size)
        normed = normed_b_ref[rows, :]
        grad = silu_back(sec[rows, :], normed * gain_b + shift_b)
        sums[0] += fold(grad * normed)
        sums[1] += fold(grad)
        pre_grad_conv_ref[rows, :] = norm_back(
            grad, normed, factor_b_ref[rows, :1], gain_b
        ).astype(LOW)

    finish(small_ref, sums, 0, 0)
    finish(small_ref, sums, 1, 1)
    for image in range(count):
        head = pre_grad_conv_ref[pl.ds(image * each * size, size), :].astype(FULL)
        tail = pre_grad_conv_ref[pl.ds((image * each + each - 1) * size, size), :].astype(FULL)
        set_edges(at_ref, edge_a_ref, edge_b_ref, image, head[:side], tail[side:])


def pre_back_kernel(
    need,
    send,
    at_ref,
    grad_conv_ref,
    got_a_ref,
    got_b_ref,
    pad,
    conv_ref,
    gain_ref,
    shift_ref,
    normed_ref,
    factor_ref,
    grad_red_ref,
    small_ref,
    grad_pad,
    taps_sum,
    sums,
):
    count, strip, side, width = pad.shape
    strip = strip - 2
    size = 2 * side
    each = strip // 2
    need(grad_conv_ref, got_a_ref, got_b_ref)
    fill_halo(at_ref, grad_pad, grad_conv_ref, got_a_ref, got_b_ref)
    need(pad, conv_ref)
    need(gain_ref, shift_ref, normed_ref, factor_ref)
    taps = tap_rows(conv_ref)
    taps_sum[...] = jnp.zeros_like(taps_sum)
    sums[...] = jnp.zeros_like(sums)
    gain, shift = (gain_ref[pl.ds(0, 1), :], shift_ref[pl.ds(0, 1), :])

    @pl.loop(0, count * each)
    def _(at):
        rows = rows_of(at, size)
        image, row = (at // each, 2 * lax.rem(at, each))
        grad = jnp.concatenate(
            [
                conv_back_row(pad, grad_pad, taps, taps_sum, image, row),
                conv_back_row(pad, grad_pad, taps, taps_sum, image, row + 1),
            ],
            axis=0,
        )
        normed = normed_ref[rows, :]
        grad = silu_back(grad, normed * gain + shift)
        sums[0] += fold(grad * normed)
        sums[1] += fold(grad)
        grad_red_ref[rows, :] = norm_back(grad, normed, factor_ref[rows, :1], gain).astype(LOW)

    for at in range(9):
        finish(small_ref, taps_sum, at, at)
    finish(small_ref, sums, 0, 9)
    finish(small_ref, sums, 1, 10)


def pair_outer_kernel(need, send, at_ref, *refs, pairs, parts):
    takes = 4 * pairs
    outs = refs[takes:]
    half, plane = (at_ref[0], at_ref[1])
    rows = outs[0].shape[0] // pairs
    for pair in range(pairs):
        left, left_far, right, right_far = refs[4 * pair : 4 * pair + 4]
        need(left, left_far, right, right_far)
        for step in range(parts):
            begin = half * (rows * parts) + flip(plane, step) * rows
            lanes = pl.ds(pl.multiple_of(begin, LANES), rows)
            total = lax.dot_general(
                left[:, lanes], right[...], (((0,), (0,)), ((), ())), preferred_element_type=FULL
            ) + lax.dot_general(
                left_far[:, lanes],
                right_far[...],
                (((0,), (0,)), ((), ())),
                preferred_element_type=FULL,
            )
            outs[step][pl.ds(pair * rows, rows), :] = total.astype(LOW)
    send(*outs)


def sum_split_kernel(need, send, at_ref, *refs, pairs, parts, pieces, along=2):
    takes, outs = (refs[:pieces], refs[pieces : pieces + parts])
    total = refs[-1]
    need(*takes)
    value = takes[0][...].astype(FULL)
    for at in range(1, pieces):
        value = value + takes[at][...].astype(FULL)
    total[...] = value
    rows = total.shape[0] // pairs // parts
    for step in range(parts):
        begin = flip(at_ref[along], step) * rows
        for pair in range(pairs):
            place = pl.ds(pl.multiple_of(pair * rows * parts + begin, SLAB), rows)
            outs[step][pl.ds(pair * rows, rows), :] = total[place, :].astype(LOW)
    send(*outs)


def assemble_kernel(*refs, pairs, planes, strips, cut):
    takes = 2 * (planes + cut)
    parts, outs = (refs[:takes], refs[takes : takes + pairs])
    full, sem = (refs[takes + pairs : takes + 2 * pairs], refs[-1])
    half, plane, row = places()
    rows = parts[0].shape[0] // pairs // strips
    block = strips * rows
    writes = []
    for pair in range(pairs):
        for at in range(2 * planes):
            side, spot = (flip(half, at // planes), flip(plane, at % planes))
            for step in range(strips):
                place = side * (planes * block) + spot * block
                if strips > 1:
                    place = place + flip(row, step) * rows
                source, begin = (at % planes, step)
                if cut and source == planes - 1 and 2 * step >= strips:
                    source, begin = (planes, step - strips // 2)
                part = parts[at // planes * (planes + cut) + source]
                full[pair][pl.ds(pl.multiple_of(place, SLAB), rows), :] = part[
                    pl.ds((begin * pairs + pair) * rows, rows), :
                ].astype(FULL)
        writes.append(pltpu.make_async_copy(full[pair], outs[pair], sem.at[pair]))
        writes[-1].start()
    for write in writes:
        write.wait()


def assemble(parts, pairs, planes, strips):
    takes = len(parts)
    out = like(2 * planes * parts[0].shape[0] // pairs, parts[0].shape[1])
    parts = [pltpu.with_memory_space_constraint(part, pltpu.VMEM) for part in parts]
    return pl.pallas_call(
        functools.partial(
            assemble_kernel, pairs=pairs, planes=planes, strips=strips, cut=takes // 2 - planes
        ),
        out_shape=[pltpu.HBM(out.shape, out.dtype)] * pairs,
        in_specs=[pl.BlockSpec(memory_space=pltpu.VMEM)] * takes,
        out_specs=[pl.BlockSpec(memory_space=pltpu.HBM)] * pairs,
        scratch_shapes=[pltpu.VMEM(out.shape, FULL)] * pairs + [pltpu.SemaphoreType.DMA((pairs,))],
        compiler_params=pltpu.CompilerParams(vmem_limit_bytes=VMEM_BYTES),
        cost_estimate=pl.CostEstimate(flops=0, bytes_accessed=0, transcendentals=0),
    )(*parts)


def small_kernel(need, send, at_ref, sums_ref, *outs):
    for place in range(2):
        conv, gain, shift, out_gain, out_shift = outs[5 * place : 5 * place + 5]
        rows = sums_ref[pl.ds(15 * place, 15), :]
        for top in range(3):
            conv[top] = rows[3 * top : 3 * top + 3]
        gain[pl.ds(0, 1), :] = rows[9:10]
        gain[pl.ds(1, 1), :] = rows[11:12]
        shift[pl.ds(0, 1), :] = rows[10:11]
        shift[pl.ds(1, 1), :] = rows[12:13]
        out_gain[...] = rows[13:14]
        out_shift[...] = rows[14:15]


class Near:
    def __init__(self, value):
        self.value = value


def like(*shape, dtype=FULL):
    return jax.ShapeDtypeStruct(shape, dtype)


def low(*shape):
    return like(*shape, dtype=LOW)


def places():
    return [lax.axis_index(axis) for axis in ("half", "im", "row")]


def call(kernel, outs, scratch, *args):
    near_in = [isinstance(arg, Near) for arg in args]
    near_out = [isinstance(out, Near) for out in outs]
    args = [arg.value if isinstance(arg, Near) else arg for arg in args]
    outs = [out.value if isinstance(out, Near) else out for out in outs]
    takes, gives = (len(args), len(outs))
    far_in = [at for at in range(takes) if not near_in[at]]
    far_out = [at for at in range(gives) if not near_out[at]]

    def body(*refs):
        given, refs = (list(refs[:takes]), refs[takes:])
        made, refs = (list(refs[:gives]), refs[gives:])
        rest = refs[len(far_in) + len(far_out) :]
        reads, writes = ({}, {})
        if far_in:
            in_sem = rest[-1]
            rest = rest[:-1]
        if far_out:
            out_sem = rest[-1]
            rest = rest[:-1]
        for place, at in enumerate(far_in):
            reads[at] = pltpu.make_async_copy(given[at], refs[place], in_sem.at[place])
            given[at] = refs[place]
        for place, at in enumerate(far_out):
            mirror = refs[len(far_in) + place]
            writes[at] = pltpu.make_async_copy(mirror, made[at], out_sem.at[place])
            made[at] = mirror
        for at in sorted(reads, key=lambda at: args[at].size):
            reads[at].start()
        started = []

        def need(*wanted):
            for at in list(reads):
                if any(given[at] is ref for ref in wanted):
                    reads.pop(at).wait()

        def send(*ready):
            for at in list(writes):
                if any(made[at] is ref for ref in ready):
                    started.append(writes.pop(at))
                    started[-1].start()

        kernel(need, send, places(), *given, *made, *rest)
        need(*given)
        send(*made)
        for write in started:
            write.wait()

    spaces = {True: pltpu.VMEM, False: pltpu.HBM}
    args = [
        pltpu.with_memory_space_constraint(arg, spaces[near]) for arg, near in zip(args, near_in)
    ]
    return pl.pallas_call(
        body,
        out_shape=[spaces[near](out.shape, out.dtype) for out, near in zip(outs, near_out)],
        in_specs=[pl.BlockSpec(memory_space=spaces[near]) for near in near_in],
        out_specs=[pl.BlockSpec(memory_space=spaces[near]) for near in near_out],
        scratch_shapes=[pltpu.VMEM(args[at].shape, args[at].dtype) for at in far_in]
        + [pltpu.VMEM(outs[at].shape, outs[at].dtype) for at in far_out]
        + [pltpu.VMEM(shape, FULL) for shape in scratch]
        + [pltpu.SemaphoreType.DMA((len(far_out),))] * bool(far_out)
        + [pltpu.SemaphoreType.DMA((len(far_in),))] * bool(far_in),
        compiler_params=pltpu.CompilerParams(vmem_limit_bytes=VMEM_BYTES),
        cost_estimate=pl.CostEstimate(flops=0, bytes_accessed=0, transcendentals=0),
    )(*args)


def edges(parity_edges):
    size = lax.axis_size("row")
    inner = [(at, at ^ 1) for at in range(size)]
    outer = [(at, at + 1) for at in range(1, size - 1, 2)]
    outer = outer + [(to, at) for at, to in outer]
    return (
        lax.ppermute(parity_edges[0], "row", inner),
        lax.ppermute(parity_edges[1], "row", outer),
    )


def swap(field):
    return lax.ppermute(field, "half", [(0, 1), (1, 0)])


def steps_of(value, axis, step):
    size = lax.axis_size(axis)
    return lax.ppermute(value, axis, [(at, at ^ step) for at in range(size)])


def share(parts, axis):
    return [parts[0]] + [steps_of(parts[at], axis, at) for at in range(1, len(parts))]


def share_same(part, axis):
    size = lax.axis_size(axis)
    return [part] + [steps_of(part, axis, at) for at in range(1, size)]


def gather_near(part):
    return [part, steps_of(part, "im", 1), steps_of(part, "im", 2)]


def gather_rest(parts):
    half = parts[0].shape[0] // 2
    return [steps_of(parts[1][:half], "im", 2), steps_of(parts[2][half:], "im", 1)]


def small_outputs(part, width):
    return [
        part[:9].reshape(3, 3, width),
        jnp.stack([part[9], part[11]]),
        jnp.stack([part[10], part[12]]),
        part[13],
        part[14],
    ]


def pair_outer(*pairs):
    size = lax.axis_size("im")
    first = pairs[0][0].value if isinstance(pairs[0][0], Near) else pairs[0][0]
    width = first.shape[1]
    rows = width // 2 // size * len(pairs)
    return list(
        call(
            functools.partial(pair_outer_kernel, pairs=len(pairs), parts=size),
            [Near(low(rows, width))] * size,
            [],
            *[ref for pair in pairs for ref in pair],
        )
    )


def sum_split(pieces, pairs):
    size = lax.axis_size("row")
    rows, width = pieces[0].shape
    return list(
        call(
            functools.partial(
                sum_split_kernel,
                pairs=pairs,
                parts=size,
                pieces=len(pieces),
            ),
            [Near(low(rows // size, width))] * size,
            [(rows, width)],
            *[Near(piece) for piece in pieces],
        )
    )


def add_low(pieces):
    total = pieces[0].astype(FULL)
    for piece in pieces[1:]:
        total = total + piece.astype(FULL)
    return total.astype(LOW)


def sum_far(left, right, axes):
    part = jnp.einsum("tm,tc->mc", left, right, preferred_element_type=FULL)
    return lax.psum(part, axes)


def shards(
    x_in,
    pre_reduce,
    pre_conv,
    pre_expand,
    pre_mid_gain,
    pre_mid_shift,
    pre_out_gain,
    pre_out_shift,
    post_reduce,
    post_conv,
    post_expand,
    post_mid_gain,
    post_mid_shift,
    post_out_gain,
    post_out_shift,
    read_weight,
    read_bias,
    cotangent,
):
    count, strip, side, width = x_in.shape
    strips = lax.axis_size("row")
    tokens = count * strip * side
    cols = side // 2
    rows = strip // 2
    slabs = count * rows
    padded = slabs * SLAB
    small = slabs * cols
    block = -(-small // SLAB) * SLAB
    features = read_weight.shape[1]
    x_low = x_in.reshape(tokens, width)
    pre_out_g, pre_out_s = (pre_out_gain[None], pre_out_shift[None])
    post_out_g, post_out_s = (post_out_gain[None], post_out_shift[None])
    pre_edge = Near(low(count, side, width))
    post_edge = Near(low(count, SLAB, width))
    quick = lax.axis_size("im") == 4 and strips == 4

    first, edge_a, edge_b, normed_a, factor_a = call(
        pre_reduce_kernel,
        [Near(low(tokens, width)), pre_edge, pre_edge, like(tokens, width), like(tokens, LANES)],
        [(tokens, width)],
        x_low,
        pre_reduce,
        pre_mid_gain,
        pre_mid_shift,
    )
    got_a, got_b = edges((edge_a, edge_b))
    (
        second,
        normed_b,
        factor_b,
        normed_c,
        factor_c,
        summed,
        pooled,
        post_first,
        edge_a,
        edge_b,
        post_normed_a,
        post_factor_a,
        pad,
    ) = call(
        pre_rest_kernel,
        [
            low(tokens, width),
            like(tokens, width),
            like(tokens, LANES),
            like(tokens, width),
            like(tokens, LANES),
            like(tokens, width),
            Near(like(padded, width)),
            Near(low(padded, width)),
            post_edge,
            post_edge,
            like(padded, width),
            like(padded, LANES),
            like(count, strip + 2, side, width),
        ],
        [(tokens, width), (side * width // LANES, LANES), (padded, width)],
        x_low,
        Near(first),
        Near(got_a),
        Near(got_b),
        pre_conv,
        pre_expand,
        pre_mid_gain,
        pre_mid_shift,
        pre_out_g,
        pre_out_s,
        post_reduce,
        post_mid_gain,
        post_mid_shift,
    )
    got_a, got_b = edges((edge_a, edge_b))
    (
        block_two,
        left_in,
        left_second,
        post_normed_b,
        post_factor_b,
        post_normed_c,
        post_factor_c,
        post_summed,
        post_pad,
    ) = call(
        functools.partial(post_rest_kernel, cols=cols),
        [
            Near(low(small, width)),
            low(block, width),
            low(block, width),
            like(padded, width),
            like(padded, LANES),
            like(padded, width),
            like(padded, LANES),
            like(padded, width),
            like(count, rows + 2, SLAB, width),
        ],
        [(padded, width), (padded, width), (block, width)],
        Near(pooled),
        Near(post_first),
        Near(got_a),
        Near(got_b),
        post_conv,
        post_expand,
        post_mid_gain,
        post_mid_shift,
        post_out_g,
        post_out_s,
    )
    whole = lax.all_gather(block_two, "row", axis=0, tiled=True)
    readout, grad_pre, *terms, d_read_b = call(
        functools.partial(readout_kernel, strips=strips),
        [
            like(*cotangent.shape, dtype=LOW),
            Near(low(strips * small, features)),
        ]
        + [Near(low(small, width))] * strips
        + [like(1, features)],
        [
            (strips * small, features),
            (strips * small, features),
            (strips * small, width),
        ],
        Near(whole),
        read_weight,
        read_bias[None],
        cotangent,
    )
    terms = share(terms, "row")
    if quick:
        parts = pair_outer(
            (Near(whole), Near(swap(whole)), Near(grad_pre), Near(swap(grad_pre)))
        )
        parts[0], *terms = tie(parts[0], *terms)
        read_parts = share(parts, "im")
    post_gs, post_ge, post_gc, edge_a, edge_b, post_small_b = call(
        functools.partial(post_back_kernel, cols=cols, strips=strips),
        [
            Near(like(padded, width)),
            Near(low(block, width)),
            Near(low(padded, width)),
            post_edge,
            post_edge,
            like(4, width),
        ],
        [(block, width), (padded, width), (padded, width), (padded, width)],
        *[Near(term) for term in terms],
        post_expand,
        post_mid_gain,
        post_mid_shift,
        post_out_g,
        post_normed_b,
        post_factor_b,
        post_normed_c,
        post_factor_c,
        post_summed,
    )
    got_a, got_b = edges((edge_a, edge_b))
    if quick:
        left_in_far, left_second_far, ge_far = (swap(left_in), swap(left_second), swap(post_ge))
        (got_a, got_b), (left_in_far, left_second_far, ge_far, *read_parts) = tie_later(
            (got_a, got_b), (left_in_far, left_second_far, ge_far, *read_parts)
        )
    (
        post_gr,
        pre_gs,
        pre_ge,
        pre_gc,
        edge_a,
        edge_b,
        post_small_a,
        pre_small_b,
    ) = call(
        functools.partial(middle_back_kernel, cols=cols),
        [
            Near(low(block, width)),
            like(tokens, width),
            Near(low(tokens, width)),
            Near(low(tokens, width)),
            pre_edge,
            pre_edge,
            like(11, width),
            like(4, width),
        ],
        [
            (count, rows + 2, SLAB, width),
            (9, 8, width),
            (padded, width),
            (side * width // LANES, LANES),
            (tokens, width),
            (2, 8, width),
            (padded, width),
            (block, width),
        ],
        Near(post_gc),
        Near(got_a),
        Near(got_b),
        post_pad,
        post_conv,
        post_reduce,
        post_mid_gain,
        post_mid_shift,
        post_normed_a,
        post_factor_a,
        Near(post_gs),
        pre_expand,
        pre_mid_gain,
        pre_mid_shift,
        pre_out_g,
        normed_b,
        factor_b,
        normed_c,
        factor_c,
        summed,
    )
    got_a, got_b = edges((edge_a, edge_b))
    if quick:
        pre_ge_far = swap(pre_ge)
        post_parts = pair_outer(
            (left_in, left_in_far, Near(post_gr), Near(swap(post_gr))),
            (left_second, left_second_far, Near(post_ge), Near(ge_far)),
        )
        post_parts = pair_outer(
            (left_in, left_in_far, Near(post_gr), Near(swap(post_gr))),
            (left_second, left_second_far, Near(post_ge), Near(ge_far)),
        )
        post_sums = [steps_of(post_parts[at], "im", at) for at in (1, 2)]
        (got_a, got_b), post_sums = tie_later((got_a, got_b), post_sums)
    pre_gr, pre_small_a = call(
        pre_back_kernel,
        [Near(low(tokens, width)), like(11, width)],
        [
            (count, strip + 2, side, width),
            (9, 8, width),
            (2, 8, width),
        ],
        Near(pre_gc),
        Near(got_a),
        Near(got_b),
        pad,
        pre_conv,
        pre_mid_gain,
        pre_mid_shift,
        normed_a,
        factor_a,
    )
    sums = jnp.concatenate([pre_small_a, pre_small_b, post_small_a, post_small_b, d_read_b])
    if quick:
        post_sums = post_sums + [steps_of(post_parts[3], "im", 3)]
        parts = pair_outer(
            (second, swap(second), Near(pre_ge), Near(swap(pre_ge))),
            (x_low, swap(x_low), Near(pre_gr), Near(swap(pre_gr))),
        )
        (parts[0], *post_sums), (sums,) = tie_later(
            (parts[0], *post_sums), (sums + swap(sums),)
        )
        post_parts = share(sum_split(post_parts[:1] + post_sums, 2), "row")
        near_parts = [steps_of(parts[at], "im", at) for at in (1, 2)]
        read_parts = gather_near(add_low(read_parts))
        sums = sums + steps_of(sums, "im", 1)
        grad_in = pre_gs + jnp.einsum("tm,cm->tc", pre_gr, pre_reduce, preferred_element_type=FULL)
        grad_in = grad_in.astype(LOW)
        post_parts, rest = tie_later(post_parts, (sums, grad_in, parts[3], *near_parts, *read_parts))
        sums, grad_in, last, *rest = rest
        near_parts, read_parts = (rest[:2], rest[2:])
        post_parts = share_same(add_low(post_parts), "row")
        last = steps_of(last, "im", 3)
        read_last = steps_of(read_parts[0], "im", 3)
        sums = sums + steps_of(sums, "im", 2)
        post_parts, (last, sums, read_last) = tie_later(post_parts, (last, sums, read_last))
        read_parts = read_parts + [read_last]
        parts = share(sum_split([parts[0]] + near_parts + [last], 2), "row")
        post_parts = gather_near(jnp.concatenate(post_parts, axis=0))
        read_bias_g = sums[30]
        sums = sums + steps_of(sums, "row", 1)
        parts, (sums, *post_parts) = tie_later(parts, (sums, *post_parts))
        parts = share_same(add_low(parts), "row")
        post_far = [swap(part) for part in post_parts]
        post_parts = post_parts + gather_rest(post_parts)
        parts, rest = tie_later(parts, (*post_parts, *post_far))
        post_parts, post_far = (rest[:5], rest[5:])
        parts = gather_near(jnp.concatenate(parts, axis=0))
        sums = sums + steps_of(sums, "row", 2)
        post_far = post_far + [swap(part) for part in post_parts[3:]]
        (*post_far, sums), parts = tie_later((*post_far, sums), parts)
        post_reduce_g, post_expand_g = assemble(post_parts + post_far, 2, 4, strips)
        (read_total,) = assemble(read_parts + [swap(part) for part in read_parts], 1, 4, 1)
        small_out = call(
            small_kernel,
            [like(3, 3, width), like(2, width), like(2, width), like(1, width), like(1, width)] * 2,
            [],
            Near(sums),
        )
        far = [swap(part) for part in parts]
        (post_reduce_g, read_total, *small_out), rest = tie_later(
            (post_reduce_g, read_total, *small_out), gather_rest(parts)
        )
        parts = parts + rest
        far = far + [swap(part) for part in rest]
        pre_expand_g, pre_reduce_g = assemble(parts + far, 2, 4, strips)
    else:
        axes = IMG + ("row",)
        post_reduce_g = sum_far(left_in, post_gr, axes)
        post_expand_g = sum_far(left_second, post_ge, axes)
        pre_expand_g = sum_far(second, pre_ge, axes)
        pre_reduce_g = sum_far(x_low, pre_gr, axes)
        read_total = sum_far(whole, grad_pre, IMG)
        read_bias_g = lax.psum(sums[30], IMG)
        sums = lax.psum(sums, axes)
        small_out = small_outputs(sums[:15], width) + small_outputs(sums[15:30], width)
        grad_in = pre_gs + jnp.einsum("tm,cm->tc", pre_gr, pre_reduce, preferred_element_type=FULL)
        grad_in = grad_in.astype(LOW)

    pre_conv_g, pre_gain_g, pre_shift_g, pre_og_g, pre_os_g = small_out[:5]
    post_conv_g, post_gain_g, post_shift_g, post_og_g, post_os_g = small_out[5:]
    return (
        readout,
        grad_in.reshape(x_in.shape),
        pre_reduce_g,
        pre_conv_g,
        pre_expand_g,
        pre_gain_g,
        pre_shift_g,
        pre_og_g.reshape(width),
        pre_os_g.reshape(width),
        post_reduce_g,
        post_conv_g,
        post_expand_g,
        post_gain_g,
        post_shift_g,
        post_og_g.reshape(width),
        post_os_g.reshape(width),
        read_total,
        read_bias_g,
    )


def solution(mesh):
    images, strips = mesh.devices.shape
    split = jax.sharding.Mesh(
        mesh.devices.reshape(images // 2, 2, strips), ("im", "half", "row")
    )
    return jax.shard_map(
        shards,
        mesh=split,
        in_specs=(P(IMG, "row", None, None),)
        + (P(),) * 14
        + (P(None, "row"), P("row"), P(IMG, None, None, "row")),
        out_specs=(P(IMG, None, None, "row"), P(IMG, "row", None, None))
        + (P(),) * 14
        + (P(None, "row"), P("row")),
        check_vma=False,
    )
```

```python
import functools

import jax
import jax.numpy as jnp
from jax import lax
from jax.experimental import pallas as pl
from jax.experimental.pallas import tpu as pltpu
from jax.sharding import PartitionSpec as P

EPSILON = 1e-06
SQRT_HALF = 0.7071067811865476
INV_SQRT_TWO_PI = 0.3989422804014327
LOW = jnp.bfloat16
FULL = jnp.float32
IMG = ("im", "half")
TILE = 256
SLAB = 16
LANES = 128
VMEM_BYTES = 24 * 1024 * 1024


def tie(*values):
    return lax.optimization_barrier(values)


def tie_later(first, second):
    first = list(tie(*first))
    out = list(tie(*first, *second))
    return (out[: len(first)], out[len(first) :])


def norm(value):
    centred = value - jnp.mean(value, axis=-1, keepdims=True)
    factor = lax.rsqrt(jnp.mean(centred * centred, axis=-1, keepdims=True) + EPSILON)
    return (centred * factor, factor)


def norm_back(grad, normed, factor, gain):
    scaled = grad * gain
    return factor * (
        scaled
        - jnp.mean(scaled, axis=-1, keepdims=True)
        - normed * jnp.mean(scaled * normed, axis=-1, keepdims=True)
    )


def gate(value):
    return 0.5 * jnp.tanh(0.5 * value) + 0.5


def silu(value):
    return value * gate(value)


def silu_back(grad, value):
    sigma = gate(value)
    return grad * sigma * (1.0 + value * (1.0 - sigma))


def flip(place, step):
    bit = 1
    while bit <= step:
        if step & bit:
            place = place + bit - 2 * bit * ((place // bit) % 2)
        bit *= 2
    return place


def wide(factor):
    return jnp.broadcast_to(factor, (factor.shape[0], LANES))


def fold(value):
    return jnp.sum(value.reshape(-1, 8, value.shape[-1]), axis=0)


def live(rows, cols):
    at = lax.broadcasted_iota(jnp.int32, (rows, 1), 0)
    return lax.rem(at, SLAB) < cols


def from_left(value):
    at = lax.broadcasted_iota(jnp.int32, (value.shape[0], 1), 0)
    return jnp.where(at == 0, 0.0, pltpu.roll(value, 1, 0))


def from_right(value):
    last = value.shape[0] - 1
    at = lax.broadcasted_iota(jnp.int32, (value.shape[0], 1), 0)
    return jnp.where(at == last, 0.0, pltpu.roll(value, last, 0))


def matmul(left_ref, right_ref, out_ref):
    @pl.loop(0, right_ref.shape[1] // TILE)
    def _(at):
        cols = pl.ds(pl.multiple_of(at * TILE, TILE), TILE)
        out_ref[:, cols] = jnp.dot(
            left_ref[...].astype(LOW), right_ref[:, cols], preferred_element_type=FULL
        )


def matmul_back(left_ref, right_ref, out_ref):
    @pl.loop(0, right_ref.shape[0] // TILE)
    def _(at):
        cols = pl.ds(pl.multiple_of(at * TILE, TILE), TILE)
        out_ref[:, cols] = lax.dot_general(
            left_ref[...].astype(LOW),
            right_ref[cols, :],
            (((1,), (1,)), ((), ())),
            preferred_element_type=FULL,
        ).astype(out_ref.dtype)


def rows_of(at, size):
    return pl.ds(pl.multiple_of(at * size, SLAB), size)


def fill_halo(at_ref, pad_ref, low_ref, got_a_ref, got_b_ref):
    count, rows, cols, width = pad_ref.shape
    rows = rows - 2
    even = lax.rem(at_ref[2], 2) == 0
    for image in range(count):
        got_a, got_b = (got_a_ref[image].astype(FULL), got_b_ref[image].astype(FULL))
        pad_ref[image, 0] = jnp.where(even, got_b, got_a)
        pad_ref[image, rows + 1] = jnp.where(even, got_a, got_b)

    size = cols if cols % SLAB == 0 else 2 * cols
    per = size // cols
    each = rows // per

    @pl.loop(0, count * each)
    def _(at):
        part = low_ref[rows_of(at, size), :].astype(FULL).reshape(per, cols, width)
        pad_ref[at // each, pl.ds(1 + per * lax.rem(at, each), per)] = part


def set_edges(at_ref, edge_a_ref, edge_b_ref, image, head, tail):
    even = lax.rem(at_ref[2], 2) == 0
    edge_a_ref[image] = jnp.where(even, tail, head).astype(LOW)
    edge_b_ref[image] = jnp.where(even, head, tail).astype(LOW)


def conv_row(pad_ref, taps, image, row):
    lines = [pad_ref[image, row + top] for top in range(3)]
    sums = [
        lines[0] * taps[left] + lines[1] * taps[3 + left] + lines[2] * taps[6 + left]
        for left in range(3)
    ]
    return from_left(sums[0]) + sums[1] + from_right(sums[2])


def conv_back_row(pad_ref, grad_ref, taps, taps_ref, image, row):
    lines = [grad_ref[image, row + top] for top in range(3)]
    sums = [
        lines[2] * taps[left] + lines[1] * taps[3 + left] + lines[0] * taps[6 + left]
        for left in range(3)
    ]
    shifted = [from_right(lines[1]), lines[1], from_left(lines[1])]
    for top in range(3):
        source = pad_ref[image, row + top]
        for left in range(3):
            taps_ref[3 * top + left] += fold(source * shifted[left])
    return from_right(sums[0]) + sums[1] + from_left(sums[2])


def pack(compact, source, out_ref, cols):
    compact[...] = jnp.zeros(compact.shape, FULL)
    for at in range(source.shape[0] // SLAB):
        compact[pl.ds(at * cols, cols), :] = source[pl.ds(at * SLAB, cols), :]
    out_ref[...] = compact[...].astype(LOW)


def narrow(pair, value):
    side = value.shape[0]
    parts = []
    for at in range(value.shape[1] // LANES):
        pair[pl.ds(at * side, side), :] = value[:, at * LANES : (at + 1) * LANES]
        parts.append(
            pair[pl.ds(at * side, side // 2, stride=2), :]
            + pair[pl.ds(at * side + 1, side // 2, stride=2), :]
        )
    return jnp.concatenate(parts, axis=1)


def widen(pair, value):
    cols = value.shape[0]
    parts = []
    for at in range(value.shape[1] // LANES):
        part = value[:, at * LANES : (at + 1) * LANES]
        pair[pl.ds(2 * cols * at, cols, stride=2), :] = part
        pair[pl.ds(2 * cols * at + 1, cols, stride=2), :] = part
        parts.append(pair[pl.ds(2 * cols * at, 2 * cols), :])
    return jnp.concatenate(parts, axis=1)


def tap_rows(conv_ref):
    lines = [conv_ref[top].astype(FULL) for top in range(3)]
    return [lines[at // 3][at % 3 : at % 3 + 1] for at in range(9)]


def finish(small_ref, sums_ref, at, place):
    small_ref[pl.ds(place, 1), :] = jnp.sum(sums_ref[at], axis=0, keepdims=True)


def pre_reduce_kernel(
    need,
    send,
    at_ref,
    x_ref, w_ref, gain_ref, shift_ref, first_ref, edge_a_ref, edge_b_ref, normed_ref, factor_ref, red
):
    count, side, width = edge_a_ref.shape
    size = 2 * side
    steps = x_ref.shape[0] // size
    need(x_ref, w_ref)
    matmul(x_ref, w_ref, red)
    need(gain_ref, shift_ref)
    gain, shift = (gain_ref[pl.ds(0, 1), :], shift_ref[pl.ds(0, 1), :])

    @pl.loop(0, steps)
    def _(at):
        rows = rows_of(at, size)
        normed, factor = norm(red[rows, :])
        normed_ref[rows, :] = normed
        factor_ref[rows, :] = wide(factor)
        first_ref[rows, :] = silu(normed * gain + shift).astype(LOW)

    each = steps // count
    for image in range(count):
        head = first_ref[pl.ds(image * each * size, size), :].astype(FULL)
        tail = first_ref[pl.ds((image * each + each - 1) * size, size), :].astype(FULL)
        set_edges(at_ref, edge_a_ref, edge_b_ref, image, head[:side], tail[side:])


def pre_rest_kernel(
    need,
    send,
    at_ref,
    x_ref,
    first_ref,
    got_a_ref,
    got_b_ref,
    conv_ref,
    expand_ref,
    gain_ref,
    shift_ref,
    out_gain_ref,
    out_shift_ref,
    reduce_ref,
    post_gain_ref,
    post_shift_ref,
    second_ref,
    normed_b_ref,
    factor_b_ref,
    normed_c_ref,
    factor_c_ref,
    summed_ref,
    pooled_ref,
    post_first_ref,
    edge_a_ref,
    edge_b_ref,
    post_normed_ref,
    post_factor_ref,
    pad,
    exp,
    pair,
    red,
):
    count, strip, side, width = pad.shape
    strip = strip - 2
    size = 2 * side
    each = strip // 2
    need(first_ref, got_a_ref, got_b_ref)
    fill_halo(at_ref, pad, first_ref, got_a_ref, got_b_ref)
    need(conv_ref, gain_ref, shift_ref)
    send(pad)
    taps = tap_rows(conv_ref)
    gain, shift = (gain_ref[pl.ds(1, 1), :], shift_ref[pl.ds(1, 1), :])

    @pl.loop(0, count * each)
    def _(at):
        rows = rows_of(at, size)
        image, row = (at // each, 2 * lax.rem(at, each))
        conv = jnp.concatenate(
            [conv_row(pad, taps, image, row), conv_row(pad, taps, image, row + 1)], axis=0
        )
        normed, factor = norm(conv)
        normed_b_ref[rows, :] = normed
        factor_b_ref[rows, :] = wide(factor)
        second_ref[rows, :] = silu(normed * gain + shift).astype(LOW)

    send(second_ref, normed_b_ref, factor_b_ref)
    need(expand_ref)
    matmul(second_ref, expand_ref, exp)
    need(x_ref, out_gain_ref, out_shift_ref)
    out_gain, out_shift = (out_gain_ref[...], out_shift_ref[...])
    cols = side // 2
    for at in range(count * each):
        rows = pl.ds(at * size, size)
        normed, factor = norm(exp[rows, :])
        normed_c_ref[rows, :] = normed
        factor_c_ref[rows, :] = wide(factor)
        summed = x_ref[rows, :].astype(FULL) + normed * out_gain + out_shift
        summed_ref[rows, :] = summed
        block = silu(summed)
        half = narrow(pair, block[:side] + block[side:])
        pooled_ref[pl.ds(at * SLAB, cols), :] = 0.25 * half
        pooled_ref[pl.ds(at * SLAB + cols, SLAB - cols), :] = jnp.zeros(
            (SLAB - cols, width), FULL
        )
    send(normed_c_ref, factor_c_ref, summed_ref)
    need(reduce_ref, post_gain_ref, post_shift_ref)
    matmul(pooled_ref, reduce_ref, red)
    normed, factor = norm(red[...])
    post_normed_ref[...] = normed
    post_factor_ref[...] = wide(factor)
    first = silu(normed * post_gain_ref[pl.ds(0, 1), :] + post_shift_ref[pl.ds(0, 1), :])
    post_first_ref[...] = jnp.where(live(red.shape[0], cols), first, 0.0).astype(LOW)
    for image in range(count):
        head = post_first_ref[pl.ds(image * each * SLAB, SLAB), :].astype(FULL)
        tail = post_first_ref[pl.ds((image * each + each - 1) * SLAB, SLAB), :].astype(FULL)
        set_edges(at_ref, edge_a_ref, edge_b_ref, image, head, tail)


def post_rest_kernel(
    need,
    send,
    at_ref,
    pooled_ref,
    first_ref,
    got_a_ref,
    got_b_ref,
    conv_ref,
    expand_ref,
    gain_ref,
    shift_ref,
    out_gain_ref,
    out_shift_ref,
    block_ref,
    left_in_ref,
    left_second_ref,
    normed_b_ref,
    factor_b_ref,
    normed_c_ref,
    factor_c_ref,
    summed_ref,
    pad,
    second,
    exp,
    compact,
    *,
    cols
):
    count, rows, _, width = pad.shape
    rows = rows - 2
    small = block_ref.shape[0]
    need(first_ref, got_a_ref, got_b_ref)
    fill_halo(at_ref, pad, first_ref, got_a_ref, got_b_ref)
    send(pad)
    need(conv_ref, gain_ref, shift_ref, pooled_ref)
    taps = tap_rows(conv_ref)
    gain, shift = (gain_ref[pl.ds(1, 1), :], shift_ref[pl.ds(1, 1), :])

    @pl.loop(0, count * rows)
    def _(at):
        place = rows_of(at, SLAB)
        normed, factor = norm(conv_row(pad, taps, at // rows, lax.rem(at, rows)))
        normed_b_ref[place, :] = normed
        factor_b_ref[place, :] = wide(factor)
        second[place, :] = silu(normed * gain + shift)

    send(normed_b_ref, factor_b_ref)
    need(expand_ref)
    matmul(second, expand_ref, exp)
    need(out_gain_ref, out_shift_ref)
    normed, factor = norm(exp[...])
    normed_c_ref[...] = normed
    factor_c_ref[...] = wide(factor)
    summed = pooled_ref[...] + normed * out_gain_ref[...] + out_shift_ref[...]
    summed_ref[...] = summed
    exp[...] = silu(summed)
    compact[...] = jnp.zeros(compact.shape, FULL)
    for at in range(count * rows):
        compact[pl.ds(at * cols, cols), :] = exp[pl.ds(at * SLAB, cols), :]
    block_ref[...] = compact[pl.ds(0, small), :].astype(LOW)
    send(block_ref, normed_c_ref, factor_c_ref, summed_ref)
    pack(compact, pooled_ref, left_in_ref, cols)
    pack(compact, second, left_second_ref, cols)


def readout_kernel(
    need,
    send,
    at_ref,
    whole_ref,
    w_ref,
    bias_ref,
    cot_ref,
    out_ref,
    grad_ref,
    *refs,
    strips
):
    slots, (bias_grad_ref, cot, out, terms_ref) = (refs[:strips], refs[strips:])
    images, lines, cols, _ = cot_ref.shape
    rows = lines // strips
    need(cot_ref)
    for at in range(images * lines):
        strip, image, row = (at // (images * rows), at // rows % images, at % rows)
        cot[pl.ds(at * cols, cols), :] = cot_ref[image, strip * rows + row].astype(FULL)
    need(whole_ref, w_ref, bias_ref)

    @pl.loop(0, w_ref.shape[1] // TILE)
    def _(at):
        lanes = pl.ds(pl.multiple_of(at * TILE, TILE), TILE)
        act = jnp.dot(whole_ref[...], w_ref[:, lanes], preferred_element_type=FULL)
        act = act + bias_ref[:, lanes]
        cdf = 0.5 * (1.0 + lax.erf(act * SQRT_HALF))
        density = jnp.exp(-0.5 * act * act) * INV_SQRT_TWO_PI
        out[:, lanes] = act * cdf
        grad = (cot[:, lanes] * (cdf + act * density)).astype(LOW)
        grad_ref[:, lanes] = grad
        bias_grad_ref[:, lanes] = jnp.sum(grad.astype(FULL), axis=0, keepdims=True)

    send(grad_ref, bias_grad_ref)
    matmul_back(grad_ref, w_ref, terms_ref)
    small = slots[0].shape[0]
    for step in range(strips):
        begin = pl.multiple_of(flip(at_ref[2], step) * small, 8)
        slots[step][...] = terms_ref[pl.ds(begin, small), :].astype(LOW)
    for at in range(images * lines):
        strip, image, row = (at // (images * rows), at // rows % images, at % rows)
        out_ref[image, strip * rows + row] = out[pl.ds(at * cols, cols), :].astype(LOW)


def post_back_kernel(
    need,
    send,
    at_ref,
    *refs,
    cols,
    strips
):
    pieces, refs = (refs[:strips], refs[strips:])
    (
    expand_ref,
    gain_ref,
    shift_ref,
    out_gain_ref,
    normed_b_ref,
    factor_b_ref,
    normed_c_ref,
    factor_c_ref,
    summed_ref,
    grad_sum_ref,
    grad_exp_ref,
    grad_conv_ref,
    edge_a_ref,
    edge_b_ref,
    small_ref,
    compact,
    spread_out,
    exp,
    sec,
    ) = refs
    count = edge_a_ref.shape[0]
    tokens, width = grad_sum_ref.shape
    each = tokens // SLAB // count
    need(*pieces)
    total = pieces[0][...].astype(FULL)
    for piece in pieces[1:]:
        total = total + piece[...].astype(FULL)
    compact[...] = jnp.zeros(compact.shape, FULL)
    compact[pl.ds(0, total.shape[0]), :] = total
    spread_out[...] = jnp.zeros((tokens, width), FULL)
    for at in range(tokens // SLAB):
        spread_out[pl.ds(at * SLAB, cols), :] = compact[pl.ds(at * cols, cols), :]
    need(summed_ref, normed_c_ref, factor_c_ref, out_gain_ref)
    grad_sum = silu_back(spread_out[...], summed_ref[...])
    grad_sum_ref[...] = grad_sum
    normed = normed_c_ref[...]
    exp[...] = norm_back(grad_sum, normed, factor_c_ref[:, :1], out_gain_ref[...])
    small_ref[pl.ds(2, 1), :] = jnp.sum(grad_sum * normed, axis=0, keepdims=True)
    small_ref[pl.ds(3, 1), :] = jnp.sum(grad_sum, axis=0, keepdims=True)
    pack(compact, exp, grad_exp_ref, cols)
    send(grad_sum_ref, grad_exp_ref)
    need(expand_ref)
    matmul_back(exp, expand_ref, sec)
    need(gain_ref, shift_ref, normed_b_ref, factor_b_ref)
    gain, shift = (gain_ref[pl.ds(1, 1), :], shift_ref[pl.ds(1, 1), :])
    normed = normed_b_ref[...]
    grad = silu_back(sec[...], normed * gain + shift)
    grad_conv_ref[...] = norm_back(grad, normed, factor_b_ref[:, :1], gain).astype(LOW)
    small_ref[pl.ds(0, 1), :] = jnp.sum(grad * normed, axis=0, keepdims=True)
    small_ref[pl.ds(1, 1), :] = jnp.sum(grad, axis=0, keepdims=True)
    for image in range(count):
        head = grad_conv_ref[pl.ds(image * each * SLAB, SLAB), :].astype(FULL)
        tail = grad_conv_ref[pl.ds((image * each + each - 1) * SLAB, SLAB), :].astype(FULL)
        set_edges(at_ref, edge_a_ref, edge_b_ref, image, head, tail)


def middle_back_kernel(
    need,
    send,
    at_ref,
    grad_conv_ref,
    got_a_ref,
    got_b_ref,
    pad,
    post_conv_ref,
    post_reduce_ref,
    post_gain_ref,
    post_shift_ref,
    post_normed_ref,
    post_factor_ref,
    post_grad_sum_ref,
    expand_ref,
    gain_ref,
    shift_ref,
    out_gain_ref,
    normed_b_ref,
    factor_b_ref,
    normed_c_ref,
    factor_c_ref,
    summed_ref,
    post_grad_red_ref,
    grad_sum_ref,
    grad_exp_ref,
    pre_grad_conv_ref,
    edge_a_ref,
    edge_b_ref,
    post_small_ref,
    small_ref,
    grad_pad,
    taps_sum,
    grad_in,
    pair,
    sec,
    sums,
    post_red,
    compact,
    *,
    cols
):
    count, side, width = edge_a_ref.shape
    need(grad_conv_ref, got_a_ref, got_b_ref)
    fill_halo(at_ref, grad_pad, grad_conv_ref, got_a_ref, got_b_ref)
    need(pad, post_conv_ref)
    need(post_gain_ref, post_shift_ref, post_normed_ref, post_factor_ref)
    taps = tap_rows(post_conv_ref)
    taps_sum[...] = jnp.zeros_like(taps_sum)
    sums[...] = jnp.zeros_like(sums)
    gain, shift = (post_gain_ref[pl.ds(0, 1), :], post_shift_ref[pl.ds(0, 1), :])
    each = post_grad_sum_ref.shape[0] // SLAB // count

    @pl.loop(0, count * each)
    def _(at):
        place = rows_of(at, SLAB)
        grad = conv_back_row(pad, grad_pad, taps, taps_sum, at // each, lax.rem(at, each))
        normed = post_normed_ref[place, :]
        grad = jnp.where(live(SLAB, cols), silu_back(grad, normed * gain + shift), 0.0)
        sums[0] += fold(grad * normed)
        sums[1] += fold(grad)
        post_red[place, :] = norm_back(grad, normed, post_factor_ref[place, :1], gain)

    for at in range(9):
        finish(post_small_ref, taps_sum, at, at)
    finish(post_small_ref, sums, 0, 9)
    finish(post_small_ref, sums, 1, 10)
    pack(compact, post_red, post_grad_red_ref, cols)
    send(post_grad_red_ref, post_small_ref)
    need(post_reduce_ref)
    matmul_back(post_red, post_reduce_ref, grad_in)
    sums[...] = jnp.zeros_like(sums)
    size = 2 * side
    need(out_gain_ref, post_grad_sum_ref, summed_ref, normed_c_ref, factor_c_ref)
    out_gain = out_gain_ref[...]
    for at in range(count * each):
        rows = pl.ds(at * size, size)
        place = pl.ds(at * SLAB, cols)
        grad = 0.25 * (post_grad_sum_ref[place, :] + grad_in[place, :])
        grad = widen(pair, grad)
        grad = jnp.concatenate([grad, grad], axis=0)
        grad_sum = silu_back(grad, summed_ref[rows, :])
        grad_sum_ref[rows, :] = grad_sum
        normed = normed_c_ref[rows, :]
        sums[0] += fold(grad_sum * normed)
        sums[1] += fold(grad_sum)
        grad_exp_ref[rows, :] = norm_back(
            grad_sum, normed, factor_c_ref[rows, :1], out_gain
        ).astype(LOW)
    finish(small_ref, sums, 0, 2)
    finish(small_ref, sums, 1, 3)
    send(grad_sum_ref, grad_exp_ref)
    need(expand_ref)
    matmul_back(grad_exp_ref, expand_ref, sec)
    need(gain_ref, shift_ref, normed_b_ref, factor_b_ref)
    sums[...] = jnp.zeros_like(sums)
    gain_b, shift_b = (gain_ref[pl.ds(1, 1), :], shift_ref[pl.ds(1, 1), :])

    @pl.loop(0, count * each)
    def _(at):
        rows = rows_of(at, size)
        normed = normed_b_ref[rows, :]
        grad = silu_back(sec[rows, :], normed * gain_b + shift_b)
        sums[0] += fold(grad * normed)
        sums[1] += fold(grad)
        pre_grad_conv_ref[rows, :] = norm_back(
            grad, normed, factor_b_ref[rows, :1], gain_b
        ).astype(LOW)

    finish(small_ref, sums, 0, 0)
    finish(small_ref, sums, 1, 1)
    for image in range(count):
        head = pre_grad_conv_ref[pl.ds(image * each * size, size), :].astype(FULL)
        tail = pre_grad_conv_ref[pl.ds((image * each + each - 1) * size, size), :].astype(FULL)
        set_edges(at_ref, edge_a_ref, edge_b_ref, image, head[:side], tail[side:])


def pre_back_kernel(
    need,
    send,
    at_ref,
    grad_conv_ref,
    got_a_ref,
    got_b_ref,
    pad,
    conv_ref,
    gain_ref,
    shift_ref,
    normed_ref,
    factor_ref,
    small_b_ref,
    post_small_a_ref,
    post_small_b_ref,
    read_bias_ref,
    grad_red_ref,
    small_ref,
    grad_pad,
    taps_sum,
    sums,
):
    count, strip, side, width = pad.shape
    strip = strip - 2
    size = 2 * side
    each = strip // 2
    need(grad_conv_ref, got_a_ref, got_b_ref)
    fill_halo(at_ref, grad_pad, grad_conv_ref, got_a_ref, got_b_ref)
    need(pad, conv_ref)
    need(gain_ref, shift_ref, normed_ref, factor_ref)
    taps = tap_rows(conv_ref)
    taps_sum[...] = jnp.zeros_like(taps_sum)
    sums[...] = jnp.zeros_like(sums)
    gain, shift = (gain_ref[pl.ds(0, 1), :], shift_ref[pl.ds(0, 1), :])

    @pl.loop(0, count * each)
    def _(at):
        rows = rows_of(at, size)
        image, row = (at // each, 2 * lax.rem(at, each))
        grad = jnp.concatenate(
            [
                conv_back_row(pad, grad_pad, taps, taps_sum, image, row),
                conv_back_row(pad, grad_pad, taps, taps_sum, image, row + 1),
            ],
            axis=0,
        )
        normed = normed_ref[rows, :]
        grad = silu_back(grad, normed * gain + shift)
        sums[0] += fold(grad * normed)
        sums[1] += fold(grad)
        grad_red_ref[rows, :] = norm_back(grad, normed, factor_ref[rows, :1], gain).astype(LOW)

    for at in range(9):
        finish(small_ref, taps_sum, at, at)
    finish(small_ref, sums, 0, 9)
    finish(small_ref, sums, 1, 10)
    need(small_b_ref, post_small_a_ref, post_small_b_ref, read_bias_ref)
    small_ref[pl.ds(11, 4), :] = small_b_ref[...]
    small_ref[pl.ds(15, 11), :] = post_small_a_ref[...]
    small_ref[pl.ds(26, 4), :] = post_small_b_ref[...]
    small_ref[pl.ds(30, 1), :] = read_bias_ref[...]
    small_ref[pl.ds(31, 1), :] = jnp.zeros_like(read_bias_ref)


def pair_outer_kernel(need, send, at_ref, *refs, pairs, parts):
    takes = 4 * pairs
    outs = refs[takes:]
    half, plane = (at_ref[0], at_ref[1])
    rows = outs[0].shape[0] // pairs
    for pair in range(pairs):
        left, left_far, right, right_far = refs[4 * pair : 4 * pair + 4]
        need(left, left_far, right, right_far)
        for step in range(parts):
            begin = half * (rows * parts) + flip(plane, step) * rows
            lanes = pl.ds(pl.multiple_of(begin, LANES), rows)
            total = lax.dot_general(
                left[:, lanes], right[...], (((0,), (0,)), ((), ())), preferred_element_type=FULL
            ) + lax.dot_general(
                left_far[:, lanes],
                right_far[...],
                (((0,), (0,)), ((), ())),
                preferred_element_type=FULL,
            )
            outs[step][pl.ds(pair * rows, rows), :] = total.astype(LOW)
    send(*outs)


def sum_split_kernel(need, send, at_ref, *refs, pairs, parts, pieces, along=2):
    takes, outs = (refs[:pieces], refs[pieces : pieces + parts])
    total = refs[-1]
    need(*takes)
    value = takes[0][...].astype(FULL)
    for at in range(1, pieces):
        value = value + takes[at][...].astype(FULL)
    total[...] = value
    rows = total.shape[0] // pairs // parts
    for step in range(parts):
        begin = flip(at_ref[along], step) * rows
        for pair in range(pairs):
            place = pl.ds(pl.multiple_of(pair * rows * parts + begin, SLAB), rows)
            outs[step][pl.ds(pair * rows, rows), :] = total[place, :].astype(LOW)
    send(*outs)


def assemble_kernel(*refs, pairs, planes, strips, cut):
    takes = 2 * (planes + cut)
    parts, outs = (refs[:takes], refs[takes : takes + pairs])
    full, sem = (refs[takes + pairs : takes + 2 * pairs], refs[-1])
    half, plane, row = places()
    rows = parts[0].shape[0] // pairs // strips
    block = strips * rows
    writes = []
    for pair in range(pairs):
        for at in range(2 * planes):
            side, spot = (flip(half, at // planes), flip(plane, at % planes))
            for step in range(strips):
                place = side * (planes * block) + spot * block
                if strips > 1:
                    place = place + flip(row, step) * rows
                source, begin = (at % planes, step)
                if cut and source == planes - 1 and 2 * step >= strips:
                    source, begin = (planes, step - strips // 2)
                part = parts[at // planes * (planes + cut) + source]
                full[pair][pl.ds(pl.multiple_of(place, SLAB), rows), :] = part[
                    pl.ds((begin * pairs + pair) * rows, rows), :
                ].astype(FULL)
        writes.append(pltpu.make_async_copy(full[pair], outs[pair], sem.at[pair]))
        writes[-1].start()
    for write in writes:
        write.wait()


def assemble(parts, pairs, planes, strips):
    takes = len(parts)
    out = like(2 * planes * parts[0].shape[0] // pairs, parts[0].shape[1])
    parts = [pltpu.with_memory_space_constraint(part, pltpu.VMEM) for part in parts]
    return pl.pallas_call(
        functools.partial(
            assemble_kernel, pairs=pairs, planes=planes, strips=strips, cut=takes // 2 - planes
        ),
        out_shape=[pltpu.HBM(out.shape, out.dtype)] * pairs,
        in_specs=[pl.BlockSpec(memory_space=pltpu.VMEM)] * takes,
        out_specs=[pl.BlockSpec(memory_space=pltpu.HBM)] * pairs,
        scratch_shapes=[pltpu.VMEM(out.shape, FULL)] * pairs + [pltpu.SemaphoreType.DMA((pairs,))],
        compiler_params=pltpu.CompilerParams(vmem_limit_bytes=VMEM_BYTES),
        cost_estimate=pl.CostEstimate(flops=0, bytes_accessed=0, transcendentals=0),
    )(*parts)


def small_kernel(need, send, at_ref, sums_ref, *outs):
    for place in range(2):
        conv, gain, shift, out_gain, out_shift = outs[5 * place : 5 * place + 5]
        rows = sums_ref[pl.ds(15 * place, 15), :]
        for top in range(3):
            conv[top] = rows[3 * top : 3 * top + 3]
        gain[pl.ds(0, 1), :] = rows[9:10]
        gain[pl.ds(1, 1), :] = rows[11:12]
        shift[pl.ds(0, 1), :] = rows[10:11]
        shift[pl.ds(1, 1), :] = rows[12:13]
        out_gain[...] = rows[13:14]
        out_shift[...] = rows[14:15]


class Near:
    def __init__(self, value):
        self.value = value


def like(*shape, dtype=FULL):
    return jax.ShapeDtypeStruct(shape, dtype)


def low(*shape):
    return like(*shape, dtype=LOW)


def places():
    return [lax.axis_index(axis) for axis in ("half", "im", "row")]


def call(kernel, outs, scratch, *args):
    near_in = [isinstance(arg, Near) for arg in args]
    near_out = [isinstance(out, Near) for out in outs]
    args = [arg.value if isinstance(arg, Near) else arg for arg in args]
    outs = [out.value if isinstance(out, Near) else out for out in outs]
    takes, gives = (len(args), len(outs))
    far_in = [at for at in range(takes) if not near_in[at]]
    far_out = [at for at in range(gives) if not near_out[at]]

    def body(*refs):
        given, refs = (list(refs[:takes]), refs[takes:])
        made, refs = (list(refs[:gives]), refs[gives:])
        rest = refs[len(far_in) + len(far_out) :]
        reads, writes = ({}, {})
        if far_in:
            in_sem = rest[-1]
            rest = rest[:-1]
        if far_out:
            out_sem = rest[-1]
            rest = rest[:-1]
        for place, at in enumerate(far_in):
            reads[at] = pltpu.make_async_copy(given[at], refs[place], in_sem.at[place])
            given[at] = refs[place]
        for place, at in enumerate(far_out):
            mirror = refs[len(far_in) + place]
            writes[at] = pltpu.make_async_copy(mirror, made[at], out_sem.at[place])
            made[at] = mirror
        for at in sorted(reads, key=lambda at: args[at].size):
            reads[at].start()
        started = []

        def need(*wanted):
            for at in list(reads):
                if any(given[at] is ref for ref in wanted):
                    reads.pop(at).wait()

        def send(*ready):
            for at in list(writes):
                if any(made[at] is ref for ref in ready):
                    started.append(writes.pop(at))
                    started[-1].start()

        kernel(need, send, places(), *given, *made, *rest)
        need(*given)
        send(*made)
        for write in started:
            write.wait()

    spaces = {True: pltpu.VMEM, False: pltpu.HBM}
    args = [
        pltpu.with_memory_space_constraint(arg, spaces[near]) for arg, near in zip(args, near_in)
    ]
    return pl.pallas_call(
        body,
        out_shape=[spaces[near](out.shape, out.dtype) for out, near in zip(outs, near_out)],
        in_specs=[pl.BlockSpec(memory_space=spaces[near]) for near in near_in],
        out_specs=[pl.BlockSpec(memory_space=spaces[near]) for near in near_out],
        scratch_shapes=[pltpu.VMEM(args[at].shape, args[at].dtype) for at in far_in]
        + [pltpu.VMEM(outs[at].shape, outs[at].dtype) for at in far_out]
        + [pltpu.VMEM(shape, FULL) for shape in scratch]
        + [pltpu.SemaphoreType.DMA((len(far_out),))] * bool(far_out)
        + [pltpu.SemaphoreType.DMA((len(far_in),))] * bool(far_in),
        compiler_params=pltpu.CompilerParams(vmem_limit_bytes=VMEM_BYTES),
        cost_estimate=pl.CostEstimate(flops=0, bytes_accessed=0, transcendentals=0),
    )(*args)


def edges(parity_edges):
    size = lax.axis_size("row")
    inner = [(at, at ^ 1) for at in range(size)]
    outer = [(at, at + 1) for at in range(1, size - 1, 2)]
    outer = outer + [(to, at) for at, to in outer]
    return (
        lax.ppermute(parity_edges[0], "row", inner),
        lax.ppermute(parity_edges[1], "row", outer),
    )


def swap(field):
    return lax.ppermute(field, "half", [(0, 1), (1, 0)])


def steps_of(value, axis, step):
    size = lax.axis_size(axis)
    return lax.ppermute(value, axis, [(at, at ^ step) for at in range(size)])


def share(parts, axis):
    return [parts[0]] + [steps_of(parts[at], axis, at) for at in range(1, len(parts))]


def share_same(part, axis):
    size = lax.axis_size(axis)
    return [part] + [steps_of(part, axis, at) for at in range(1, size)]


def gather_near(part):
    return [part, steps_of(part, "im", 1), steps_of(part, "im", 2)]


def gather_rest(parts):
    half = parts[0].shape[0] // 2
    return [steps_of(parts[1][:half], "im", 2), steps_of(parts[2][half:], "im", 1)]


def small_outputs(part, width):
    return [
        part[:9].reshape(3, 3, width),
        jnp.stack([part[9], part[11]]),
        jnp.stack([part[10], part[12]]),
        part[13],
        part[14],
    ]


def pair_outer(*pairs):
    size = lax.axis_size("im")
    first = pairs[0][0].value if isinstance(pairs[0][0], Near) else pairs[0][0]
    width = first.shape[1]
    rows = width // 2 // size * len(pairs)
    return list(
        call(
            functools.partial(pair_outer_kernel, pairs=len(pairs), parts=size),
            [Near(low(rows, width))] * size,
            [],
            *[ref for pair in pairs for ref in pair],
        )
    )


def sum_split(pieces, pairs):
    size = lax.axis_size("row")
    rows, width = pieces[0].shape
    return list(
        call(
            functools.partial(
                sum_split_kernel,
                pairs=pairs,
                parts=size,
                pieces=len(pieces),
            ),
            [Near(low(rows // size, width))] * size,
            [(rows, width)],
            *[Near(piece) for piece in pieces],
        )
    )


def add_low(pieces):
    total = pieces[0].astype(FULL)
    for piece in pieces[1:]:
        total = total + piece.astype(FULL)
    return total.astype(LOW)


def sum_far(left, right, axes):
    part = jnp.einsum("tm,tc->mc", left, right, preferred_element_type=FULL)
    return lax.psum(part, axes)


def shards(
    x_in,
    pre_reduce,
    pre_conv,
    pre_expand,
    pre_mid_gain,
    pre_mid_shift,
    pre_out_gain,
    pre_out_shift,
    post_reduce,
    post_conv,
    post_expand,
    post_mid_gain,
    post_mid_shift,
    post_out_gain,
    post_out_shift,
    read_weight,
    read_bias,
    cotangent,
):
    count, strip, side, width = x_in.shape
    strips = lax.axis_size("row")
    tokens = count * strip * side
    cols = side // 2
    rows = strip // 2
    slabs = count * rows
    padded = slabs * SLAB
    small = slabs * cols
    block = -(-small // SLAB) * SLAB
    features = read_weight.shape[1]
    x_low = x_in.reshape(tokens, width)
    pre_out_g, pre_out_s = (pre_out_gain[None], pre_out_shift[None])
    post_out_g, post_out_s = (post_out_gain[None], post_out_shift[None])
    pre_edge = Near(low(count, side, width))
    post_edge = Near(low(count, SLAB, width))
    quick = lax.axis_size("im") == 4 and strips == 4

    first, edge_a, edge_b, normed_a, factor_a = call(
        pre_reduce_kernel,
        [Near(low(tokens, width)), pre_edge, pre_edge, like(tokens, width), like(tokens, LANES)],
        [(tokens, width)],
        x_low,
        pre_reduce,
        pre_mid_gain,
        pre_mid_shift,
    )
    got_a, got_b = edges((edge_a, edge_b))
    (
        second,
        normed_b,
        factor_b,
        normed_c,
        factor_c,
        summed,
        pooled,
        post_first,
        edge_a,
        edge_b,
        post_normed_a,
        post_factor_a,
        pad,
    ) = call(
        pre_rest_kernel,
        [
            low(tokens, width),
            like(tokens, width),
            like(tokens, LANES),
            like(tokens, width),
            like(tokens, LANES),
            like(tokens, width),
            Near(like(padded, width)),
            Near(low(padded, width)),
            post_edge,
            post_edge,
            like(padded, width),
            like(padded, LANES),
            like(count, strip + 2, side, width),
        ],
        [(tokens, width), (side * width // LANES, LANES), (padded, width)],
        x_low,
        Near(first),
        Near(got_a),
        Near(got_b),
        pre_conv,
        pre_expand,
        pre_mid_gain,
        pre_mid_shift,
        pre_out_g,
        pre_out_s,
        post_reduce,
        post_mid_gain,
        post_mid_shift,
    )
    got_a, got_b = edges((edge_a, edge_b))
    (
        block_two,
        left_in,
        left_second,
        post_normed_b,
        post_factor_b,
        post_normed_c,
        post_factor_c,
        post_summed,
        post_pad,
    ) = call(
        functools.partial(post_rest_kernel, cols=cols),
        [
            Near(low(small, width)),
            low(block, width),
            low(block, width),
            like(padded, width),
            like(padded, LANES),
            like(padded, width),
            like(padded, LANES),
            like(padded, width),
            like(count, rows + 2, SLAB, width),
        ],
        [(padded, width), (padded, width), (block, width)],
        Near(pooled),
        Near(post_first),
        Near(got_a),
        Near(got_b),
        post_conv,
        post_expand,
        post_mid_gain,
        post_mid_shift,
        post_out_g,
        post_out_s,
    )
    whole = lax.all_gather(block_two, "row", axis=0, tiled=True)
    readout, grad_pre, *terms, d_read_b = call(
        functools.partial(readout_kernel, strips=strips),
        [
            like(*cotangent.shape, dtype=LOW),
            Near(low(strips * small, features)),
        ]
        + [Near(low(small, width))] * strips
        + [like(1, features)],
        [
            (strips * small, features),
            (strips * small, features),
            (strips * small, width),
        ],
        Near(whole),
        read_weight,
        read_bias[None],
        cotangent,
    )
    terms = share(terms, "row")
    if quick:
        parts = pair_outer(
            (Near(whole), Near(swap(whole)), Near(grad_pre), Near(swap(grad_pre)))
        )
        parts[0], *terms = tie(parts[0], *terms)
        read_parts = share(parts, "im")
    post_gs, post_ge, post_gc, edge_a, edge_b, post_small_b = call(
        functools.partial(post_back_kernel, cols=cols, strips=strips),
        [
            Near(like(padded, width)),
            Near(low(block, width)),
            Near(low(padded, width)),
            post_edge,
            post_edge,
            like(4, width),
        ],
        [(block, width), (padded, width), (padded, width), (padded, width)],
        *[Near(term) for term in terms],
        post_expand,
        post_mid_gain,
        post_mid_shift,
        post_out_g,
        post_normed_b,
        post_factor_b,
        post_normed_c,
        post_factor_c,
        post_summed,
    )
    got_a, got_b = edges((edge_a, edge_b))
    if quick:
        (got_a, got_b), read_parts = tie_later((got_a, got_b), read_parts)
    (
        post_gr,
        pre_gs,
        pre_ge,
        pre_gc,
        edge_a,
        edge_b,
        post_small_a,
        pre_small_b,
    ) = call(
        functools.partial(middle_back_kernel, cols=cols),
        [
            Near(low(block, width)),
            like(tokens, width),
            Near(low(tokens, width)),
            Near(low(tokens, width)),
            pre_edge,
            pre_edge,
            like(11, width),
            like(4, width),
        ],
        [
            (count, rows + 2, SLAB, width),
            (9, 8, width),
            (padded, width),
            (side * width // LANES, LANES),
            (tokens, width),
            (2, 8, width),
            (padded, width),
            (block, width),
        ],
        Near(post_gc),
        Near(got_a),
        Near(got_b),
        post_pad,
        post_conv,
        post_reduce,
        post_mid_gain,
        post_mid_shift,
        post_normed_a,
        post_factor_a,
        Near(post_gs),
        pre_expand,
        pre_mid_gain,
        pre_mid_shift,
        pre_out_g,
        normed_b,
        factor_b,
        normed_c,
        factor_c,
        summed,
    )
    got_a, got_b = edges((edge_a, edge_b))
    if quick:
        pre_ge_far = swap(pre_ge)
        post_parts = pair_outer(
            (left_in, swap(left_in), Near(post_gr), Near(swap(post_gr))),
            (left_second, swap(left_second), Near(post_ge), Near(swap(post_ge))),
        )
        post_parts = pair_outer(
            (left_in, swap(left_in), Near(post_gr), Near(swap(post_gr))),
            (left_second, swap(left_second), Near(post_ge), Near(swap(post_ge))),
        )
        post_sums = [steps_of(post_parts[at], "im", at) for at in (1, 2)]
        (got_a, got_b), post_sums = tie_later((got_a, got_b), post_sums)
    pre_gr, sums = call(
        pre_back_kernel,
        [Near(low(tokens, width)), Near(like(32, width))],
        [
            (count, strip + 2, side, width),
            (9, 8, width),
            (2, 8, width),
        ],
        Near(pre_gc),
        Near(got_a),
        Near(got_b),
        pad,
        pre_conv,
        pre_mid_gain,
        pre_mid_shift,
        normed_a,
        factor_a,
        pre_small_b,
        post_small_a,
        post_small_b,
        d_read_b,
    )
    if quick:
        post_sums = post_sums + [steps_of(post_parts[3], "im", 3)]
        parts = pair_outer(
            (second, swap(second), Near(pre_ge), Near(swap(pre_ge))),
            (x_low, swap(x_low), Near(pre_gr), Near(swap(pre_gr))),
        )
        parts[0], sums = tie(parts[0], sums + swap(sums))
        alone = lax.broadcasted_iota(jnp.int32, sums.shape, 0) >= 30
        for step in (1, 2):
            sums = sums + jnp.where(alone, 0.0, steps_of(sums, "row", step))
        (parts[0], *post_sums), (sums, *read_parts) = tie_later(
            (parts[0], *post_sums), (sums, *read_parts)
        )
        post_parts = share(sum_split(post_parts[:1] + post_sums, 2), "row")
        near_parts = [steps_of(parts[at], "im", at) for at in (1, 2)]
        grad_in = pre_gs + jnp.einsum("tm,cm->tc", pre_gr, pre_reduce, preferred_element_type=FULL)
        grad_in = grad_in.astype(LOW)
        post_parts, (grad_in, last, *rest) = tie_later(
            post_parts, (grad_in, parts[3], *near_parts, *read_parts)
        )
        near_parts, read_parts = (rest[:2], rest[2:])
        post_parts = share_same(add_low(post_parts), "row")
        last = steps_of(last, "im", 3)
        post_parts, (last, *read_parts) = tie_later(post_parts, (last, *read_parts))
        parts = share(sum_split([parts[0]] + near_parts + [last], 2), "row")
        post_parts = gather_near(jnp.concatenate(post_parts, axis=0))
        read_parts = gather_near(add_low(read_parts))
        parts, rest = tie_later(parts, (*post_parts, *read_parts))
        post_parts, read_parts = (rest[:3], rest[3:])
        parts = share_same(add_low(parts), "row")
        read_parts.append(steps_of(read_parts[0], "im", 3))
        post_parts = post_parts + gather_rest(post_parts)
        parts, rest = tie_later(parts, (*post_parts, *read_parts, sums))
        post_parts, read_parts, sums = (rest[:5], rest[5:9], rest[9])
        parts = gather_near(jnp.concatenate(parts, axis=0))
        parts, post_parts = tie_later(parts, post_parts)
        post_far = [swap(part) for part in post_parts]
        post_reduce_g, post_expand_g = assemble(post_parts + post_far, 2, 4, strips)
        (read_total,) = assemble(read_parts + [swap(part) for part in read_parts], 1, 4, 1)
        far = [swap(part) for part in parts]
        rest = gather_rest(parts)
        for step in (1, 2):
            sums = sums + steps_of(sums, "im", step)
        (post_reduce_g, read_total), rest = tie_later((post_reduce_g, read_total), rest)
        parts = parts + rest
        far = far + [swap(part) for part in rest]
        far[4], sums = tie(far[4], sums)
        small_out = call(
            small_kernel,
            [like(3, 3, width), like(2, width), like(2, width), like(1, width), like(1, width)] * 2,
            [],
            Near(sums),
        )
        pre_expand_g, pre_reduce_g = assemble(parts + far, 2, 4, strips)
        read_bias_g = sums[30]
    else:
        axes = IMG + ("row",)
        post_reduce_g = sum_far(left_in, post_gr, axes)
        post_expand_g = sum_far(left_second, post_ge, axes)
        pre_expand_g = sum_far(second, pre_ge, axes)
        pre_reduce_g = sum_far(x_low, pre_gr, axes)
        read_total = sum_far(whole, grad_pre, IMG)
        read_bias_g = lax.psum(sums[30], IMG)
        sums = lax.psum(sums[:30], axes)
        small_out = small_outputs(sums[:15], width) + small_outputs(sums[15:30], width)
        grad_in = pre_gs + jnp.einsum("tm,cm->tc", pre_gr, pre_reduce, preferred_element_type=FULL)
        grad_in = grad_in.astype(LOW)

    pre_conv_g, pre_gain_g, pre_shift_g, pre_og_g, pre_os_g = small_out[:5]
    post_conv_g, post_gain_g, post_shift_g, post_og_g, post_os_g = small_out[5:]
    return (
        readout,
        grad_in.reshape(x_in.shape),
        pre_reduce_g,
        pre_conv_g,
        pre_expand_g,
        pre_gain_g,
        pre_shift_g,
        pre_og_g.reshape(width),
        pre_os_g.reshape(width),
        post_reduce_g,
        post_conv_g,
        post_expand_g,
        post_gain_g,
        post_shift_g,
        post_og_g.reshape(width),
        post_os_g.reshape(width),
        read_total,
        read_bias_g,
    )


def solution(mesh):
    images, strips = mesh.devices.shape
    split = jax.sharding.Mesh(
        mesh.devices.reshape(images // 2, 2, strips), ("im", "half", "row")
    )
    return jax.shard_map(
        shards,
        mesh=split,
        in_specs=(P(IMG, "row", None, None),)
        + (P(),) * 14
        + (P(None, "row"), P("row"), P(IMG, None, None, "row")),
        out_specs=(P(IMG, None, None, "row"), P(IMG, "row", None, None))
        + (P(),) * 14
        + (P(None, "row"), P("row")),
        check_vma=False,
    )
```

```python
import functools

import jax
import jax.numpy as jnp
from jax import lax
from jax.experimental import pallas as pl
from jax.experimental.pallas import tpu as pltpu
from jax.sharding import PartitionSpec as P

EPSILON = 1e-06
SQRT_HALF = 0.7071067811865476
INV_SQRT_TWO_PI = 0.3989422804014327
LOW = jnp.bfloat16
FULL = jnp.float32
IMG = ("im", "half")
TILE = 256
SLAB = 16
LANES = 128
VMEM_BYTES = 24 * 1024 * 1024


def tie(*values):
    return lax.optimization_barrier(values)


def tie_later(first, second):
    first = list(tie(*first))
    out = list(tie(*first, *second))
    return (out[: len(first)], out[len(first) :])


def norm(value):
    centred = value - jnp.mean(value, axis=-1, keepdims=True)
    factor = lax.rsqrt(jnp.mean(centred * centred, axis=-1, keepdims=True) + EPSILON)
    return (centred * factor, factor)


def norm_back(grad, normed, factor, gain):
    scaled = grad * gain
    return factor * (
        scaled
        - jnp.mean(scaled, axis=-1, keepdims=True)
        - normed * jnp.mean(scaled * normed, axis=-1, keepdims=True)
    )


def gate(value):
    return 0.5 * jnp.tanh(0.5 * value) + 0.5


def silu(value):
    return value * gate(value)


def silu_back(grad, value):
    sigma = gate(value)
    return grad * sigma * (1.0 + value * (1.0 - sigma))


def flip(place, step):
    bit = 1
    while bit <= step:
        if step & bit:
            place = place + bit - 2 * bit * ((place // bit) % 2)
        bit *= 2
    return place


def wide(factor):
    return jnp.broadcast_to(factor, (factor.shape[0], LANES))


def fold(value):
    return jnp.sum(value.reshape(-1, 8, value.shape[-1]), axis=0)


def live(rows, cols):
    at = lax.broadcasted_iota(jnp.int32, (rows, 1), 0)
    return lax.rem(at, SLAB) < cols


def from_left(value):
    at = lax.broadcasted_iota(jnp.int32, (value.shape[0], 1), 0)
    return jnp.where(at == 0, 0.0, pltpu.roll(value, 1, 0))


def from_right(value):
    last = value.shape[0] - 1
    at = lax.broadcasted_iota(jnp.int32, (value.shape[0], 1), 0)
    return jnp.where(at == last, 0.0, pltpu.roll(value, last, 0))


def matmul(left_ref, right_ref, out_ref):
    @pl.loop(0, right_ref.shape[1] // TILE)
    def _(at):
        cols = pl.ds(pl.multiple_of(at * TILE, TILE), TILE)
        out_ref[:, cols] = jnp.dot(
            left_ref[...].astype(LOW), right_ref[:, cols], preferred_element_type=FULL
        )


def matmul_back(left_ref, right_ref, out_ref):
    @pl.loop(0, right_ref.shape[0] // TILE)
    def _(at):
        cols = pl.ds(pl.multiple_of(at * TILE, TILE), TILE)
        out_ref[:, cols] = lax.dot_general(
            left_ref[...].astype(LOW),
            right_ref[cols, :],
            (((1,), (1,)), ((), ())),
            preferred_element_type=FULL,
        ).astype(out_ref.dtype)


def rows_of(at, size):
    return pl.ds(pl.multiple_of(at * size, SLAB), size)


def fill_halo(at_ref, pad_ref, low_ref, got_a_ref, got_b_ref):
    count, rows, cols, width = pad_ref.shape
    rows = rows - 2
    even = lax.rem(at_ref[2], 2) == 0
    for image in range(count):
        got_a, got_b = (got_a_ref[image].astype(FULL), got_b_ref[image].astype(FULL))
        pad_ref[image, 0] = jnp.where(even, got_b, got_a)
        pad_ref[image, rows + 1] = jnp.where(even, got_a, got_b)

    size = cols if cols % SLAB == 0 else 2 * cols
    per = size // cols
    each = rows // per

    @pl.loop(0, count * each)
    def _(at):
        part = low_ref[rows_of(at, size), :].astype(FULL).reshape(per, cols, width)
        pad_ref[at // each, pl.ds(1 + per * lax.rem(at, each), per)] = part


def set_edges(at_ref, edge_a_ref, edge_b_ref, image, head, tail):
    even = lax.rem(at_ref[2], 2) == 0
    edge_a_ref[image] = jnp.where(even, tail, head).astype(LOW)
    edge_b_ref[image] = jnp.where(even, head, tail).astype(LOW)


def conv_row(pad_ref, taps, image, row):
    lines = [pad_ref[image, row + top] for top in range(3)]
    sums = [
        lines[0] * taps[left] + lines[1] * taps[3 + left] + lines[2] * taps[6 + left]
        for left in range(3)
    ]
    return from_left(sums[0]) + sums[1] + from_right(sums[2])


def conv_back_row(pad_ref, grad_ref, taps, taps_ref, image, row):
    lines = [grad_ref[image, row + top] for top in range(3)]
    sums = [
        lines[2] * taps[left] + lines[1] * taps[3 + left] + lines[0] * taps[6 + left]
        for left in range(3)
    ]
    shifted = [from_right(lines[1]), lines[1], from_left(lines[1])]
    for top in range(3):
        source = pad_ref[image, row + top]
        for left in range(3):
            taps_ref[3 * top + left] += fold(source * shifted[left])
    return from_right(sums[0]) + sums[1] + from_left(sums[2])


def pack(compact, source, out_ref, cols):
    compact[...] = jnp.zeros(compact.shape, FULL)
    for at in range(source.shape[0] // SLAB):
        compact[pl.ds(at * cols, cols), :] = source[pl.ds(at * SLAB, cols), :]
    out_ref[...] = compact[...].astype(LOW)


def narrow(pair, value):
    side = value.shape[0]
    parts = []
    for at in range(value.shape[1] // LANES):
        pair[pl.ds(at * side, side), :] = value[:, at * LANES : (at + 1) * LANES]
        parts.append(
            pair[pl.ds(at * side, side // 2, stride=2), :]
            + pair[pl.ds(at * side + 1, side // 2, stride=2), :]
        )
    return jnp.concatenate(parts, axis=1)


def widen(pair, value):
    cols = value.shape[0]
    parts = []
    for at in range(value.shape[1] // LANES):
        part = value[:, at * LANES : (at + 1) * LANES]
        pair[pl.ds(2 * cols * at, cols, stride=2), :] = part
        pair[pl.ds(2 * cols * at + 1, cols, stride=2), :] = part
        parts.append(pair[pl.ds(2 * cols * at, 2 * cols), :])
    return jnp.concatenate(parts, axis=1)


def tap_rows(conv_ref):
    lines = [conv_ref[top].astype(FULL) for top in range(3)]
    return [lines[at // 3][at % 3 : at % 3 + 1] for at in range(9)]


def finish(small_ref, sums_ref, at, place):
    small_ref[pl.ds(place, 1), :] = jnp.sum(sums_ref[at], axis=0, keepdims=True)


def pre_reduce_kernel(
    need,
    send,
    at_ref,
    x_ref, w_ref, gain_ref, shift_ref, first_ref, edge_a_ref, edge_b_ref, normed_ref, factor_ref, red
):
    count, side, width = edge_a_ref.shape
    size = 2 * side
    steps = x_ref.shape[0] // size
    need(x_ref, w_ref)
    matmul(x_ref, w_ref, red)
    need(gain_ref, shift_ref)
    gain, shift = (gain_ref[pl.ds(0, 1), :], shift_ref[pl.ds(0, 1), :])

    @pl.loop(0, steps)
    def _(at):
        rows = rows_of(at, size)
        normed, factor = norm(red[rows, :])
        normed_ref[rows, :] = normed
        factor_ref[rows, :] = wide(factor)
        first_ref[rows, :] = silu(normed * gain + shift).astype(LOW)

    each = steps // count
    for image in range(count):
        head = first_ref[pl.ds(image * each * size, size), :].astype(FULL)
        tail = first_ref[pl.ds((image * each + each - 1) * size, size), :].astype(FULL)
        set_edges(at_ref, edge_a_ref, edge_b_ref, image, head[:side], tail[side:])


def pre_rest_kernel(
    need,
    send,
    at_ref,
    x_ref,
    first_ref,
    got_a_ref,
    got_b_ref,
    conv_ref,
    expand_ref,
    gain_ref,
    shift_ref,
    out_gain_ref,
    out_shift_ref,
    reduce_ref,
    post_gain_ref,
    post_shift_ref,
    second_ref,
    normed_b_ref,
    factor_b_ref,
    normed_c_ref,
    factor_c_ref,
    summed_ref,
    pooled_ref,
    post_first_ref,
    edge_a_ref,
    edge_b_ref,
    post_normed_ref,
    post_factor_ref,
    pad,
    exp,
    pair,
    red,
):
    count, strip, side, width = pad.shape
    strip = strip - 2
    size = 2 * side
    each = strip // 2
    need(first_ref, got_a_ref, got_b_ref)
    fill_halo(at_ref, pad, first_ref, got_a_ref, got_b_ref)
    need(conv_ref, gain_ref, shift_ref)
    send(pad)
    taps = tap_rows(conv_ref)
    gain, shift = (gain_ref[pl.ds(1, 1), :], shift_ref[pl.ds(1, 1), :])

    @pl.loop(0, count * each)
    def _(at):
        rows = rows_of(at, size)
        image, row = (at // each, 2 * lax.rem(at, each))
        conv = jnp.concatenate(
            [conv_row(pad, taps, image, row), conv_row(pad, taps, image, row + 1)], axis=0
        )
        normed, factor = norm(conv)
        normed_b_ref[rows, :] = normed
        factor_b_ref[rows, :] = wide(factor)
        second_ref[rows, :] = silu(normed * gain + shift).astype(LOW)

    send(second_ref, normed_b_ref, factor_b_ref)
    need(expand_ref)
    matmul(second_ref, expand_ref, exp)
    need(x_ref, out_gain_ref, out_shift_ref)
    out_gain, out_shift = (out_gain_ref[...], out_shift_ref[...])
    cols = side // 2
    for at in range(count * each):
        rows = pl.ds(at * size, size)
        normed, factor = norm(exp[rows, :])
        normed_c_ref[rows, :] = normed
        factor_c_ref[rows, :] = wide(factor)
        summed = x_ref[rows, :].astype(FULL) + normed * out_gain + out_shift
        summed_ref[rows, :] = summed
        block = silu(summed)
        half = narrow(pair, block[:side] + block[side:])
        pooled_ref[pl.ds(at * SLAB, cols), :] = 0.25 * half
        pooled_ref[pl.ds(at * SLAB + cols, SLAB - cols), :] = jnp.zeros(
            (SLAB - cols, width), FULL
        )
    send(normed_c_ref, factor_c_ref, summed_ref)
    need(reduce_ref, post_gain_ref, post_shift_ref)
    matmul(pooled_ref, reduce_ref, red)
    normed, factor = norm(red[...])
    post_normed_ref[...] = normed
    post_factor_ref[...] = wide(factor)
    first = silu(normed * post_gain_ref[pl.ds(0, 1), :] + post_shift_ref[pl.ds(0, 1), :])
    post_first_ref[...] = jnp.where(live(red.shape[0], cols), first, 0.0).astype(LOW)
    for image in range(count):
        head = post_first_ref[pl.ds(image * each * SLAB, SLAB), :].astype(FULL)
        tail = post_first_ref[pl.ds((image * each + each - 1) * SLAB, SLAB), :].astype(FULL)
        set_edges(at_ref, edge_a_ref, edge_b_ref, image, head, tail)


def post_rest_kernel(
    need,
    send,
    at_ref,
    pooled_ref,
    first_ref,
    got_a_ref,
    got_b_ref,
    conv_ref,
    expand_ref,
    gain_ref,
    shift_ref,
    out_gain_ref,
    out_shift_ref,
    block_ref,
    left_in_ref,
    left_second_ref,
    normed_b_ref,
    factor_b_ref,
    normed_c_ref,
    factor_c_ref,
    summed_ref,
    pad,
    second,
    exp,
    compact,
    *,
    cols
):
    count, rows, _, width = pad.shape
    rows = rows - 2
    small = block_ref.shape[0]
    need(first_ref, got_a_ref, got_b_ref)
    fill_halo(at_ref, pad, first_ref, got_a_ref, got_b_ref)
    send(pad)
    need(conv_ref, gain_ref, shift_ref, pooled_ref)
    taps = tap_rows(conv_ref)
    gain, shift = (gain_ref[pl.ds(1, 1), :], shift_ref[pl.ds(1, 1), :])

    @pl.loop(0, count * rows)
    def _(at):
        place = rows_of(at, SLAB)
        normed, factor = norm(conv_row(pad, taps, at // rows, lax.rem(at, rows)))
        normed_b_ref[place, :] = normed
        factor_b_ref[place, :] = wide(factor)
        second[place, :] = silu(normed * gain + shift)

    send(normed_b_ref, factor_b_ref)
    need(expand_ref)
    matmul(second, expand_ref, exp)
    need(out_gain_ref, out_shift_ref)
    normed, factor = norm(exp[...])
    normed_c_ref[...] = normed
    factor_c_ref[...] = wide(factor)
    summed = pooled_ref[...] + normed * out_gain_ref[...] + out_shift_ref[...]
    summed_ref[...] = summed
    exp[...] = silu(summed)
    compact[...] = jnp.zeros(compact.shape, FULL)
    for at in range(count * rows):
        compact[pl.ds(at * cols, cols), :] = exp[pl.ds(at * SLAB, cols), :]
    block_ref[...] = compact[pl.ds(0, small), :].astype(LOW)
    send(block_ref, normed_c_ref, factor_c_ref, summed_ref)
    pack(compact, pooled_ref, left_in_ref, cols)
    pack(compact, second, left_second_ref, cols)


def readout_kernel(
    need,
    send,
    at_ref,
    whole_ref,
    w_ref,
    bias_ref,
    cot_ref,
    out_ref,
    grad_ref,
    *refs,
    strips
):
    slots, (bias_grad_ref, cot, out, terms_ref) = (refs[:strips], refs[strips:])
    images, lines, cols, _ = cot_ref.shape
    rows = lines // strips
    need(cot_ref)
    for at in range(images * lines):
        strip, image, row = (at // (images * rows), at // rows % images, at % rows)
        cot[pl.ds(at * cols, cols), :] = cot_ref[image, strip * rows + row].astype(FULL)
    need(whole_ref, w_ref, bias_ref)

    @pl.loop(0, w_ref.shape[1] // TILE)
    def _(at):
        lanes = pl.ds(pl.multiple_of(at * TILE, TILE), TILE)
        act = jnp.dot(whole_ref[...], w_ref[:, lanes], preferred_element_type=FULL)
        act = act + bias_ref[:, lanes]
        cdf = 0.5 * (1.0 + lax.erf(act * SQRT_HALF))
        density = jnp.exp(-0.5 * act * act) * INV_SQRT_TWO_PI
        out[:, lanes] = act * cdf
        grad = (cot[:, lanes] * (cdf + act * density)).astype(LOW)
        grad_ref[:, lanes] = grad
        bias_grad_ref[:, lanes] = jnp.sum(grad.astype(FULL), axis=0, keepdims=True)

    send(grad_ref, bias_grad_ref)
    matmul_back(grad_ref, w_ref, terms_ref)
    small = slots[0].shape[0]
    for step in range(strips):
        begin = pl.multiple_of(flip(at_ref[2], step) * small, 8)
        slots[step][...] = terms_ref[pl.ds(begin, small), :].astype(LOW)
    for at in range(images * lines):
        strip, image, row = (at // (images * rows), at // rows % images, at % rows)
        out_ref[image, strip * rows + row] = out[pl.ds(at * cols, cols), :].astype(LOW)


def post_back_kernel(
    need,
    send,
    at_ref,
    *refs,
    cols,
    strips
):
    pieces, refs = (refs[:strips], refs[strips:])
    (
    expand_ref,
    gain_ref,
    shift_ref,
    out_gain_ref,
    normed_b_ref,
    factor_b_ref,
    normed_c_ref,
    factor_c_ref,
    summed_ref,
    grad_sum_ref,
    grad_exp_ref,
    grad_conv_ref,
    edge_a_ref,
    edge_b_ref,
    small_ref,
    compact,
    spread_out,
    exp,
    sec,
    ) = refs
    count = edge_a_ref.shape[0]
    tokens, width = grad_sum_ref.shape
    each = tokens // SLAB // count
    need(*pieces)
    total = pieces[0][...].astype(FULL)
    for piece in pieces[1:]:
        total = total + piece[...].astype(FULL)
    compact[...] = jnp.zeros(compact.shape, FULL)
    compact[pl.ds(0, total.shape[0]), :] = total
    spread_out[...] = jnp.zeros((tokens, width), FULL)
    for at in range(tokens // SLAB):
        spread_out[pl.ds(at * SLAB, cols), :] = compact[pl.ds(at * cols, cols), :]
    need(summed_ref, normed_c_ref, factor_c_ref, out_gain_ref)
    grad_sum = silu_back(spread_out[...], summed_ref[...])
    grad_sum_ref[...] = grad_sum
    normed = normed_c_ref[...]
    exp[...] = norm_back(grad_sum, normed, factor_c_ref[:, :1], out_gain_ref[...])
    small_ref[pl.ds(2, 1), :] = jnp.sum(grad_sum * normed, axis=0, keepdims=True)
    small_ref[pl.ds(3, 1), :] = jnp.sum(grad_sum, axis=0, keepdims=True)
    pack(compact, exp, grad_exp_ref, cols)
    send(grad_sum_ref, grad_exp_ref)
    need(expand_ref)
    matmul_back(exp, expand_ref, sec)
    need(gain_ref, shift_ref, normed_b_ref, factor_b_ref)
    gain, shift = (gain_ref[pl.ds(1, 1), :], shift_ref[pl.ds(1, 1), :])
    normed = normed_b_ref[...]
    grad = silu_back(sec[...], normed * gain + shift)
    grad_conv_ref[...] = norm_back(grad, normed, factor_b_ref[:, :1], gain).astype(LOW)
    small_ref[pl.ds(0, 1), :] = jnp.sum(grad * normed, axis=0, keepdims=True)
    small_ref[pl.ds(1, 1), :] = jnp.sum(grad, axis=0, keepdims=True)
    for image in range(count):
        head = grad_conv_ref[pl.ds(image * each * SLAB, SLAB), :].astype(FULL)
        tail = grad_conv_ref[pl.ds((image * each + each - 1) * SLAB, SLAB), :].astype(FULL)
        set_edges(at_ref, edge_a_ref, edge_b_ref, image, head, tail)


def middle_back_kernel(
    need,
    send,
    at_ref,
    grad_conv_ref,
    got_a_ref,
    got_b_ref,
    pad,
    post_conv_ref,
    post_reduce_ref,
    post_gain_ref,
    post_shift_ref,
    post_normed_ref,
    post_factor_ref,
    post_grad_sum_ref,
    expand_ref,
    gain_ref,
    shift_ref,
    out_gain_ref,
    normed_b_ref,
    factor_b_ref,
    normed_c_ref,
    factor_c_ref,
    summed_ref,
    post_grad_red_ref,
    grad_sum_ref,
    grad_exp_ref,
    pre_grad_conv_ref,
    edge_a_ref,
    edge_b_ref,
    post_small_ref,
    small_ref,
    grad_pad,
    taps_sum,
    grad_in,
    pair,
    sec,
    sums,
    post_red,
    compact,
    *,
    cols
):
    count, side, width = edge_a_ref.shape
    need(grad_conv_ref, got_a_ref, got_b_ref)
    fill_halo(at_ref, grad_pad, grad_conv_ref, got_a_ref, got_b_ref)
    need(pad, post_conv_ref)
    need(post_gain_ref, post_shift_ref, post_normed_ref, post_factor_ref)
    taps = tap_rows(post_conv_ref)
    taps_sum[...] = jnp.zeros_like(taps_sum)
    sums[...] = jnp.zeros_like(sums)
    gain, shift = (post_gain_ref[pl.ds(0, 1), :], post_shift_ref[pl.ds(0, 1), :])
    each = post_grad_sum_ref.shape[0] // SLAB // count

    @pl.loop(0, count * each)
    def _(at):
        place = rows_of(at, SLAB)
        grad = conv_back_row(pad, grad_pad, taps, taps_sum, at // each, lax.rem(at, each))
        normed = post_normed_ref[place, :]
        grad = jnp.where(live(SLAB, cols), silu_back(grad, normed * gain + shift), 0.0)
        sums[0] += fold(grad * normed)
        sums[1] += fold(grad)
        post_red[place, :] = norm_back(grad, normed, post_factor_ref[place, :1], gain)

    for at in range(9):
        finish(post_small_ref, taps_sum, at, at)
    finish(post_small_ref, sums, 0, 9)
    finish(post_small_ref, sums, 1, 10)
    pack(compact, post_red, post_grad_red_ref, cols)
    send(post_grad_red_ref, post_small_ref)
    need(post_reduce_ref)
    matmul_back(post_red, post_reduce_ref, grad_in)
    sums[...] = jnp.zeros_like(sums)
    size = 2 * side
    need(out_gain_ref, post_grad_sum_ref, summed_ref, normed_c_ref, factor_c_ref)
    out_gain = out_gain_ref[...]
    for at in range(count * each):
        rows = pl.ds(at * size, size)
        place = pl.ds(at * SLAB, cols)
        grad = 0.25 * (post_grad_sum_ref[place, :] + grad_in[place, :])
        grad = widen(pair, grad)
        grad = jnp.concatenate([grad, grad], axis=0)
        grad_sum = silu_back(grad, summed_ref[rows, :])
        grad_sum_ref[rows, :] = grad_sum
        normed = normed_c_ref[rows, :]
        sums[0] += fold(grad_sum * normed)
        sums[1] += fold(grad_sum)
        grad_exp_ref[rows, :] = norm_back(
            grad_sum, normed, factor_c_ref[rows, :1], out_gain
        ).astype(LOW)
    finish(small_ref, sums, 0, 2)
    finish(small_ref, sums, 1, 3)
    send(grad_sum_ref, grad_exp_ref)
    need(expand_ref)
    matmul_back(grad_exp_ref, expand_ref, sec)
    need(gain_ref, shift_ref, normed_b_ref, factor_b_ref)
    sums[...] = jnp.zeros_like(sums)
    gain_b, shift_b = (gain_ref[pl.ds(1, 1), :], shift_ref[pl.ds(1, 1), :])

    @pl.loop(0, count * each)
    def _(at):
        rows = rows_of(at, size)
        normed = normed_b_ref[rows, :]
        grad = silu_back(sec[rows, :], normed * gain_b + shift_b)
        sums[0] += fold(grad * normed)
        sums[1] += fold(grad)
        pre_grad_conv_ref[rows, :] = norm_back(
            grad, normed, factor_b_ref[rows, :1], gain_b
        ).astype(LOW)

    finish(small_ref, sums, 0, 0)
    finish(small_ref, sums, 1, 1)
    for image in range(count):
        head = pre_grad_conv_ref[pl.ds(image * each * size, size), :].astype(FULL)
        tail = pre_grad_conv_ref[pl.ds((image * each + each - 1) * size, size), :].astype(FULL)
        set_edges(at_ref, edge_a_ref, edge_b_ref, image, head[:side], tail[side:])


def pre_back_kernel(
    need,
    send,
    at_ref,
    grad_conv_ref,
    got_a_ref,
    got_b_ref,
    pad,
    conv_ref,
    gain_ref,
    shift_ref,
    normed_ref,
    factor_ref,
    small_b_ref,
    post_small_a_ref,
    post_small_b_ref,
    read_bias_ref,
    grad_red_ref,
    small_ref,
    grad_pad,
    taps_sum,
    sums,
):
    count, strip, side, width = pad.shape
    strip = strip - 2
    size = 2 * side
    each = strip // 2
    need(grad_conv_ref, got_a_ref, got_b_ref)
    fill_halo(at_ref, grad_pad, grad_conv_ref, got_a_ref, got_b_ref)
    need(pad, conv_ref)
    need(gain_ref, shift_ref, normed_ref, factor_ref)
    taps = tap_rows(conv_ref)
    taps_sum[...] = jnp.zeros_like(taps_sum)
    sums[...] = jnp.zeros_like(sums)
    gain, shift = (gain_ref[pl.ds(0, 1), :], shift_ref[pl.ds(0, 1), :])

    @pl.loop(0, count * each)
    def _(at):
        rows = rows_of(at, size)
        image, row = (at // each, 2 * lax.rem(at, each))
        grad = jnp.concatenate(
            [
                conv_back_row(pad, grad_pad, taps, taps_sum, image, row),
                conv_back_row(pad, grad_pad, taps, taps_sum, image, row + 1),
            ],
            axis=0,
        )
        normed = normed_ref[rows, :]
        grad = silu_back(grad, normed * gain + shift)
        sums[0] += fold(grad * normed)
        sums[1] += fold(grad)
        grad_red_ref[rows, :] = norm_back(grad, normed, factor_ref[rows, :1], gain).astype(LOW)

    for at in range(9):
        finish(small_ref, taps_sum, at, at)
    finish(small_ref, sums, 0, 9)
    finish(small_ref, sums, 1, 10)
    need(small_b_ref, post_small_a_ref, post_small_b_ref, read_bias_ref)
    small_ref[pl.ds(11, 4), :] = small_b_ref[...]
    small_ref[pl.ds(15, 11), :] = post_small_a_ref[...]
    small_ref[pl.ds(26, 4), :] = post_small_b_ref[...]
    small_ref[pl.ds(30, 1), :] = read_bias_ref[...]
    small_ref[pl.ds(31, 1), :] = jnp.zeros_like(read_bias_ref)


def pair_outer_kernel(need, send, at_ref, *refs, pairs, parts):
    takes = 4 * pairs
    outs = refs[takes:]
    half, plane = (at_ref[0], at_ref[1])
    rows = outs[0].shape[0] // pairs
    for pair in range(pairs):
        left, left_far, right, right_far = refs[4 * pair : 4 * pair + 4]
        need(left, left_far, right, right_far)
        for step in range(parts):
            begin = half * (rows * parts) + flip(plane, step) * rows
            lanes = pl.ds(pl.multiple_of(begin, LANES), rows)
            total = lax.dot_general(
                left[:, lanes], right[...], (((0,), (0,)), ((), ())), preferred_element_type=FULL
            ) + lax.dot_general(
                left_far[:, lanes],
                right_far[...],
                (((0,), (0,)), ((), ())),
                preferred_element_type=FULL,
            )
            outs[step][pl.ds(pair * rows, rows), :] = total.astype(LOW)
    send(*outs)


def sum_split_kernel(need, send, at_ref, *refs, pairs, parts, pieces, along=2):
    takes, outs = (refs[:pieces], refs[pieces : pieces + parts])
    total = refs[-1]
    need(*takes)
    value = takes[0][...].astype(FULL)
    for at in range(1, pieces):
        value = value + takes[at][...].astype(FULL)
    total[...] = value
    rows = total.shape[0] // pairs // parts
    for step in range(parts):
        begin = flip(at_ref[along], step) * rows
        for pair in range(pairs):
            place = pl.ds(pl.multiple_of(pair * rows * parts + begin, SLAB), rows)
            outs[step][pl.ds(pair * rows, rows), :] = total[place, :].astype(LOW)
    send(*outs)


def assemble_kernel(*refs, pairs, planes, strips, cut):
    takes = 2 * (planes + cut)
    parts, outs = (refs[:takes], refs[takes : takes + pairs])
    full, sem = (refs[takes + pairs : takes + 2 * pairs], refs[-1])
    half, plane, row = places()
    rows = parts[0].shape[0] // pairs // strips
    block = strips * rows
    writes = []
    for pair in range(pairs):
        for at in range(2 * planes):
            side, spot = (flip(half, at // planes), flip(plane, at % planes))
            for step in range(strips):
                place = side * (planes * block) + spot * block
                if strips > 1:
                    place = place + flip(row, step) * rows
                source, begin = (at % planes, step)
                if cut and source == planes - 1 and 2 * step >= strips:
                    source, begin = (planes, step - strips // 2)
                part = parts[at // planes * (planes + cut) + source]
                full[pair][pl.ds(pl.multiple_of(place, SLAB), rows), :] = part[
                    pl.ds((begin * pairs + pair) * rows, rows), :
                ].astype(FULL)
        writes.append(pltpu.make_async_copy(full[pair], outs[pair], sem.at[pair]))
        writes[-1].start()
    for write in writes:
        write.wait()


def assemble(parts, pairs, planes, strips):
    takes = len(parts)
    out = like(2 * planes * parts[0].shape[0] // pairs, parts[0].shape[1])
    parts = [pltpu.with_memory_space_constraint(part, pltpu.VMEM) for part in parts]
    return pl.pallas_call(
        functools.partial(
            assemble_kernel, pairs=pairs, planes=planes, strips=strips, cut=takes // 2 - planes
        ),
        out_shape=[pltpu.HBM(out.shape, out.dtype)] * pairs,
        in_specs=[pl.BlockSpec(memory_space=pltpu.VMEM)] * takes,
        out_specs=[pl.BlockSpec(memory_space=pltpu.HBM)] * pairs,
        scratch_shapes=[pltpu.VMEM(out.shape, FULL)] * pairs + [pltpu.SemaphoreType.DMA((pairs,))],
        compiler_params=pltpu.CompilerParams(vmem_limit_bytes=VMEM_BYTES),
        cost_estimate=pl.CostEstimate(flops=0, bytes_accessed=0, transcendentals=0),
    )(*parts)


def small_kernel(need, send, at_ref, sums_ref, *outs):
    for place in range(2):
        conv, gain, shift, out_gain, out_shift = outs[5 * place : 5 * place + 5]
        rows = sums_ref[pl.ds(15 * place, 15), :]
        for top in range(3):
            conv[top] = rows[3 * top : 3 * top + 3]
        gain[pl.ds(0, 1), :] = rows[9:10]
        gain[pl.ds(1, 1), :] = rows[11:12]
        shift[pl.ds(0, 1), :] = rows[10:11]
        shift[pl.ds(1, 1), :] = rows[12:13]
        out_gain[...] = rows[13:14]
        out_shift[...] = rows[14:15]


class Near:
    def __init__(self, value):
        self.value = value


def like(*shape, dtype=FULL):
    return jax.ShapeDtypeStruct(shape, dtype)


def low(*shape):
    return like(*shape, dtype=LOW)


def places():
    return [lax.axis_index(axis) for axis in ("half", "im", "row")]


def call(kernel, outs, scratch, *args):
    near_in = [isinstance(arg, Near) for arg in args]
    near_out = [isinstance(out, Near) for out in outs]
    args = [arg.value if isinstance(arg, Near) else arg for arg in args]
    outs = [out.value if isinstance(out, Near) else out for out in outs]
    takes, gives = (len(args), len(outs))
    far_in = [at for at in range(takes) if not near_in[at]]
    far_out = [at for at in range(gives) if not near_out[at]]

    def body(*refs):
        given, refs = (list(refs[:takes]), refs[takes:])
        made, refs = (list(refs[:gives]), refs[gives:])
        rest = refs[len(far_in) + len(far_out) :]
        reads, writes = ({}, {})
        if far_in:
            in_sem = rest[-1]
            rest = rest[:-1]
        if far_out:
            out_sem = rest[-1]
            rest = rest[:-1]
        for place, at in enumerate(far_in):
            reads[at] = pltpu.make_async_copy(given[at], refs[place], in_sem.at[place])
            given[at] = refs[place]
        for place, at in enumerate(far_out):
            mirror = refs[len(far_in) + place]
            writes[at] = pltpu.make_async_copy(mirror, made[at], out_sem.at[place])
            made[at] = mirror
        for at in sorted(reads, key=lambda at: args[at].size):
            reads[at].start()
        started = []

        def need(*wanted):
            for at in list(reads):
                if any(given[at] is ref for ref in wanted):
                    reads.pop(at).wait()

        def send(*ready):
            for at in list(writes):
                if any(made[at] is ref for ref in ready):
                    started.append(writes.pop(at))
                    started[-1].start()

        kernel(need, send, places(), *given, *made, *rest)
        need(*given)
        send(*made)
        for write in started:
            write.wait()

    spaces = {True: pltpu.VMEM, False: pltpu.HBM}
    args = [
        pltpu.with_memory_space_constraint(arg, spaces[near]) for arg, near in zip(args, near_in)
    ]
    return pl.pallas_call(
        body,
        out_shape=[spaces[near](out.shape, out.dtype) for out, near in zip(outs, near_out)],
        in_specs=[pl.BlockSpec(memory_space=spaces[near]) for near in near_in],
        out_specs=[pl.BlockSpec(memory_space=spaces[near]) for near in near_out],
        scratch_shapes=[pltpu.VMEM(args[at].shape, args[at].dtype) for at in far_in]
        + [pltpu.VMEM(outs[at].shape, outs[at].dtype) for at in far_out]
        + [pltpu.VMEM(shape, FULL) for shape in scratch]
        + [pltpu.SemaphoreType.DMA((len(far_out),))] * bool(far_out)
        + [pltpu.SemaphoreType.DMA((len(far_in),))] * bool(far_in),
        compiler_params=pltpu.CompilerParams(vmem_limit_bytes=VMEM_BYTES),
        cost_estimate=pl.CostEstimate(flops=0, bytes_accessed=0, transcendentals=0),
    )(*args)


def edges(parity_edges):
    size = lax.axis_size("row")
    inner = [(at, at ^ 1) for at in range(size)]
    outer = [(at, at + 1) for at in range(1, size - 1, 2)]
    outer = outer + [(to, at) for at, to in outer]
    return (
        lax.ppermute(parity_edges[0], "row", inner),
        lax.ppermute(parity_edges[1], "row", outer),
    )


def swap(field):
    return lax.ppermute(field, "half", [(0, 1), (1, 0)])


def steps_of(value, axis, step):
    size = lax.axis_size(axis)
    return lax.ppermute(value, axis, [(at, at ^ step) for at in range(size)])


def share(parts, axis):
    return [parts[0]] + [steps_of(parts[at], axis, at) for at in range(1, len(parts))]


def share_same(part, axis):
    size = lax.axis_size(axis)
    return [part] + [steps_of(part, axis, at) for at in range(1, size)]


def gather_near(part):
    return [part, steps_of(part, "im", 1), steps_of(part, "im", 2)]


def gather_rest(parts):
    half = parts[0].shape[0] // 2
    return [steps_of(parts[1][:half], "im", 2), steps_of(parts[2][half:], "im", 1)]


def small_outputs(part, width):
    return [
        part[:9].reshape(3, 3, width),
        jnp.stack([part[9], part[11]]),
        jnp.stack([part[10], part[12]]),
        part[13],
        part[14],
    ]


def pair_outer(*pairs):
    size = lax.axis_size("im")
    first = pairs[0][0].value if isinstance(pairs[0][0], Near) else pairs[0][0]
    width = first.shape[1]
    rows = width // 2 // size * len(pairs)
    return list(
        call(
            functools.partial(pair_outer_kernel, pairs=len(pairs), parts=size),
            [Near(low(rows, width))] * size,
            [],
            *[ref for pair in pairs for ref in pair],
        )
    )


def sum_split(pieces, pairs):
    size = lax.axis_size("row")
    rows, width = pieces[0].shape
    return list(
        call(
            functools.partial(
                sum_split_kernel,
                pairs=pairs,
                parts=size,
                pieces=len(pieces),
            ),
            [Near(low(rows // size, width))] * size,
            [(rows, width)],
            *[Near(piece) for piece in pieces],
        )
    )


def add_low(pieces):
    total = pieces[0].astype(FULL)
    for piece in pieces[1:]:
        total = total + piece.astype(FULL)
    return total.astype(LOW)


def sum_far(left, right, axes):
    part = jnp.einsum("tm,tc->mc", left, right, preferred_element_type=FULL)
    return lax.psum(part, axes)


def shards(
    x_in,
    pre_reduce,
    pre_conv,
    pre_expand,
    pre_mid_gain,
    pre_mid_shift,
    pre_out_gain,
    pre_out_shift,
    post_reduce,
    post_conv,
    post_expand,
    post_mid_gain,
    post_mid_shift,
    post_out_gain,
    post_out_shift,
    read_weight,
    read_bias,
    cotangent,
):
    count, strip, side, width = x_in.shape
    strips = lax.axis_size("row")
    tokens = count * strip * side
    cols = side // 2
    rows = strip // 2
    slabs = count * rows
    padded = slabs * SLAB
    small = slabs * cols
    block = -(-small // SLAB) * SLAB
    features = read_weight.shape[1]
    x_low = x_in.reshape(tokens, width)
    pre_out_g, pre_out_s = (pre_out_gain[None], pre_out_shift[None])
    post_out_g, post_out_s = (post_out_gain[None], post_out_shift[None])
    pre_edge = Near(low(count, side, width))
    post_edge = Near(low(count, SLAB, width))
    quick = lax.axis_size("im") == 4 and strips == 4

    first, edge_a, edge_b, normed_a, factor_a = call(
        pre_reduce_kernel,
        [Near(low(tokens, width)), pre_edge, pre_edge, like(tokens, width), like(tokens, LANES)],
        [(tokens, width)],
        x_low,
        pre_reduce,
        pre_mid_gain,
        pre_mid_shift,
    )
    got_a, got_b = edges((edge_a, edge_b))
    (
        second,
        normed_b,
        factor_b,
        normed_c,
        factor_c,
        summed,
        pooled,
        post_first,
        edge_a,
        edge_b,
        post_normed_a,
        post_factor_a,
        pad,
    ) = call(
        pre_rest_kernel,
        [
            low(tokens, width),
            like(tokens, width),
            like(tokens, LANES),
            like(tokens, width),
            like(tokens, LANES),
            like(tokens, width),
            Near(like(padded, width)),
            Near(low(padded, width)),
            post_edge,
            post_edge,
            like(padded, width),
            like(padded, LANES),
            like(count, strip + 2, side, width),
        ],
        [(tokens, width), (side * width // LANES, LANES), (padded, width)],
        x_low,
        Near(first),
        Near(got_a),
        Near(got_b),
        pre_conv,
        pre_expand,
        pre_mid_gain,
        pre_mid_shift,
        pre_out_g,
        pre_out_s,
        post_reduce,
        post_mid_gain,
        post_mid_shift,
    )
    got_a, got_b = edges((edge_a, edge_b))
    (
        block_two,
        left_in,
        left_second,
        post_normed_b,
        post_factor_b,
        post_normed_c,
        post_factor_c,
        post_summed,
        post_pad,
    ) = call(
        functools.partial(post_rest_kernel, cols=cols),
        [
            Near(low(small, width)),
            low(block, width),
            low(block, width),
            like(padded, width),
            like(padded, LANES),
            like(padded, width),
            like(padded, LANES),
            like(padded, width),
            like(count, rows + 2, SLAB, width),
        ],
        [(padded, width), (padded, width), (block, width)],
        Near(pooled),
        Near(post_first),
        Near(got_a),
        Near(got_b),
        post_conv,
        post_expand,
        post_mid_gain,
        post_mid_shift,
        post_out_g,
        post_out_s,
    )
    whole = lax.all_gather(block_two, "row", axis=0, tiled=True)
    readout, grad_pre, *terms, d_read_b = call(
        functools.partial(readout_kernel, strips=strips),
        [
            like(*cotangent.shape, dtype=LOW),
            Near(low(strips * small, features)),
        ]
        + [Near(low(small, width))] * strips
        + [like(1, features)],
        [
            (strips * small, features),
            (strips * small, features),
            (strips * small, width),
        ],
        Near(whole),
        read_weight,
        read_bias[None],
        cotangent,
    )
    terms = share(terms, "row")
    post_gs, post_ge, post_gc, edge_a, edge_b, post_small_b = call(
        functools.partial(post_back_kernel, cols=cols, strips=strips),
        [
            Near(like(padded, width)),
            Near(low(block, width)),
            Near(low(padded, width)),
            post_edge,
            post_edge,
            like(4, width),
        ],
        [(block, width), (padded, width), (padded, width), (padded, width)],
        *[Near(term) for term in terms],
        post_expand,
        post_mid_gain,
        post_mid_shift,
        post_out_g,
        post_normed_b,
        post_factor_b,
        post_normed_c,
        post_factor_c,
        post_summed,
    )
    if quick:
        edge_a, whole, grad_pre = tie(edge_a, whole, grad_pre)
    got_a, got_b = edges((edge_a, edge_b))
    if quick:
        read_slots = pair_outer(
            (Near(whole), Near(swap(whole)), Near(grad_pre), Near(swap(grad_pre)))
        )
        read_parts = [read_slots[0]] + [steps_of(read_slots[at], "im", at) for at in (1, 2)]
        (got_a, got_b), (*read_parts, read_last) = tie_later(
            (got_a, got_b), (*read_parts, read_slots[3])
        )
    (
        post_gr,
        pre_gs,
        pre_ge,
        pre_gc,
        edge_a,
        edge_b,
        post_small_a,
        pre_small_b,
    ) = call(
        functools.partial(middle_back_kernel, cols=cols),
        [
            Near(low(block, width)),
            like(tokens, width),
            Near(low(tokens, width)),
            Near(low(tokens, width)),
            pre_edge,
            pre_edge,
            like(11, width),
            like(4, width),
        ],
        [
            (count, rows + 2, SLAB, width),
            (9, 8, width),
            (padded, width),
            (side * width // LANES, LANES),
            (tokens, width),
            (2, 8, width),
            (padded, width),
            (block, width),
        ],
        Near(post_gc),
        Near(got_a),
        Near(got_b),
        post_pad,
        post_conv,
        post_reduce,
        post_mid_gain,
        post_mid_shift,
        post_normed_a,
        post_factor_a,
        Near(post_gs),
        pre_expand,
        pre_mid_gain,
        pre_mid_shift,
        pre_out_g,
        normed_b,
        factor_b,
        normed_c,
        factor_c,
        summed,
    )
    got_a, got_b = edges((edge_a, edge_b))
    if quick:
        pre_ge_far = swap(pre_ge)
        post_parts = pair_outer(
            (left_in, swap(left_in), Near(post_gr), Near(swap(post_gr))),
            (left_second, swap(left_second), Near(post_ge), Near(swap(post_ge))),
        )
        post_parts = pair_outer(
            (left_in, swap(left_in), Near(post_gr), Near(swap(post_gr))),
            (left_second, swap(left_second), Near(post_ge), Near(swap(post_ge))),
        )
        post_sums = [steps_of(post_parts[at], "im", at) for at in (1, 2)]
        (got_a, got_b), (*post_sums, read_last) = tie_later(
            (got_a, got_b), (*post_sums, steps_of(read_last, "im", 3))
        )
        read_parts = read_parts + [read_last]
    pre_gr, sums = call(
        pre_back_kernel,
        [Near(low(tokens, width)), Near(like(32, width))],
        [
            (count, strip + 2, side, width),
            (9, 8, width),
            (2, 8, width),
        ],
        Near(pre_gc),
        Near(got_a),
        Near(got_b),
        pad,
        pre_conv,
        pre_mid_gain,
        pre_mid_shift,
        normed_a,
        factor_a,
        pre_small_b,
        post_small_a,
        post_small_b,
        d_read_b,
    )
    if quick:
        post_sums = post_sums + [steps_of(post_parts[3], "im", 3)]
        far = swap(pre_gr)
        far, *post_sums = tie(far, *post_sums)
        post_parts = share(sum_split(post_parts[:1] + post_sums, 2), "row")
        parts = pair_outer(
            (second, swap(second), Near(pre_ge), Near(swap(pre_ge))),
            (x_low, swap(x_low), Near(pre_gr), Near(far)),
        )
        sums = sums + swap(sums)
        near_parts = [steps_of(parts[at], "im", at) for at in (1, 2)]
        grad_in = pre_gs + jnp.einsum("tm,cm->tc", pre_gr, pre_reduce, preferred_element_type=FULL)
        grad_in = grad_in.astype(LOW)
        post_parts, (grad_in, last, *rest) = tie_later(
            post_parts, (grad_in, parts[3], *near_parts, *read_parts)
        )
        near_parts, read_parts = (rest[:2], rest[2:])
        post_parts = share_same(add_low(post_parts), "row")
        last = steps_of(last, "im", 3)
        post_parts, (last, *read_parts) = tie_later(post_parts, (last, *read_parts))
        parts = share(sum_split([parts[0]] + near_parts + [last], 2), "row")
        post_parts = gather_near(jnp.concatenate(post_parts, axis=0))
        read_parts = gather_near(add_low(read_parts))
        parts, rest = tie_later(parts, (*post_parts, *read_parts))
        post_parts, read_parts = (rest[:3], rest[3:])
        parts = share_same(add_low(parts), "row")
        read_parts.append(steps_of(read_parts[0], "im", 3))
        post_parts = post_parts + gather_rest(post_parts)
        parts, rest = tie_later(parts, (*post_parts, *read_parts, sums))
        post_parts, read_parts, sums = (rest[:5], rest[5:9], rest[9])
        parts = gather_near(jnp.concatenate(parts, axis=0))
        alone = lax.broadcasted_iota(jnp.int32, sums.shape, 0) >= 30
        for step in (1, 2):
            sums = sums + jnp.where(alone, 0.0, steps_of(sums, "row", step))
        parts, (sums, *post_parts) = tie_later(parts, (sums, *post_parts))
        post_far = [swap(part) for part in post_parts]
        far = [swap(part) for part in parts]
        rest, (sums, *others) = tie_later(gather_rest(parts), (sums, *post_far, *far))
        post_far, far = (others[:5], others[5:])
        for step in (1, 2):
            sums = sums + steps_of(sums, "im", step)
        parts = parts + rest
        far = far + [swap(part) for part in rest]
        post_reduce_g, post_expand_g = assemble(post_parts + post_far, 2, 4, strips)
        (read_total,) = assemble(read_parts + [swap(part) for part in read_parts], 1, 4, 1)
        (post_reduce_g, read_total), (sums, *far) = tie_later(
            (post_reduce_g, read_total), (sums, *far)
        )
        small_out = call(
            small_kernel,
            [like(3, 3, width), like(2, width), like(2, width), like(1, width), like(1, width)] * 2,
            [],
            Near(sums),
        )
        pre_expand_g, pre_reduce_g = assemble(parts + far, 2, 4, strips)
        read_bias_g = sums[30]
    else:
        axes = IMG + ("row",)
        post_reduce_g = sum_far(left_in, post_gr, axes)
        post_expand_g = sum_far(left_second, post_ge, axes)
        pre_expand_g = sum_far(second, pre_ge, axes)
        pre_reduce_g = sum_far(x_low, pre_gr, axes)
        read_total = sum_far(whole, grad_pre, IMG)
        read_bias_g = lax.psum(sums[30], IMG)
        sums = lax.psum(sums[:30], axes)
        small_out = small_outputs(sums[:15], width) + small_outputs(sums[15:30], width)
        grad_in = pre_gs + jnp.einsum("tm,cm->tc", pre_gr, pre_reduce, preferred_element_type=FULL)
        grad_in = grad_in.astype(LOW)

    pre_conv_g, pre_gain_g, pre_shift_g, pre_og_g, pre_os_g = small_out[:5]
    post_conv_g, post_gain_g, post_shift_g, post_og_g, post_os_g = small_out[5:]
    return (
        readout,
        grad_in.reshape(x_in.shape),
        pre_reduce_g,
        pre_conv_g,
        pre_expand_g,
        pre_gain_g,
        pre_shift_g,
        pre_og_g.reshape(width),
        pre_os_g.reshape(width),
        post_reduce_g,
        post_conv_g,
        post_expand_g,
        post_gain_g,
        post_shift_g,
        post_og_g.reshape(width),
        post_os_g.reshape(width),
        read_total,
        read_bias_g,
    )


def solution(mesh):
    images, strips = mesh.devices.shape
    split = jax.sharding.Mesh(
        mesh.devices.reshape(images // 2, 2, strips), ("im", "half", "row")
    )
    return jax.shard_map(
        shards,
        mesh=split,
        in_specs=(P(IMG, "row", None, None),)
        + (P(),) * 14
        + (P(None, "row"), P("row"), P(IMG, None, None, "row")),
        out_specs=(P(IMG, None, None, "row"), P(IMG, "row", None, None))
        + (P(),) * 14
        + (P(None, "row"), P("row")),
        check_vma=False,
    )
```

```python
import functools

import jax
import jax.numpy as jnp
from jax import lax
from jax.experimental import pallas as pl
from jax.experimental.pallas import tpu as pltpu
from jax.sharding import PartitionSpec as P

EPSILON = 1e-06
SQRT_HALF = 0.7071067811865476
INV_SQRT_TWO_PI = 0.3989422804014327
LOW = jnp.bfloat16
FULL = jnp.float32
IMG = ("im", "half")
TILE = 256
SLAB = 16
LANES = 128
VMEM_BYTES = 24 * 1024 * 1024


def tie(*values):
    return lax.optimization_barrier(values)


def tie_later(first, second):
    first = list(tie(*first))
    out = list(tie(*first, *second))
    return (out[: len(first)], out[len(first) :])


def norm(value):
    centred = value - jnp.mean(value, axis=-1, keepdims=True)
    factor = lax.rsqrt(jnp.mean(centred * centred, axis=-1, keepdims=True) + EPSILON)
    return (centred * factor, factor)


def norm_back(grad, normed, factor, gain):
    scaled = grad * gain
    return factor * (
        scaled
        - jnp.mean(scaled, axis=-1, keepdims=True)
        - normed * jnp.mean(scaled * normed, axis=-1, keepdims=True)
    )


def gate(value):
    return 0.5 * jnp.tanh(0.5 * value) + 0.5


def silu(value):
    return value * gate(value)


def silu_back(grad, value):
    sigma = gate(value)
    return grad * sigma * (1.0 + value * (1.0 - sigma))


def flip(place, step):
    bit = 1
    while bit <= step:
        if step & bit:
            place = place + bit - 2 * bit * ((place // bit) % 2)
        bit *= 2
    return place


def wide(factor):
    return jnp.broadcast_to(factor, (factor.shape[0], LANES))


def fold(value):
    return jnp.sum(value.reshape(-1, 8, value.shape[-1]), axis=0)


def live(rows, cols):
    at = lax.broadcasted_iota(jnp.int32, (rows, 1), 0)
    return lax.rem(at, SLAB) < cols


def from_left(value):
    at = lax.broadcasted_iota(jnp.int32, (value.shape[0], 1), 0)
    return jnp.where(at == 0, 0.0, pltpu.roll(value, 1, 0))


def from_right(value):
    last = value.shape[0] - 1
    at = lax.broadcasted_iota(jnp.int32, (value.shape[0], 1), 0)
    return jnp.where(at == last, 0.0, pltpu.roll(value, last, 0))


def matmul(left_ref, right_ref, out_ref):
    @pl.loop(0, right_ref.shape[1] // TILE)
    def _(at):
        cols = pl.ds(pl.multiple_of(at * TILE, TILE), TILE)
        out_ref[:, cols] = jnp.dot(
            left_ref[...].astype(LOW), right_ref[:, cols], preferred_element_type=FULL
        )


def matmul_back(left_ref, right_ref, out_ref):
    @pl.loop(0, right_ref.shape[0] // TILE)
    def _(at):
        cols = pl.ds(pl.multiple_of(at * TILE, TILE), TILE)
        out_ref[:, cols] = lax.dot_general(
            left_ref[...].astype(LOW),
            right_ref[cols, :],
            (((1,), (1,)), ((), ())),
            preferred_element_type=FULL,
        ).astype(out_ref.dtype)


def rows_of(at, size):
    return pl.ds(pl.multiple_of(at * size, SLAB), size)


def fill_halo(at_ref, pad_ref, low_ref, got_a_ref, got_b_ref):
    count, rows, cols, width = pad_ref.shape
    rows = rows - 2
    even = lax.rem(at_ref[2], 2) == 0
    for image in range(count):
        got_a, got_b = (got_a_ref[image].astype(FULL), got_b_ref[image].astype(FULL))
        pad_ref[image, 0] = jnp.where(even, got_b, got_a)
        pad_ref[image, rows + 1] = jnp.where(even, got_a, got_b)

    size = cols if cols % SLAB == 0 else 2 * cols
    per = size // cols
    each = rows // per

    @pl.loop(0, count * each)
    def _(at):
        part = low_ref[rows_of(at, size), :].astype(FULL).reshape(per, cols, width)
        pad_ref[at // each, pl.ds(1 + per * lax.rem(at, each), per)] = part


def set_edges(at_ref, edge_a_ref, edge_b_ref, image, head, tail):
    even = lax.rem(at_ref[2], 2) == 0
    edge_a_ref[image] = jnp.where(even, tail, head).astype(LOW)
    edge_b_ref[image] = jnp.where(even, head, tail).astype(LOW)


def conv_row(pad_ref, taps, image, row):
    lines = [pad_ref[image, row + top] for top in range(3)]
    sums = [
        lines[0] * taps[left] + lines[1] * taps[3 + left] + lines[2] * taps[6 + left]
        for left in range(3)
    ]
    return from_left(sums[0]) + sums[1] + from_right(sums[2])


def conv_back_row(pad_ref, grad_ref, taps, taps_ref, image, row):
    lines = [grad_ref[image, row + top] for top in range(3)]
    sums = [
        lines[2] * taps[left] + lines[1] * taps[3 + left] + lines[0] * taps[6 + left]
        for left in range(3)
    ]
    shifted = [from_right(lines[1]), lines[1], from_left(lines[1])]
    for top in range(3):
        source = pad_ref[image, row + top]
        for left in range(3):
            taps_ref[3 * top + left] += fold(source * shifted[left])
    return from_right(sums[0]) + sums[1] + from_left(sums[2])


def pack(compact, source, out_ref, cols):
    compact[...] = jnp.zeros(compact.shape, FULL)
    for at in range(source.shape[0] // SLAB):
        compact[pl.ds(at * cols, cols), :] = source[pl.ds(at * SLAB, cols), :]
    out_ref[...] = compact[...].astype(LOW)


def narrow(pair, value):
    side = value.shape[0]
    parts = []
    for at in range(value.shape[1] // LANES):
        pair[pl.ds(at * side, side), :] = value[:, at * LANES : (at + 1) * LANES]
        parts.append(
            pair[pl.ds(at * side, side // 2, stride=2), :]
            + pair[pl.ds(at * side + 1, side // 2, stride=2), :]
        )
    return jnp.concatenate(parts, axis=1)


def widen(pair, value):
    cols = value.shape[0]
    parts = []
    for at in range(value.shape[1] // LANES):
        part = value[:, at * LANES : (at + 1) * LANES]
        pair[pl.ds(2 * cols * at, cols, stride=2), :] = part
        pair[pl.ds(2 * cols * at + 1, cols, stride=2), :] = part
        parts.append(pair[pl.ds(2 * cols * at, 2 * cols), :])
    return jnp.concatenate(parts, axis=1)


def tap_rows(conv_ref):
    lines = [conv_ref[top].astype(FULL) for top in range(3)]
    return [lines[at // 3][at % 3 : at % 3 + 1] for at in range(9)]


def finish(small_ref, sums_ref, at, place):
    small_ref[pl.ds(place, 1), :] = jnp.sum(sums_ref[at], axis=0, keepdims=True)


def pre_reduce_kernel(
    need,
    send,
    at_ref,
    x_ref, w_ref, gain_ref, shift_ref, first_ref, edge_a_ref, edge_b_ref, normed_ref, factor_ref, red
):
    count, side, width = edge_a_ref.shape
    size = 2 * side
    steps = x_ref.shape[0] // size
    need(x_ref, w_ref)
    matmul(x_ref, w_ref, red)
    need(gain_ref, shift_ref)
    gain, shift = (gain_ref[pl.ds(0, 1), :], shift_ref[pl.ds(0, 1), :])

    @pl.loop(0, steps)
    def _(at):
        rows = rows_of(at, size)
        normed, factor = norm(red[rows, :])
        normed_ref[rows, :] = normed
        factor_ref[rows, :] = wide(factor)
        first_ref[rows, :] = silu(normed * gain + shift).astype(LOW)

    each = steps // count
    for image in range(count):
        head = first_ref[pl.ds(image * each * size, size), :].astype(FULL)
        tail = first_ref[pl.ds((image * each + each - 1) * size, size), :].astype(FULL)
        set_edges(at_ref, edge_a_ref, edge_b_ref, image, head[:side], tail[side:])


def pre_rest_kernel(
    need,
    send,
    at_ref,
    x_ref,
    first_ref,
    got_a_ref,
    got_b_ref,
    conv_ref,
    expand_ref,
    gain_ref,
    shift_ref,
    out_gain_ref,
    out_shift_ref,
    reduce_ref,
    post_gain_ref,
    post_shift_ref,
    second_ref,
    normed_b_ref,
    factor_b_ref,
    normed_c_ref,
    factor_c_ref,
    summed_ref,
    pooled_ref,
    post_first_ref,
    edge_a_ref,
    edge_b_ref,
    post_normed_ref,
    post_factor_ref,
    pad,
    exp,
    pair,
    red,
):
    count, strip, side, width = pad.shape
    strip = strip - 2
    size = 2 * side
    each = strip // 2
    need(first_ref, got_a_ref, got_b_ref)
    fill_halo(at_ref, pad, first_ref, got_a_ref, got_b_ref)
    need(conv_ref, gain_ref, shift_ref)
    send(pad)
    taps = tap_rows(conv_ref)
    gain, shift = (gain_ref[pl.ds(1, 1), :], shift_ref[pl.ds(1, 1), :])

    @pl.loop(0, count * each)
    def _(at):
        rows = rows_of(at, size)
        image, row = (at // each, 2 * lax.rem(at, each))
        conv = jnp.concatenate(
            [conv_row(pad, taps, image, row), conv_row(pad, taps, image, row + 1)], axis=0
        )
        normed, factor = norm(conv)
        normed_b_ref[rows, :] = normed
        factor_b_ref[rows, :] = wide(factor)
        second_ref[rows, :] = silu(normed * gain + shift).astype(LOW)

    send(second_ref, normed_b_ref, factor_b_ref)
    need(expand_ref)
    matmul(second_ref, expand_ref, exp)
    need(x_ref, out_gain_ref, out_shift_ref)
    out_gain, out_shift = (out_gain_ref[...], out_shift_ref[...])
    cols = side // 2
    for at in range(count * each):
        rows = pl.ds(at * size, size)
        normed, factor = norm(exp[rows, :])
        normed_c_ref[rows, :] = normed
        factor_c_ref[rows, :] = wide(factor)
        summed = x_ref[rows, :].astype(FULL) + normed * out_gain + out_shift
        summed_ref[rows, :] = summed
        block = silu(summed)
        half = narrow(pair, block[:side] + block[side:])
        pooled_ref[pl.ds(at * SLAB, cols), :] = 0.25 * half
        pooled_ref[pl.ds(at * SLAB + cols, SLAB - cols), :] = jnp.zeros(
            (SLAB - cols, width), FULL
        )
    send(normed_c_ref, factor_c_ref, summed_ref)
    need(reduce_ref, post_gain_ref, post_shift_ref)
    matmul(pooled_ref, reduce_ref, red)
    normed, factor = norm(red[...])
    post_normed_ref[...] = normed
    post_factor_ref[...] = wide(factor)
    first = silu(normed * post_gain_ref[pl.ds(0, 1), :] + post_shift_ref[pl.ds(0, 1), :])
    post_first_ref[...] = jnp.where(live(red.shape[0], cols), first, 0.0).astype(LOW)
    for image in range(count):
        head = post_first_ref[pl.ds(image * each * SLAB, SLAB), :].astype(FULL)
        tail = post_first_ref[pl.ds((image * each + each - 1) * SLAB, SLAB), :].astype(FULL)
        set_edges(at_ref, edge_a_ref, edge_b_ref, image, head, tail)


def post_rest_kernel(
    need,
    send,
    at_ref,
    pooled_ref,
    first_ref,
    got_a_ref,
    got_b_ref,
    conv_ref,
    expand_ref,
    gain_ref,
    shift_ref,
    out_gain_ref,
    out_shift_ref,
    block_ref,
    left_in_ref,
    left_second_ref,
    normed_b_ref,
    factor_b_ref,
    normed_c_ref,
    factor_c_ref,
    summed_ref,
    pad,
    second,
    exp,
    compact,
    *,
    cols
):
    count, rows, _, width = pad.shape
    rows = rows - 2
    small = block_ref.shape[0]
    need(first_ref, got_a_ref, got_b_ref)
    fill_halo(at_ref, pad, first_ref, got_a_ref, got_b_ref)
    send(pad)
    need(conv_ref, gain_ref, shift_ref, pooled_ref)
    taps = tap_rows(conv_ref)
    gain, shift = (gain_ref[pl.ds(1, 1), :], shift_ref[pl.ds(1, 1), :])

    @pl.loop(0, count * rows)
    def _(at):
        place = rows_of(at, SLAB)
        normed, factor = norm(conv_row(pad, taps, at // rows, lax.rem(at, rows)))
        normed_b_ref[place, :] = normed
        factor_b_ref[place, :] = wide(factor)
        second[place, :] = silu(normed * gain + shift)

    send(normed_b_ref, factor_b_ref)
    need(expand_ref)
    matmul(second, expand_ref, exp)
    need(out_gain_ref, out_shift_ref)
    normed, factor = norm(exp[...])
    normed_c_ref[...] = normed
    factor_c_ref[...] = wide(factor)
    summed = pooled_ref[...] + normed * out_gain_ref[...] + out_shift_ref[...]
    summed_ref[...] = summed
    exp[...] = silu(summed)
    compact[...] = jnp.zeros(compact.shape, FULL)
    for at in range(count * rows):
        compact[pl.ds(at * cols, cols), :] = exp[pl.ds(at * SLAB, cols), :]
    block_ref[...] = compact[pl.ds(0, small), :].astype(LOW)
    send(block_ref, normed_c_ref, factor_c_ref, summed_ref)
    pack(compact, pooled_ref, left_in_ref, cols)
    pack(compact, second, left_second_ref, cols)


def readout_kernel(
    need,
    send,
    at_ref,
    whole_ref,
    w_ref,
    bias_ref,
    cot_ref,
    out_ref,
    grad_ref,
    *refs,
    strips
):
    slots, (bias_grad_ref, cot, out, terms_ref) = (refs[:strips], refs[strips:])
    images, lines, cols, _ = cot_ref.shape
    rows = lines // strips
    need(cot_ref)
    for at in range(images * lines):
        strip, image, row = (at // (images * rows), at // rows % images, at % rows)
        cot[pl.ds(at * cols, cols), :] = cot_ref[image, strip * rows + row].astype(FULL)
    need(whole_ref, w_ref, bias_ref)

    @pl.loop(0, w_ref.shape[1] // TILE)
    def _(at):
        lanes = pl.ds(pl.multiple_of(at * TILE, TILE), TILE)
        act = jnp.dot(whole_ref[...], w_ref[:, lanes], preferred_element_type=FULL)
        act = act + bias_ref[:, lanes]
        cdf = 0.5 * (1.0 + lax.erf(act * SQRT_HALF))
        density = jnp.exp(-0.5 * act * act) * INV_SQRT_TWO_PI
        out[:, lanes] = act * cdf
        grad = (cot[:, lanes] * (cdf + act * density)).astype(LOW)
        grad_ref[:, lanes] = grad
        bias_grad_ref[:, lanes] = jnp.sum(grad.astype(FULL), axis=0, keepdims=True)

    send(grad_ref, bias_grad_ref)
    matmul_back(grad_ref, w_ref, terms_ref)
    small = slots[0].shape[0]
    for step in range(strips):
        begin = pl.multiple_of(flip(at_ref[2], step) * small, 8)
        slots[step][...] = terms_ref[pl.ds(begin, small), :].astype(LOW)
    for at in range(images * lines):
        strip, image, row = (at // (images * rows), at // rows % images, at % rows)
        out_ref[image, strip * rows + row] = out[pl.ds(at * cols, cols), :].astype(LOW)


def post_back_kernel(
    need,
    send,
    at_ref,
    *refs,
    cols,
    strips
):
    pieces, refs = (refs[:strips], refs[strips:])
    (
    expand_ref,
    gain_ref,
    shift_ref,
    out_gain_ref,
    normed_b_ref,
    factor_b_ref,
    normed_c_ref,
    factor_c_ref,
    summed_ref,
    grad_sum_ref,
    grad_exp_ref,
    grad_conv_ref,
    edge_a_ref,
    edge_b_ref,
    small_ref,
    compact,
    spread_out,
    exp,
    sec,
    ) = refs
    count = edge_a_ref.shape[0]
    tokens, width = grad_sum_ref.shape
    each = tokens // SLAB // count
    need(*pieces)
    total = pieces[0][...].astype(FULL)
    for piece in pieces[1:]:
        total = total + piece[...].astype(FULL)
    compact[...] = jnp.zeros(compact.shape, FULL)
    compact[pl.ds(0, total.shape[0]), :] = total
    spread_out[...] = jnp.zeros((tokens, width), FULL)
    for at in range(tokens // SLAB):
        spread_out[pl.ds(at * SLAB, cols), :] = compact[pl.ds(at * cols, cols), :]
    need(summed_ref, normed_c_ref, factor_c_ref, out_gain_ref)
    grad_sum = silu_back(spread_out[...], summed_ref[...])
    grad_sum_ref[...] = grad_sum
    normed = normed_c_ref[...]
    exp[...] = norm_back(grad_sum, normed, factor_c_ref[:, :1], out_gain_ref[...])
    small_ref[pl.ds(2, 1), :] = jnp.sum(grad_sum * normed, axis=0, keepdims=True)
    small_ref[pl.ds(3, 1), :] = jnp.sum(grad_sum, axis=0, keepdims=True)
    pack(compact, exp, grad_exp_ref, cols)
    send(grad_sum_ref, grad_exp_ref)
    need(expand_ref)
    matmul_back(exp, expand_ref, sec)
    need(gain_ref, shift_ref, normed_b_ref, factor_b_ref)
    gain, shift = (gain_ref[pl.ds(1, 1), :], shift_ref[pl.ds(1, 1), :])
    normed = normed_b_ref[...]
    grad = silu_back(sec[...], normed * gain + shift)
    grad_conv_ref[...] = norm_back(grad, normed, factor_b_ref[:, :1], gain).astype(LOW)
    small_ref[pl.ds(0, 1), :] = jnp.sum(grad * normed, axis=0, keepdims=True)
    small_ref[pl.ds(1, 1), :] = jnp.sum(grad, axis=0, keepdims=True)
    for image in range(count):
        head = grad_conv_ref[pl.ds(image * each * SLAB, SLAB), :].astype(FULL)
        tail = grad_conv_ref[pl.ds((image * each + each - 1) * SLAB, SLAB), :].astype(FULL)
        set_edges(at_ref, edge_a_ref, edge_b_ref, image, head, tail)


def middle_back_kernel(
    need,
    send,
    at_ref,
    grad_conv_ref,
    got_a_ref,
    got_b_ref,
    pad,
    post_conv_ref,
    post_reduce_ref,
    post_gain_ref,
    post_shift_ref,
    post_normed_ref,
    post_factor_ref,
    post_grad_sum_ref,
    expand_ref,
    gain_ref,
    shift_ref,
    out_gain_ref,
    normed_b_ref,
    factor_b_ref,
    normed_c_ref,
    factor_c_ref,
    summed_ref,
    post_grad_red_ref,
    grad_sum_ref,
    grad_exp_ref,
    pre_grad_conv_ref,
    edge_a_ref,
    edge_b_ref,
    post_small_ref,
    small_ref,
    grad_pad,
    taps_sum,
    grad_in,
    pair,
    sec,
    sums,
    post_red,
    compact,
    *,
    cols
):
    count, side, width = edge_a_ref.shape
    need(grad_conv_ref, got_a_ref, got_b_ref)
    fill_halo(at_ref, grad_pad, grad_conv_ref, got_a_ref, got_b_ref)
    need(pad, post_conv_ref)
    need(post_gain_ref, post_shift_ref, post_normed_ref, post_factor_ref)
    taps = tap_rows(post_conv_ref)
    taps_sum[...] = jnp.zeros_like(taps_sum)
    sums[...] = jnp.zeros_like(sums)
    gain, shift = (post_gain_ref[pl.ds(0, 1), :], post_shift_ref[pl.ds(0, 1), :])
    each = post_grad_sum_ref.shape[0] // SLAB // count

    @pl.loop(0, count * each)
    def _(at):
        place = rows_of(at, SLAB)
        grad = conv_back_row(pad, grad_pad, taps, taps_sum, at // each, lax.rem(at, each))
        normed = post_normed_ref[place, :]
        grad = jnp.where(live(SLAB, cols), silu_back(grad, normed * gain + shift), 0.0)
        sums[0] += fold(grad * normed)
        sums[1] += fold(grad)
        post_red[place, :] = norm_back(grad, normed, post_factor_ref[place, :1], gain)

    for at in range(9):
        finish(post_small_ref, taps_sum, at, at)
    finish(post_small_ref, sums, 0, 9)
    finish(post_small_ref, sums, 1, 10)
    pack(compact, post_red, post_grad_red_ref, cols)
    send(post_grad_red_ref, post_small_ref)
    need(post_reduce_ref)
    matmul_back(post_red, post_reduce_ref, grad_in)
    sums[...] = jnp.zeros_like(sums)
    size = 2 * side
    need(out_gain_ref, post_grad_sum_ref, summed_ref, normed_c_ref, factor_c_ref)
    out_gain = out_gain_ref[...]
    for at in range(count * each):
        rows = pl.ds(at * size, size)
        place = pl.ds(at * SLAB, cols)
        grad = 0.25 * (post_grad_sum_ref[place, :] + grad_in[place, :])
        grad = widen(pair, grad)
        grad = jnp.concatenate([grad, grad], axis=0)
        grad_sum = silu_back(grad, summed_ref[rows, :])
        grad_sum_ref[rows, :] = grad_sum
        normed = normed_c_ref[rows, :]
        sums[0] += fold(grad_sum * normed)
        sums[1] += fold(grad_sum)
        grad_exp_ref[rows, :] = norm_back(
            grad_sum, normed, factor_c_ref[rows, :1], out_gain
        ).astype(LOW)
    finish(small_ref, sums, 0, 2)
    finish(small_ref, sums, 1, 3)
    send(grad_sum_ref, grad_exp_ref)
    need(expand_ref)
    matmul_back(grad_exp_ref, expand_ref, sec)
    need(gain_ref, shift_ref, normed_b_ref, factor_b_ref)
    sums[...] = jnp.zeros_like(sums)
    gain_b, shift_b = (gain_ref[pl.ds(1, 1), :], shift_ref[pl.ds(1, 1), :])

    @pl.loop(0, count * each)
    def _(at):
        rows = rows_of(at, size)
        normed = normed_b_ref[rows, :]
        grad = silu_back(sec[rows, :], normed * gain_b + shift_b)
        sums[0] += fold(grad * normed)
        sums[1] += fold(grad)
        pre_grad_conv_ref[rows, :] = norm_back(
            grad, normed, factor_b_ref[rows, :1], gain_b
        ).astype(LOW)

    finish(small_ref, sums, 0, 0)
    finish(small_ref, sums, 1, 1)
    for image in range(count):
        head = pre_grad_conv_ref[pl.ds(image * each * size, size), :].astype(FULL)
        tail = pre_grad_conv_ref[pl.ds((image * each + each - 1) * size, size), :].astype(FULL)
        set_edges(at_ref, edge_a_ref, edge_b_ref, image, head[:side], tail[side:])


def pre_back_kernel(
    need,
    send,
    at_ref,
    grad_conv_ref,
    got_a_ref,
    got_b_ref,
    pad,
    conv_ref,
    gain_ref,
    shift_ref,
    normed_ref,
    factor_ref,
    small_b_ref,
    post_small_a_ref,
    post_small_b_ref,
    read_bias_ref,
    grad_red_ref,
    small_ref,
    grad_pad,
    taps_sum,
    sums,
):
    count, strip, side, width = pad.shape
    strip = strip - 2
    size = 2 * side
    each = strip // 2
    need(grad_conv_ref, got_a_ref, got_b_ref)
    fill_halo(at_ref, grad_pad, grad_conv_ref, got_a_ref, got_b_ref)
    need(pad, conv_ref)
    need(gain_ref, shift_ref, normed_ref, factor_ref)
    taps = tap_rows(conv_ref)
    taps_sum[...] = jnp.zeros_like(taps_sum)
    sums[...] = jnp.zeros_like(sums)
    gain, shift = (gain_ref[pl.ds(0, 1), :], shift_ref[pl.ds(0, 1), :])

    @pl.loop(0, count * each)
    def _(at):
        rows = rows_of(at, size)
        image, row = (at // each, 2 * lax.rem(at, each))
        grad = jnp.concatenate(
            [
                conv_back_row(pad, grad_pad, taps, taps_sum, image, row),
                conv_back_row(pad, grad_pad, taps, taps_sum, image, row + 1),
            ],
            axis=0,
        )
        normed = normed_ref[rows, :]
        grad = silu_back(grad, normed * gain + shift)
        sums[0] += fold(grad * normed)
        sums[1] += fold(grad)
        grad_red_ref[rows, :] = norm_back(grad, normed, factor_ref[rows, :1], gain).astype(LOW)

    for at in range(9):
        finish(small_ref, taps_sum, at, at)
    finish(small_ref, sums, 0, 9)
    finish(small_ref, sums, 1, 10)
    need(small_b_ref, post_small_a_ref, post_small_b_ref, read_bias_ref)
    small_ref[pl.ds(11, 4), :] = small_b_ref[...]
    small_ref[pl.ds(15, 11), :] = post_small_a_ref[...]
    small_ref[pl.ds(26, 4), :] = post_small_b_ref[...]
    small_ref[pl.ds(30, 1), :] = read_bias_ref[...]
    small_ref[pl.ds(31, 1), :] = jnp.zeros_like(read_bias_ref)


def pair_outer_kernel(need, send, at_ref, *refs, pairs, parts):
    takes = 4 * pairs
    outs = refs[takes:]
    half, plane = (at_ref[0], at_ref[1])
    rows = outs[0].shape[0] // pairs
    for pair in range(pairs):
        left, left_far, right, right_far = refs[4 * pair : 4 * pair + 4]
        need(left, left_far, right, right_far)
        for step in range(parts):
            begin = half * (rows * parts) + flip(plane, step) * rows
            lanes = pl.ds(pl.multiple_of(begin, LANES), rows)
            total = lax.dot_general(
                left[:, lanes], right[...], (((0,), (0,)), ((), ())), preferred_element_type=FULL
            ) + lax.dot_general(
                left_far[:, lanes],
                right_far[...],
                (((0,), (0,)), ((), ())),
                preferred_element_type=FULL,
            )
            outs[step][pl.ds(pair * rows, rows), :] = total.astype(LOW)
    send(*outs)


def sum_split_kernel(need, send, at_ref, *refs, pairs, parts, pieces, along=2):
    takes, outs = (refs[:pieces], refs[pieces : pieces + parts])
    total = refs[-1]
    need(*takes)
    value = takes[0][...].astype(FULL)
    for at in range(1, pieces):
        value = value + takes[at][...].astype(FULL)
    total[...] = value
    rows = total.shape[0] // pairs // parts
    for step in range(parts):
        begin = flip(at_ref[along], step) * rows
        for pair in range(pairs):
            place = pl.ds(pl.multiple_of(pair * rows * parts + begin, SLAB), rows)
            outs[step][pl.ds(pair * rows, rows), :] = total[place, :].astype(LOW)
    send(*outs)


def assemble_kernel(*refs, spans, pairs, planes, strips):
    takes = len(spans)
    parts, outs = (refs[:takes], refs[takes : takes + pairs])
    full, sem = (refs[takes + pairs : takes + 2 * pairs], refs[-1])
    half, plane, row = places()
    rows = spans[0] // pairs // strips
    block = strips * rows
    pieces = []
    for part, span in zip(parts, spans):
        pieces += [(part, begin) for begin in range(0, span, pairs * rows)]
    writes = []
    for pair in range(pairs):
        for at in range(2 * planes * strips):
            near, step = (at // strips, at % strips)
            side, spot = (flip(half, near // planes), flip(plane, near % planes))
            place = side * (planes * block) + spot * block
            if strips > 1:
                place = place + flip(row, step) * rows
            part, begin = pieces[at]
            full[pair][pl.ds(pl.multiple_of(place, SLAB), rows), :] = part[
                pl.ds(begin + pair * rows, rows), :
            ].astype(FULL)
        writes.append(pltpu.make_async_copy(full[pair], outs[pair], sem.at[pair]))
        writes[-1].start()
    for write in writes:
        write.wait()


def assemble(parts, far, pairs, planes, strips):
    out = like(2 * planes * parts[0].shape[0] // pairs, parts[0].shape[1])
    parts = [pltpu.with_memory_space_constraint(part, pltpu.VMEM) for part in parts + far]
    return pl.pallas_call(
        functools.partial(
            assemble_kernel,
            spans=[part.shape[0] for part in parts],
            pairs=pairs,
            planes=planes,
            strips=strips,
        ),
        out_shape=[pltpu.HBM(out.shape, out.dtype)] * pairs,
        in_specs=[pl.BlockSpec(memory_space=pltpu.VMEM)] * len(parts),
        out_specs=[pl.BlockSpec(memory_space=pltpu.HBM)] * pairs,
        scratch_shapes=[pltpu.VMEM(out.shape, FULL)] * pairs + [pltpu.SemaphoreType.DMA((pairs,))],
        compiler_params=pltpu.CompilerParams(vmem_limit_bytes=VMEM_BYTES),
        cost_estimate=pl.CostEstimate(flops=0, bytes_accessed=0, transcendentals=0),
    )(*parts)


def small_kernel(need, send, at_ref, sums_ref, *outs):
    for place in range(2):
        conv, gain, shift, out_gain, out_shift = outs[5 * place : 5 * place + 5]
        rows = sums_ref[pl.ds(15 * place, 15), :]
        for top in range(3):
            conv[top] = rows[3 * top : 3 * top + 3]
        gain[pl.ds(0, 1), :] = rows[9:10]
        gain[pl.ds(1, 1), :] = rows[11:12]
        shift[pl.ds(0, 1), :] = rows[10:11]
        shift[pl.ds(1, 1), :] = rows[12:13]
        out_gain[...] = rows[13:14]
        out_shift[...] = rows[14:15]


class Near:
    def __init__(self, value):
        self.value = value


def like(*shape, dtype=FULL):
    return jax.ShapeDtypeStruct(shape, dtype)


def low(*shape):
    return like(*shape, dtype=LOW)


def places():
    return [lax.axis_index(axis) for axis in ("half", "im", "row")]


def call(kernel, outs, scratch, *args):
    near_in = [isinstance(arg, Near) for arg in args]
    near_out = [isinstance(out, Near) for out in outs]
    args = [arg.value if isinstance(arg, Near) else arg for arg in args]
    outs = [out.value if isinstance(out, Near) else out for out in outs]
    takes, gives = (len(args), len(outs))
    far_in = [at for at in range(takes) if not near_in[at]]
    far_out = [at for at in range(gives) if not near_out[at]]

    def body(*refs):
        given, refs = (list(refs[:takes]), refs[takes:])
        made, refs = (list(refs[:gives]), refs[gives:])
        rest = refs[len(far_in) + len(far_out) :]
        reads, writes = ({}, {})
        if far_in:
            in_sem = rest[-1]
            rest = rest[:-1]
        if far_out:
            out_sem = rest[-1]
            rest = rest[:-1]
        for place, at in enumerate(far_in):
            reads[at] = pltpu.make_async_copy(given[at], refs[place], in_sem.at[place])
            given[at] = refs[place]
        for place, at in enumerate(far_out):
            mirror = refs[len(far_in) + place]
            writes[at] = pltpu.make_async_copy(mirror, made[at], out_sem.at[place])
            made[at] = mirror
        for at in sorted(reads, key=lambda at: args[at].size):
            reads[at].start()
        started = []

        def need(*wanted):
            for at in list(reads):
                if any(given[at] is ref for ref in wanted):
                    reads.pop(at).wait()

        def send(*ready):
            for at in list(writes):
                if any(made[at] is ref for ref in ready):
                    started.append(writes.pop(at))
                    started[-1].start()

        kernel(need, send, places(), *given, *made, *rest)
        need(*given)
        send(*made)
        for write in started:
            write.wait()

    spaces = {True: pltpu.VMEM, False: pltpu.HBM}
    args = [
        pltpu.with_memory_space_constraint(arg, spaces[near]) for arg, near in zip(args, near_in)
    ]
    return pl.pallas_call(
        body,
        out_shape=[spaces[near](out.shape, out.dtype) for out, near in zip(outs, near_out)],
        in_specs=[pl.BlockSpec(memory_space=spaces[near]) for near in near_in],
        out_specs=[pl.BlockSpec(memory_space=spaces[near]) for near in near_out],
        scratch_shapes=[pltpu.VMEM(args[at].shape, args[at].dtype) for at in far_in]
        + [pltpu.VMEM(outs[at].shape, outs[at].dtype) for at in far_out]
        + [pltpu.VMEM(shape, FULL) for shape in scratch]
        + [pltpu.SemaphoreType.DMA((len(far_out),))] * bool(far_out)
        + [pltpu.SemaphoreType.DMA((len(far_in),))] * bool(far_in),
        compiler_params=pltpu.CompilerParams(vmem_limit_bytes=VMEM_BYTES),
        cost_estimate=pl.CostEstimate(flops=0, bytes_accessed=0, transcendentals=0),
    )(*args)


def edges(parity_edges):
    size = lax.axis_size("row")
    inner = [(at, at ^ 1) for at in range(size)]
    outer = [(at, at + 1) for at in range(1, size - 1, 2)]
    outer = outer + [(to, at) for at, to in outer]
    return (
        lax.ppermute(parity_edges[0], "row", inner),
        lax.ppermute(parity_edges[1], "row", outer),
    )


def swap(field):
    return lax.ppermute(field, "half", [(0, 1), (1, 0)])


def steps_of(value, axis, step):
    size = lax.axis_size(axis)
    return lax.ppermute(value, axis, [(at, at ^ step) for at in range(size)])


def share(parts, axis):
    return [parts[0]] + [steps_of(parts[at], axis, at) for at in range(1, len(parts))]


def share_same(part, axis):
    size = lax.axis_size(axis)
    return [part] + [steps_of(part, axis, at) for at in range(1, size)]


def gather_near(part):
    return [part, steps_of(part, "im", 1), steps_of(part, "im", 2)]


def gather_rest(parts):
    half = parts[0].shape[0] // 2
    return [steps_of(parts[1][:half], "im", 2), steps_of(parts[2][half:], "im", 1)]


def small_outputs(part, width):
    return [
        part[:9].reshape(3, 3, width),
        jnp.stack([part[9], part[11]]),
        jnp.stack([part[10], part[12]]),
        part[13],
        part[14],
    ]


def pair_outer(*pairs):
    size = lax.axis_size("im")
    first = pairs[0][0].value if isinstance(pairs[0][0], Near) else pairs[0][0]
    width = first.shape[1]
    rows = width // 2 // size * len(pairs)
    return list(
        call(
            functools.partial(pair_outer_kernel, pairs=len(pairs), parts=size),
            [Near(low(rows, width))] * size,
            [],
            *[ref for pair in pairs for ref in pair],
        )
    )


def sum_split(pieces, pairs):
    size = lax.axis_size("row")
    rows, width = pieces[0].shape
    return list(
        call(
            functools.partial(
                sum_split_kernel,
                pairs=pairs,
                parts=size,
                pieces=len(pieces),
            ),
            [Near(low(rows // size, width))] * size,
            [(rows, width)],
            *[Near(piece) for piece in pieces],
        )
    )


def add_low(pieces):
    total = pieces[0].astype(FULL)
    for piece in pieces[1:]:
        total = total + piece.astype(FULL)
    return total.astype(LOW)


def sum_far(left, right, axes):
    part = jnp.einsum("tm,tc->mc", left, right, preferred_element_type=FULL)
    return lax.psum(part, axes)


def shards(
    x_in,
    pre_reduce,
    pre_conv,
    pre_expand,
    pre_mid_gain,
    pre_mid_shift,
    pre_out_gain,
    pre_out_shift,
    post_reduce,
    post_conv,
    post_expand,
    post_mid_gain,
    post_mid_shift,
    post_out_gain,
    post_out_shift,
    read_weight,
    read_bias,
    cotangent,
):
    count, strip, side, width = x_in.shape
    strips = lax.axis_size("row")
    tokens = count * strip * side
    cols = side // 2
    rows = strip // 2
    slabs = count * rows
    padded = slabs * SLAB
    small = slabs * cols
    block = -(-small // SLAB) * SLAB
    features = read_weight.shape[1]
    x_low = x_in.reshape(tokens, width)
    pre_out_g, pre_out_s = (pre_out_gain[None], pre_out_shift[None])
    post_out_g, post_out_s = (post_out_gain[None], post_out_shift[None])
    pre_edge = Near(low(count, side, width))
    post_edge = Near(low(count, SLAB, width))
    quick = lax.axis_size("im") == 4 and strips == 4

    first, edge_a, edge_b, normed_a, factor_a = call(
        pre_reduce_kernel,
        [Near(low(tokens, width)), pre_edge, pre_edge, like(tokens, width), like(tokens, LANES)],
        [(tokens, width)],
        x_low,
        pre_reduce,
        pre_mid_gain,
        pre_mid_shift,
    )
    got_a, got_b = edges((edge_a, edge_b))
    (
        second,
        normed_b,
        factor_b,
        normed_c,
        factor_c,
        summed,
        pooled,
        post_first,
        edge_a,
        edge_b,
        post_normed_a,
        post_factor_a,
        pad,
    ) = call(
        pre_rest_kernel,
        [
            low(tokens, width),
            like(tokens, width),
            like(tokens, LANES),
            like(tokens, width),
            like(tokens, LANES),
            like(tokens, width),
            Near(like(padded, width)),
            Near(low(padded, width)),
            post_edge,
            post_edge,
            like(padded, width),
            like(padded, LANES),
            like(count, strip + 2, side, width),
        ],
        [(tokens, width), (side * width // LANES, LANES), (padded, width)],
        x_low,
        Near(first),
        Near(got_a),
        Near(got_b),
        pre_conv,
        pre_expand,
        pre_mid_gain,
        pre_mid_shift,
        pre_out_g,
        pre_out_s,
        post_reduce,
        post_mid_gain,
        post_mid_shift,
    )
    got_a, got_b = edges((edge_a, edge_b))
    (
        block_two,
        left_in,
        left_second,
        post_normed_b,
        post_factor_b,
        post_normed_c,
        post_factor_c,
        post_summed,
        post_pad,
    ) = call(
        functools.partial(post_rest_kernel, cols=cols),
        [
            Near(low(small, width)),
            low(block, width),
            low(block, width),
            like(padded, width),
            like(padded, LANES),
            like(padded, width),
            like(padded, LANES),
            like(padded, width),
            like(count, rows + 2, SLAB, width),
        ],
        [(padded, width), (padded, width), (block, width)],
        Near(pooled),
        Near(post_first),
        Near(got_a),
        Near(got_b),
        post_conv,
        post_expand,
        post_mid_gain,
        post_mid_shift,
        post_out_g,
        post_out_s,
    )
    whole = lax.all_gather(block_two, "row", axis=0, tiled=True)
    readout, grad_pre, *terms, d_read_b = call(
        functools.partial(readout_kernel, strips=strips),
        [
            like(*cotangent.shape, dtype=LOW),
            Near(low(strips * small, features)),
        ]
        + [Near(low(small, width))] * strips
        + [like(1, features)],
        [
            (strips * small, features),
            (strips * small, features),
            (strips * small, width),
        ],
        Near(whole),
        read_weight,
        read_bias[None],
        cotangent,
    )
    terms = share(terms, "row")
    post_gs, post_ge, post_gc, edge_a, edge_b, post_small_b = call(
        functools.partial(post_back_kernel, cols=cols, strips=strips),
        [
            Near(like(padded, width)),
            Near(low(block, width)),
            Near(low(padded, width)),
            post_edge,
            post_edge,
            like(4, width),
        ],
        [(block, width), (padded, width), (padded, width), (padded, width)],
        *[Near(term) for term in terms],
        post_expand,
        post_mid_gain,
        post_mid_shift,
        post_out_g,
        post_normed_b,
        post_factor_b,
        post_normed_c,
        post_factor_c,
        post_summed,
    )
    if quick:
        edge_a, whole, grad_pre = tie(edge_a, whole, grad_pre)
    got_a, got_b = edges((edge_a, edge_b))
    if quick:
        read_slots = pair_outer(
            (Near(whole), Near(swap(whole)), Near(grad_pre), Near(swap(grad_pre)))
        )
        read_parts = [read_slots[0]] + [steps_of(read_slots[at], "im", at) for at in (1, 2)]
        (got_a, got_b), (*read_parts, read_last) = tie_later(
            (got_a, got_b), (*read_parts, read_slots[3])
        )
    (
        post_gr,
        pre_gs,
        pre_ge,
        pre_gc,
        edge_a,
        edge_b,
        post_small_a,
        pre_small_b,
    ) = call(
        functools.partial(middle_back_kernel, cols=cols),
        [
            Near(low(block, width)),
            like(tokens, width),
            Near(low(tokens, width)),
            Near(low(tokens, width)),
            pre_edge,
            pre_edge,
            like(11, width),
            like(4, width),
        ],
        [
            (count, rows + 2, SLAB, width),
            (9, 8, width),
            (padded, width),
            (side * width // LANES, LANES),
            (tokens, width),
            (2, 8, width),
            (padded, width),
            (block, width),
        ],
        Near(post_gc),
        Near(got_a),
        Near(got_b),
        post_pad,
        post_conv,
        post_reduce,
        post_mid_gain,
        post_mid_shift,
        post_normed_a,
        post_factor_a,
        Near(post_gs),
        pre_expand,
        pre_mid_gain,
        pre_mid_shift,
        pre_out_g,
        normed_b,
        factor_b,
        normed_c,
        factor_c,
        summed,
    )
    got_a, got_b = edges((edge_a, edge_b))
    if quick:
        pre_ge_far = swap(pre_ge)
        post_parts = pair_outer(
            (left_in, swap(left_in), Near(post_gr), Near(swap(post_gr))),
            (left_second, swap(left_second), Near(post_ge), Near(swap(post_ge))),
        )
        post_parts = pair_outer(
            (left_in, swap(left_in), Near(post_gr), Near(swap(post_gr))),
            (left_second, swap(left_second), Near(post_ge), Near(swap(post_ge))),
        )
        post_sums = share(post_parts, "im")[1:]
        (got_a, got_b), post_sums = tie_later((got_a, got_b), post_sums)
    pre_gr, sums = call(
        pre_back_kernel,
        [Near(low(tokens, width)), Near(like(32, width))],
        [
            (count, strip + 2, side, width),
            (9, 8, width),
            (2, 8, width),
        ],
        Near(pre_gc),
        Near(got_a),
        Near(got_b),
        pad,
        pre_conv,
        pre_mid_gain,
        pre_mid_shift,
        normed_a,
        factor_a,
        pre_small_b,
        post_small_a,
        post_small_b,
        d_read_b,
    )
    if quick:
        far = swap(pre_gr)
        post_parts = sum_split(post_parts[:1] + post_sums, 2)
        post_parts[0], far = tie(post_parts[0], far)
        post_parts = share(post_parts, "row")
        parts = pair_outer(
            (second, swap(second), Near(pre_ge), Near(swap(pre_ge))),
            (x_low, swap(x_low), Near(pre_gr), Near(far)),
        )
        parts[0], sums = tie(parts[0], sums + swap(sums))
        read_parts = read_parts + [steps_of(read_last, "im", 3)]
        near_parts = [steps_of(parts[at], "im", at) for at in (1, 2)]
        grad_in = pre_gs + jnp.einsum("tm,cm->tc", pre_gr, pre_reduce, preferred_element_type=FULL)
        grad_in = grad_in.astype(LOW)
        post_parts, (grad_in, last, *rest) = tie_later(
            post_parts, (grad_in, parts[3], *near_parts, *read_parts)
        )
        near_parts, read_parts = (rest[:2], rest[2:])
        post_parts = share_same(add_low(post_parts), "row")
        last = steps_of(last, "im", 3)
        post_parts, (last, *read_parts) = tie_later(post_parts, (last, *read_parts))
        parts = share(sum_split([parts[0]] + near_parts + [last], 2), "row")
        post_parts = gather_near(jnp.concatenate(post_parts, axis=0))
        read_parts = gather_near(add_low(read_parts))
        parts, rest = tie_later(parts, (*post_parts, *read_parts))
        post_parts, read_parts = (rest[:3], rest[3:])
        parts = share_same(add_low(parts), "row")
        read_parts.append(steps_of(read_parts[0], "im", 3))
        post_parts = post_parts + gather_rest(post_parts)
        parts, rest = tie_later(parts, (*post_parts, *read_parts, sums))
        post_parts, read_parts, sums = (rest[:5], rest[5:9], rest[9])
        parts = gather_near(jnp.concatenate(parts, axis=0))
        alone = lax.broadcasted_iota(jnp.int32, sums.shape, 0) >= 30
        for step in (1, 2):
            sums = sums + jnp.where(alone, 0.0, steps_of(sums, "row", step))
        parts, (sums, *post_parts) = tie_later(parts, (sums, *post_parts))
        far = swap(jnp.concatenate(parts, axis=0))
        post_far = swap(jnp.concatenate(post_parts, axis=0))
        read_far = swap(jnp.concatenate(read_parts, axis=0))
        sums = sums + steps_of(sums, "im", 1)
        far, post_far, read_far, sums, *rest = tie(
            far, post_far, read_far, sums, *gather_rest(parts)
        )
        far_rest = swap(jnp.concatenate(rest, axis=0))
        sums = sums + steps_of(sums, "im", 2)
        post_reduce_g, post_expand_g = assemble(post_parts, [post_far], 2, 4, strips)
        (read_total,) = assemble(read_parts, [read_far], 1, 4, 1)
        (post_reduce_g, read_total), (sums, far_rest) = tie_later(
            (post_reduce_g, read_total), (sums, far_rest)
        )
        small_out = call(
            small_kernel,
            [like(3, 3, width), like(2, width), like(2, width), like(1, width), like(1, width)] * 2,
            [],
            Near(sums),
        )
        pre_expand_g, pre_reduce_g = assemble(parts + rest, [far, far_rest], 2, 4, strips)
        read_bias_g = sums[30]
    else:
        axes = IMG + ("row",)
        post_reduce_g = sum_far(left_in, post_gr, axes)
        post_expand_g = sum_far(left_second, post_ge, axes)
        pre_expand_g = sum_far(second, pre_ge, axes)
        pre_reduce_g = sum_far(x_low, pre_gr, axes)
        read_total = sum_far(whole, grad_pre, IMG)
        read_bias_g = lax.psum(sums[30], IMG)
        sums = lax.psum(sums[:30], axes)
        small_out = small_outputs(sums[:15], width) + small_outputs(sums[15:30], width)
        grad_in = pre_gs + jnp.einsum("tm,cm->tc", pre_gr, pre_reduce, preferred_element_type=FULL)
        grad_in = grad_in.astype(LOW)

    pre_conv_g, pre_gain_g, pre_shift_g, pre_og_g, pre_os_g = small_out[:5]
    post_conv_g, post_gain_g, post_shift_g, post_og_g, post_os_g = small_out[5:]
    return (
        readout,
        grad_in.reshape(x_in.shape),
        pre_reduce_g,
        pre_conv_g,
        pre_expand_g,
        pre_gain_g,
        pre_shift_g,
        pre_og_g.reshape(width),
        pre_os_g.reshape(width),
        post_reduce_g,
        post_conv_g,
        post_expand_g,
        post_gain_g,
        post_shift_g,
        post_og_g.reshape(width),
        post_os_g.reshape(width),
        read_total,
        read_bias_g,
    )


def solution(mesh):
    images, strips = mesh.devices.shape
    split = jax.sharding.Mesh(
        mesh.devices.reshape(images // 2, 2, strips), ("im", "half", "row")
    )
    return jax.shard_map(
        shards,
        mesh=split,
        in_specs=(P(IMG, "row", None, None),)
        + (P(),) * 14
        + (P(None, "row"), P("row"), P(IMG, None, None, "row")),
        out_specs=(P(IMG, None, None, "row"), P(IMG, "row", None, None))
        + (P(),) * 14
        + (P(None, "row"), P("row")),
        check_vma=False,
    )
```

```python
import functools

import jax
import jax.numpy as jnp
from jax import lax
from jax.experimental import pallas as pl
from jax.experimental.pallas import tpu as pltpu
from jax.sharding import PartitionSpec as P

EPSILON = 1e-06
SQRT_HALF = 0.7071067811865476
INV_SQRT_TWO_PI = 0.3989422804014327
LOW = jnp.bfloat16
FULL = jnp.float32
IMG = ("im", "half")
TILE = 256
SLAB = 16
LANES = 128
VMEM_BYTES = 24 * 1024 * 1024


def tie(*values):
    return lax.optimization_barrier(values)


def tie_later(first, second):
    first = list(tie(*first))
    out = list(tie(*first, *second))
    return (out[: len(first)], out[len(first) :])


def norm(value):
    centred = value - jnp.mean(value, axis=-1, keepdims=True)
    factor = lax.rsqrt(jnp.mean(centred * centred, axis=-1, keepdims=True) + EPSILON)
    return (centred * factor, factor)


def norm_back(grad, normed, factor, gain):
    scaled = grad * gain
    return factor * (
        scaled
        - jnp.mean(scaled, axis=-1, keepdims=True)
        - normed * jnp.mean(scaled * normed, axis=-1, keepdims=True)
    )


def gate(value):
    return 0.5 * jnp.tanh(0.5 * value) + 0.5


def silu(value):
    return value * gate(value)


def silu_back(grad, value):
    sigma = gate(value)
    return grad * sigma * (1.0 + value * (1.0 - sigma))


def flip(place, step):
    bit = 1
    while bit <= step:
        if step & bit:
            place = place + bit - 2 * bit * ((place // bit) % 2)
        bit *= 2
    return place


def wide(factor):
    return jnp.broadcast_to(factor, (factor.shape[0], LANES))


def fold(value):
    return jnp.sum(value.reshape(-1, 8, value.shape[-1]), axis=0)


def live(rows, cols):
    at = lax.broadcasted_iota(jnp.int32, (rows, 1), 0)
    return lax.rem(at, SLAB) < cols


def from_left(value):
    at = lax.broadcasted_iota(jnp.int32, (value.shape[0], 1), 0)
    return jnp.where(at == 0, 0.0, pltpu.roll(value, 1, 0))


def from_right(value):
    last = value.shape[0] - 1
    at = lax.broadcasted_iota(jnp.int32, (value.shape[0], 1), 0)
    return jnp.where(at == last, 0.0, pltpu.roll(value, last, 0))


def matmul(left_ref, right_ref, out_ref):
    @pl.loop(0, right_ref.shape[1] // TILE)
    def _(at):
        cols = pl.ds(pl.multiple_of(at * TILE, TILE), TILE)
        out_ref[:, cols] = jnp.dot(
            left_ref[...].astype(LOW), right_ref[:, cols], preferred_element_type=FULL
        )


def matmul_back(left_ref, right_ref, out_ref):
    @pl.loop(0, right_ref.shape[0] // TILE)
    def _(at):
        cols = pl.ds(pl.multiple_of(at * TILE, TILE), TILE)
        out_ref[:, cols] = lax.dot_general(
            left_ref[...].astype(LOW),
            right_ref[cols, :],
            (((1,), (1,)), ((), ())),
            preferred_element_type=FULL,
        ).astype(out_ref.dtype)


def rows_of(at, size):
    return pl.ds(pl.multiple_of(at * size, SLAB), size)


def fill_halo(at_ref, pad_ref, low_ref, got_a_ref, got_b_ref):
    count, rows, cols, width = pad_ref.shape
    rows = rows - 2
    even = lax.rem(at_ref[2], 2) == 0
    for image in range(count):
        got_a, got_b = (got_a_ref[image].astype(FULL), got_b_ref[image].astype(FULL))
        pad_ref[image, 0] = jnp.where(even, got_b, got_a)
        pad_ref[image, rows + 1] = jnp.where(even, got_a, got_b)

    size = cols if cols % SLAB == 0 else 2 * cols
    per = size // cols
    each = rows // per

    @pl.loop(0, count * each)
    def _(at):
        part = low_ref[rows_of(at, size), :].astype(FULL).reshape(per, cols, width)
        pad_ref[at // each, pl.ds(1 + per * lax.rem(at, each), per)] = part


def set_edges(at_ref, edge_a_ref, edge_b_ref, image, head, tail):
    even = lax.rem(at_ref[2], 2) == 0
    edge_a_ref[image] = jnp.where(even, tail, head).astype(LOW)
    edge_b_ref[image] = jnp.where(even, head, tail).astype(LOW)


def conv_row(pad_ref, taps, image, row):
    lines = [pad_ref[image, row + top] for top in range(3)]
    sums = [
        lines[0] * taps[left] + lines[1] * taps[3 + left] + lines[2] * taps[6 + left]
        for left in range(3)
    ]
    return from_left(sums[0]) + sums[1] + from_right(sums[2])


def conv_back_row(pad_ref, grad_ref, taps, taps_ref, image, row):
    lines = [grad_ref[image, row + top] for top in range(3)]
    sums = [
        lines[2] * taps[left] + lines[1] * taps[3 + left] + lines[0] * taps[6 + left]
        for left in range(3)
    ]
    shifted = [from_right(lines[1]), lines[1], from_left(lines[1])]
    for top in range(3):
        source = pad_ref[image, row + top]
        for left in range(3):
            taps_ref[3 * top + left] += fold(source * shifted[left])
    return from_right(sums[0]) + sums[1] + from_left(sums[2])


def pack(compact, source, out_ref, cols):
    compact[...] = jnp.zeros(compact.shape, FULL)
    for at in range(source.shape[0] // SLAB):
        compact[pl.ds(at * cols, cols), :] = source[pl.ds(at * SLAB, cols), :]
    out_ref[...] = compact[...].astype(LOW)


def narrow(pair, value):
    side = value.shape[0]
    parts = []
    for at in range(value.shape[1] // LANES):
        pair[pl.ds(at * side, side), :] = value[:, at * LANES : (at + 1) * LANES]
        parts.append(
            pair[pl.ds(at * side, side // 2, stride=2), :]
            + pair[pl.ds(at * side + 1, side // 2, stride=2), :]
        )
    return jnp.concatenate(parts, axis=1)


def widen(pair, value):
    cols = value.shape[0]
    parts = []
    for at in range(value.shape[1] // LANES):
        part = value[:, at * LANES : (at + 1) * LANES]
        pair[pl.ds(2 * cols * at, cols, stride=2), :] = part
        pair[pl.ds(2 * cols * at + 1, cols, stride=2), :] = part
        parts.append(pair[pl.ds(2 * cols * at, 2 * cols), :])
    return jnp.concatenate(parts, axis=1)


def tap_rows(conv_ref):
    lines = [conv_ref[top].astype(FULL) for top in range(3)]
    return [lines[at // 3][at % 3 : at % 3 + 1] for at in range(9)]


def finish(small_ref, sums_ref, at, place):
    small_ref[pl.ds(place, 1), :] = jnp.sum(sums_ref[at], axis=0, keepdims=True)


def pre_reduce_kernel(
    need,
    send,
    at_ref,
    x_ref, w_ref, gain_ref, shift_ref, first_ref, edge_a_ref, edge_b_ref, normed_ref, factor_ref, red
):
    count, side, width = edge_a_ref.shape
    size = 2 * side
    steps = x_ref.shape[0] // size
    need(x_ref, w_ref)
    matmul(x_ref, w_ref, red)
    need(gain_ref, shift_ref)
    gain, shift = (gain_ref[pl.ds(0, 1), :], shift_ref[pl.ds(0, 1), :])

    @pl.loop(0, steps)
    def _(at):
        rows = rows_of(at, size)
        normed, factor = norm(red[rows, :])
        normed_ref[rows, :] = normed
        factor_ref[rows, :] = wide(factor)
        first_ref[rows, :] = silu(normed * gain + shift).astype(LOW)

    each = steps // count
    for image in range(count):
        head = first_ref[pl.ds(image * each * size, size), :].astype(FULL)
        tail = first_ref[pl.ds((image * each + each - 1) * size, size), :].astype(FULL)
        set_edges(at_ref, edge_a_ref, edge_b_ref, image, head[:side], tail[side:])


def pre_rest_kernel(
    need,
    send,
    at_ref,
    x_ref,
    first_ref,
    got_a_ref,
    got_b_ref,
    conv_ref,
    expand_ref,
    gain_ref,
    shift_ref,
    out_gain_ref,
    out_shift_ref,
    reduce_ref,
    post_gain_ref,
    post_shift_ref,
    second_ref,
    normed_b_ref,
    factor_b_ref,
    normed_c_ref,
    factor_c_ref,
    summed_ref,
    pooled_ref,
    post_first_ref,
    edge_a_ref,
    edge_b_ref,
    post_normed_ref,
    post_factor_ref,
    pad,
    exp,
    pair,
    red,
):
    count, strip, side, width = pad.shape
    strip = strip - 2
    size = 2 * side
    each = strip // 2
    need(first_ref, got_a_ref, got_b_ref)
    fill_halo(at_ref, pad, first_ref, got_a_ref, got_b_ref)
    need(conv_ref, gain_ref, shift_ref)
    send(pad)
    taps = tap_rows(conv_ref)
    gain, shift = (gain_ref[pl.ds(1, 1), :], shift_ref[pl.ds(1, 1), :])

    @pl.loop(0, count * each)
    def _(at):
        rows = rows_of(at, size)
        image, row = (at // each, 2 * lax.rem(at, each))
        conv = jnp.concatenate(
            [conv_row(pad, taps, image, row), conv_row(pad, taps, image, row + 1)], axis=0
        )
        normed, factor = norm(conv)
        normed_b_ref[rows, :] = normed
        factor_b_ref[rows, :] = wide(factor)
        second_ref[rows, :] = silu(normed * gain + shift).astype(LOW)

    send(second_ref, normed_b_ref, factor_b_ref)
    need(expand_ref)
    matmul(second_ref, expand_ref, exp)
    need(x_ref, out_gain_ref, out_shift_ref)
    out_gain, out_shift = (out_gain_ref[...], out_shift_ref[...])
    cols = side // 2
    for at in range(count * each):
        rows = pl.ds(at * size, size)
        normed, factor = norm(exp[rows, :])
        normed_c_ref[rows, :] = normed
        factor_c_ref[rows, :] = wide(factor)
        summed = x_ref[rows, :].astype(FULL) + normed * out_gain + out_shift
        summed_ref[rows, :] = summed
        block = silu(summed)
        half = narrow(pair, block[:side] + block[side:])
        pooled_ref[pl.ds(at * SLAB, cols), :] = 0.25 * half
        pooled_ref[pl.ds(at * SLAB + cols, SLAB - cols), :] = jnp.zeros(
            (SLAB - cols, width), FULL
        )
    send(normed_c_ref, factor_c_ref, summed_ref)
    need(reduce_ref, post_gain_ref, post_shift_ref)
    matmul(pooled_ref, reduce_ref, red)
    normed, factor = norm(red[...])
    post_normed_ref[...] = normed
    post_factor_ref[...] = wide(factor)
    first = silu(normed * post_gain_ref[pl.ds(0, 1), :] + post_shift_ref[pl.ds(0, 1), :])
    post_first_ref[...] = jnp.where(live(red.shape[0], cols), first, 0.0).astype(LOW)
    for image in range(count):
        head = post_first_ref[pl.ds(image * each * SLAB, SLAB), :].astype(FULL)
        tail = post_first_ref[pl.ds((image * each + each - 1) * SLAB, SLAB), :].astype(FULL)
        set_edges(at_ref, edge_a_ref, edge_b_ref, image, head, tail)


def post_rest_kernel(
    need,
    send,
    at_ref,
    pooled_ref,
    first_ref,
    got_a_ref,
    got_b_ref,
    conv_ref,
    expand_ref,
    gain_ref,
    shift_ref,
    out_gain_ref,
    out_shift_ref,
    block_ref,
    left_in_ref,
    left_second_ref,
    normed_b_ref,
    factor_b_ref,
    normed_c_ref,
    factor_c_ref,
    summed_ref,
    pad,
    second,
    exp,
    compact,
    *,
    cols
):
    count, rows, _, width = pad.shape
    rows = rows - 2
    small = block_ref.shape[0]
    need(first_ref, got_a_ref, got_b_ref)
    fill_halo(at_ref, pad, first_ref, got_a_ref, got_b_ref)
    send(pad)
    need(conv_ref, gain_ref, shift_ref, pooled_ref)
    taps = tap_rows(conv_ref)
    gain, shift = (gain_ref[pl.ds(1, 1), :], shift_ref[pl.ds(1, 1), :])

    @pl.loop(0, count * rows)
    def _(at):
        place = rows_of(at, SLAB)
        normed, factor = norm(conv_row(pad, taps, at // rows, lax.rem(at, rows)))
        normed_b_ref[place, :] = normed
        factor_b_ref[place, :] = wide(factor)
        second[place, :] = silu(normed * gain + shift)

    send(normed_b_ref, factor_b_ref)
    need(expand_ref)
    matmul(second, expand_ref, exp)
    need(out_gain_ref, out_shift_ref)
    normed, factor = norm(exp[...])
    normed_c_ref[...] = normed
    factor_c_ref[...] = wide(factor)
    summed = pooled_ref[...] + normed * out_gain_ref[...] + out_shift_ref[...]
    summed_ref[...] = summed
    exp[...] = silu(summed)
    compact[...] = jnp.zeros(compact.shape, FULL)
    for at in range(count * rows):
        compact[pl.ds(at * cols, cols), :] = exp[pl.ds(at * SLAB, cols), :]
    block_ref[...] = compact[pl.ds(0, small), :].astype(LOW)
    send(block_ref, normed_c_ref, factor_c_ref, summed_ref)
    pack(compact, pooled_ref, left_in_ref, cols)
    pack(compact, second, left_second_ref, cols)


def readout_kernel(
    need,
    send,
    at_ref,
    whole_ref,
    w_ref,
    bias_ref,
    cot_ref,
    out_ref,
    grad_ref,
    *refs,
    strips
):
    slots, (bias_grad_ref, cot, out, terms_ref) = (refs[:strips], refs[strips:])
    images, lines, cols, _ = cot_ref.shape
    rows = lines // strips
    need(cot_ref)
    for at in range(images * lines):
        strip, image, row = (at // (images * rows), at // rows % images, at % rows)
        cot[pl.ds(at * cols, cols), :] = cot_ref[image, strip * rows + row].astype(FULL)
    need(whole_ref, w_ref, bias_ref)

    @pl.loop(0, w_ref.shape[1] // TILE)
    def _(at):
        lanes = pl.ds(pl.multiple_of(at * TILE, TILE), TILE)
        act = jnp.dot(whole_ref[...], w_ref[:, lanes], preferred_element_type=FULL)
        act = act + bias_ref[:, lanes]
        cdf = 0.5 * (1.0 + lax.erf(act * SQRT_HALF))
        density = jnp.exp(-0.5 * act * act) * INV_SQRT_TWO_PI
        out[:, lanes] = act * cdf
        grad = (cot[:, lanes] * (cdf + act * density)).astype(LOW)
        grad_ref[:, lanes] = grad
        bias_grad_ref[:, lanes] = jnp.sum(grad.astype(FULL), axis=0, keepdims=True)

    send(grad_ref, bias_grad_ref)
    matmul_back(grad_ref, w_ref, terms_ref)
    small = slots[0].shape[0]
    for step in range(strips):
        begin = pl.multiple_of(flip(at_ref[2], step) * small, 8)
        slots[step][...] = terms_ref[pl.ds(begin, small), :].astype(LOW)
    for at in range(images * lines):
        strip, image, row = (at // (images * rows), at // rows % images, at % rows)
        out_ref[image, strip * rows + row] = out[pl.ds(at * cols, cols), :].astype(LOW)


def post_back_kernel(
    need,
    send,
    at_ref,
    *refs,
    cols,
    strips
):
    pieces, refs = (refs[:strips], refs[strips:])
    (
    expand_ref,
    gain_ref,
    shift_ref,
    out_gain_ref,
    normed_b_ref,
    factor_b_ref,
    normed_c_ref,
    factor_c_ref,
    summed_ref,
    grad_sum_ref,
    grad_exp_ref,
    grad_conv_ref,
    edge_a_ref,
    edge_b_ref,
    small_ref,
    compact,
    spread_out,
    exp,
    sec,
    ) = refs
    count = edge_a_ref.shape[0]
    tokens, width = grad_sum_ref.shape
    each = tokens // SLAB // count
    need(*pieces)
    total = pieces[0][...].astype(FULL)
    for piece in pieces[1:]:
        total = total + piece[...].astype(FULL)
    compact[...] = jnp.zeros(compact.shape, FULL)
    compact[pl.ds(0, total.shape[0]), :] = total
    spread_out[...] = jnp.zeros((tokens, width), FULL)
    for at in range(tokens // SLAB):
        spread_out[pl.ds(at * SLAB, cols), :] = compact[pl.ds(at * cols, cols), :]
    need(summed_ref, normed_c_ref, factor_c_ref, out_gain_ref)
    grad_sum = silu_back(spread_out[...], summed_ref[...])
    grad_sum_ref[...] = grad_sum
    normed = normed_c_ref[...]
    exp[...] = norm_back(grad_sum, normed, factor_c_ref[:, :1], out_gain_ref[...])
    small_ref[pl.ds(2, 1), :] = jnp.sum(grad_sum * normed, axis=0, keepdims=True)
    small_ref[pl.ds(3, 1), :] = jnp.sum(grad_sum, axis=0, keepdims=True)
    pack(compact, exp, grad_exp_ref, cols)
    send(grad_sum_ref, grad_exp_ref)
    need(expand_ref)
    matmul_back(exp, expand_ref, sec)
    need(gain_ref, shift_ref, normed_b_ref, factor_b_ref)
    gain, shift = (gain_ref[pl.ds(1, 1), :], shift_ref[pl.ds(1, 1), :])
    normed = normed_b_ref[...]
    grad = silu_back(sec[...], normed * gain + shift)
    grad_conv_ref[...] = norm_back(grad, normed, factor_b_ref[:, :1], gain).astype(LOW)
    small_ref[pl.ds(0, 1), :] = jnp.sum(grad * normed, axis=0, keepdims=True)
    small_ref[pl.ds(1, 1), :] = jnp.sum(grad, axis=0, keepdims=True)
    for image in range(count):
        head = grad_conv_ref[pl.ds(image * each * SLAB, SLAB), :].astype(FULL)
        tail = grad_conv_ref[pl.ds((image * each + each - 1) * SLAB, SLAB), :].astype(FULL)
        set_edges(at_ref, edge_a_ref, edge_b_ref, image, head, tail)


def middle_back_kernel(
    need,
    send,
    at_ref,
    grad_conv_ref,
    got_a_ref,
    got_b_ref,
    pad,
    post_conv_ref,
    post_reduce_ref,
    post_gain_ref,
    post_shift_ref,
    post_normed_ref,
    post_factor_ref,
    post_grad_sum_ref,
    expand_ref,
    gain_ref,
    shift_ref,
    out_gain_ref,
    normed_b_ref,
    factor_b_ref,
    normed_c_ref,
    factor_c_ref,
    summed_ref,
    post_grad_red_ref,
    grad_sum_ref,
    grad_exp_ref,
    pre_grad_conv_ref,
    edge_a_ref,
    edge_b_ref,
    post_small_ref,
    small_ref,
    grad_pad,
    taps_sum,
    grad_in,
    pair,
    sec,
    sums,
    post_red,
    compact,
    *,
    cols
):
    count, side, width = edge_a_ref.shape
    need(grad_conv_ref, got_a_ref, got_b_ref)
    fill_halo(at_ref, grad_pad, grad_conv_ref, got_a_ref, got_b_ref)
    need(pad, post_conv_ref)
    need(post_gain_ref, post_shift_ref, post_normed_ref, post_factor_ref)
    taps = tap_rows(post_conv_ref)
    taps_sum[...] = jnp.zeros_like(taps_sum)
    sums[...] = jnp.zeros_like(sums)
    gain, shift = (post_gain_ref[pl.ds(0, 1), :], post_shift_ref[pl.ds(0, 1), :])
    each = post_grad_sum_ref.shape[0] // SLAB // count

    @pl.loop(0, count * each)
    def _(at):
        place = rows_of(at, SLAB)
        grad = conv_back_row(pad, grad_pad, taps, taps_sum, at // each, lax.rem(at, each))
        normed = post_normed_ref[place, :]
        grad = jnp.where(live(SLAB, cols), silu_back(grad, normed * gain + shift), 0.0)
        sums[0] += fold(grad * normed)
        sums[1] += fold(grad)
        post_red[place, :] = norm_back(grad, normed, post_factor_ref[place, :1], gain)

    for at in range(9):
        finish(post_small_ref, taps_sum, at, at)
    finish(post_small_ref, sums, 0, 9)
    finish(post_small_ref, sums, 1, 10)
    pack(compact, post_red, post_grad_red_ref, cols)
    send(post_grad_red_ref, post_small_ref)
    need(post_reduce_ref)
    matmul_back(post_red, post_reduce_ref, grad_in)
    sums[...] = jnp.zeros_like(sums)
    size = 2 * side
    need(out_gain_ref, post_grad_sum_ref, summed_ref, normed_c_ref, factor_c_ref)
    out_gain = out_gain_ref[...]
    for at in range(count * each):
        rows = pl.ds(at * size, size)
        place = pl.ds(at * SLAB, cols)
        grad = 0.25 * (post_grad_sum_ref[place, :] + grad_in[place, :])
        grad = widen(pair, grad)
        grad = jnp.concatenate([grad, grad], axis=0)
        grad_sum = silu_back(grad, summed_ref[rows, :])
        grad_sum_ref[rows, :] = grad_sum
        normed = normed_c_ref[rows, :]
        sums[0] += fold(grad_sum * normed)
        sums[1] += fold(grad_sum)
        grad_exp_ref[rows, :] = norm_back(
            grad_sum, normed, factor_c_ref[rows, :1], out_gain
        ).astype(LOW)
    finish(small_ref, sums, 0, 2)
    finish(small_ref, sums, 1, 3)
    send(grad_sum_ref, grad_exp_ref)
    need(expand_ref)
    matmul_back(grad_exp_ref, expand_ref, sec)
    need(gain_ref, shift_ref, normed_b_ref, factor_b_ref)
    sums[...] = jnp.zeros_like(sums)
    gain_b, shift_b = (gain_ref[pl.ds(1, 1), :], shift_ref[pl.ds(1, 1), :])

    @pl.loop(0, count * each)
    def _(at):
        rows = rows_of(at, size)
        normed = normed_b_ref[rows, :]
        grad = silu_back(sec[rows, :], normed * gain_b + shift_b)
        sums[0] += fold(grad * normed)
        sums[1] += fold(grad)
        pre_grad_conv_ref[rows, :] = norm_back(
            grad, normed, factor_b_ref[rows, :1], gain_b
        ).astype(LOW)

    finish(small_ref, sums, 0, 0)
    finish(small_ref, sums, 1, 1)
    for image in range(count):
        head = pre_grad_conv_ref[pl.ds(image * each * size, size), :].astype(FULL)
        tail = pre_grad_conv_ref[pl.ds((image * each + each - 1) * size, size), :].astype(FULL)
        set_edges(at_ref, edge_a_ref, edge_b_ref, image, head[:side], tail[side:])


def pre_back_kernel(
    need,
    send,
    at_ref,
    grad_conv_ref,
    got_a_ref,
    got_b_ref,
    pad,
    conv_ref,
    gain_ref,
    shift_ref,
    normed_ref,
    factor_ref,
    small_b_ref,
    post_small_a_ref,
    post_small_b_ref,
    read_bias_ref,
    grad_red_ref,
    small_ref,
    grad_pad,
    taps_sum,
    sums,
):
    count, strip, side, width = pad.shape
    strip = strip - 2
    size = 2 * side
    each = strip // 2
    need(grad_conv_ref, got_a_ref, got_b_ref)
    fill_halo(at_ref, grad_pad, grad_conv_ref, got_a_ref, got_b_ref)
    need(pad, conv_ref)
    need(gain_ref, shift_ref, normed_ref, factor_ref)
    taps = tap_rows(conv_ref)
    taps_sum[...] = jnp.zeros_like(taps_sum)
    sums[...] = jnp.zeros_like(sums)
    gain, shift = (gain_ref[pl.ds(0, 1), :], shift_ref[pl.ds(0, 1), :])

    @pl.loop(0, count * each)
    def _(at):
        rows = rows_of(at, size)
        image, row = (at // each, 2 * lax.rem(at, each))
        grad = jnp.concatenate(
            [
                conv_back_row(pad, grad_pad, taps, taps_sum, image, row),
                conv_back_row(pad, grad_pad, taps, taps_sum, image, row + 1),
            ],
            axis=0,
        )
        normed = normed_ref[rows, :]
        grad = silu_back(grad, normed * gain + shift)
        sums[0] += fold(grad * normed)
        sums[1] += fold(grad)
        grad_red_ref[rows, :] = norm_back(grad, normed, factor_ref[rows, :1], gain).astype(LOW)

    for at in range(9):
        finish(small_ref, taps_sum, at, at)
    finish(small_ref, sums, 0, 9)
    finish(small_ref, sums, 1, 10)
    need(small_b_ref, post_small_a_ref, post_small_b_ref, read_bias_ref)
    small_ref[pl.ds(11, 4), :] = small_b_ref[...]
    small_ref[pl.ds(15, 11), :] = post_small_a_ref[...]
    small_ref[pl.ds(26, 4), :] = post_small_b_ref[...]
    small_ref[pl.ds(30, 1), :] = read_bias_ref[...]
    small_ref[pl.ds(31, 1), :] = jnp.zeros_like(read_bias_ref)


def pair_outer_kernel(need, send, at_ref, *refs, pairs, parts):
    takes = 4 * pairs
    outs = refs[takes:]
    half, plane = (at_ref[0], at_ref[1])
    rows = outs[0].shape[0] // pairs
    for pair in range(pairs):
        left, left_far, right, right_far = refs[4 * pair : 4 * pair + 4]
        need(left, left_far, right, right_far)
        for step in range(parts):
            begin = half * (rows * parts) + flip(plane, step) * rows
            lanes = pl.ds(pl.multiple_of(begin, LANES), rows)
            total = lax.dot_general(
                left[:, lanes], right[...], (((0,), (0,)), ((), ())), preferred_element_type=FULL
            ) + lax.dot_general(
                left_far[:, lanes],
                right_far[...],
                (((0,), (0,)), ((), ())),
                preferred_element_type=FULL,
            )
            outs[step][pl.ds(pair * rows, rows), :] = total.astype(LOW)
    send(*outs)


def sum_split_kernel(need, send, at_ref, *refs, pairs, parts, pieces, along=2):
    takes, outs = (refs[:pieces], refs[pieces : pieces + parts])
    total = refs[-1]
    need(*takes)
    value = takes[0][...].astype(FULL)
    for at in range(1, pieces):
        value = value + takes[at][...].astype(FULL)
    total[...] = value
    rows = total.shape[0] // pairs // parts
    for step in range(parts):
        begin = flip(at_ref[along], step) * rows
        for pair in range(pairs):
            place = pl.ds(pl.multiple_of(pair * rows * parts + begin, SLAB), rows)
            outs[step][pl.ds(pair * rows, rows), :] = total[place, :].astype(LOW)
    send(*outs)


def assemble_kernel(*refs, spans, pairs, planes, strips):
    takes = len(spans)
    parts, outs = (refs[:takes], refs[takes : takes + pairs])
    full, sem = (refs[takes + pairs : takes + 2 * pairs], refs[-1])
    half, plane, row = places()
    rows = spans[0] // pairs // strips
    block = strips * rows
    pieces = []
    for part, span in zip(parts, spans):
        pieces += [(part, begin) for begin in range(0, span, pairs * rows)]
    writes = []
    for pair in range(pairs):
        for at in range(2 * planes * strips):
            near, step = (at // strips, at % strips)
            side, spot = (flip(half, near // planes), flip(plane, near % planes))
            place = side * (planes * block) + spot * block
            if strips > 1:
                place = place + flip(row, step) * rows
            part, begin = pieces[at]
            full[pair][pl.ds(pl.multiple_of(place, SLAB), rows), :] = part[
                pl.ds(begin + pair * rows, rows), :
            ].astype(FULL)
        writes.append(pltpu.make_async_copy(full[pair], outs[pair], sem.at[pair]))
        writes[-1].start()
    for write in writes:
        write.wait()


def assemble(parts, far, pairs, planes, strips):
    out = like(2 * planes * parts[0].shape[0] // pairs, parts[0].shape[1])
    parts = [pltpu.with_memory_space_constraint(part, pltpu.VMEM) for part in parts + far]
    return pl.pallas_call(
        functools.partial(
            assemble_kernel,
            spans=[part.shape[0] for part in parts],
            pairs=pairs,
            planes=planes,
            strips=strips,
        ),
        out_shape=[pltpu.HBM(out.shape, out.dtype)] * pairs,
        in_specs=[pl.BlockSpec(memory_space=pltpu.VMEM)] * len(parts),
        out_specs=[pl.BlockSpec(memory_space=pltpu.HBM)] * pairs,
        scratch_shapes=[pltpu.VMEM(out.shape, FULL)] * pairs + [pltpu.SemaphoreType.DMA((pairs,))],
        compiler_params=pltpu.CompilerParams(vmem_limit_bytes=VMEM_BYTES),
        cost_estimate=pl.CostEstimate(flops=0, bytes_accessed=0, transcendentals=0),
    )(*parts)


def small_kernel(need, send, at_ref, sums_ref, *outs):
    for place in range(2):
        conv, gain, shift, out_gain, out_shift = outs[5 * place : 5 * place + 5]
        rows = sums_ref[pl.ds(15 * place, 15), :]
        for top in range(3):
            conv[top] = rows[3 * top : 3 * top + 3]
        gain[pl.ds(0, 1), :] = rows[9:10]
        gain[pl.ds(1, 1), :] = rows[11:12]
        shift[pl.ds(0, 1), :] = rows[10:11]
        shift[pl.ds(1, 1), :] = rows[12:13]
        out_gain[...] = rows[13:14]
        out_shift[...] = rows[14:15]


class Near:
    def __init__(self, value):
        self.value = value


def like(*shape, dtype=FULL):
    return jax.ShapeDtypeStruct(shape, dtype)


def low(*shape):
    return like(*shape, dtype=LOW)


def places():
    return [lax.axis_index(axis) for axis in ("half", "im", "row")]


def call(kernel, outs, scratch, *args):
    near_in = [isinstance(arg, Near) for arg in args]
    near_out = [isinstance(out, Near) for out in outs]
    args = [arg.value if isinstance(arg, Near) else arg for arg in args]
    outs = [out.value if isinstance(out, Near) else out for out in outs]
    takes, gives = (len(args), len(outs))
    far_in = [at for at in range(takes) if not near_in[at]]
    far_out = [at for at in range(gives) if not near_out[at]]

    def body(*refs):
        given, refs = (list(refs[:takes]), refs[takes:])
        made, refs = (list(refs[:gives]), refs[gives:])
        rest = refs[len(far_in) + len(far_out) :]
        reads, writes = ({}, {})
        if far_in:
            in_sem = rest[-1]
            rest = rest[:-1]
        if far_out:
            out_sem = rest[-1]
            rest = rest[:-1]
        for place, at in enumerate(far_in):
            reads[at] = pltpu.make_async_copy(given[at], refs[place], in_sem.at[place])
            given[at] = refs[place]
        for place, at in enumerate(far_out):
            mirror = refs[len(far_in) + place]
            writes[at] = pltpu.make_async_copy(mirror, made[at], out_sem.at[place])
            made[at] = mirror
        for at in sorted(reads, key=lambda at: args[at].size):
            reads[at].start()
        started = []

        def need(*wanted):
            for at in list(reads):
                if any(given[at] is ref for ref in wanted):
                    reads.pop(at).wait()

        def send(*ready):
            for at in list(writes):
                if any(made[at] is ref for ref in ready):
                    started.append(writes.pop(at))
                    started[-1].start()

        kernel(need, send, places(), *given, *made, *rest)
        need(*given)
        send(*made)
        for write in started:
            write.wait()

    spaces = {True: pltpu.VMEM, False: pltpu.HBM}
    args = [
        pltpu.with_memory_space_constraint(arg, spaces[near]) for arg, near in zip(args, near_in)
    ]
    return pl.pallas_call(
        body,
        out_shape=[spaces[near](out.shape, out.dtype) for out, near in zip(outs, near_out)],
        in_specs=[pl.BlockSpec(memory_space=spaces[near]) for near in near_in],
        out_specs=[pl.BlockSpec(memory_space=spaces[near]) for near in near_out],
        scratch_shapes=[pltpu.VMEM(args[at].shape, args[at].dtype) for at in far_in]
        + [pltpu.VMEM(outs[at].shape, outs[at].dtype) for at in far_out]
        + [pltpu.VMEM(shape, FULL) for shape in scratch]
        + [pltpu.SemaphoreType.DMA((len(far_out),))] * bool(far_out)
        + [pltpu.SemaphoreType.DMA((len(far_in),))] * bool(far_in),
        compiler_params=pltpu.CompilerParams(vmem_limit_bytes=VMEM_BYTES),
        cost_estimate=pl.CostEstimate(flops=0, bytes_accessed=0, transcendentals=0),
    )(*args)


def edges(parity_edges):
    size = lax.axis_size("row")
    inner = [(at, at ^ 1) for at in range(size)]
    outer = [(at, at + 1) for at in range(1, size - 1, 2)]
    outer = outer + [(to, at) for at, to in outer]
    return (
        lax.ppermute(parity_edges[0], "row", inner),
        lax.ppermute(parity_edges[1], "row", outer),
    )


def swap(field):
    return lax.ppermute(field, "half", [(0, 1), (1, 0)])


def steps_of(value, axis, step):
    size = lax.axis_size(axis)
    return lax.ppermute(value, axis, [(at, at ^ step) for at in range(size)])


def share(parts, axis):
    return [parts[0]] + [steps_of(parts[at], axis, at) for at in range(1, len(parts))]


def share_same(part, axis):
    size = lax.axis_size(axis)
    return [part] + [steps_of(part, axis, at) for at in range(1, size)]


def gather_near(part):
    return [part, steps_of(part, "im", 1), steps_of(part, "im", 2)]


def gather_rest(parts):
    half = parts[0].shape[0] // 2
    return [steps_of(parts[1][:half], "im", 2), steps_of(parts[2][half:], "im", 1)]


def small_outputs(part, width):
    return [
        part[:9].reshape(3, 3, width),
        jnp.stack([part[9], part[11]]),
        jnp.stack([part[10], part[12]]),
        part[13],
        part[14],
    ]


def pair_outer(*pairs):
    size = lax.axis_size("im")
    first = pairs[0][0].value if isinstance(pairs[0][0], Near) else pairs[0][0]
    width = first.shape[1]
    rows = width // 2 // size * len(pairs)
    return list(
        call(
            functools.partial(pair_outer_kernel, pairs=len(pairs), parts=size),
            [Near(low(rows, width))] * size,
            [],
            *[ref for pair in pairs for ref in pair],
        )
    )


def sum_split(pieces, pairs):
    size = lax.axis_size("row")
    rows, width = pieces[0].shape
    return list(
        call(
            functools.partial(
                sum_split_kernel,
                pairs=pairs,
                parts=size,
                pieces=len(pieces),
            ),
            [Near(low(rows // size, width))] * size,
            [(rows, width)],
            *[Near(piece) for piece in pieces],
        )
    )


def add_low(pieces):
    total = pieces[0].astype(FULL)
    for piece in pieces[1:]:
        total = total + piece.astype(FULL)
    return total.astype(LOW)


def sum_far(left, right, axes):
    part = jnp.einsum("tm,tc->mc", left, right, preferred_element_type=FULL)
    return lax.psum(part, axes)


def shards(
    x_in,
    pre_reduce,
    pre_conv,
    pre_expand,
    pre_mid_gain,
    pre_mid_shift,
    pre_out_gain,
    pre_out_shift,
    post_reduce,
    post_conv,
    post_expand,
    post_mid_gain,
    post_mid_shift,
    post_out_gain,
    post_out_shift,
    read_weight,
    read_bias,
    cotangent,
):
    count, strip, side, width = x_in.shape
    strips = lax.axis_size("row")
    tokens = count * strip * side
    cols = side // 2
    rows = strip // 2
    slabs = count * rows
    padded = slabs * SLAB
    small = slabs * cols
    block = -(-small // SLAB) * SLAB
    features = read_weight.shape[1]
    x_low = x_in.reshape(tokens, width)
    pre_out_g, pre_out_s = (pre_out_gain[None], pre_out_shift[None])
    post_out_g, post_out_s = (post_out_gain[None], post_out_shift[None])
    pre_edge = Near(low(count, side, width))
    post_edge = Near(low(count, SLAB, width))
    quick = lax.axis_size("im") == 4 and strips == 4

    first, edge_a, edge_b, normed_a, factor_a = call(
        pre_reduce_kernel,
        [Near(low(tokens, width)), pre_edge, pre_edge, like(tokens, width), like(tokens, LANES)],
        [(tokens, width)],
        x_low,
        pre_reduce,
        pre_mid_gain,
        pre_mid_shift,
    )
    got_a, got_b = edges((edge_a, edge_b))
    (
        second,
        normed_b,
        factor_b,
        normed_c,
        factor_c,
        summed,
        pooled,
        post_first,
        edge_a,
        edge_b,
        post_normed_a,
        post_factor_a,
        pad,
    ) = call(
        pre_rest_kernel,
        [
            low(tokens, width),
            like(tokens, width),
            like(tokens, LANES),
            like(tokens, width),
            like(tokens, LANES),
            like(tokens, width),
            Near(like(padded, width)),
            Near(low(padded, width)),
            post_edge,
            post_edge,
            like(padded, width),
            like(padded, LANES),
            like(count, strip + 2, side, width),
        ],
        [(tokens, width), (side * width // LANES, LANES), (padded, width)],
        x_low,
        Near(first),
        Near(got_a),
        Near(got_b),
        pre_conv,
        pre_expand,
        pre_mid_gain,
        pre_mid_shift,
        pre_out_g,
        pre_out_s,
        post_reduce,
        post_mid_gain,
        post_mid_shift,
    )
    got_a, got_b = edges((edge_a, edge_b))
    (
        block_two,
        left_in,
        left_second,
        post_normed_b,
        post_factor_b,
        post_normed_c,
        post_factor_c,
        post_summed,
        post_pad,
    ) = call(
        functools.partial(post_rest_kernel, cols=cols),
        [
            Near(low(small, width)),
            low(block, width),
            low(block, width),
            like(padded, width),
            like(padded, LANES),
            like(padded, width),
            like(padded, LANES),
            like(padded, width),
            like(count, rows + 2, SLAB, width),
        ],
        [(padded, width), (padded, width), (block, width)],
        Near(pooled),
        Near(post_first),
        Near(got_a),
        Near(got_b),
        post_conv,
        post_expand,
        post_mid_gain,
        post_mid_shift,
        post_out_g,
        post_out_s,
    )
    whole = lax.all_gather(block_two, "row", axis=0, tiled=True)
    readout, grad_pre, *terms, d_read_b = call(
        functools.partial(readout_kernel, strips=strips),
        [
            like(*cotangent.shape, dtype=LOW),
            Near(low(strips * small, features)),
        ]
        + [Near(low(small, width))] * strips
        + [like(1, features)],
        [
            (strips * small, features),
            (strips * small, features),
            (strips * small, width),
        ],
        Near(whole),
        read_weight,
        read_bias[None],
        cotangent,
    )
    terms = share(terms, "row")
    post_gs, post_ge, post_gc, edge_a, edge_b, post_small_b = call(
        functools.partial(post_back_kernel, cols=cols, strips=strips),
        [
            Near(like(padded, width)),
            Near(low(block, width)),
            Near(low(padded, width)),
            post_edge,
            post_edge,
            like(4, width),
        ],
        [(block, width), (padded, width), (padded, width), (padded, width)],
        *[Near(term) for term in terms],
        post_expand,
        post_mid_gain,
        post_mid_shift,
        post_out_g,
        post_normed_b,
        post_factor_b,
        post_normed_c,
        post_factor_c,
        post_summed,
    )
    got_a, got_b = edges((edge_a, edge_b))
    (
        post_gr,
        pre_gs,
        pre_ge,
        pre_gc,
        edge_a,
        edge_b,
        post_small_a,
        pre_small_b,
    ) = call(
        functools.partial(middle_back_kernel, cols=cols),
        [
            Near(low(block, width)),
            like(tokens, width),
            Near(low(tokens, width)),
            Near(low(tokens, width)),
            pre_edge,
            pre_edge,
            like(11, width),
            like(4, width),
        ],
        [
            (count, rows + 2, SLAB, width),
            (9, 8, width),
            (padded, width),
            (side * width // LANES, LANES),
            (tokens, width),
            (2, 8, width),
            (padded, width),
            (block, width),
        ],
        Near(post_gc),
        Near(got_a),
        Near(got_b),
        post_pad,
        post_conv,
        post_reduce,
        post_mid_gain,
        post_mid_shift,
        post_normed_a,
        post_factor_a,
        Near(post_gs),
        pre_expand,
        pre_mid_gain,
        pre_mid_shift,
        pre_out_g,
        normed_b,
        factor_b,
        normed_c,
        factor_c,
        summed,
    )
    if quick:
        edge_a, left_in, left_second, post_ge, whole, grad_pre = tie(
            edge_a, left_in, left_second, post_ge, whole, grad_pre
        )
    got_a, got_b = edges((edge_a, edge_b))
    if quick:
        post_parts = pair_outer(
            (left_in, swap(left_in), Near(post_gr), Near(swap(post_gr))),
            (left_second, swap(left_second), Near(post_ge), Near(swap(post_ge))),
        )
        post_sums = share(post_parts, "im")[1:]
        got_a, whole, grad_pre = tie(got_a, whole, grad_pre)
        read_parts = pair_outer(
            (Near(whole), Near(swap(whole)), Near(grad_pre), Near(swap(grad_pre)))
        )
        (got_a, got_b), rest = tie_later((got_a, got_b), (*post_sums, *read_parts))
        post_sums, read_parts = (rest[:3], rest[3:])
    pre_gr, sums = call(
        pre_back_kernel,
        [Near(low(tokens, width)), Near(like(32, width))],
        [
            (count, strip + 2, side, width),
            (9, 8, width),
            (2, 8, width),
        ],
        Near(pre_gc),
        Near(got_a),
        Near(got_b),
        pad,
        pre_conv,
        pre_mid_gain,
        pre_mid_shift,
        normed_a,
        factor_a,
        pre_small_b,
        post_small_a,
        post_small_b,
        d_read_b,
    )
    if quick:
        far = swap(pre_gr)
        post_parts = sum_split(post_parts[:1] + post_sums, 2)
        post_parts[0], far = tie(post_parts[0], far)
        post_parts = share(post_parts, "row")
        parts = pair_outer(
            (second, swap(second), Near(pre_ge), Near(swap(pre_ge))),
            (x_low, swap(x_low), Near(pre_gr), Near(far)),
        )
        parts[0], sums = tie(parts[0], sums + swap(sums))
        read_last = read_parts[3]
        read_parts = read_parts[:1] + [steps_of(read_parts[at], "im", at) for at in (1, 2)]
        near_parts = [steps_of(parts[at], "im", at) for at in (1, 2)]
        grad_in = pre_gs + jnp.einsum("tm,cm->tc", pre_gr, pre_reduce, preferred_element_type=FULL)
        grad_in = grad_in.astype(LOW)
        post_parts, (grad_in, last, read_last, *rest) = tie_later(
            post_parts, (grad_in, parts[3], read_last, *near_parts, *read_parts)
        )
        near_parts, read_parts = (rest[:2], rest[2:])
        post_parts = share_same(add_low(post_parts), "row")
        last = steps_of(last, "im", 3)
        read_parts = read_parts + [steps_of(read_last, "im", 3)]
        post_parts, (last, *read_parts) = tie_later(post_parts, (last, *read_parts))
        parts = share(sum_split([parts[0]] + near_parts + [last], 2), "row")
        post_parts = gather_near(jnp.concatenate(post_parts, axis=0))
        read_parts = gather_near(add_low(read_parts))
        parts, rest = tie_later(parts, (*post_parts, *read_parts))
        post_parts, read_parts = (rest[:3], rest[3:])
        parts = share_same(add_low(parts), "row")
        read_parts.append(steps_of(read_parts[0], "im", 3))
        post_parts = post_parts + gather_rest(post_parts)
        parts, rest = tie_later(parts, (*post_parts, *read_parts, sums))
        post_parts, read_parts, sums = (rest[:5], rest[5:9], rest[9])
        parts = gather_near(jnp.concatenate(parts, axis=0))
        alone = lax.broadcasted_iota(jnp.int32, sums.shape, 0) >= 30
        for step in (1, 2):
            sums = sums + jnp.where(alone, 0.0, steps_of(sums, "row", step))
        parts, (sums, *post_parts) = tie_later(parts, (sums, *post_parts))
        far = swap(jnp.concatenate(parts, axis=0))
        post_far = swap(jnp.concatenate(post_parts, axis=0))
        read_far = swap(jnp.concatenate(read_parts, axis=0))
        far, post_far, read_far = tie(far, post_far, read_far)
        post_reduce_g, post_expand_g = assemble(post_parts, [post_far], 2, 4, strips)
        (read_total,) = assemble(read_parts, [read_far], 1, 4, 1)
        (post_reduce_g, read_total), (sums, *rest) = tie_later(
            (post_reduce_g, read_total), (sums, *gather_rest(parts))
        )
        far_rest = swap(jnp.concatenate(rest, axis=0))
        for step in (1, 2):
            sums = sums + steps_of(sums, "im", step)
        small_out = call(
            small_kernel,
            [like(3, 3, width), like(2, width), like(2, width), like(1, width), like(1, width)] * 2,
            [],
            Near(sums),
        )
        pre_expand_g, pre_reduce_g = assemble(parts + rest, [far, far_rest], 2, 4, strips)
        read_bias_g = sums[30]
    else:
        axes = IMG + ("row",)
        post_reduce_g = sum_far(left_in, post_gr, axes)
        post_expand_g = sum_far(left_second, post_ge, axes)
        pre_expand_g = sum_far(second, pre_ge, axes)
        pre_reduce_g = sum_far(x_low, pre_gr, axes)
        read_total = sum_far(whole, grad_pre, IMG)
        read_bias_g = lax.psum(sums[30], IMG)
        sums = lax.psum(sums[:30], axes)
        small_out = small_outputs(sums[:15], width) + small_outputs(sums[15:30], width)
        grad_in = pre_gs + jnp.einsum("tm,cm->tc", pre_gr, pre_reduce, preferred_element_type=FULL)
        grad_in = grad_in.astype(LOW)

    pre_conv_g, pre_gain_g, pre_shift_g, pre_og_g, pre_os_g = small_out[:5]
    post_conv_g, post_gain_g, post_shift_g, post_og_g, post_os_g = small_out[5:]
    return (
        readout,
        grad_in.reshape(x_in.shape),
        pre_reduce_g,
        pre_conv_g,
        pre_expand_g,
        pre_gain_g,
        pre_shift_g,
        pre_og_g.reshape(width),
        pre_os_g.reshape(width),
        post_reduce_g,
        post_conv_g,
        post_expand_g,
        post_gain_g,
        post_shift_g,
        post_og_g.reshape(width),
        post_os_g.reshape(width),
        read_total,
        read_bias_g,
    )


def solution(mesh):
    images, strips = mesh.devices.shape
    split = jax.sharding.Mesh(
        mesh.devices.reshape(images // 2, 2, strips), ("im", "half", "row")
    )
    return jax.shard_map(
        shards,
        mesh=split,
        in_specs=(P(IMG, "row", None, None),)
        + (P(),) * 14
        + (P(None, "row"), P("row"), P(IMG, None, None, "row")),
        out_specs=(P(IMG, None, None, "row"), P(IMG, "row", None, None))
        + (P(),) * 14
        + (P(None, "row"), P("row")),
        check_vma=False,
    )
```

```python
import functools

import jax
import jax.numpy as jnp
from jax import lax
from jax.experimental import pallas as pl
from jax.experimental.pallas import tpu as pltpu
from jax.sharding import PartitionSpec as P

EPSILON = 1e-06
SQRT_HALF = 0.7071067811865476
INV_SQRT_TWO_PI = 0.3989422804014327
LOW = jnp.bfloat16
FULL = jnp.float32
IMG = ("im", "half")
TILE = 256
SLAB = 16
LANES = 128
VMEM_BYTES = 24 * 1024 * 1024


def tie(*values):
    return lax.optimization_barrier(values)


def tie_later(first, second):
    first = list(tie(*first))
    out = list(tie(*first, *second))
    return (out[: len(first)], out[len(first) :])


def norm(value):
    centred = value - jnp.mean(value, axis=-1, keepdims=True)
    factor = lax.rsqrt(jnp.mean(centred * centred, axis=-1, keepdims=True) + EPSILON)
    return (centred * factor, factor)


def norm_back(grad, normed, factor, gain):
    scaled = grad * gain
    return factor * (
        scaled
        - jnp.mean(scaled, axis=-1, keepdims=True)
        - normed * jnp.mean(scaled * normed, axis=-1, keepdims=True)
    )


def gate(value):
    return 0.5 * jnp.tanh(0.5 * value) + 0.5


def silu(value):
    return value * gate(value)


def silu_back(grad, value):
    sigma = gate(value)
    return grad * sigma * (1.0 + value * (1.0 - sigma))


def flip(place, step):
    bit = 1
    while bit <= step:
        if step & bit:
            place = place + bit - 2 * bit * ((place // bit) % 2)
        bit *= 2
    return place


def wide(factor):
    return jnp.broadcast_to(factor, (factor.shape[0], LANES))


def fold(value):
    return jnp.sum(value.reshape(-1, 8, value.shape[-1]), axis=0)


def live(rows, cols):
    at = lax.broadcasted_iota(jnp.int32, (rows, 1), 0)
    return lax.rem(at, SLAB) < cols


def from_left(value):
    at = lax.broadcasted_iota(jnp.int32, (value.shape[0], 1), 0)
    return jnp.where(at == 0, 0.0, pltpu.roll(value, 1, 0))


def from_right(value):
    last = value.shape[0] - 1
    at = lax.broadcasted_iota(jnp.int32, (value.shape[0], 1), 0)
    return jnp.where(at == last, 0.0, pltpu.roll(value, last, 0))


def matmul(left_ref, right_ref, out_ref):
    @pl.loop(0, right_ref.shape[1] // TILE)
    def _(at):
        cols = pl.ds(pl.multiple_of(at * TILE, TILE), TILE)
        out_ref[:, cols] = jnp.dot(
            left_ref[...].astype(LOW), right_ref[:, cols], preferred_element_type=FULL
        )


def matmul_back(left_ref, right_ref, out_ref):
    @pl.loop(0, right_ref.shape[0] // TILE)
    def _(at):
        cols = pl.ds(pl.multiple_of(at * TILE, TILE), TILE)
        out_ref[:, cols] = lax.dot_general(
            left_ref[...].astype(LOW),
            right_ref[cols, :],
            (((1,), (1,)), ((), ())),
            preferred_element_type=FULL,
        ).astype(out_ref.dtype)


def rows_of(at, size):
    return pl.ds(pl.multiple_of(at * size, SLAB), size)


def fill_halo(at_ref, pad_ref, low_ref, got_a_ref, got_b_ref):
    count, rows, cols, width = pad_ref.shape
    rows = rows - 2
    even = lax.rem(at_ref[2], 2) == 0
    for image in range(count):
        got_a, got_b = (got_a_ref[image].astype(FULL), got_b_ref[image].astype(FULL))
        pad_ref[image, 0] = jnp.where(even, got_b, got_a)
        pad_ref[image, rows + 1] = jnp.where(even, got_a, got_b)

    size = cols if cols % SLAB == 0 else 2 * cols
    per = size // cols
    each = rows // per

    @pl.loop(0, count * each)
    def _(at):
        part = low_ref[rows_of(at, size), :].astype(FULL).reshape(per, cols, width)
        pad_ref[at // each, pl.ds(1 + per * lax.rem(at, each), per)] = part


def set_edges(at_ref, edge_a_ref, edge_b_ref, image, head, tail):
    even = lax.rem(at_ref[2], 2) == 0
    edge_a_ref[image] = jnp.where(even, tail, head).astype(LOW)
    edge_b_ref[image] = jnp.where(even, head, tail).astype(LOW)


def conv_row(pad_ref, taps, image, row):
    lines = [pad_ref[image, row + top] for top in range(3)]
    sums = [
        lines[0] * taps[left] + lines[1] * taps[3 + left] + lines[2] * taps[6 + left]
        for left in range(3)
    ]
    return from_left(sums[0]) + sums[1] + from_right(sums[2])


def conv_back_row(pad_ref, grad_ref, taps, taps_ref, image, row):
    lines = [grad_ref[image, row + top] for top in range(3)]
    sums = [
        lines[2] * taps[left] + lines[1] * taps[3 + left] + lines[0] * taps[6 + left]
        for left in range(3)
    ]
    shifted = [from_right(lines[1]), lines[1], from_left(lines[1])]
    for top in range(3):
        source = pad_ref[image, row + top]
        for left in range(3):
            taps_ref[3 * top + left] += fold(source * shifted[left])
    return from_right(sums[0]) + sums[1] + from_left(sums[2])


def pack(compact, source, out_ref, cols):
    compact[...] = jnp.zeros(compact.shape, FULL)
    for at in range(source.shape[0] // SLAB):
        compact[pl.ds(at * cols, cols), :] = source[pl.ds(at * SLAB, cols), :]
    out_ref[...] = compact[...].astype(LOW)


def narrow(pair, value):
    side = value.shape[0]
    parts = []
    for at in range(value.shape[1] // LANES):
        pair[pl.ds(at * side, side), :] = value[:, at * LANES : (at + 1) * LANES]
        parts.append(
            pair[pl.ds(at * side, side // 2, stride=2), :]
            + pair[pl.ds(at * side + 1, side // 2, stride=2), :]
        )
    return jnp.concatenate(parts, axis=1)


def widen(pair, value):
    cols = value.shape[0]
    parts = []
    for at in range(value.shape[1] // LANES):
        part = value[:, at * LANES : (at + 1) * LANES]
        pair[pl.ds(2 * cols * at, cols, stride=2), :] = part
        pair[pl.ds(2 * cols * at + 1, cols, stride=2), :] = part
        parts.append(pair[pl.ds(2 * cols * at, 2 * cols), :])
    return jnp.concatenate(parts, axis=1)


def tap_rows(conv_ref):
    lines = [conv_ref[top].astype(FULL) for top in range(3)]
    return [lines[at // 3][at % 3 : at % 3 + 1] for at in range(9)]


def finish(small_ref, sums_ref, at, place):
    small_ref[pl.ds(place, 1), :] = jnp.sum(sums_ref[at], axis=0, keepdims=True)


def pre_reduce_kernel(
    need,
    send,
    at_ref,
    x_ref, w_ref, gain_ref, shift_ref, first_ref, edge_a_ref, edge_b_ref, normed_ref, factor_ref, red
):
    count, side, width = edge_a_ref.shape
    size = 2 * side
    steps = x_ref.shape[0] // size
    need(x_ref, w_ref)
    matmul(x_ref, w_ref, red)
    need(gain_ref, shift_ref)
    gain, shift = (gain_ref[pl.ds(0, 1), :], shift_ref[pl.ds(0, 1), :])

    @pl.loop(0, steps)
    def _(at):
        rows = rows_of(at, size)
        normed, factor = norm(red[rows, :])
        normed_ref[rows, :] = normed
        factor_ref[rows, :] = wide(factor)
        first_ref[rows, :] = silu(normed * gain + shift).astype(LOW)

    each = steps // count
    for image in range(count):
        head = first_ref[pl.ds(image * each * size, size), :].astype(FULL)
        tail = first_ref[pl.ds((image * each + each - 1) * size, size), :].astype(FULL)
        set_edges(at_ref, edge_a_ref, edge_b_ref, image, head[:side], tail[side:])


def pre_rest_kernel(
    need,
    send,
    at_ref,
    x_ref,
    first_ref,
    got_a_ref,
    got_b_ref,
    conv_ref,
    expand_ref,
    gain_ref,
    shift_ref,
    out_gain_ref,
    out_shift_ref,
    reduce_ref,
    post_gain_ref,
    post_shift_ref,
    second_ref,
    normed_b_ref,
    factor_b_ref,
    normed_c_ref,
    factor_c_ref,
    summed_ref,
    pooled_ref,
    post_first_ref,
    edge_a_ref,
    edge_b_ref,
    post_normed_ref,
    post_factor_ref,
    pad,
    exp,
    pair,
    red,
):
    count, strip, side, width = pad.shape
    strip = strip - 2
    size = 2 * side
    each = strip // 2
    need(first_ref, got_a_ref, got_b_ref)
    fill_halo(at_ref, pad, first_ref, got_a_ref, got_b_ref)
    need(conv_ref, gain_ref, shift_ref)
    send(pad)
    taps = tap_rows(conv_ref)
    gain, shift = (gain_ref[pl.ds(1, 1), :], shift_ref[pl.ds(1, 1), :])

    @pl.loop(0, count * each)
    def _(at):
        rows = rows_of(at, size)
        image, row = (at // each, 2 * lax.rem(at, each))
        conv = jnp.concatenate(
            [conv_row(pad, taps, image, row), conv_row(pad, taps, image, row + 1)], axis=0
        )
        normed, factor = norm(conv)
        normed_b_ref[rows, :] = normed
        factor_b_ref[rows, :] = wide(factor)
        second_ref[rows, :] = silu(normed * gain + shift).astype(LOW)

    send(second_ref, normed_b_ref, factor_b_ref)
    need(expand_ref)
    matmul(second_ref, expand_ref, exp)
    need(x_ref, out_gain_ref, out_shift_ref)
    out_gain, out_shift = (out_gain_ref[...], out_shift_ref[...])
    cols = side // 2
    for at in range(count * each):
        rows = pl.ds(at * size, size)
        normed, factor = norm(exp[rows, :])
        normed_c_ref[rows, :] = normed
        factor_c_ref[rows, :] = wide(factor)
        summed = x_ref[rows, :].astype(FULL) + normed * out_gain + out_shift
        summed_ref[rows, :] = summed
        block = silu(summed)
        half = narrow(pair, block[:side] + block[side:])
        pooled_ref[pl.ds(at * SLAB, cols), :] = 0.25 * half
        pooled_ref[pl.ds(at * SLAB + cols, SLAB - cols), :] = jnp.zeros(
            (SLAB - cols, width), FULL
        )
    send(normed_c_ref, factor_c_ref, summed_ref)
    need(reduce_ref, post_gain_ref, post_shift_ref)
    matmul(pooled_ref, reduce_ref, red)
    normed, factor = norm(red[...])
    post_normed_ref[...] = normed
    post_factor_ref[...] = wide(factor)
    first = silu(normed * post_gain_ref[pl.ds(0, 1), :] + post_shift_ref[pl.ds(0, 1), :])
    post_first_ref[...] = jnp.where(live(red.shape[0], cols), first, 0.0).astype(LOW)
    for image in range(count):
        head = post_first_ref[pl.ds(image * each * SLAB, SLAB), :].astype(FULL)
        tail = post_first_ref[pl.ds((image * each + each - 1) * SLAB, SLAB), :].astype(FULL)
        set_edges(at_ref, edge_a_ref, edge_b_ref, image, head, tail)


def post_rest_kernel(
    need,
    send,
    at_ref,
    pooled_ref,
    first_ref,
    got_a_ref,
    got_b_ref,
    conv_ref,
    expand_ref,
    gain_ref,
    shift_ref,
    out_gain_ref,
    out_shift_ref,
    block_ref,
    left_in_ref,
    left_second_ref,
    normed_b_ref,
    factor_b_ref,
    normed_c_ref,
    factor_c_ref,
    summed_ref,
    pad,
    second,
    exp,
    compact,
    *,
    cols
):
    count, rows, _, width = pad.shape
    rows = rows - 2
    small = block_ref.shape[0]
    need(first_ref, got_a_ref, got_b_ref)
    fill_halo(at_ref, pad, first_ref, got_a_ref, got_b_ref)
    send(pad)
    need(conv_ref, gain_ref, shift_ref, pooled_ref)
    taps = tap_rows(conv_ref)
    gain, shift = (gain_ref[pl.ds(1, 1), :], shift_ref[pl.ds(1, 1), :])

    @pl.loop(0, count * rows)
    def _(at):
        place = rows_of(at, SLAB)
        normed, factor = norm(conv_row(pad, taps, at // rows, lax.rem(at, rows)))
        normed_b_ref[place, :] = normed
        factor_b_ref[place, :] = wide(factor)
        second[place, :] = silu(normed * gain + shift)

    send(normed_b_ref, factor_b_ref)
    need(expand_ref)
    matmul(second, expand_ref, exp)
    need(out_gain_ref, out_shift_ref)
    normed, factor = norm(exp[...])
    normed_c_ref[...] = normed
    factor_c_ref[...] = wide(factor)
    summed = pooled_ref[...] + normed * out_gain_ref[...] + out_shift_ref[...]
    summed_ref[...] = summed
    exp[...] = silu(summed)
    compact[...] = jnp.zeros(compact.shape, FULL)
    for at in range(count * rows):
        compact[pl.ds(at * cols, cols), :] = exp[pl.ds(at * SLAB, cols), :]
    block_ref[...] = compact[pl.ds(0, small), :].astype(LOW)
    send(block_ref, normed_c_ref, factor_c_ref, summed_ref)
    pack(compact, pooled_ref, left_in_ref, cols)
    pack(compact, second, left_second_ref, cols)


def readout_kernel(
    need,
    send,
    at_ref,
    whole_ref,
    w_ref,
    bias_ref,
    cot_ref,
    out_ref,
    grad_ref,
    *refs,
    strips
):
    slots, (bias_grad_ref, cot, out, terms_ref) = (refs[:strips], refs[strips:])
    images, lines, cols, _ = cot_ref.shape
    rows = lines // strips
    need(cot_ref)
    for at in range(images * lines):
        strip, image, row = (at // (images * rows), at // rows % images, at % rows)
        cot[pl.ds(at * cols, cols), :] = cot_ref[image, strip * rows + row].astype(FULL)
    need(whole_ref, w_ref, bias_ref)

    @pl.loop(0, w_ref.shape[1] // TILE)
    def _(at):
        lanes = pl.ds(pl.multiple_of(at * TILE, TILE), TILE)
        act = jnp.dot(whole_ref[...], w_ref[:, lanes], preferred_element_type=FULL)
        act = act + bias_ref[:, lanes]
        cdf = 0.5 * (1.0 + lax.erf(act * SQRT_HALF))
        density = jnp.exp(-0.5 * act * act) * INV_SQRT_TWO_PI
        out[:, lanes] = act * cdf
        grad = (cot[:, lanes] * (cdf + act * density)).astype(LOW)
        grad_ref[:, lanes] = grad
        bias_grad_ref[:, lanes] = jnp.sum(grad.astype(FULL), axis=0, keepdims=True)

    send(grad_ref, bias_grad_ref)
    matmul_back(grad_ref, w_ref, terms_ref)
    small = slots[0].shape[0]
    for step in range(strips):
        begin = pl.multiple_of(flip(at_ref[2], step) * small, 8)
        slots[step][...] = terms_ref[pl.ds(begin, small), :].astype(LOW)
    for at in range(images * lines):
        strip, image, row = (at // (images * rows), at // rows % images, at % rows)
        out_ref[image, strip * rows + row] = out[pl.ds(at * cols, cols), :].astype(LOW)


def post_back_kernel(
    need,
    send,
    at_ref,
    *refs,
    cols,
    strips
):
    pieces, refs = (refs[:strips], refs[strips:])
    (
    expand_ref,
    gain_ref,
    shift_ref,
    out_gain_ref,
    normed_b_ref,
    factor_b_ref,
    normed_c_ref,
    factor_c_ref,
    summed_ref,
    grad_sum_ref,
    grad_exp_ref,
    grad_conv_ref,
    edge_a_ref,
    edge_b_ref,
    small_ref,
    compact,
    spread_out,
    exp,
    sec,
    ) = refs
    count = edge_a_ref.shape[0]
    tokens, width = grad_sum_ref.shape
    each = tokens // SLAB // count
    need(*pieces)
    total = pieces[0][...].astype(FULL)
    for piece in pieces[1:]:
        total = total + piece[...].astype(FULL)
    compact[...] = jnp.zeros(compact.shape, FULL)
    compact[pl.ds(0, total.shape[0]), :] = total
    spread_out[...] = jnp.zeros((tokens, width), FULL)
    for at in range(tokens // SLAB):
        spread_out[pl.ds(at * SLAB, cols), :] = compact[pl.ds(at * cols, cols), :]
    need(summed_ref, normed_c_ref, factor_c_ref, out_gain_ref)
    grad_sum = silu_back(spread_out[...], summed_ref[...])
    grad_sum_ref[...] = grad_sum
    normed = normed_c_ref[...]
    exp[...] = norm_back(grad_sum, normed, factor_c_ref[:, :1], out_gain_ref[...])
    small_ref[pl.ds(2, 1), :] = jnp.sum(grad_sum * normed, axis=0, keepdims=True)
    small_ref[pl.ds(3, 1), :] = jnp.sum(grad_sum, axis=0, keepdims=True)
    pack(compact, exp, grad_exp_ref, cols)
    send(grad_sum_ref, grad_exp_ref)
    need(expand_ref)
    matmul_back(exp, expand_ref, sec)
    need(gain_ref, shift_ref, normed_b_ref, factor_b_ref)
    gain, shift = (gain_ref[pl.ds(1, 1), :], shift_ref[pl.ds(1, 1), :])
    normed = normed_b_ref[...]
    grad = silu_back(sec[...], normed * gain + shift)
    grad_conv_ref[...] = norm_back(grad, normed, factor_b_ref[:, :1], gain).astype(LOW)
    small_ref[pl.ds(0, 1), :] = jnp.sum(grad * normed, axis=0, keepdims=True)
    small_ref[pl.ds(1, 1), :] = jnp.sum(grad, axis=0, keepdims=True)
    for image in range(count):
        head = grad_conv_ref[pl.ds(image * each * SLAB, SLAB), :].astype(FULL)
        tail = grad_conv_ref[pl.ds((image * each + each - 1) * SLAB, SLAB), :].astype(FULL)
        set_edges(at_ref, edge_a_ref, edge_b_ref, image, head, tail)


def middle_back_kernel(
    need,
    send,
    at_ref,
    grad_conv_ref,
    got_a_ref,
    got_b_ref,
    pad,
    post_conv_ref,
    post_reduce_ref,
    post_gain_ref,
    post_shift_ref,
    post_normed_ref,
    post_factor_ref,
    post_grad_sum_ref,
    expand_ref,
    gain_ref,
    shift_ref,
    out_gain_ref,
    normed_b_ref,
    factor_b_ref,
    normed_c_ref,
    factor_c_ref,
    summed_ref,
    post_grad_red_ref,
    grad_sum_ref,
    grad_exp_ref,
    pre_grad_conv_ref,
    edge_a_ref,
    edge_b_ref,
    post_small_ref,
    small_ref,
    grad_pad,
    taps_sum,
    grad_in,
    pair,
    sec,
    sums,
    post_red,
    compact,
    *,
    cols
):
    count, side, width = edge_a_ref.shape
    need(grad_conv_ref, got_a_ref, got_b_ref)
    fill_halo(at_ref, grad_pad, grad_conv_ref, got_a_ref, got_b_ref)
    need(pad, post_conv_ref)
    need(post_gain_ref, post_shift_ref, post_normed_ref, post_factor_ref)
    taps = tap_rows(post_conv_ref)
    taps_sum[...] = jnp.zeros_like(taps_sum)
    sums[...] = jnp.zeros_like(sums)
    gain, shift = (post_gain_ref[pl.ds(0, 1), :], post_shift_ref[pl.ds(0, 1), :])
    each = post_grad_sum_ref.shape[0] // SLAB // count

    @pl.loop(0, count * each)
    def _(at):
        place = rows_of(at, SLAB)
        grad = conv_back_row(pad, grad_pad, taps, taps_sum, at // each, lax.rem(at, each))
        normed = post_normed_ref[place, :]
        grad = jnp.where(live(SLAB, cols), silu_back(grad, normed * gain + shift), 0.0)
        sums[0] += fold(grad * normed)
        sums[1] += fold(grad)
        post_red[place, :] = norm_back(grad, normed, post_factor_ref[place, :1], gain)

    for at in range(9):
        finish(post_small_ref, taps_sum, at, at)
    finish(post_small_ref, sums, 0, 9)
    finish(post_small_ref, sums, 1, 10)
    pack(compact, post_red, post_grad_red_ref, cols)
    send(post_grad_red_ref, post_small_ref)
    need(post_reduce_ref)
    matmul_back(post_red, post_reduce_ref, grad_in)
    sums[...] = jnp.zeros_like(sums)
    size = 2 * side
    need(out_gain_ref, post_grad_sum_ref, summed_ref, normed_c_ref, factor_c_ref)
    out_gain = out_gain_ref[...]
    for at in range(count * each):
        rows = pl.ds(at * size, size)
        place = pl.ds(at * SLAB, cols)
        grad = 0.25 * (post_grad_sum_ref[place, :] + grad_in[place, :])
        grad = widen(pair, grad)
        grad = jnp.concatenate([grad, grad], axis=0)
        grad_sum = silu_back(grad, summed_ref[rows, :])
        grad_sum_ref[rows, :] = grad_sum
        normed = normed_c_ref[rows, :]
        sums[0] += fold(grad_sum * normed)
        sums[1] += fold(grad_sum)
        grad_exp_ref[rows, :] = norm_back(
            grad_sum, normed, factor_c_ref[rows, :1], out_gain
        ).astype(LOW)
    finish(small_ref, sums, 0, 2)
    finish(small_ref, sums, 1, 3)
    send(grad_sum_ref, grad_exp_ref)
    need(expand_ref)
    matmul_back(grad_exp_ref, expand_ref, sec)
    need(gain_ref, shift_ref, normed_b_ref, factor_b_ref)
    sums[...] = jnp.zeros_like(sums)
    gain_b, shift_b = (gain_ref[pl.ds(1, 1), :], shift_ref[pl.ds(1, 1), :])

    @pl.loop(0, count * each)
    def _(at):
        rows = rows_of(at, size)
        normed = normed_b_ref[rows, :]
        grad = silu_back(sec[rows, :], normed * gain_b + shift_b)
        sums[0] += fold(grad * normed)
        sums[1] += fold(grad)
        pre_grad_conv_ref[rows, :] = norm_back(
            grad, normed, factor_b_ref[rows, :1], gain_b
        ).astype(LOW)

    finish(small_ref, sums, 0, 0)
    finish(small_ref, sums, 1, 1)
    for image in range(count):
        head = pre_grad_conv_ref[pl.ds(image * each * size, size), :].astype(FULL)
        tail = pre_grad_conv_ref[pl.ds((image * each + each - 1) * size, size), :].astype(FULL)
        set_edges(at_ref, edge_a_ref, edge_b_ref, image, head[:side], tail[side:])


def pre_back_kernel(
    need,
    send,
    at_ref,
    grad_conv_ref,
    got_a_ref,
    got_b_ref,
    pad,
    conv_ref,
    gain_ref,
    shift_ref,
    normed_ref,
    factor_ref,
    small_b_ref,
    post_small_a_ref,
    post_small_b_ref,
    read_bias_ref,
    grad_red_ref,
    small_ref,
    grad_pad,
    taps_sum,
    sums,
):
    count, strip, side, width = pad.shape
    strip = strip - 2
    size = 2 * side
    each = strip // 2
    need(grad_conv_ref, got_a_ref, got_b_ref)
    fill_halo(at_ref, grad_pad, grad_conv_ref, got_a_ref, got_b_ref)
    need(pad, conv_ref)
    need(gain_ref, shift_ref, normed_ref, factor_ref)
    taps = tap_rows(conv_ref)
    taps_sum[...] = jnp.zeros_like(taps_sum)
    sums[...] = jnp.zeros_like(sums)
    gain, shift = (gain_ref[pl.ds(0, 1), :], shift_ref[pl.ds(0, 1), :])

    @pl.loop(0, count * each)
    def _(at):
        rows = rows_of(at, size)
        image, row = (at // each, 2 * lax.rem(at, each))
        grad = jnp.concatenate(
            [
                conv_back_row(pad, grad_pad, taps, taps_sum, image, row),
                conv_back_row(pad, grad_pad, taps, taps_sum, image, row + 1),
            ],
            axis=0,
        )
        normed = normed_ref[rows, :]
        grad = silu_back(grad, normed * gain + shift)
        sums[0] += fold(grad * normed)
        sums[1] += fold(grad)
        grad_red_ref[rows, :] = norm_back(grad, normed, factor_ref[rows, :1], gain).astype(LOW)

    for at in range(9):
        finish(small_ref, taps_sum, at, at)
    finish(small_ref, sums, 0, 9)
    finish(small_ref, sums, 1, 10)
    need(small_b_ref, post_small_a_ref, post_small_b_ref, read_bias_ref)
    small_ref[pl.ds(11, 4), :] = small_b_ref[...]
    small_ref[pl.ds(15, 11), :] = post_small_a_ref[...]
    small_ref[pl.ds(26, 4), :] = post_small_b_ref[...]
    small_ref[pl.ds(30, 1), :] = read_bias_ref[...]
    small_ref[pl.ds(31, 1), :] = jnp.zeros_like(read_bias_ref)


def pair_outer_kernel(need, send, at_ref, *refs, pairs, parts):
    takes = 4 * pairs
    outs = refs[takes:]
    half, plane = (at_ref[0], at_ref[1])
    rows = outs[0].shape[0] // pairs
    for pair in range(pairs):
        left, left_far, right, right_far = refs[4 * pair : 4 * pair + 4]
        need(left, left_far, right, right_far)
        for step in range(parts):
            begin = half * (rows * parts) + flip(plane, step) * rows
            lanes = pl.ds(pl.multiple_of(begin, LANES), rows)
            total = lax.dot_general(
                left[:, lanes], right[...], (((0,), (0,)), ((), ())), preferred_element_type=FULL
            ) + lax.dot_general(
                left_far[:, lanes],
                right_far[...],
                (((0,), (0,)), ((), ())),
                preferred_element_type=FULL,
            )
            outs[step][pl.ds(pair * rows, rows), :] = total.astype(LOW)
    send(*outs)


def sum_split_kernel(need, send, at_ref, *refs, pairs, parts, pieces, along=2):
    takes, outs = (refs[:pieces], refs[pieces : pieces + parts])
    total = refs[-1]
    need(*takes)
    value = takes[0][...].astype(FULL)
    for at in range(1, pieces):
        value = value + takes[at][...].astype(FULL)
    total[...] = value
    rows = total.shape[0] // pairs // parts
    for step in range(parts):
        begin = flip(at_ref[along], step) * rows
        for pair in range(pairs):
            place = pl.ds(pl.multiple_of(pair * rows * parts + begin, SLAB), rows)
            outs[step][pl.ds(pair * rows, rows), :] = total[place, :].astype(LOW)
    send(*outs)


def assemble_kernel(*refs, spans, pairs, planes, strips):
    takes = len(spans)
    parts, outs = (refs[:takes], refs[takes : takes + pairs])
    full, sem = (refs[takes + pairs : takes + 2 * pairs], refs[-1])
    half, plane, row = places()
    rows = spans[0] // pairs // strips
    block = strips * rows
    pieces = []
    for part, span in zip(parts, spans):
        pieces += [(part, begin) for begin in range(0, span, pairs * rows)]
    writes = []
    for pair in range(pairs):
        for at in range(2 * planes * strips):
            near, step = (at // strips, at % strips)
            side, spot = (flip(half, near // planes), flip(plane, near % planes))
            place = side * (planes * block) + spot * block
            if strips > 1:
                place = place + flip(row, step) * rows
            part, begin = pieces[at]
            full[pair][pl.ds(pl.multiple_of(place, SLAB), rows), :] = part[
                pl.ds(begin + pair * rows, rows), :
            ].astype(FULL)
        writes.append(pltpu.make_async_copy(full[pair], outs[pair], sem.at[pair]))
        writes[-1].start()
    for write in writes:
        write.wait()


def assemble(parts, far, pairs, planes, strips):
    out = like(2 * planes * parts[0].shape[0] // pairs, parts[0].shape[1])
    parts = [pltpu.with_memory_space_constraint(part, pltpu.VMEM) for part in parts + far]
    return pl.pallas_call(
        functools.partial(
            assemble_kernel,
            spans=[part.shape[0] for part in parts],
            pairs=pairs,
            planes=planes,
            strips=strips,
        ),
        out_shape=[pltpu.HBM(out.shape, out.dtype)] * pairs,
        in_specs=[pl.BlockSpec(memory_space=pltpu.VMEM)] * len(parts),
        out_specs=[pl.BlockSpec(memory_space=pltpu.HBM)] * pairs,
        scratch_shapes=[pltpu.VMEM(out.shape, FULL)] * pairs + [pltpu.SemaphoreType.DMA((pairs,))],
        compiler_params=pltpu.CompilerParams(vmem_limit_bytes=VMEM_BYTES),
        cost_estimate=pl.CostEstimate(flops=0, bytes_accessed=0, transcendentals=0),
    )(*parts)


def small_kernel(need, send, at_ref, sums_ref, *outs):
    for place in range(2):
        conv, gain, shift, out_gain, out_shift = outs[5 * place : 5 * place + 5]
        rows = sums_ref[pl.ds(15 * place, 15), :]
        for top in range(3):
            conv[top] = rows[3 * top : 3 * top + 3]
        gain[pl.ds(0, 1), :] = rows[9:10]
        gain[pl.ds(1, 1), :] = rows[11:12]
        shift[pl.ds(0, 1), :] = rows[10:11]
        shift[pl.ds(1, 1), :] = rows[12:13]
        out_gain[...] = rows[13:14]
        out_shift[...] = rows[14:15]


class Near:
    def __init__(self, value):
        self.value = value


def like(*shape, dtype=FULL):
    return jax.ShapeDtypeStruct(shape, dtype)


def low(*shape):
    return like(*shape, dtype=LOW)


def places():
    return [lax.axis_index(axis) for axis in ("half", "im", "row")]


def call(kernel, outs, scratch, *args):
    near_in = [isinstance(arg, Near) for arg in args]
    near_out = [isinstance(out, Near) for out in outs]
    args = [arg.value if isinstance(arg, Near) else arg for arg in args]
    outs = [out.value if isinstance(out, Near) else out for out in outs]
    takes, gives = (len(args), len(outs))
    far_in = [at for at in range(takes) if not near_in[at]]
    far_out = [at for at in range(gives) if not near_out[at]]

    def body(*refs):
        given, refs = (list(refs[:takes]), refs[takes:])
        made, refs = (list(refs[:gives]), refs[gives:])
        rest = refs[len(far_in) + len(far_out) :]
        reads, writes = ({}, {})
        if far_in:
            in_sem = rest[-1]
            rest = rest[:-1]
        if far_out:
            out_sem = rest[-1]
            rest = rest[:-1]
        for place, at in enumerate(far_in):
            reads[at] = pltpu.make_async_copy(given[at], refs[place], in_sem.at[place])
            given[at] = refs[place]
        for place, at in enumerate(far_out):
            mirror = refs[len(far_in) + place]
            writes[at] = pltpu.make_async_copy(mirror, made[at], out_sem.at[place])
            made[at] = mirror
        for at in sorted(reads, key=lambda at: args[at].size):
            reads[at].start()
        started = []

        def need(*wanted):
            for at in list(reads):
                if any(given[at] is ref for ref in wanted):
                    reads.pop(at).wait()

        def send(*ready):
            for at in list(writes):
                if any(made[at] is ref for ref in ready):
                    started.append(writes.pop(at))
                    started[-1].start()

        kernel(need, send, places(), *given, *made, *rest)
        need(*given)
        send(*made)
        for write in started:
            write.wait()

    spaces = {True: pltpu.VMEM, False: pltpu.HBM}
    args = [
        pltpu.with_memory_space_constraint(arg, spaces[near]) for arg, near in zip(args, near_in)
    ]
    return pl.pallas_call(
        body,
        out_shape=[spaces[near](out.shape, out.dtype) for out, near in zip(outs, near_out)],
        in_specs=[pl.BlockSpec(memory_space=spaces[near]) for near in near_in],
        out_specs=[pl.BlockSpec(memory_space=spaces[near]) for near in near_out],
        scratch_shapes=[pltpu.VMEM(args[at].shape, args[at].dtype) for at in far_in]
        + [pltpu.VMEM(outs[at].shape, outs[at].dtype) for at in far_out]
        + [pltpu.VMEM(shape, FULL) for shape in scratch]
        + [pltpu.SemaphoreType.DMA((len(far_out),))] * bool(far_out)
        + [pltpu.SemaphoreType.DMA((len(far_in),))] * bool(far_in),
        compiler_params=pltpu.CompilerParams(vmem_limit_bytes=VMEM_BYTES),
        cost_estimate=pl.CostEstimate(flops=0, bytes_accessed=0, transcendentals=0),
    )(*args)


def edges(parity_edges):
    size = lax.axis_size("row")
    inner = [(at, at ^ 1) for at in range(size)]
    outer = [(at, at + 1) for at in range(1, size - 1, 2)]
    outer = outer + [(to, at) for at, to in outer]
    return (
        lax.ppermute(parity_edges[0], "row", inner),
        lax.ppermute(parity_edges[1], "row", outer),
    )


def swap(field):
    return lax.ppermute(field, "half", [(0, 1), (1, 0)])


def steps_of(value, axis, step):
    size = lax.axis_size(axis)
    return lax.ppermute(value, axis, [(at, at ^ step) for at in range(size)])


def share(parts, axis):
    return [parts[0]] + [steps_of(parts[at], axis, at) for at in range(1, len(parts))]


def share_same(part, axis):
    size = lax.axis_size(axis)
    return [part] + [steps_of(part, axis, at) for at in range(1, size)]


def gather_near(part):
    return [part, steps_of(part, "im", 1), steps_of(part, "im", 2)]


def gather_rest(parts):
    half = parts[0].shape[0] // 2
    return [steps_of(parts[1][:half], "im", 2), steps_of(parts[2][half:], "im", 1)]


def small_outputs(part, width):
    return [
        part[:9].reshape(3, 3, width),
        jnp.stack([part[9], part[11]]),
        jnp.stack([part[10], part[12]]),
        part[13],
        part[14],
    ]


def pair_outer(*pairs):
    size = lax.axis_size("im")
    first = pairs[0][0].value if isinstance(pairs[0][0], Near) else pairs[0][0]
    width = first.shape[1]
    rows = width // 2 // size * len(pairs)
    return list(
        call(
            functools.partial(pair_outer_kernel, pairs=len(pairs), parts=size),
            [Near(low(rows, width))] * size,
            [],
            *[ref for pair in pairs for ref in pair],
        )
    )


def sum_split(pieces, pairs):
    size = lax.axis_size("row")
    rows, width = pieces[0].shape
    return list(
        call(
            functools.partial(
                sum_split_kernel,
                pairs=pairs,
                parts=size,
                pieces=len(pieces),
            ),
            [Near(low(rows // size, width))] * size,
            [(rows, width)],
            *[Near(piece) for piece in pieces],
        )
    )


def add_low(pieces):
    total = pieces[0].astype(FULL)
    for piece in pieces[1:]:
        total = total + piece.astype(FULL)
    return total.astype(LOW)


def sum_far(left, right, axes):
    part = jnp.einsum("tm,tc->mc", left, right, preferred_element_type=FULL)
    return lax.psum(part, axes)


def shards(
    x_in,
    pre_reduce,
    pre_conv,
    pre_expand,
    pre_mid_gain,
    pre_mid_shift,
    pre_out_gain,
    pre_out_shift,
    post_reduce,
    post_conv,
    post_expand,
    post_mid_gain,
    post_mid_shift,
    post_out_gain,
    post_out_shift,
    read_weight,
    read_bias,
    cotangent,
):
    count, strip, side, width = x_in.shape
    strips = lax.axis_size("row")
    tokens = count * strip * side
    cols = side // 2
    rows = strip // 2
    slabs = count * rows
    padded = slabs * SLAB
    small = slabs * cols
    block = -(-small // SLAB) * SLAB
    features = read_weight.shape[1]
    x_low = x_in.reshape(tokens, width)
    pre_out_g, pre_out_s = (pre_out_gain[None], pre_out_shift[None])
    post_out_g, post_out_s = (post_out_gain[None], post_out_shift[None])
    pre_edge = Near(low(count, side, width))
    post_edge = Near(low(count, SLAB, width))
    quick = lax.axis_size("im") == 4 and strips == 4

    first, edge_a, edge_b, normed_a, factor_a = call(
        pre_reduce_kernel,
        [Near(low(tokens, width)), pre_edge, pre_edge, like(tokens, width), like(tokens, LANES)],
        [(tokens, width)],
        x_low,
        pre_reduce,
        pre_mid_gain,
        pre_mid_shift,
    )
    got_a, got_b = edges((edge_a, edge_b))
    (
        second,
        normed_b,
        factor_b,
        normed_c,
        factor_c,
        summed,
        pooled,
        post_first,
        edge_a,
        edge_b,
        post_normed_a,
        post_factor_a,
        pad,
    ) = call(
        pre_rest_kernel,
        [
            low(tokens, width),
            like(tokens, width),
            like(tokens, LANES),
            like(tokens, width),
            like(tokens, LANES),
            like(tokens, width),
            Near(like(padded, width)),
            Near(low(padded, width)),
            post_edge,
            post_edge,
            like(padded, width),
            like(padded, LANES),
            like(count, strip + 2, side, width),
        ],
        [(tokens, width), (side * width // LANES, LANES), (padded, width)],
        x_low,
        Near(first),
        Near(got_a),
        Near(got_b),
        pre_conv,
        pre_expand,
        pre_mid_gain,
        pre_mid_shift,
        pre_out_g,
        pre_out_s,
        post_reduce,
        post_mid_gain,
        post_mid_shift,
    )
    got_a, got_b = edges((edge_a, edge_b))
    (
        block_two,
        left_in,
        left_second,
        post_normed_b,
        post_factor_b,
        post_normed_c,
        post_factor_c,
        post_summed,
        post_pad,
    ) = call(
        functools.partial(post_rest_kernel, cols=cols),
        [
            Near(low(small, width)),
            low(block, width),
            low(block, width),
            like(padded, width),
            like(padded, LANES),
            like(padded, width),
            like(padded, LANES),
            like(padded, width),
            like(count, rows + 2, SLAB, width),
        ],
        [(padded, width), (padded, width), (block, width)],
        Near(pooled),
        Near(post_first),
        Near(got_a),
        Near(got_b),
        post_conv,
        post_expand,
        post_mid_gain,
        post_mid_shift,
        post_out_g,
        post_out_s,
    )
    whole = lax.all_gather(block_two, "row", axis=0, tiled=True)
    readout, grad_pre, *terms, d_read_b = call(
        functools.partial(readout_kernel, strips=strips),
        [
            like(*cotangent.shape, dtype=LOW),
            Near(low(strips * small, features)),
        ]
        + [Near(low(small, width))] * strips
        + [like(1, features)],
        [
            (strips * small, features),
            (strips * small, features),
            (strips * small, width),
        ],
        Near(whole),
        read_weight,
        read_bias[None],
        cotangent,
    )
    terms = share(terms, "row")
    post_gs, post_ge, post_gc, edge_a, edge_b, post_small_b = call(
        functools.partial(post_back_kernel, cols=cols, strips=strips),
        [
            Near(like(padded, width)),
            Near(low(block, width)),
            Near(low(padded, width)),
            post_edge,
            post_edge,
            like(4, width),
        ],
        [(block, width), (padded, width), (padded, width), (padded, width)],
        *[Near(term) for term in terms],
        post_expand,
        post_mid_gain,
        post_mid_shift,
        post_out_g,
        post_normed_b,
        post_factor_b,
        post_normed_c,
        post_factor_c,
        post_summed,
    )
    got_a, got_b = edges((edge_a, edge_b))
    (
        post_gr,
        pre_gs,
        pre_ge,
        pre_gc,
        edge_a,
        edge_b,
        post_small_a,
        pre_small_b,
    ) = call(
        functools.partial(middle_back_kernel, cols=cols),
        [
            Near(low(block, width)),
            like(tokens, width),
            Near(low(tokens, width)),
            Near(low(tokens, width)),
            pre_edge,
            pre_edge,
            like(11, width),
            like(4, width),
        ],
        [
            (count, rows + 2, SLAB, width),
            (9, 8, width),
            (padded, width),
            (side * width // LANES, LANES),
            (tokens, width),
            (2, 8, width),
            (padded, width),
            (block, width),
        ],
        Near(post_gc),
        Near(got_a),
        Near(got_b),
        post_pad,
        post_conv,
        post_reduce,
        post_mid_gain,
        post_mid_shift,
        post_normed_a,
        post_factor_a,
        Near(post_gs),
        pre_expand,
        pre_mid_gain,
        pre_mid_shift,
        pre_out_g,
        normed_b,
        factor_b,
        normed_c,
        factor_c,
        summed,
    )
    if quick:
        edge_a, left_in, left_second, post_ge, whole, grad_pre = tie(
            edge_a, left_in, left_second, post_ge, whole, grad_pre
        )
    got_a, got_b = edges((edge_a, edge_b))
    if quick:
        post_parts = pair_outer(
            (left_in, swap(left_in), Near(post_gr), Near(swap(post_gr))),
            (left_second, swap(left_second), Near(post_ge), Near(swap(post_ge))),
        )
        post_sums = share(post_parts, "im")[1:]
        post_parts[0], whole, grad_pre = tie(post_parts[0], whole, grad_pre)
        read_parts = pair_outer(
            (Near(whole), Near(swap(whole)), Near(grad_pre), Near(swap(grad_pre)))
        )
        (got_a, got_b), rest = tie_later((got_a, got_b), (*post_sums, *read_parts))
        post_sums, read_parts = (rest[:3], rest[3:])
    pre_gr, sums = call(
        pre_back_kernel,
        [Near(low(tokens, width)), Near(like(32, width))],
        [
            (count, strip + 2, side, width),
            (9, 8, width),
            (2, 8, width),
        ],
        Near(pre_gc),
        Near(got_a),
        Near(got_b),
        pad,
        pre_conv,
        pre_mid_gain,
        pre_mid_shift,
        normed_a,
        factor_a,
        pre_small_b,
        post_small_a,
        post_small_b,
        d_read_b,
    )
    if quick:
        far = swap(pre_gr)
        post_parts = sum_split(post_parts[:1] + post_sums, 2)
        post_parts[0], far = tie(post_parts[0], far)
        post_parts = share(post_parts, "row")
        parts = pair_outer(
            (second, swap(second), Near(pre_ge), Near(swap(pre_ge))),
            (x_low, swap(x_low), Near(pre_gr), Near(far)),
        )
        parts[0], sums = tie(parts[0], sums + swap(sums))
        read_last = read_parts[3]
        read_parts = read_parts[:1] + [steps_of(read_parts[at], "im", at) for at in (1, 2)]
        near_parts = [steps_of(parts[at], "im", at) for at in (1, 2)]
        grad_in = pre_gs + jnp.einsum("tm,cm->tc", pre_gr, pre_reduce, preferred_element_type=FULL)
        grad_in = grad_in.astype(LOW)
        post_parts, (grad_in, last, read_last, *rest) = tie_later(
            post_parts, (grad_in, parts[3], read_last, *near_parts, *read_parts)
        )
        near_parts, read_parts = (rest[:2], rest[2:])
        post_parts = share_same(add_low(post_parts), "row")
        last = steps_of(last, "im", 3)
        read_parts = read_parts + [steps_of(read_last, "im", 3)]
        post_parts, (last, *read_parts) = tie_later(post_parts, (last, *read_parts))
        parts = share(sum_split([parts[0]] + near_parts + [last], 2), "row")
        post_parts = gather_near(jnp.concatenate(post_parts, axis=0))
        read_parts = gather_near(add_low(read_parts))
        parts, rest = tie_later(parts, (*post_parts, *read_parts))
        post_parts, read_parts = (rest[:3], rest[3:])
        parts = share_same(add_low(parts), "row")
        read_parts.append(steps_of(read_parts[0], "im", 3))
        post_parts = post_parts + gather_rest(post_parts)
        parts, rest = tie_later(parts, (*post_parts, *read_parts, sums))
        post_parts, read_parts, sums = (rest[:5], rest[5:9], rest[9])
        parts = gather_near(jnp.concatenate(parts, axis=0))
        alone = lax.broadcasted_iota(jnp.int32, sums.shape, 0) >= 30
        for step in (1, 2):
            sums = sums + jnp.where(alone, 0.0, steps_of(sums, "row", step))
        sums = sums + steps_of(sums, "im", 1)
        parts, (sums, *post_parts) = tie_later(parts, (sums, *post_parts))
        far = swap(jnp.concatenate(parts, axis=0))
        post_far = swap(jnp.concatenate(post_parts, axis=0))
        read_far = swap(jnp.concatenate(read_parts, axis=0))
        far, post_far, read_far = tie(far, post_far, read_far)
        post_reduce_g, post_expand_g = assemble(post_parts, [post_far], 2, 4, strips)
        (read_total,) = assemble(read_parts, [read_far], 1, 4, 1)
        (post_reduce_g, read_total), (sums, *rest) = tie_later(
            (post_reduce_g, read_total), (sums, *gather_rest(parts))
        )
        far_rest = swap(jnp.concatenate(rest, axis=0))
        sums = sums + steps_of(sums, "im", 2)
        small_out = call(
            small_kernel,
            [like(3, 3, width), like(2, width), like(2, width), like(1, width), like(1, width)] * 2,
            [],
            Near(sums),
        )
        pre_expand_g, pre_reduce_g = assemble(parts + rest, [far, far_rest], 2, 4, strips)
        read_bias_g = sums[30]
    else:
        axes = IMG + ("row",)
        post_reduce_g = sum_far(left_in, post_gr, axes)
        post_expand_g = sum_far(left_second, post_ge, axes)
        pre_expand_g = sum_far(second, pre_ge, axes)
        pre_reduce_g = sum_far(x_low, pre_gr, axes)
        read_total = sum_far(whole, grad_pre, IMG)
        read_bias_g = lax.psum(sums[30], IMG)
        sums = lax.psum(sums[:30], axes)
        small_out = small_outputs(sums[:15], width) + small_outputs(sums[15:30], width)
        grad_in = pre_gs + jnp.einsum("tm,cm->tc", pre_gr, pre_reduce, preferred_element_type=FULL)
        grad_in = grad_in.astype(LOW)

    pre_conv_g, pre_gain_g, pre_shift_g, pre_og_g, pre_os_g = small_out[:5]
    post_conv_g, post_gain_g, post_shift_g, post_og_g, post_os_g = small_out[5:]
    return (
        readout,
        grad_in.reshape(x_in.shape),
        pre_reduce_g,
        pre_conv_g,
        pre_expand_g,
        pre_gain_g,
        pre_shift_g,
        pre_og_g.reshape(width),
        pre_os_g.reshape(width),
        post_reduce_g,
        post_conv_g,
        post_expand_g,
        post_gain_g,
        post_shift_g,
        post_og_g.reshape(width),
        post_os_g.reshape(width),
        read_total,
        read_bias_g,
    )


def solution(mesh):
    images, strips = mesh.devices.shape
    split = jax.sharding.Mesh(
        mesh.devices.reshape(images // 2, 2, strips), ("im", "half", "row")
    )
    return jax.shard_map(
        shards,
        mesh=split,
        in_specs=(P(IMG, "row", None, None),)
        + (P(),) * 14
        + (P(None, "row"), P("row"), P(IMG, None, None, "row")),
        out_specs=(P(IMG, None, None, "row"), P(IMG, "row", None, None))
        + (P(),) * 14
        + (P(None, "row"), P("row")),
        check_vma=False,
    )
```

```python
import functools

import jax
import jax.numpy as jnp
from jax import lax
from jax.experimental import pallas as pl
from jax.experimental.pallas import tpu as pltpu
from jax.sharding import PartitionSpec as P

EPSILON = 1e-06
SQRT_HALF = 0.7071067811865476
INV_SQRT_TWO_PI = 0.3989422804014327
LOW = jnp.bfloat16
FULL = jnp.float32
IMG = ("im", "half")
TILE = 256
SLAB = 16
LANES = 128
VMEM_BYTES = 24 * 1024 * 1024


def tie(*values):
    return lax.optimization_barrier(values)


def tie_later(first, second):
    first = list(tie(*first))
    out = list(tie(*first, *second))
    return (out[: len(first)], out[len(first) :])


def norm(value):
    centred = value - jnp.mean(value, axis=-1, keepdims=True)
    factor = lax.rsqrt(jnp.mean(centred * centred, axis=-1, keepdims=True) + EPSILON)
    return (centred * factor, factor)


def norm_back(grad, normed, factor, gain):
    scaled = grad * gain
    return factor * (
        scaled
        - jnp.mean(scaled, axis=-1, keepdims=True)
        - normed * jnp.mean(scaled * normed, axis=-1, keepdims=True)
    )


def gate(value):
    return 0.5 * jnp.tanh(0.5 * value) + 0.5


def silu(value):
    return value * gate(value)


def silu_back(grad, value):
    sigma = gate(value)
    return grad * sigma * (1.0 + value * (1.0 - sigma))


def flip(place, step):
    bit = 1
    while bit <= step:
        if step & bit:
            place = place + bit - 2 * bit * ((place // bit) % 2)
        bit *= 2
    return place


def wide(factor):
    return jnp.broadcast_to(factor, (factor.shape[0], LANES))


def fold(value):
    return jnp.sum(value.reshape(-1, 8, value.shape[-1]), axis=0)


def live(rows, cols):
    at = lax.broadcasted_iota(jnp.int32, (rows, 1), 0)
    return lax.rem(at, SLAB) < cols


def from_left(value):
    at = lax.broadcasted_iota(jnp.int32, (value.shape[0], 1), 0)
    return jnp.where(at == 0, 0.0, pltpu.roll(value, 1, 0))


def from_right(value):
    last = value.shape[0] - 1
    at = lax.broadcasted_iota(jnp.int32, (value.shape[0], 1), 0)
    return jnp.where(at == last, 0.0, pltpu.roll(value, last, 0))


def matmul(left_ref, right_ref, out_ref):
    @pl.loop(0, right_ref.shape[1] // TILE)
    def _(at):
        cols = pl.ds(pl.multiple_of(at * TILE, TILE), TILE)
        out_ref[:, cols] = jnp.dot(
            left_ref[...].astype(LOW), right_ref[:, cols], preferred_element_type=FULL
        )


def matmul_back(left_ref, right_ref, out_ref):
    @pl.loop(0, right_ref.shape[0] // TILE)
    def _(at):
        cols = pl.ds(pl.multiple_of(at * TILE, TILE), TILE)
        out_ref[:, cols] = lax.dot_general(
            left_ref[...].astype(LOW),
            right_ref[cols, :],
            (((1,), (1,)), ((), ())),
            preferred_element_type=FULL,
        ).astype(out_ref.dtype)


def rows_of(at, size):
    return pl.ds(pl.multiple_of(at * size, SLAB), size)


def fill_halo(at_ref, pad_ref, low_ref, got_a_ref, got_b_ref):
    count, rows, cols, width = pad_ref.shape
    rows = rows - 2
    even = lax.rem(at_ref[2], 2) == 0
    for image in range(count):
        got_a, got_b = (got_a_ref[image].astype(FULL), got_b_ref[image].astype(FULL))
        pad_ref[image, 0] = jnp.where(even, got_b, got_a)
        pad_ref[image, rows + 1] = jnp.where(even, got_a, got_b)

    size = cols if cols % SLAB == 0 else 2 * cols
    per = size // cols
    each = rows // per

    @pl.loop(0, count * each)
    def _(at):
        part = low_ref[rows_of(at, size), :].astype(FULL).reshape(per, cols, width)
        pad_ref[at // each, pl.ds(1 + per * lax.rem(at, each), per)] = part


def set_edges(at_ref, edge_a_ref, edge_b_ref, image, head, tail):
    even = lax.rem(at_ref[2], 2) == 0
    edge_a_ref[image] = jnp.where(even, tail, head).astype(LOW)
    edge_b_ref[image] = jnp.where(even, head, tail).astype(LOW)


def conv_row(pad_ref, taps, image, row):
    lines = [pad_ref[image, row + top] for top in range(3)]
    sums = [
        lines[0] * taps[left] + lines[1] * taps[3 + left] + lines[2] * taps[6 + left]
        for left in range(3)
    ]
    return from_left(sums[0]) + sums[1] + from_right(sums[2])


def conv_back_row(pad_ref, grad_ref, taps, taps_ref, image, row):
    lines = [grad_ref[image, row + top] for top in range(3)]
    sums = [
        lines[2] * taps[left] + lines[1] * taps[3 + left] + lines[0] * taps[6 + left]
        for left in range(3)
    ]
    shifted = [from_right(lines[1]), lines[1], from_left(lines[1])]
    for top in range(3):
        source = pad_ref[image, row + top]
        for left in range(3):
            taps_ref[3 * top + left] += fold(source * shifted[left])
    return from_right(sums[0]) + sums[1] + from_left(sums[2])


def pack(compact, source, out_ref, cols):
    compact[...] = jnp.zeros(compact.shape, FULL)
    for at in range(source.shape[0] // SLAB):
        compact[pl.ds(at * cols, cols), :] = source[pl.ds(at * SLAB, cols), :]
    out_ref[...] = compact[...].astype(LOW)


def narrow(pair, value):
    side = value.shape[0]
    parts = []
    for at in range(value.shape[1] // LANES):
        pair[pl.ds(at * side, side), :] = value[:, at * LANES : (at + 1) * LANES]
        parts.append(
            pair[pl.ds(at * side, side // 2, stride=2), :]
            + pair[pl.ds(at * side + 1, side // 2, stride=2), :]
        )
    return jnp.concatenate(parts, axis=1)


def widen(pair, value):
    cols = value.shape[0]
    parts = []
    for at in range(value.shape[1] // LANES):
        part = value[:, at * LANES : (at + 1) * LANES]
        pair[pl.ds(2 * cols * at, cols, stride=2), :] = part
        pair[pl.ds(2 * cols * at + 1, cols, stride=2), :] = part
        parts.append(pair[pl.ds(2 * cols * at, 2 * cols), :])
    return jnp.concatenate(parts, axis=1)


def tap_rows(conv_ref):
    lines = [conv_ref[top].astype(FULL) for top in range(3)]
    return [lines[at // 3][at % 3 : at % 3 + 1] for at in range(9)]


def finish(small_ref, sums_ref, at, place):
    small_ref[pl.ds(place, 1), :] = jnp.sum(sums_ref[at], axis=0, keepdims=True)


def pre_reduce_kernel(
    need,
    send,
    at_ref,
    x_ref, w_ref, gain_ref, shift_ref, first_ref, edge_a_ref, edge_b_ref, normed_ref, factor_ref, red
):
    count, side, width = edge_a_ref.shape
    size = 2 * side
    steps = x_ref.shape[0] // size
    need(x_ref, w_ref)
    matmul(x_ref, w_ref, red)
    need(gain_ref, shift_ref)
    gain, shift = (gain_ref[pl.ds(0, 1), :], shift_ref[pl.ds(0, 1), :])

    @pl.loop(0, steps)
    def _(at):
        rows = rows_of(at, size)
        normed, factor = norm(red[rows, :])
        normed_ref[rows, :] = normed
        factor_ref[rows, :] = wide(factor)
        first_ref[rows, :] = silu(normed * gain + shift).astype(LOW)

    each = steps // count
    for image in range(count):
        head = first_ref[pl.ds(image * each * size, size), :].astype(FULL)
        tail = first_ref[pl.ds((image * each + each - 1) * size, size), :].astype(FULL)
        set_edges(at_ref, edge_a_ref, edge_b_ref, image, head[:side], tail[side:])


def pre_rest_kernel(
    need,
    send,
    at_ref,
    x_ref,
    first_ref,
    got_a_ref,
    got_b_ref,
    conv_ref,
    expand_ref,
    gain_ref,
    shift_ref,
    out_gain_ref,
    out_shift_ref,
    reduce_ref,
    post_gain_ref,
    post_shift_ref,
    second_ref,
    normed_b_ref,
    factor_b_ref,
    normed_c_ref,
    factor_c_ref,
    summed_ref,
    pooled_ref,
    post_first_ref,
    edge_a_ref,
    edge_b_ref,
    post_normed_ref,
    post_factor_ref,
    pad,
    exp,
    pair,
    red,
):
    count, strip, side, width = pad.shape
    strip = strip - 2
    size = 2 * side
    each = strip // 2
    need(first_ref, got_a_ref, got_b_ref)
    fill_halo(at_ref, pad, first_ref, got_a_ref, got_b_ref)
    need(conv_ref, gain_ref, shift_ref)
    send(pad)
    taps = tap_rows(conv_ref)
    gain, shift = (gain_ref[pl.ds(1, 1), :], shift_ref[pl.ds(1, 1), :])

    @pl.loop(0, count * each)
    def _(at):
        rows = rows_of(at, size)
        image, row = (at // each, 2 * lax.rem(at, each))
        conv = jnp.concatenate(
            [conv_row(pad, taps, image, row), conv_row(pad, taps, image, row + 1)], axis=0
        )
        normed, factor = norm(conv)
        normed_b_ref[rows, :] = normed
        factor_b_ref[rows, :] = wide(factor)
        second_ref[rows, :] = silu(normed * gain + shift).astype(LOW)

    send(second_ref, normed_b_ref, factor_b_ref)
    need(expand_ref)
    matmul(second_ref, expand_ref, exp)
    need(x_ref, out_gain_ref, out_shift_ref)
    out_gain, out_shift = (out_gain_ref[...], out_shift_ref[...])
    cols = side // 2
    for at in range(count * each):
        rows = pl.ds(at * size, size)
        normed, factor = norm(exp[rows, :])
        normed_c_ref[rows, :] = normed
        factor_c_ref[rows, :] = wide(factor)
        summed = x_ref[rows, :].astype(FULL) + normed * out_gain + out_shift
        summed_ref[rows, :] = summed
        block = silu(summed)
        half = narrow(pair, block[:side] + block[side:])
        pooled_ref[pl.ds(at * SLAB, cols), :] = 0.25 * half
        pooled_ref[pl.ds(at * SLAB + cols, SLAB - cols), :] = jnp.zeros(
            (SLAB - cols, width), FULL
        )
    send(normed_c_ref, factor_c_ref, summed_ref)
    need(reduce_ref, post_gain_ref, post_shift_ref)
    matmul(pooled_ref, reduce_ref, red)
    normed, factor = norm(red[...])
    post_normed_ref[...] = normed
    post_factor_ref[...] = wide(factor)
    first = silu(normed * post_gain_ref[pl.ds(0, 1), :] + post_shift_ref[pl.ds(0, 1), :])
    post_first_ref[...] = jnp.where(live(red.shape[0], cols), first, 0.0).astype(LOW)
    for image in range(count):
        head = post_first_ref[pl.ds(image * each * SLAB, SLAB), :].astype(FULL)
        tail = post_first_ref[pl.ds((image * each + each - 1) * SLAB, SLAB), :].astype(FULL)
        set_edges(at_ref, edge_a_ref, edge_b_ref, image, head, tail)


def post_rest_kernel(
    need,
    send,
    at_ref,
    pooled_ref,
    first_ref,
    got_a_ref,
    got_b_ref,
    conv_ref,
    expand_ref,
    gain_ref,
    shift_ref,
    out_gain_ref,
    out_shift_ref,
    block_ref,
    left_in_ref,
    left_second_ref,
    normed_b_ref,
    factor_b_ref,
    normed_c_ref,
    factor_c_ref,
    summed_ref,
    pad,
    second,
    exp,
    compact,
    *,
    cols
):
    count, rows, _, width = pad.shape
    rows = rows - 2
    small = block_ref.shape[0]
    need(first_ref, got_a_ref, got_b_ref)
    fill_halo(at_ref, pad, first_ref, got_a_ref, got_b_ref)
    send(pad)
    need(conv_ref, gain_ref, shift_ref, pooled_ref)
    taps = tap_rows(conv_ref)
    gain, shift = (gain_ref[pl.ds(1, 1), :], shift_ref[pl.ds(1, 1), :])

    @pl.loop(0, count * rows)
    def _(at):
        place = rows_of(at, SLAB)
        normed, factor = norm(conv_row(pad, taps, at // rows, lax.rem(at, rows)))
        normed_b_ref[place, :] = normed
        factor_b_ref[place, :] = wide(factor)
        second[place, :] = silu(normed * gain + shift)

    send(normed_b_ref, factor_b_ref)
    need(expand_ref)
    matmul(second, expand_ref, exp)
    need(out_gain_ref, out_shift_ref)
    normed, factor = norm(exp[...])
    normed_c_ref[...] = normed
    factor_c_ref[...] = wide(factor)
    summed = pooled_ref[...] + normed * out_gain_ref[...] + out_shift_ref[...]
    summed_ref[...] = summed
    exp[...] = silu(summed)
    compact[...] = jnp.zeros(compact.shape, FULL)
    for at in range(count * rows):
        compact[pl.ds(at * cols, cols), :] = exp[pl.ds(at * SLAB, cols), :]
    block_ref[...] = compact[pl.ds(0, small), :].astype(LOW)
    send(block_ref, normed_c_ref, factor_c_ref, summed_ref)
    pack(compact, pooled_ref, left_in_ref, cols)
    pack(compact, second, left_second_ref, cols)


def readout_kernel(
    need,
    send,
    at_ref,
    whole_ref,
    w_ref,
    bias_ref,
    cot_ref,
    out_ref,
    grad_ref,
    *refs,
    strips
):
    slots, (bias_grad_ref, cot, out, terms_ref) = (refs[:strips], refs[strips:])
    images, lines, cols, _ = cot_ref.shape
    rows = lines // strips
    need(cot_ref)
    for at in range(images * lines):
        strip, image, row = (at // (images * rows), at // rows % images, at % rows)
        cot[pl.ds(at * cols, cols), :] = cot_ref[image, strip * rows + row].astype(FULL)
    need(whole_ref, w_ref, bias_ref)

    @pl.loop(0, w_ref.shape[1] // TILE)
    def _(at):
        lanes = pl.ds(pl.multiple_of(at * TILE, TILE), TILE)
        act = jnp.dot(whole_ref[...], w_ref[:, lanes], preferred_element_type=FULL)
        act = act + bias_ref[:, lanes]
        cdf = 0.5 * (1.0 + lax.erf(act * SQRT_HALF))
        density = jnp.exp(-0.5 * act * act) * INV_SQRT_TWO_PI
        out[:, lanes] = act * cdf
        grad = (cot[:, lanes] * (cdf + act * density)).astype(LOW)
        grad_ref[:, lanes] = grad
        bias_grad_ref[:, lanes] = jnp.sum(grad.astype(FULL), axis=0, keepdims=True)

    send(grad_ref, bias_grad_ref)
    matmul_back(grad_ref, w_ref, terms_ref)
    small = slots[0].shape[0]
    for step in range(strips):
        begin = pl.multiple_of(flip(at_ref[2], step) * small, 8)
        slots[step][...] = terms_ref[pl.ds(begin, small), :].astype(LOW)
    for at in range(images * lines):
        strip, image, row = (at // (images * rows), at // rows % images, at % rows)
        out_ref[image, strip * rows + row] = out[pl.ds(at * cols, cols), :].astype(LOW)


def post_back_kernel(
    need,
    send,
    at_ref,
    *refs,
    cols,
    strips
):
    pieces, refs = (refs[:strips], refs[strips:])
    (
    expand_ref,
    gain_ref,
    shift_ref,
    out_gain_ref,
    normed_b_ref,
    factor_b_ref,
    normed_c_ref,
    factor_c_ref,
    summed_ref,
    grad_sum_ref,
    grad_exp_ref,
    grad_conv_ref,
    edge_a_ref,
    edge_b_ref,
    small_ref,
    compact,
    spread_out,
    exp,
    sec,
    ) = refs
    count = edge_a_ref.shape[0]
    tokens, width = grad_sum_ref.shape
    each = tokens // SLAB // count
    need(*pieces)
    total = pieces[0][...].astype(FULL)
    for piece in pieces[1:]:
        total = total + piece[...].astype(FULL)
    compact[...] = jnp.zeros(compact.shape, FULL)
    compact[pl.ds(0, total.shape[0]), :] = total
    spread_out[...] = jnp.zeros((tokens, width), FULL)
    for at in range(tokens // SLAB):
        spread_out[pl.ds(at * SLAB, cols), :] = compact[pl.ds(at * cols, cols), :]
    need(summed_ref, normed_c_ref, factor_c_ref, out_gain_ref)
    grad_sum = silu_back(spread_out[...], summed_ref[...])
    grad_sum_ref[...] = grad_sum
    normed = normed_c_ref[...]
    exp[...] = norm_back(grad_sum, normed, factor_c_ref[:, :1], out_gain_ref[...])
    small_ref[pl.ds(2, 1), :] = jnp.sum(grad_sum * normed, axis=0, keepdims=True)
    small_ref[pl.ds(3, 1), :] = jnp.sum(grad_sum, axis=0, keepdims=True)
    pack(compact, exp, grad_exp_ref, cols)
    send(grad_sum_ref, grad_exp_ref)
    need(expand_ref)
    matmul_back(exp, expand_ref, sec)
    need(gain_ref, shift_ref, normed_b_ref, factor_b_ref)
    gain, shift = (gain_ref[pl.ds(1, 1), :], shift_ref[pl.ds(1, 1), :])
    normed = normed_b_ref[...]
    grad = silu_back(sec[...], normed * gain + shift)
    grad_conv_ref[...] = norm_back(grad, normed, factor_b_ref[:, :1], gain).astype(LOW)
    small_ref[pl.ds(0, 1), :] = jnp.sum(grad * normed, axis=0, keepdims=True)
    small_ref[pl.ds(1, 1), :] = jnp.sum(grad, axis=0, keepdims=True)
    for image in range(count):
        head = grad_conv_ref[pl.ds(image * each * SLAB, SLAB), :].astype(FULL)
        tail = grad_conv_ref[pl.ds((image * each + each - 1) * SLAB, SLAB), :].astype(FULL)
        set_edges(at_ref, edge_a_ref, edge_b_ref, image, head, tail)


def middle_back_kernel(
    need,
    send,
    at_ref,
    grad_conv_ref,
    got_a_ref,
    got_b_ref,
    pad,
    post_conv_ref,
    post_reduce_ref,
    post_gain_ref,
    post_shift_ref,
    post_normed_ref,
    post_factor_ref,
    post_grad_sum_ref,
    expand_ref,
    gain_ref,
    shift_ref,
    out_gain_ref,
    normed_b_ref,
    factor_b_ref,
    normed_c_ref,
    factor_c_ref,
    summed_ref,
    post_grad_red_ref,
    grad_sum_ref,
    grad_exp_ref,
    pre_grad_conv_ref,
    edge_a_ref,
    edge_b_ref,
    post_small_ref,
    small_ref,
    grad_pad,
    taps_sum,
    grad_in,
    pair,
    sec,
    sums,
    post_red,
    compact,
    *,
    cols
):
    count, side, width = edge_a_ref.shape
    need(grad_conv_ref, got_a_ref, got_b_ref)
    fill_halo(at_ref, grad_pad, grad_conv_ref, got_a_ref, got_b_ref)
    need(pad, post_conv_ref)
    need(post_gain_ref, post_shift_ref, post_normed_ref, post_factor_ref)
    taps = tap_rows(post_conv_ref)
    taps_sum[...] = jnp.zeros_like(taps_sum)
    sums[...] = jnp.zeros_like(sums)
    gain, shift = (post_gain_ref[pl.ds(0, 1), :], post_shift_ref[pl.ds(0, 1), :])
    each = post_grad_sum_ref.shape[0] // SLAB // count

    @pl.loop(0, count * each)
    def _(at):
        place = rows_of(at, SLAB)
        grad = conv_back_row(pad, grad_pad, taps, taps_sum, at // each, lax.rem(at, each))
        normed = post_normed_ref[place, :]
        grad = jnp.where(live(SLAB, cols), silu_back(grad, normed * gain + shift), 0.0)
        sums[0] += fold(grad * normed)
        sums[1] += fold(grad)
        post_red[place, :] = norm_back(grad, normed, post_factor_ref[place, :1], gain)

    for at in range(9):
        finish(post_small_ref, taps_sum, at, at)
    finish(post_small_ref, sums, 0, 9)
    finish(post_small_ref, sums, 1, 10)
    pack(compact, post_red, post_grad_red_ref, cols)
    send(post_grad_red_ref, post_small_ref)
    need(post_reduce_ref)
    matmul_back(post_red, post_reduce_ref, grad_in)
    sums[...] = jnp.zeros_like(sums)
    size = 2 * side
    need(out_gain_ref, post_grad_sum_ref, summed_ref, normed_c_ref, factor_c_ref)
    out_gain = out_gain_ref[...]
    for at in range(count * each):
        rows = pl.ds(at * size, size)
        place = pl.ds(at * SLAB, cols)
        grad = 0.25 * (post_grad_sum_ref[place, :] + grad_in[place, :])
        grad = widen(pair, grad)
        grad = jnp.concatenate([grad, grad], axis=0)
        grad_sum = silu_back(grad, summed_ref[rows, :])
        grad_sum_ref[rows, :] = grad_sum
        normed = normed_c_ref[rows, :]
        sums[0] += fold(grad_sum * normed)
        sums[1] += fold(grad_sum)
        grad_exp_ref[rows, :] = norm_back(
            grad_sum, normed, factor_c_ref[rows, :1], out_gain
        ).astype(LOW)
    finish(small_ref, sums, 0, 2)
    finish(small_ref, sums, 1, 3)
    send(grad_sum_ref, grad_exp_ref)
    need(expand_ref)
    matmul_back(grad_exp_ref, expand_ref, sec)
    need(gain_ref, shift_ref, normed_b_ref, factor_b_ref)
    sums[...] = jnp.zeros_like(sums)
    gain_b, shift_b = (gain_ref[pl.ds(1, 1), :], shift_ref[pl.ds(1, 1), :])

    @pl.loop(0, count * each)
    def _(at):
        rows = rows_of(at, size)
        normed = normed_b_ref[rows, :]
        grad = silu_back(sec[rows, :], normed * gain_b + shift_b)
        sums[0] += fold(grad * normed)
        sums[1] += fold(grad)
        pre_grad_conv_ref[rows, :] = norm_back(
            grad, normed, factor_b_ref[rows, :1], gain_b
        ).astype(LOW)

    finish(small_ref, sums, 0, 0)
    finish(small_ref, sums, 1, 1)
    for image in range(count):
        head = pre_grad_conv_ref[pl.ds(image * each * size, size), :].astype(FULL)
        tail = pre_grad_conv_ref[pl.ds((image * each + each - 1) * size, size), :].astype(FULL)
        set_edges(at_ref, edge_a_ref, edge_b_ref, image, head[:side], tail[side:])


def pre_back_kernel(
    need,
    send,
    at_ref,
    grad_conv_ref,
    got_a_ref,
    got_b_ref,
    pad,
    conv_ref,
    gain_ref,
    shift_ref,
    normed_ref,
    factor_ref,
    small_b_ref,
    post_small_a_ref,
    post_small_b_ref,
    read_bias_ref,
    grad_red_ref,
    small_ref,
    grad_pad,
    taps_sum,
    sums,
):
    count, strip, side, width = pad.shape
    strip = strip - 2
    size = 2 * side
    each = strip // 2
    need(grad_conv_ref, got_a_ref, got_b_ref)
    fill_halo(at_ref, grad_pad, grad_conv_ref, got_a_ref, got_b_ref)
    need(pad, conv_ref)
    need(gain_ref, shift_ref, normed_ref, factor_ref)
    taps = tap_rows(conv_ref)
    taps_sum[...] = jnp.zeros_like(taps_sum)
    sums[...] = jnp.zeros_like(sums)
    gain, shift = (gain_ref[pl.ds(0, 1), :], shift_ref[pl.ds(0, 1), :])

    @pl.loop(0, count * each)
    def _(at):
        rows = rows_of(at, size)
        image, row = (at // each, 2 * lax.rem(at, each))
        grad = jnp.concatenate(
            [
                conv_back_row(pad, grad_pad, taps, taps_sum, image, row),
                conv_back_row(pad, grad_pad, taps, taps_sum, image, row + 1),
            ],
            axis=0,
        )
        normed = normed_ref[rows, :]
        grad = silu_back(grad, normed * gain + shift)
        sums[0] += fold(grad * normed)
        sums[1] += fold(grad)
        grad_red_ref[rows, :] = norm_back(grad, normed, factor_ref[rows, :1], gain).astype(LOW)

    for at in range(9):
        finish(small_ref, taps_sum, at, at)
    finish(small_ref, sums, 0, 9)
    finish(small_ref, sums, 1, 10)
    need(small_b_ref, post_small_a_ref, post_small_b_ref, read_bias_ref)
    small_ref[pl.ds(11, 4), :] = small_b_ref[...]
    small_ref[pl.ds(15, 11), :] = post_small_a_ref[...]
    small_ref[pl.ds(26, 4), :] = post_small_b_ref[...]
    small_ref[pl.ds(30, 1), :] = read_bias_ref[...]
    small_ref[pl.ds(31, 1), :] = jnp.zeros_like(read_bias_ref)


def pair_outer_kernel(need, send, at_ref, *refs, pairs, parts):
    takes = 4 * pairs
    outs = refs[takes:]
    half, plane = (at_ref[0], at_ref[1])
    rows = outs[0].shape[0] // pairs
    for pair in range(pairs):
        left, left_far, right, right_far = refs[4 * pair : 4 * pair + 4]
        need(left, left_far, right, right_far)
        for step in range(parts):
            begin = half * (rows * parts) + flip(plane, step) * rows
            lanes = pl.ds(pl.multiple_of(begin, LANES), rows)
            total = lax.dot_general(
                left[:, lanes], right[...], (((0,), (0,)), ((), ())), preferred_element_type=FULL
            ) + lax.dot_general(
                left_far[:, lanes],
                right_far[...],
                (((0,), (0,)), ((), ())),
                preferred_element_type=FULL,
            )
            outs[step][pl.ds(pair * rows, rows), :] = total.astype(LOW)
    send(*outs)


def sum_split_kernel(need, send, at_ref, *refs, pairs, parts, pieces, along=2):
    takes, outs = (refs[:pieces], refs[pieces : pieces + parts])
    total = refs[-1]
    need(*takes)
    value = takes[0][...].astype(FULL)
    for at in range(1, pieces):
        value = value + takes[at][...].astype(FULL)
    total[...] = value
    rows = total.shape[0] // pairs // parts
    for step in range(parts):
        begin = flip(at_ref[along], step) * rows
        for pair in range(pairs):
            place = pl.ds(pl.multiple_of(pair * rows * parts + begin, SLAB), rows)
            outs[step][pl.ds(pair * rows, rows), :] = total[place, :].astype(LOW)
    send(*outs)


def assemble_kernel(*refs, spans, pairs, planes, strips):
    takes = len(spans)
    parts, outs = (refs[:takes], refs[takes : takes + pairs])
    full, sem = (refs[takes + pairs : takes + 2 * pairs], refs[-1])
    half, plane, row = places()
    rows = spans[0] // pairs // strips
    block = strips * rows
    pieces = []
    for part, span in zip(parts, spans):
        pieces += [(part, begin) for begin in range(0, span, pairs * rows)]
    writes = []
    for pair in range(pairs):
        for at in range(2 * planes * strips):
            near, step = (at // strips, at % strips)
            side, spot = (flip(half, near // planes), flip(plane, near % planes))
            place = side * (planes * block) + spot * block
            if strips > 1:
                place = place + flip(row, step) * rows
            part, begin = pieces[at]
            full[pair][pl.ds(pl.multiple_of(place, SLAB), rows), :] = part[
                pl.ds(begin + pair * rows, rows), :
            ].astype(FULL)
        writes.append(pltpu.make_async_copy(full[pair], outs[pair], sem.at[pair]))
        writes[-1].start()
    for write in writes:
        write.wait()


def assemble(parts, far, pairs, planes, strips):
    out = like(2 * planes * parts[0].shape[0] // pairs, parts[0].shape[1])
    parts = [pltpu.with_memory_space_constraint(part, pltpu.VMEM) for part in parts + far]
    return pl.pallas_call(
        functools.partial(
            assemble_kernel,
            spans=[part.shape[0] for part in parts],
            pairs=pairs,
            planes=planes,
            strips=strips,
        ),
        out_shape=[pltpu.HBM(out.shape, out.dtype)] * pairs,
        in_specs=[pl.BlockSpec(memory_space=pltpu.VMEM)] * len(parts),
        out_specs=[pl.BlockSpec(memory_space=pltpu.HBM)] * pairs,
        scratch_shapes=[pltpu.VMEM(out.shape, FULL)] * pairs + [pltpu.SemaphoreType.DMA((pairs,))],
        compiler_params=pltpu.CompilerParams(vmem_limit_bytes=VMEM_BYTES),
        cost_estimate=pl.CostEstimate(flops=0, bytes_accessed=0, transcendentals=0),
    )(*parts)


def small_kernel(need, send, at_ref, sums_ref, *outs):
    for place in range(2):
        conv, gain, shift, out_gain, out_shift = outs[5 * place : 5 * place + 5]
        rows = sums_ref[pl.ds(15 * place, 15), :]
        for top in range(3):
            conv[top] = rows[3 * top : 3 * top + 3]
        gain[pl.ds(0, 1), :] = rows[9:10]
        gain[pl.ds(1, 1), :] = rows[11:12]
        shift[pl.ds(0, 1), :] = rows[10:11]
        shift[pl.ds(1, 1), :] = rows[12:13]
        out_gain[...] = rows[13:14]
        out_shift[...] = rows[14:15]


class Near:
    def __init__(self, value):
        self.value = value


def like(*shape, dtype=FULL):
    return jax.ShapeDtypeStruct(shape, dtype)


def low(*shape):
    return like(*shape, dtype=LOW)


def places():
    return [lax.axis_index(axis) for axis in ("half", "im", "row")]


def call(kernel, outs, scratch, *args):
    near_in = [isinstance(arg, Near) for arg in args]
    near_out = [isinstance(out, Near) for out in outs]
    args = [arg.value if isinstance(arg, Near) else arg for arg in args]
    outs = [out.value if isinstance(out, Near) else out for out in outs]
    takes, gives = (len(args), len(outs))
    far_in = [at for at in range(takes) if not near_in[at]]
    far_out = [at for at in range(gives) if not near_out[at]]

    def body(*refs):
        given, refs = (list(refs[:takes]), refs[takes:])
        made, refs = (list(refs[:gives]), refs[gives:])
        rest = refs[len(far_in) + len(far_out) :]
        reads, writes = ({}, {})
        if far_in:
            in_sem = rest[-1]
            rest = rest[:-1]
        if far_out:
            out_sem = rest[-1]
            rest = rest[:-1]
        for place, at in enumerate(far_in):
            reads[at] = pltpu.make_async_copy(given[at], refs[place], in_sem.at[place])
            given[at] = refs[place]
        for place, at in enumerate(far_out):
            mirror = refs[len(far_in) + place]
            writes[at] = pltpu.make_async_copy(mirror, made[at], out_sem.at[place])
            made[at] = mirror
        for at in sorted(reads, key=lambda at: args[at].size):
            reads[at].start()
        started = []

        def need(*wanted):
            for at in list(reads):
                if any(given[at] is ref for ref in wanted):
                    reads.pop(at).wait()

        def send(*ready):
            for at in list(writes):
                if any(made[at] is ref for ref in ready):
                    started.append(writes.pop(at))
                    started[-1].start()

        kernel(need, send, places(), *given, *made, *rest)
        need(*given)
        send(*made)
        for write in started:
            write.wait()

    spaces = {True: pltpu.VMEM, False: pltpu.HBM}
    args = [
        pltpu.with_memory_space_constraint(arg, spaces[near]) for arg, near in zip(args, near_in)
    ]
    return pl.pallas_call(
        body,
        out_shape=[spaces[near](out.shape, out.dtype) for out, near in zip(outs, near_out)],
        in_specs=[pl.BlockSpec(memory_space=spaces[near]) for near in near_in],
        out_specs=[pl.BlockSpec(memory_space=spaces[near]) for near in near_out],
        scratch_shapes=[pltpu.VMEM(args[at].shape, args[at].dtype) for at in far_in]
        + [pltpu.VMEM(outs[at].shape, outs[at].dtype) for at in far_out]
        + [pltpu.VMEM(shape, FULL) for shape in scratch]
        + [pltpu.SemaphoreType.DMA((len(far_out),))] * bool(far_out)
        + [pltpu.SemaphoreType.DMA((len(far_in),))] * bool(far_in),
        compiler_params=pltpu.CompilerParams(vmem_limit_bytes=VMEM_BYTES),
        cost_estimate=pl.CostEstimate(flops=0, bytes_accessed=0, transcendentals=0),
    )(*args)


def edges(parity_edges):
    size = lax.axis_size("row")
    inner = [(at, at ^ 1) for at in range(size)]
    outer = [(at, at + 1) for at in range(1, size - 1, 2)]
    outer = outer + [(to, at) for at, to in outer]
    return (
        lax.ppermute(parity_edges[0], "row", inner),
        lax.ppermute(parity_edges[1], "row", outer),
    )


def swap(field):
    return lax.ppermute(field, "half", [(0, 1), (1, 0)])


def steps_of(value, axis, step):
    size = lax.axis_size(axis)
    return lax.ppermute(value, axis, [(at, at ^ step) for at in range(size)])


def share(parts, axis):
    return [parts[0]] + [steps_of(parts[at], axis, at) for at in range(1, len(parts))]


def share_same(part, axis):
    size = lax.axis_size(axis)
    return [part] + [steps_of(part, axis, at) for at in range(1, size)]


def gather_near(part):
    return [part, steps_of(part, "im", 1), steps_of(part, "im", 2)]


def gather_rest(parts):
    half = parts[0].shape[0] // 2
    return [steps_of(parts[1][:half], "im", 2), steps_of(parts[2][half:], "im", 1)]


def small_outputs(part, width):
    return [
        part[:9].reshape(3, 3, width),
        jnp.stack([part[9], part[11]]),
        jnp.stack([part[10], part[12]]),
        part[13],
        part[14],
    ]


def pair_outer(*pairs):
    size = lax.axis_size("im")
    first = pairs[0][0].value if isinstance(pairs[0][0], Near) else pairs[0][0]
    width = first.shape[1]
    rows = width // 2 // size * len(pairs)
    return list(
        call(
            functools.partial(pair_outer_kernel, pairs=len(pairs), parts=size),
            [Near(low(rows, width))] * size,
            [],
            *[ref for pair in pairs for ref in pair],
        )
    )


def sum_split(pieces, pairs):
    size = lax.axis_size("row")
    rows, width = pieces[0].shape
    return list(
        call(
            functools.partial(
                sum_split_kernel,
                pairs=pairs,
                parts=size,
                pieces=len(pieces),
            ),
            [Near(low(rows // size, width))] * size,
            [(rows, width)],
            *[Near(piece) for piece in pieces],
        )
    )


def add_low(pieces):
    total = pieces[0].astype(FULL)
    for piece in pieces[1:]:
        total = total + piece.astype(FULL)
    return total.astype(LOW)


def sum_far(left, right, axes):
    part = jnp.einsum("tm,tc->mc", left, right, preferred_element_type=FULL)
    return lax.psum(part, axes)


def shards(
    x_in,
    pre_reduce,
    pre_conv,
    pre_expand,
    pre_mid_gain,
    pre_mid_shift,
    pre_out_gain,
    pre_out_shift,
    post_reduce,
    post_conv,
    post_expand,
    post_mid_gain,
    post_mid_shift,
    post_out_gain,
    post_out_shift,
    read_weight,
    read_bias,
    cotangent,
):
    count, strip, side, width = x_in.shape
    strips = lax.axis_size("row")
    tokens = count * strip * side
    cols = side // 2
    rows = strip // 2
    slabs = count * rows
    padded = slabs * SLAB
    small = slabs * cols
    block = -(-small // SLAB) * SLAB
    features = read_weight.shape[1]
    x_low = x_in.reshape(tokens, width)
    pre_out_g, pre_out_s = (pre_out_gain[None], pre_out_shift[None])
    post_out_g, post_out_s = (post_out_gain[None], post_out_shift[None])
    pre_edge = Near(low(count, side, width))
    post_edge = Near(low(count, SLAB, width))
    quick = lax.axis_size("im") == 4 and strips == 4

    first, edge_a, edge_b, normed_a, factor_a = call(
        pre_reduce_kernel,
        [Near(low(tokens, width)), pre_edge, pre_edge, like(tokens, width), like(tokens, LANES)],
        [(tokens, width)],
        x_low,
        pre_reduce,
        pre_mid_gain,
        pre_mid_shift,
    )
    got_a, got_b = edges((edge_a, edge_b))
    (
        second,
        normed_b,
        factor_b,
        normed_c,
        factor_c,
        summed,
        pooled,
        post_first,
        edge_a,
        edge_b,
        post_normed_a,
        post_factor_a,
        pad,
    ) = call(
        pre_rest_kernel,
        [
            low(tokens, width),
            like(tokens, width),
            like(tokens, LANES),
            like(tokens, width),
            like(tokens, LANES),
            like(tokens, width),
            Near(like(padded, width)),
            Near(low(padded, width)),
            post_edge,
            post_edge,
            like(padded, width),
            like(padded, LANES),
            like(count, strip + 2, side, width),
        ],
        [(tokens, width), (side * width // LANES, LANES), (padded, width)],
        x_low,
        Near(first),
        Near(got_a),
        Near(got_b),
        pre_conv,
        pre_expand,
        pre_mid_gain,
        pre_mid_shift,
        pre_out_g,
        pre_out_s,
        post_reduce,
        post_mid_gain,
        post_mid_shift,
    )
    got_a, got_b = edges((edge_a, edge_b))
    (
        block_two,
        left_in,
        left_second,
        post_normed_b,
        post_factor_b,
        post_normed_c,
        post_factor_c,
        post_summed,
        post_pad,
    ) = call(
        functools.partial(post_rest_kernel, cols=cols),
        [
            Near(low(small, width)),
            low(block, width),
            low(block, width),
            like(padded, width),
            like(padded, LANES),
            like(padded, width),
            like(padded, LANES),
            like(padded, width),
            like(count, rows + 2, SLAB, width),
        ],
        [(padded, width), (padded, width), (block, width)],
        Near(pooled),
        Near(post_first),
        Near(got_a),
        Near(got_b),
        post_conv,
        post_expand,
        post_mid_gain,
        post_mid_shift,
        post_out_g,
        post_out_s,
    )
    whole = lax.all_gather(block_two, "row", axis=0, tiled=True)
    readout, grad_pre, *terms, d_read_b = call(
        functools.partial(readout_kernel, strips=strips),
        [
            like(*cotangent.shape, dtype=LOW),
            Near(low(strips * small, features)),
        ]
        + [Near(low(small, width))] * strips
        + [like(1, features)],
        [
            (strips * small, features),
            (strips * small, features),
            (strips * small, width),
        ],
        Near(whole),
        read_weight,
        read_bias[None],
        cotangent,
    )
    terms = share(terms, "row")
    post_gs, post_ge, post_gc, edge_a, edge_b, post_small_b = call(
        functools.partial(post_back_kernel, cols=cols, strips=strips),
        [
            Near(like(padded, width)),
            Near(low(block, width)),
            Near(low(padded, width)),
            post_edge,
            post_edge,
            like(4, width),
        ],
        [(block, width), (padded, width), (padded, width), (padded, width)],
        *[Near(term) for term in terms],
        post_expand,
        post_mid_gain,
        post_mid_shift,
        post_out_g,
        post_normed_b,
        post_factor_b,
        post_normed_c,
        post_factor_c,
        post_summed,
    )
    if quick:
        edge_a, whole, grad_pre = tie(edge_a, whole, grad_pre)
    got_a, got_b = edges((edge_a, edge_b))
    if quick:
        read_slots = pair_outer(
            (Near(whole), Near(swap(whole)), Near(grad_pre), Near(swap(grad_pre)))
        )
        read_parts = [read_slots[0]] + [steps_of(read_slots[at], "im", at) for at in (1, 2)]
        (got_a, got_b), (*read_parts, read_last) = tie_later(
            (got_a, got_b), (*read_parts, read_slots[3])
        )
    (
        post_gr,
        pre_gs,
        pre_ge,
        pre_gc,
        edge_a,
        edge_b,
        post_small_a,
        pre_small_b,
    ) = call(
        functools.partial(middle_back_kernel, cols=cols),
        [
            Near(low(block, width)),
            like(tokens, width),
            Near(low(tokens, width)),
            Near(low(tokens, width)),
            pre_edge,
            pre_edge,
            like(11, width),
            like(4, width),
        ],
        [
            (count, rows + 2, SLAB, width),
            (9, 8, width),
            (padded, width),
            (side * width // LANES, LANES),
            (tokens, width),
            (2, 8, width),
            (padded, width),
            (block, width),
        ],
        Near(post_gc),
        Near(got_a),
        Near(got_b),
        post_pad,
        post_conv,
        post_reduce,
        post_mid_gain,
        post_mid_shift,
        post_normed_a,
        post_factor_a,
        Near(post_gs),
        pre_expand,
        pre_mid_gain,
        pre_mid_shift,
        pre_out_g,
        normed_b,
        factor_b,
        normed_c,
        factor_c,
        summed,
    )
    got_a, got_b = edges((edge_a, edge_b))
    if quick:
        post_parts = pair_outer(
            (left_in, swap(left_in), Near(post_gr), Near(swap(post_gr))),
            (left_second, swap(left_second), Near(post_ge), Near(swap(post_ge))),
        )
        post_sums = share(post_parts, "im")[1:]
        (got_a, got_b), post_sums = tie_later((got_a, got_b), post_sums)
    pre_gr, sums = call(
        pre_back_kernel,
        [Near(low(tokens, width)), Near(like(32, width))],
        [
            (count, strip + 2, side, width),
            (9, 8, width),
            (2, 8, width),
        ],
        Near(pre_gc),
        Near(got_a),
        Near(got_b),
        pad,
        pre_conv,
        pre_mid_gain,
        pre_mid_shift,
        normed_a,
        factor_a,
        pre_small_b,
        post_small_a,
        post_small_b,
        d_read_b,
    )
    if quick:
        far = swap(pre_gr)
        post_parts = sum_split(post_parts[:1] + post_sums, 2)
        post_parts[0], far = tie(post_parts[0], far)
        post_parts = share(post_parts, "row")
        parts = pair_outer(
            (second, swap(second), Near(pre_ge), Near(swap(pre_ge))),
            (x_low, swap(x_low), Near(pre_gr), Near(far)),
        )
        parts[0], sums = tie(parts[0], sums + swap(sums))
        read_parts = read_parts + [steps_of(read_last, "im", 3)]
        near_parts = [steps_of(parts[at], "im", at) for at in (1, 2)]
        grad_in = pre_gs + jnp.einsum("tm,cm->tc", pre_gr, pre_reduce, preferred_element_type=FULL)
        grad_in = grad_in.astype(LOW)
        post_parts, (grad_in, last, *rest) = tie_later(
            post_parts, (grad_in, parts[3], *near_parts, *read_parts)
        )
        near_parts, read_parts = (rest[:2], rest[2:])
        post_parts = share_same(add_low(post_parts), "row")
        last = steps_of(last, "im", 3)
        post_parts, (last, *read_parts) = tie_later(post_parts, (last, *read_parts))
        parts = share(sum_split([parts[0]] + near_parts + [last], 2), "row")
        post_parts = gather_near(jnp.concatenate(post_parts, axis=0))
        read_parts = gather_near(add_low(read_parts))
        parts, rest = tie_later(parts, (*post_parts, *read_parts))
        post_parts, read_parts = (rest[:3], rest[3:])
        parts = share_same(add_low(parts), "row")
        read_parts.append(steps_of(read_parts[0], "im", 3))
        post_parts = post_parts + gather_rest(post_parts)
        parts, rest = tie_later(parts, (*post_parts, *read_parts, sums))
        post_parts, read_parts, sums = (rest[:5], rest[5:9], rest[9])
        parts = gather_near(jnp.concatenate(parts, axis=0))
        alone = lax.broadcasted_iota(jnp.int32, sums.shape, 0) >= 30
        for step in (1, 2):
            sums = sums + jnp.where(alone, 0.0, steps_of(sums, "row", step))
        post_far = swap(jnp.concatenate(post_parts, axis=0))
        read_far = swap(jnp.concatenate(read_parts, axis=0))
        parts, (sums, post_far, read_far, *post_parts) = tie_later(
            parts, (sums, post_far, read_far, *post_parts)
        )
        far = swap(jnp.concatenate(parts, axis=0))
        post_reduce_g, post_expand_g = assemble(post_parts, [post_far], 2, 4, strips)
        (read_total,) = assemble(read_parts, [read_far], 1, 4, 1)
        (post_reduce_g, read_total), (far, sums, *rest) = tie_later(
            (post_reduce_g, read_total), (far, sums, *gather_rest(parts))
        )
        far_rest = swap(jnp.concatenate(rest, axis=0))
        first, *others = share_same(sums, "im")
        sums = (first + others[0]) + (others[1] + others[2])
        small_out = call(
            small_kernel,
            [like(3, 3, width), like(2, width), like(2, width), like(1, width), like(1, width)] * 2,
            [],
            Near(sums),
        )
        pre_expand_g, pre_reduce_g = assemble(parts + rest, [far, far_rest], 2, 4, strips)
        read_bias_g = sums[30]
    else:
        axes = IMG + ("row",)
        post_reduce_g = sum_far(left_in, post_gr, axes)
        post_expand_g = sum_far(left_second, post_ge, axes)
        pre_expand_g = sum_far(second, pre_ge, axes)
        pre_reduce_g = sum_far(x_low, pre_gr, axes)
        read_total = sum_far(whole, grad_pre, IMG)
        read_bias_g = lax.psum(sums[30], IMG)
        sums = lax.psum(sums[:30], axes)
        small_out = small_outputs(sums[:15], width) + small_outputs(sums[15:30], width)
        grad_in = pre_gs + jnp.einsum("tm,cm->tc", pre_gr, pre_reduce, preferred_element_type=FULL)
        grad_in = grad_in.astype(LOW)

    pre_conv_g, pre_gain_g, pre_shift_g, pre_og_g, pre_os_g = small_out[:5]
    post_conv_g, post_gain_g, post_shift_g, post_og_g, post_os_g = small_out[5:]
    return (
        readout,
        grad_in.reshape(x_in.shape),
        pre_reduce_g,
        pre_conv_g,
        pre_expand_g,
        pre_gain_g,
        pre_shift_g,
        pre_og_g.reshape(width),
        pre_os_g.reshape(width),
        post_reduce_g,
        post_conv_g,
        post_expand_g,
        post_gain_g,
        post_shift_g,
        post_og_g.reshape(width),
        post_os_g.reshape(width),
        read_total,
        read_bias_g,
    )


def solution(mesh):
    images, strips = mesh.devices.shape
    split = jax.sharding.Mesh(
        mesh.devices.reshape(images // 2, 2, strips), ("im", "half", "row")
    )
    return jax.shard_map(
        shards,
        mesh=split,
        in_specs=(P(IMG, "row", None, None),)
        + (P(),) * 14
        + (P(None, "row"), P("row"), P(IMG, None, None, "row")),
        out_specs=(P(IMG, None, None, "row"), P(IMG, "row", None, None))
        + (P(),) * 14
        + (P(None, "row"), P("row")),
        check_vma=False,
    )
```

```python
import functools

import jax
import jax.numpy as jnp
from jax import lax
from jax.experimental import pallas as pl
from jax.experimental.pallas import tpu as pltpu
from jax.sharding import PartitionSpec as P

EPSILON = 1e-06
SQRT_HALF = 0.7071067811865476
INV_SQRT_TWO_PI = 0.3989422804014327
LOW = jnp.bfloat16
FULL = jnp.float32
IMG = ("im", "half")
TILE = 256
SLAB = 16
LANES = 128
VMEM_BYTES = 24 * 1024 * 1024


def tie(*values):
    return lax.optimization_barrier(values)


def tie_later(first, second):
    first = list(tie(*first))
    out = list(tie(*first, *second))
    return (out[: len(first)], out[len(first) :])


def norm(value):
    centred = value - jnp.mean(value, axis=-1, keepdims=True)
    factor = lax.rsqrt(jnp.mean(centred * centred, axis=-1, keepdims=True) + EPSILON)
    return (centred * factor, factor)


def norm_back(grad, normed, factor, gain):
    scaled = grad * gain
    return factor * (
        scaled
        - jnp.mean(scaled, axis=-1, keepdims=True)
        - normed * jnp.mean(scaled * normed, axis=-1, keepdims=True)
    )


def gate(value):
    return 0.5 * jnp.tanh(0.5 * value) + 0.5


def silu(value):
    return value * gate(value)


def silu_back(grad, value):
    sigma = gate(value)
    return grad * sigma * (1.0 + value * (1.0 - sigma))


def flip(place, step):
    bit = 1
    while bit <= step:
        if step & bit:
            place = place + bit - 2 * bit * ((place // bit) % 2)
        bit *= 2
    return place


def wide(factor):
    return jnp.broadcast_to(factor, (factor.shape[0], LANES))


def fold(value):
    return jnp.sum(value.reshape(-1, 8, value.shape[-1]), axis=0)


def live(rows, cols):
    at = lax.broadcasted_iota(jnp.int32, (rows, 1), 0)
    return lax.rem(at, SLAB) < cols


def from_left(value):
    at = lax.broadcasted_iota(jnp.int32, (value.shape[0], 1), 0)
    return jnp.where(at == 0, 0.0, pltpu.roll(value, 1, 0))


def from_right(value):
    last = value.shape[0] - 1
    at = lax.broadcasted_iota(jnp.int32, (value.shape[0], 1), 0)
    return jnp.where(at == last, 0.0, pltpu.roll(value, last, 0))


def matmul(left_ref, right_ref, out_ref):
    @pl.loop(0, right_ref.shape[1] // TILE)
    def _(at):
        cols = pl.ds(pl.multiple_of(at * TILE, TILE), TILE)
        out_ref[:, cols] = jnp.dot(
            left_ref[...].astype(LOW), right_ref[:, cols], preferred_element_type=FULL
        )


def matmul_back(left_ref, right_ref, out_ref):
    @pl.loop(0, right_ref.shape[0] // TILE)
    def _(at):
        cols = pl.ds(pl.multiple_of(at * TILE, TILE), TILE)
        out_ref[:, cols] = lax.dot_general(
            left_ref[...].astype(LOW),
            right_ref[cols, :],
            (((1,), (1,)), ((), ())),
            preferred_element_type=FULL,
        ).astype(out_ref.dtype)


def rows_of(at, size):
    return pl.ds(pl.multiple_of(at * size, SLAB), size)


def fill_halo(at_ref, pad_ref, low_ref, got_a_ref, got_b_ref):
    count, rows, cols, width = pad_ref.shape
    rows = rows - 2
    even = lax.rem(at_ref[2], 2) == 0
    for image in range(count):
        got_a, got_b = (got_a_ref[image].astype(FULL), got_b_ref[image].astype(FULL))
        pad_ref[image, 0] = jnp.where(even, got_b, got_a)
        pad_ref[image, rows + 1] = jnp.where(even, got_a, got_b)

    size = cols if cols % SLAB == 0 else 2 * cols
    per = size // cols
    each = rows // per

    @pl.loop(0, count * each)
    def _(at):
        part = low_ref[rows_of(at, size), :].astype(FULL).reshape(per, cols, width)
        pad_ref[at // each, pl.ds(1 + per * lax.rem(at, each), per)] = part


def set_edges(at_ref, edge_a_ref, edge_b_ref, image, head, tail):
    even = lax.rem(at_ref[2], 2) == 0
    edge_a_ref[image] = jnp.where(even, tail, head).astype(LOW)
    edge_b_ref[image] = jnp.where(even, head, tail).astype(LOW)


def conv_row(pad_ref, taps, image, row):
    lines = [pad_ref[image, row + top] for top in range(3)]
    sums = [
        lines[0] * taps[left] + lines[1] * taps[3 + left] + lines[2] * taps[6 + left]
        for left in range(3)
    ]
    return from_left(sums[0]) + sums[1] + from_right(sums[2])


def conv_back_row(pad_ref, grad_ref, taps, taps_ref, image, row):
    lines = [grad_ref[image, row + top] for top in range(3)]
    sums = [
        lines[2] * taps[left] + lines[1] * taps[3 + left] + lines[0] * taps[6 + left]
        for left in range(3)
    ]
    shifted = [from_right(lines[1]), lines[1], from_left(lines[1])]
    for top in range(3):
        source = pad_ref[image, row + top]
        for left in range(3):
            taps_ref[3 * top + left] += fold(source * shifted[left])
    return from_right(sums[0]) + sums[1] + from_left(sums[2])


def pack(compact, source, out_ref, cols):
    compact[...] = jnp.zeros(compact.shape, FULL)
    for at in range(source.shape[0] // SLAB):
        compact[pl.ds(at * cols, cols), :] = source[pl.ds(at * SLAB, cols), :]
    out_ref[...] = compact[...].astype(LOW)


def narrow(pair, value):
    side = value.shape[0]
    parts = []
    for at in range(value.shape[1] // LANES):
        pair[pl.ds(at * side, side), :] = value[:, at * LANES : (at + 1) * LANES]
        parts.append(
            pair[pl.ds(at * side, side // 2, stride=2), :]
            + pair[pl.ds(at * side + 1, side // 2, stride=2), :]
        )
    return jnp.concatenate(parts, axis=1)


def widen(pair, value):
    cols = value.shape[0]
    parts = []
    for at in range(value.shape[1] // LANES):
        part = value[:, at * LANES : (at + 1) * LANES]
        pair[pl.ds(2 * cols * at, cols, stride=2), :] = part
        pair[pl.ds(2 * cols * at + 1, cols, stride=2), :] = part
        parts.append(pair[pl.ds(2 * cols * at, 2 * cols), :])
    return jnp.concatenate(parts, axis=1)


def tap_rows(conv_ref):
    lines = [conv_ref[top].astype(FULL) for top in range(3)]
    return [lines[at // 3][at % 3 : at % 3 + 1] for at in range(9)]


def finish(small_ref, sums_ref, at, place):
    small_ref[pl.ds(place, 1), :] = jnp.sum(sums_ref[at], axis=0, keepdims=True)


def pre_reduce_kernel(
    need,
    send,
    at_ref,
    x_ref, w_ref, gain_ref, shift_ref, first_ref, edge_a_ref, edge_b_ref, normed_ref, factor_ref, red
):
    count, side, width = edge_a_ref.shape
    size = 2 * side
    steps = x_ref.shape[0] // size
    need(x_ref, w_ref)
    matmul(x_ref, w_ref, red)
    need(gain_ref, shift_ref)
    gain, shift = (gain_ref[pl.ds(0, 1), :], shift_ref[pl.ds(0, 1), :])

    @pl.loop(0, steps)
    def _(at):
        rows = rows_of(at, size)
        normed, factor = norm(red[rows, :])
        normed_ref[rows, :] = normed
        factor_ref[rows, :] = wide(factor)
        first_ref[rows, :] = silu(normed * gain + shift).astype(LOW)

    each = steps // count
    for image in range(count):
        head = first_ref[pl.ds(image * each * size, size), :].astype(FULL)
        tail = first_ref[pl.ds((image * each + each - 1) * size, size), :].astype(FULL)
        set_edges(at_ref, edge_a_ref, edge_b_ref, image, head[:side], tail[side:])


def pre_rest_kernel(
    need,
    send,
    at_ref,
    x_ref,
    first_ref,
    got_a_ref,
    got_b_ref,
    conv_ref,
    expand_ref,
    gain_ref,
    shift_ref,
    out_gain_ref,
    out_shift_ref,
    reduce_ref,
    post_gain_ref,
    post_shift_ref,
    second_ref,
    normed_b_ref,
    factor_b_ref,
    normed_c_ref,
    factor_c_ref,
    summed_ref,
    pooled_ref,
    post_first_ref,
    edge_a_ref,
    edge_b_ref,
    post_normed_ref,
    post_factor_ref,
    pad,
    exp,
    pair,
    red,
):
    count, strip, side, width = pad.shape
    strip = strip - 2
    size = 2 * side
    each = strip // 2
    need(first_ref, got_a_ref, got_b_ref)
    fill_halo(at_ref, pad, first_ref, got_a_ref, got_b_ref)
    need(conv_ref, gain_ref, shift_ref)
    send(pad)
    taps = tap_rows(conv_ref)
    gain, shift = (gain_ref[pl.ds(1, 1), :], shift_ref[pl.ds(1, 1), :])

    @pl.loop(0, count * each)
    def _(at):
        rows = rows_of(at, size)
        image, row = (at // each, 2 * lax.rem(at, each))
        conv = jnp.concatenate(
            [conv_row(pad, taps, image, row), conv_row(pad, taps, image, row + 1)], axis=0
        )
        normed, factor = norm(conv)
        normed_b_ref[rows, :] = normed
        factor_b_ref[rows, :] = wide(factor)
        second_ref[rows, :] = silu(normed * gain + shift).astype(LOW)

    send(second_ref, normed_b_ref, factor_b_ref)
    need(expand_ref)
    matmul(second_ref, expand_ref, exp)
    need(x_ref, out_gain_ref, out_shift_ref)
    out_gain, out_shift = (out_gain_ref[...], out_shift_ref[...])
    cols = side // 2
    for at in range(count * each):
        rows = pl.ds(at * size, size)
        normed, factor = norm(exp[rows, :])
        normed_c_ref[rows, :] = normed
        factor_c_ref[rows, :] = wide(factor)
        summed = x_ref[rows, :].astype(FULL) + normed * out_gain + out_shift
        summed_ref[rows, :] = summed
        block = silu(summed)
        half = narrow(pair, block[:side] + block[side:])
        pooled_ref[pl.ds(at * SLAB, cols), :] = 0.25 * half
        pooled_ref[pl.ds(at * SLAB + cols, SLAB - cols), :] = jnp.zeros(
            (SLAB - cols, width), FULL
        )
    send(normed_c_ref, factor_c_ref, summed_ref)
    need(reduce_ref, post_gain_ref, post_shift_ref)
    matmul(pooled_ref, reduce_ref, red)
    normed, factor = norm(red[...])
    post_normed_ref[...] = normed
    post_factor_ref[...] = wide(factor)
    first = silu(normed * post_gain_ref[pl.ds(0, 1), :] + post_shift_ref[pl.ds(0, 1), :])
    post_first_ref[...] = jnp.where(live(red.shape[0], cols), first, 0.0).astype(LOW)
    for image in range(count):
        head = post_first_ref[pl.ds(image * each * SLAB, SLAB), :].astype(FULL)
        tail = post_first_ref[pl.ds((image * each + each - 1) * SLAB, SLAB), :].astype(FULL)
        set_edges(at_ref, edge_a_ref, edge_b_ref, image, head, tail)


def post_rest_kernel(
    need,
    send,
    at_ref,
    pooled_ref,
    first_ref,
    got_a_ref,
    got_b_ref,
    conv_ref,
    expand_ref,
    gain_ref,
    shift_ref,
    out_gain_ref,
    out_shift_ref,
    block_ref,
    left_in_ref,
    left_second_ref,
    normed_b_ref,
    factor_b_ref,
    normed_c_ref,
    factor_c_ref,
    summed_ref,
    pad,
    second,
    exp,
    compact,
    *,
    cols
):
    count, rows, _, width = pad.shape
    rows = rows - 2
    small = block_ref.shape[0]
    need(first_ref, got_a_ref, got_b_ref)
    fill_halo(at_ref, pad, first_ref, got_a_ref, got_b_ref)
    send(pad)
    need(conv_ref, gain_ref, shift_ref, pooled_ref)
    taps = tap_rows(conv_ref)
    gain, shift = (gain_ref[pl.ds(1, 1), :], shift_ref[pl.ds(1, 1), :])

    @pl.loop(0, count * rows)
    def _(at):
        place = rows_of(at, SLAB)
        normed, factor = norm(conv_row(pad, taps, at // rows, lax.rem(at, rows)))
        normed_b_ref[place, :] = normed
        factor_b_ref[place, :] = wide(factor)
        second[place, :] = silu(normed * gain + shift)

    send(normed_b_ref, factor_b_ref)
    need(expand_ref)
    matmul(second, expand_ref, exp)
    need(out_gain_ref, out_shift_ref)
    normed, factor = norm(exp[...])
    normed_c_ref[...] = normed
    factor_c_ref[...] = wide(factor)
    summed = pooled_ref[...] + normed * out_gain_ref[...] + out_shift_ref[...]
    summed_ref[...] = summed
    exp[...] = silu(summed)
    compact[...] = jnp.zeros(compact.shape, FULL)
    for at in range(count * rows):
        compact[pl.ds(at * cols, cols), :] = exp[pl.ds(at * SLAB, cols), :]
    block_ref[...] = compact[pl.ds(0, small), :].astype(LOW)
    send(block_ref, normed_c_ref, factor_c_ref, summed_ref)
    pack(compact, pooled_ref, left_in_ref, cols)
    pack(compact, second, left_second_ref, cols)


def readout_kernel(
    need,
    send,
    at_ref,
    whole_ref,
    w_ref,
    bias_ref,
    cot_ref,
    out_ref,
    grad_ref,
    *refs,
    strips
):
    slots, (bias_grad_ref, cot, out, terms_ref) = (refs[:strips], refs[strips:])
    images, lines, cols, _ = cot_ref.shape
    rows = lines // strips
    need(cot_ref)
    for at in range(images * lines):
        strip, image, row = (at // (images * rows), at // rows % images, at % rows)
        cot[pl.ds(at * cols, cols), :] = cot_ref[image, strip * rows + row].astype(FULL)
    need(whole_ref, w_ref, bias_ref)

    @pl.loop(0, w_ref.shape[1] // TILE)
    def _(at):
        lanes = pl.ds(pl.multiple_of(at * TILE, TILE), TILE)
        act = jnp.dot(whole_ref[...], w_ref[:, lanes], preferred_element_type=FULL)
        act = act + bias_ref[:, lanes]
        cdf = 0.5 * (1.0 + lax.erf(act * SQRT_HALF))
        density = jnp.exp(-0.5 * act * act) * INV_SQRT_TWO_PI
        out[:, lanes] = act * cdf
        grad = (cot[:, lanes] * (cdf + act * density)).astype(LOW)
        grad_ref[:, lanes] = grad
        bias_grad_ref[:, lanes] = jnp.sum(grad.astype(FULL), axis=0, keepdims=True)

    send(grad_ref, bias_grad_ref)
    matmul_back(grad_ref, w_ref, terms_ref)
    small = slots[0].shape[0]
    for step in range(strips):
        begin = pl.multiple_of(flip(at_ref[2], step) * small, 8)
        slots[step][...] = terms_ref[pl.ds(begin, small), :].astype(LOW)
    for at in range(images * lines):
        strip, image, row = (at // (images * rows), at // rows % images, at % rows)
        out_ref[image, strip * rows + row] = out[pl.ds(at * cols, cols), :].astype(LOW)


def post_back_kernel(
    need,
    send,
    at_ref,
    *refs,
    cols,
    strips
):
    pieces, refs = (refs[:strips], refs[strips:])
    (
    expand_ref,
    gain_ref,
    shift_ref,
    out_gain_ref,
    normed_b_ref,
    factor_b_ref,
    normed_c_ref,
    factor_c_ref,
    summed_ref,
    grad_sum_ref,
    grad_exp_ref,
    grad_conv_ref,
    edge_a_ref,
    edge_b_ref,
    small_ref,
    compact,
    spread_out,
    exp,
    sec,
    ) = refs
    count = edge_a_ref.shape[0]
    tokens, width = grad_sum_ref.shape
    each = tokens // SLAB // count
    need(*pieces)
    total = pieces[0][...].astype(FULL)
    for piece in pieces[1:]:
        total = total + piece[...].astype(FULL)
    compact[...] = jnp.zeros(compact.shape, FULL)
    compact[pl.ds(0, total.shape[0]), :] = total
    spread_out[...] = jnp.zeros((tokens, width), FULL)
    for at in range(tokens // SLAB):
        spread_out[pl.ds(at * SLAB, cols), :] = compact[pl.ds(at * cols, cols), :]
    need(summed_ref, normed_c_ref, factor_c_ref, out_gain_ref)
    grad_sum = silu_back(spread_out[...], summed_ref[...])
    grad_sum_ref[...] = grad_sum
    normed = normed_c_ref[...]
    exp[...] = norm_back(grad_sum, normed, factor_c_ref[:, :1], out_gain_ref[...])
    small_ref[pl.ds(2, 1), :] = jnp.sum(grad_sum * normed, axis=0, keepdims=True)
    small_ref[pl.ds(3, 1), :] = jnp.sum(grad_sum, axis=0, keepdims=True)
    pack(compact, exp, grad_exp_ref, cols)
    send(grad_sum_ref, grad_exp_ref)
    need(expand_ref)
    matmul_back(exp, expand_ref, sec)
    need(gain_ref, shift_ref, normed_b_ref, factor_b_ref)
    gain, shift = (gain_ref[pl.ds(1, 1), :], shift_ref[pl.ds(1, 1), :])
    normed = normed_b_ref[...]
    grad = silu_back(sec[...], normed * gain + shift)
    grad_conv_ref[...] = norm_back(grad, normed, factor_b_ref[:, :1], gain).astype(LOW)
    small_ref[pl.ds(0, 1), :] = jnp.sum(grad * normed, axis=0, keepdims=True)
    small_ref[pl.ds(1, 1), :] = jnp.sum(grad, axis=0, keepdims=True)
    for image in range(count):
        head = grad_conv_ref[pl.ds(image * each * SLAB, SLAB), :].astype(FULL)
        tail = grad_conv_ref[pl.ds((image * each + each - 1) * SLAB, SLAB), :].astype(FULL)
        set_edges(at_ref, edge_a_ref, edge_b_ref, image, head, tail)


def middle_back_kernel(
    need,
    send,
    at_ref,
    grad_conv_ref,
    got_a_ref,
    got_b_ref,
    pad,
    post_conv_ref,
    post_reduce_ref,
    post_gain_ref,
    post_shift_ref,
    post_normed_ref,
    post_factor_ref,
    post_grad_sum_ref,
    expand_ref,
    gain_ref,
    shift_ref,
    out_gain_ref,
    normed_b_ref,
    factor_b_ref,
    normed_c_ref,
    factor_c_ref,
    summed_ref,
    post_grad_red_ref,
    grad_sum_ref,
    grad_exp_ref,
    pre_grad_conv_ref,
    edge_a_ref,
    edge_b_ref,
    post_small_ref,
    small_ref,
    grad_pad,
    taps_sum,
    grad_in,
    pair,
    sec,
    sums,
    post_red,
    compact,
    *,
    cols
):
    count, side, width = edge_a_ref.shape
    need(grad_conv_ref, got_a_ref, got_b_ref)
    fill_halo(at_ref, grad_pad, grad_conv_ref, got_a_ref, got_b_ref)
    need(pad, post_conv_ref)
    need(post_gain_ref, post_shift_ref, post_normed_ref, post_factor_ref)
    taps = tap_rows(post_conv_ref)
    taps_sum[...] = jnp.zeros_like(taps_sum)
    sums[...] = jnp.zeros_like(sums)
    gain, shift = (post_gain_ref[pl.ds(0, 1), :], post_shift_ref[pl.ds(0, 1), :])
    each = post_grad_sum_ref.shape[0] // SLAB // count

    @pl.loop(0, count * each)
    def _(at):
        place = rows_of(at, SLAB)
        grad = conv_back_row(pad, grad_pad, taps, taps_sum, at // each, lax.rem(at, each))
        normed = post_normed_ref[place, :]
        grad = jnp.where(live(SLAB, cols), silu_back(grad, normed * gain + shift), 0.0)
        sums[0] += fold(grad * normed)
        sums[1] += fold(grad)
        post_red[place, :] = norm_back(grad, normed, post_factor_ref[place, :1], gain)

    for at in range(9):
        finish(post_small_ref, taps_sum, at, at)
    finish(post_small_ref, sums, 0, 9)
    finish(post_small_ref, sums, 1, 10)
    pack(compact, post_red, post_grad_red_ref, cols)
    send(post_grad_red_ref, post_small_ref)
    need(post_reduce_ref)
    matmul_back(post_red, post_reduce_ref, grad_in)
    sums[...] = jnp.zeros_like(sums)
    size = 2 * side
    need(out_gain_ref, post_grad_sum_ref, summed_ref, normed_c_ref, factor_c_ref)
    out_gain = out_gain_ref[...]
    for at in range(count * each):
        rows = pl.ds(at * size, size)
        place = pl.ds(at * SLAB, cols)
        grad = 0.25 * (post_grad_sum_ref[place, :] + grad_in[place, :])
        grad = widen(pair, grad)
        grad = jnp.concatenate([grad, grad], axis=0)
        grad_sum = silu_back(grad, summed_ref[rows, :])
        grad_sum_ref[rows, :] = grad_sum
        normed = normed_c_ref[rows, :]
        sums[0] += fold(grad_sum * normed)
        sums[1] += fold(grad_sum)
        grad_exp_ref[rows, :] = norm_back(
            grad_sum, normed, factor_c_ref[rows, :1], out_gain
        ).astype(LOW)
    finish(small_ref, sums, 0, 2)
    finish(small_ref, sums, 1, 3)
    send(grad_sum_ref, grad_exp_ref)
    need(expand_ref)
    matmul_back(grad_exp_ref, expand_ref, sec)
    need(gain_ref, shift_ref, normed_b_ref, factor_b_ref)
    sums[...] = jnp.zeros_like(sums)
    gain_b, shift_b = (gain_ref[pl.ds(1, 1), :], shift_ref[pl.ds(1, 1), :])

    @pl.loop(0, count * each)
    def _(at):
        rows = rows_of(at, size)
        normed = normed_b_ref[rows, :]
        grad = silu_back(sec[rows, :], normed * gain_b + shift_b)
        sums[0] += fold(grad * normed)
        sums[1] += fold(grad)
        pre_grad_conv_ref[rows, :] = norm_back(
            grad, normed, factor_b_ref[rows, :1], gain_b
        ).astype(LOW)

    finish(small_ref, sums, 0, 0)
    finish(small_ref, sums, 1, 1)
    for image in range(count):
        head = pre_grad_conv_ref[pl.ds(image * each * size, size), :].astype(FULL)
        tail = pre_grad_conv_ref[pl.ds((image * each + each - 1) * size, size), :].astype(FULL)
        set_edges(at_ref, edge_a_ref, edge_b_ref, image, head[:side], tail[side:])


def pre_back_kernel(
    need,
    send,
    at_ref,
    grad_conv_ref,
    got_a_ref,
    got_b_ref,
    pad,
    conv_ref,
    gain_ref,
    shift_ref,
    normed_ref,
    factor_ref,
    small_b_ref,
    post_small_a_ref,
    post_small_b_ref,
    read_bias_ref,
    grad_red_ref,
    small_ref,
    grad_pad,
    taps_sum,
    sums,
):
    count, strip, side, width = pad.shape
    strip = strip - 2
    size = 2 * side
    each = strip // 2
    need(grad_conv_ref, got_a_ref, got_b_ref)
    fill_halo(at_ref, grad_pad, grad_conv_ref, got_a_ref, got_b_ref)
    need(pad, conv_ref)
    need(gain_ref, shift_ref, normed_ref, factor_ref)
    taps = tap_rows(conv_ref)
    taps_sum[...] = jnp.zeros_like(taps_sum)
    sums[...] = jnp.zeros_like(sums)
    gain, shift = (gain_ref[pl.ds(0, 1), :], shift_ref[pl.ds(0, 1), :])

    @pl.loop(0, count * each)
    def _(at):
        rows = rows_of(at, size)
        image, row = (at // each, 2 * lax.rem(at, each))
        grad = jnp.concatenate(
            [
                conv_back_row(pad, grad_pad, taps, taps_sum, image, row),
                conv_back_row(pad, grad_pad, taps, taps_sum, image, row + 1),
            ],
            axis=0,
        )
        normed = normed_ref[rows, :]
        grad = silu_back(grad, normed * gain + shift)
        sums[0] += fold(grad * normed)
        sums[1] += fold(grad)
        grad_red_ref[rows, :] = norm_back(grad, normed, factor_ref[rows, :1], gain).astype(LOW)

    for at in range(9):
        finish(small_ref, taps_sum, at, at)
    finish(small_ref, sums, 0, 9)
    finish(small_ref, sums, 1, 10)
    need(small_b_ref, post_small_a_ref, post_small_b_ref, read_bias_ref)
    small_ref[pl.ds(11, 4), :] = small_b_ref[...]
    small_ref[pl.ds(15, 11), :] = post_small_a_ref[...]
    small_ref[pl.ds(26, 4), :] = post_small_b_ref[...]
    small_ref[pl.ds(30, 1), :] = read_bias_ref[...]
    small_ref[pl.ds(31, 1), :] = jnp.zeros_like(read_bias_ref)


def pair_outer_kernel(need, send, at_ref, *refs, pairs, parts):
    takes = 4 * pairs
    outs = refs[takes:]
    half, plane = (at_ref[0], at_ref[1])
    rows = outs[0].shape[0] // pairs
    for pair in range(pairs):
        left, left_far, right, right_far = refs[4 * pair : 4 * pair + 4]
        need(left, left_far, right, right_far)
        for step in range(parts):
            begin = half * (rows * parts) + flip(plane, step) * rows
            lanes = pl.ds(pl.multiple_of(begin, LANES), rows)
            total = lax.dot_general(
                left[:, lanes], right[...], (((0,), (0,)), ((), ())), preferred_element_type=FULL
            ) + lax.dot_general(
                left_far[:, lanes],
                right_far[...],
                (((0,), (0,)), ((), ())),
                preferred_element_type=FULL,
            )
            outs[step][pl.ds(pair * rows, rows), :] = total.astype(LOW)
    send(*outs)


def sum_split_kernel(need, send, at_ref, *refs, pairs, parts, pieces, along=2):
    takes, outs = (refs[:pieces], refs[pieces : pieces + parts])
    total = refs[-1]
    need(*takes)
    value = takes[0][...].astype(FULL)
    for at in range(1, pieces):
        value = value + takes[at][...].astype(FULL)
    total[...] = value
    rows = total.shape[0] // pairs // parts
    for step in range(parts):
        begin = flip(at_ref[along], step) * rows
        for pair in range(pairs):
            place = pl.ds(pl.multiple_of(pair * rows * parts + begin, SLAB), rows)
            outs[step][pl.ds(pair * rows, rows), :] = total[place, :].astype(LOW)
    send(*outs)


def assemble_kernel(*refs, spans, pairs, planes, strips):
    takes = len(spans)
    parts, outs = (refs[:takes], refs[takes : takes + pairs])
    full, sem = (refs[takes + pairs : takes + 2 * pairs], refs[-1])
    half, plane, row = places()
    rows = spans[0] // pairs // strips
    block = strips * rows
    pieces = []
    for part, span in zip(parts, spans):
        pieces += [(part, begin) for begin in range(0, span, pairs * rows)]
    writes = []
    for pair in range(pairs):
        for at in range(2 * planes * strips):
            near, step = (at // strips, at % strips)
            side, spot = (flip(half, near // planes), flip(plane, near % planes))
            place = side * (planes * block) + spot * block
            if strips > 1:
                place = place + flip(row, step) * rows
            part, begin = pieces[at]
            full[pair][pl.ds(pl.multiple_of(place, SLAB), rows), :] = part[
                pl.ds(begin + pair * rows, rows), :
            ].astype(FULL)
        writes.append(pltpu.make_async_copy(full[pair], outs[pair], sem.at[pair]))
        writes[-1].start()
    for write in writes:
        write.wait()


def assemble(parts, far, pairs, planes, strips):
    out = like(2 * planes * parts[0].shape[0] // pairs, parts[0].shape[1])
    parts = [pltpu.with_memory_space_constraint(part, pltpu.VMEM) for part in parts + far]
    return pl.pallas_call(
        functools.partial(
            assemble_kernel,
            spans=[part.shape[0] for part in parts],
            pairs=pairs,
            planes=planes,
            strips=strips,
        ),
        out_shape=[pltpu.HBM(out.shape, out.dtype)] * pairs,
        in_specs=[pl.BlockSpec(memory_space=pltpu.VMEM)] * len(parts),
        out_specs=[pl.BlockSpec(memory_space=pltpu.HBM)] * pairs,
        scratch_shapes=[pltpu.VMEM(out.shape, FULL)] * pairs + [pltpu.SemaphoreType.DMA((pairs,))],
        compiler_params=pltpu.CompilerParams(vmem_limit_bytes=VMEM_BYTES),
        cost_estimate=pl.CostEstimate(flops=0, bytes_accessed=0, transcendentals=0),
    )(*parts)


def small_kernel(need, send, at_ref, sums_ref, *outs):
    for place in range(2):
        conv, gain, shift, out_gain, out_shift = outs[5 * place : 5 * place + 5]
        rows = sums_ref[pl.ds(15 * place, 15), :]
        for top in range(3):
            conv[top] = rows[3 * top : 3 * top + 3]
        gain[pl.ds(0, 1), :] = rows[9:10]
        gain[pl.ds(1, 1), :] = rows[11:12]
        shift[pl.ds(0, 1), :] = rows[10:11]
        shift[pl.ds(1, 1), :] = rows[12:13]
        out_gain[...] = rows[13:14]
        out_shift[...] = rows[14:15]


class Near:
    def __init__(self, value):
        self.value = value


def like(*shape, dtype=FULL):
    return jax.ShapeDtypeStruct(shape, dtype)


def low(*shape):
    return like(*shape, dtype=LOW)


def places():
    return [lax.axis_index(axis) for axis in ("half", "im", "row")]


def call(kernel, outs, scratch, *args):
    near_in = [isinstance(arg, Near) for arg in args]
    near_out = [isinstance(out, Near) for out in outs]
    args = [arg.value if isinstance(arg, Near) else arg for arg in args]
    outs = [out.value if isinstance(out, Near) else out for out in outs]
    takes, gives = (len(args), len(outs))
    far_in = [at for at in range(takes) if not near_in[at]]
    far_out = [at for at in range(gives) if not near_out[at]]

    def body(*refs):
        given, refs = (list(refs[:takes]), refs[takes:])
        made, refs = (list(refs[:gives]), refs[gives:])
        rest = refs[len(far_in) + len(far_out) :]
        reads, writes = ({}, {})
        if far_in:
            in_sem = rest[-1]
            rest = rest[:-1]
        if far_out:
            out_sem = rest[-1]
            rest = rest[:-1]
        for place, at in enumerate(far_in):
            reads[at] = pltpu.make_async_copy(given[at], refs[place], in_sem.at[place])
            given[at] = refs[place]
        for place, at in enumerate(far_out):
            mirror = refs[len(far_in) + place]
            writes[at] = pltpu.make_async_copy(mirror, made[at], out_sem.at[place])
            made[at] = mirror
        for at in sorted(reads, key=lambda at: args[at].size):
            reads[at].start()
        started = []

        def need(*wanted):
            for at in list(reads):
                if any(given[at] is ref for ref in wanted):
                    reads.pop(at).wait()

        def send(*ready):
            for at in list(writes):
                if any(made[at] is ref for ref in ready):
                    started.append(writes.pop(at))
                    started[-1].start()

        kernel(need, send, places(), *given, *made, *rest)
        need(*given)
        send(*made)
        for write in started:
            write.wait()

    spaces = {True: pltpu.VMEM, False: pltpu.HBM}
    args = [
        pltpu.with_memory_space_constraint(arg, spaces[near]) for arg, near in zip(args, near_in)
    ]
    return pl.pallas_call(
        body,
        out_shape=[spaces[near](out.shape, out.dtype) for out, near in zip(outs, near_out)],
        in_specs=[pl.BlockSpec(memory_space=spaces[near]) for near in near_in],
        out_specs=[pl.BlockSpec(memory_space=spaces[near]) for near in near_out],
        scratch_shapes=[pltpu.VMEM(args[at].shape, args[at].dtype) for at in far_in]
        + [pltpu.VMEM(outs[at].shape, outs[at].dtype) for at in far_out]
        + [pltpu.VMEM(shape, FULL) for shape in scratch]
        + [pltpu.SemaphoreType.DMA((len(far_out),))] * bool(far_out)
        + [pltpu.SemaphoreType.DMA((len(far_in),))] * bool(far_in),
        compiler_params=pltpu.CompilerParams(vmem_limit_bytes=VMEM_BYTES),
        cost_estimate=pl.CostEstimate(flops=0, bytes_accessed=0, transcendentals=0),
    )(*args)


def edges(parity_edges):
    size = lax.axis_size("row")
    inner = [(at, at ^ 1) for at in range(size)]
    outer = [(at, at + 1) for at in range(1, size - 1, 2)]
    outer = outer + [(to, at) for at, to in outer]
    return (
        lax.ppermute(parity_edges[0], "row", inner),
        lax.ppermute(parity_edges[1], "row", outer),
    )


def swap(field):
    return lax.ppermute(field, "half", [(0, 1), (1, 0)])


def steps_of(value, axis, step):
    size = lax.axis_size(axis)
    return lax.ppermute(value, axis, [(at, at ^ step) for at in range(size)])


def share(parts, axis):
    return [parts[0]] + [steps_of(parts[at], axis, at) for at in range(1, len(parts))]


def share_same(part, axis):
    size = lax.axis_size(axis)
    return [part] + [steps_of(part, axis, at) for at in range(1, size)]


def gather_near(part):
    return [part, steps_of(part, "im", 1), steps_of(part, "im", 2)]


def gather_rest(parts):
    half = parts[0].shape[0] // 2
    return [steps_of(parts[1][:half], "im", 2), steps_of(parts[2][half:], "im", 1)]


def small_outputs(part, width):
    return [
        part[:9].reshape(3, 3, width),
        jnp.stack([part[9], part[11]]),
        jnp.stack([part[10], part[12]]),
        part[13],
        part[14],
    ]


def pair_outer(*pairs):
    size = lax.axis_size("im")
    first = pairs[0][0].value if isinstance(pairs[0][0], Near) else pairs[0][0]
    width = first.shape[1]
    rows = width // 2 // size * len(pairs)
    return list(
        call(
            functools.partial(pair_outer_kernel, pairs=len(pairs), parts=size),
            [Near(low(rows, width))] * size,
            [],
            *[ref for pair in pairs for ref in pair],
        )
    )


def sum_split(pieces, pairs):
    size = lax.axis_size("row")
    rows, width = pieces[0].shape
    return list(
        call(
            functools.partial(
                sum_split_kernel,
                pairs=pairs,
                parts=size,
                pieces=len(pieces),
            ),
            [Near(low(rows // size, width))] * size,
            [(rows, width)],
            *[Near(piece) for piece in pieces],
        )
    )


def add_low(pieces):
    total = pieces[0].astype(FULL)
    for piece in pieces[1:]:
        total = total + piece.astype(FULL)
    return total.astype(LOW)


def sum_far(left, right, axes):
    part = jnp.einsum("tm,tc->mc", left, right, preferred_element_type=FULL)
    return lax.psum(part, axes)


def shards(
    x_in,
    pre_reduce,
    pre_conv,
    pre_expand,
    pre_mid_gain,
    pre_mid_shift,
    pre_out_gain,
    pre_out_shift,
    post_reduce,
    post_conv,
    post_expand,
    post_mid_gain,
    post_mid_shift,
    post_out_gain,
    post_out_shift,
    read_weight,
    read_bias,
    cotangent,
):
    count, strip, side, width = x_in.shape
    strips = lax.axis_size("row")
    tokens = count * strip * side
    cols = side // 2
    rows = strip // 2
    slabs = count * rows
    padded = slabs * SLAB
    small = slabs * cols
    block = -(-small // SLAB) * SLAB
    features = read_weight.shape[1]
    x_low = x_in.reshape(tokens, width)
    pre_out_g, pre_out_s = (pre_out_gain[None], pre_out_shift[None])
    post_out_g, post_out_s = (post_out_gain[None], post_out_shift[None])
    pre_edge = Near(low(count, side, width))
    post_edge = Near(low(count, SLAB, width))
    quick = lax.axis_size("im") == 4 and strips == 4

    first, edge_a, edge_b, normed_a, factor_a = call(
        pre_reduce_kernel,
        [Near(low(tokens, width)), pre_edge, pre_edge, like(tokens, width), like(tokens, LANES)],
        [(tokens, width)],
        x_low,
        pre_reduce,
        pre_mid_gain,
        pre_mid_shift,
    )
    got_a, got_b = edges((edge_a, edge_b))
    (
        second,
        normed_b,
        factor_b,
        normed_c,
        factor_c,
        summed,
        pooled,
        post_first,
        edge_a,
        edge_b,
        post_normed_a,
        post_factor_a,
        pad,
    ) = call(
        pre_rest_kernel,
        [
            low(tokens, width),
            like(tokens, width),
            like(tokens, LANES),
            like(tokens, width),
            like(tokens, LANES),
            like(tokens, width),
            Near(like(padded, width)),
            Near(low(padded, width)),
            post_edge,
            post_edge,
            like(padded, width),
            like(padded, LANES),
            like(count, strip + 2, side, width),
        ],
        [(tokens, width), (side * width // LANES, LANES), (padded, width)],
        x_low,
        Near(first),
        Near(got_a),
        Near(got_b),
        pre_conv,
        pre_expand,
        pre_mid_gain,
        pre_mid_shift,
        pre_out_g,
        pre_out_s,
        post_reduce,
        post_mid_gain,
        post_mid_shift,
    )
    got_a, got_b = edges((edge_a, edge_b))
    (
        block_two,
        left_in,
        left_second,
        post_normed_b,
        post_factor_b,
        post_normed_c,
        post_factor_c,
        post_summed,
        post_pad,
    ) = call(
        functools.partial(post_rest_kernel, cols=cols),
        [
            Near(low(small, width)),
            low(block, width),
            low(block, width),
            like(padded, width),
            like(padded, LANES),
            like(padded, width),
            like(padded, LANES),
            like(padded, width),
            like(count, rows + 2, SLAB, width),
        ],
        [(padded, width), (padded, width), (block, width)],
        Near(pooled),
        Near(post_first),
        Near(got_a),
        Near(got_b),
        post_conv,
        post_expand,
        post_mid_gain,
        post_mid_shift,
        post_out_g,
        post_out_s,
    )
    whole = lax.all_gather(block_two, "row", axis=0, tiled=True)
    readout, grad_pre, *terms, d_read_b = call(
        functools.partial(readout_kernel, strips=strips),
        [
            like(*cotangent.shape, dtype=LOW),
            Near(low(strips * small, features)),
        ]
        + [Near(low(small, width))] * strips
        + [like(1, features)],
        [
            (strips * small, features),
            (strips * small, features),
            (strips * small, width),
        ],
        Near(whole),
        read_weight,
        read_bias[None],
        cotangent,
    )
    terms = share(terms, "row")
    post_gs, post_ge, post_gc, edge_a, edge_b, post_small_b = call(
        functools.partial(post_back_kernel, cols=cols, strips=strips),
        [
            Near(like(padded, width)),
            Near(low(block, width)),
            Near(low(padded, width)),
            post_edge,
            post_edge,
            like(4, width),
        ],
        [(block, width), (padded, width), (padded, width), (padded, width)],
        *[Near(term) for term in terms],
        post_expand,
        post_mid_gain,
        post_mid_shift,
        post_out_g,
        post_normed_b,
        post_factor_b,
        post_normed_c,
        post_factor_c,
        post_summed,
    )
    if quick:
        edge_a, whole, grad_pre = tie(edge_a, whole, grad_pre)
    got_a, got_b = edges((edge_a, edge_b))
    if quick:
        read_slots = pair_outer(
            (Near(whole), Near(swap(whole)), Near(grad_pre), Near(swap(grad_pre)))
        )
        read_parts = [read_slots[0]] + [steps_of(read_slots[at], "im", at) for at in (1, 2)]
        (got_a, got_b), (*read_parts, read_last) = tie_later(
            (got_a, got_b), (*read_parts, read_slots[3])
        )
    (
        post_gr,
        pre_gs,
        pre_ge,
        pre_gc,
        edge_a,
        edge_b,
        post_small_a,
        pre_small_b,
    ) = call(
        functools.partial(middle_back_kernel, cols=cols),
        [
            Near(low(block, width)),
            like(tokens, width),
            Near(low(tokens, width)),
            Near(low(tokens, width)),
            pre_edge,
            pre_edge,
            like(11, width),
            like(4, width),
        ],
        [
            (count, rows + 2, SLAB, width),
            (9, 8, width),
            (padded, width),
            (side * width // LANES, LANES),
            (tokens, width),
            (2, 8, width),
            (padded, width),
            (block, width),
        ],
        Near(post_gc),
        Near(got_a),
        Near(got_b),
        post_pad,
        post_conv,
        post_reduce,
        post_mid_gain,
        post_mid_shift,
        post_normed_a,
        post_factor_a,
        Near(post_gs),
        pre_expand,
        pre_mid_gain,
        pre_mid_shift,
        pre_out_g,
        normed_b,
        factor_b,
        normed_c,
        factor_c,
        summed,
    )
    got_a, got_b = edges((edge_a, edge_b))
    if quick:
        post_parts = pair_outer(
            (left_in, swap(left_in), Near(post_gr), Near(swap(post_gr))),
            (left_second, swap(left_second), Near(post_ge), Near(swap(post_ge))),
        )
        post_sums = share(post_parts, "im")[1:]
        (got_a, got_b), post_sums = tie_later((got_a, got_b), post_sums)
    pre_gr, sums = call(
        pre_back_kernel,
        [Near(low(tokens, width)), Near(like(32, width))],
        [
            (count, strip + 2, side, width),
            (9, 8, width),
            (2, 8, width),
        ],
        Near(pre_gc),
        Near(got_a),
        Near(got_b),
        pad,
        pre_conv,
        pre_mid_gain,
        pre_mid_shift,
        normed_a,
        factor_a,
        pre_small_b,
        post_small_a,
        post_small_b,
        d_read_b,
    )
    if quick:
        far = swap(pre_gr)
        post_parts = sum_split(post_parts[:1] + post_sums, 2)
        post_parts[0], far = tie(post_parts[0], far)
        post_parts = share(post_parts, "row")
        parts = pair_outer(
            (second, swap(second), Near(pre_ge), Near(swap(pre_ge))),
            (x_low, swap(x_low), Near(pre_gr), Near(far)),
        )
        parts[0], sums = tie(parts[0], sums + swap(sums))
        read_parts = read_parts + [steps_of(read_last, "im", 3)]
        near_parts = [steps_of(parts[at], "im", at) for at in (1, 2)]
        grad_in = pre_gs + jnp.einsum("tm,cm->tc", pre_gr, pre_reduce, preferred_element_type=FULL)
        grad_in = grad_in.astype(LOW)
        post_parts, (grad_in, last, *rest) = tie_later(
            post_parts, (grad_in, parts[3], *near_parts, *read_parts)
        )
        near_parts, read_parts = (rest[:2], rest[2:])
        post_parts = share_same(add_low(post_parts), "row")
        last = steps_of(last, "im", 3)
        post_parts, (last, *read_parts) = tie_later(post_parts, (last, *read_parts))
        parts = share(sum_split([parts[0]] + near_parts + [last], 2), "row")
        post_parts = gather_near(jnp.concatenate(post_parts, axis=0))
        read_parts = gather_near(add_low(read_parts))
        parts, rest = tie_later(parts, (*post_parts, *read_parts))
        post_parts, read_parts = (rest[:3], rest[3:])
        parts = share_same(add_low(parts), "row")
        read_parts.append(steps_of(read_parts[0], "im", 3))
        post_parts = post_parts + gather_rest(post_parts)
        parts, rest = tie_later(parts, (*post_parts, *read_parts, sums))
        post_parts, read_parts, sums = (rest[:5], rest[5:9], rest[9])
        parts = gather_near(jnp.concatenate(parts, axis=0))
        alone = lax.broadcasted_iota(jnp.int32, sums.shape, 0) >= 30
        for step in (1, 2):
            sums = sums + jnp.where(alone, 0.0, steps_of(sums, "row", step))
        post_far = swap(jnp.concatenate(post_parts, axis=0))
        read_far = swap(jnp.concatenate(read_parts, axis=0))
        parts, (sums, post_far, read_far, *post_parts) = tie_later(
            parts, (sums, post_far, read_far, *post_parts)
        )
        far = swap(jnp.concatenate(parts, axis=0))
        post_reduce_g, post_expand_g = assemble(post_parts, [post_far], 2, 4, strips)
        (read_total,) = assemble(read_parts, [read_far], 1, 4, 1)
        (post_reduce_g, read_total), (*others, far, sums) = tie_later(
            (post_reduce_g, read_total),
            (*gather_rest(parts), *share_same(sums, "im")[1:], far, sums),
        )
        far_rest = swap(jnp.concatenate(others[:2], axis=0))
        rest = others[:2]
        sums = (sums + others[2]) + (others[3] + others[4])
        small_out = call(
            small_kernel,
            [like(3, 3, width), like(2, width), like(2, width), like(1, width), like(1, width)] * 2,
            [],
            Near(sums),
        )
        pre_expand_g, pre_reduce_g = assemble(parts + rest, [far, far_rest], 2, 4, strips)
        read_bias_g = sums[30]
    else:
        axes = IMG + ("row",)
        post_reduce_g = sum_far(left_in, post_gr, axes)
        post_expand_g = sum_far(left_second, post_ge, axes)
        pre_expand_g = sum_far(second, pre_ge, axes)
        pre_reduce_g = sum_far(x_low, pre_gr, axes)
        read_total = sum_far(whole, grad_pre, IMG)
        read_bias_g = lax.psum(sums[30], IMG)
        sums = lax.psum(sums[:30], axes)
        small_out = small_outputs(sums[:15], width) + small_outputs(sums[15:30], width)
        grad_in = pre_gs + jnp.einsum("tm,cm->tc", pre_gr, pre_reduce, preferred_element_type=FULL)
        grad_in = grad_in.astype(LOW)

    pre_conv_g, pre_gain_g, pre_shift_g, pre_og_g, pre_os_g = small_out[:5]
    post_conv_g, post_gain_g, post_shift_g, post_og_g, post_os_g = small_out[5:]
    return (
        readout,
        grad_in.reshape(x_in.shape),
        pre_reduce_g,
        pre_conv_g,
        pre_expand_g,
        pre_gain_g,
        pre_shift_g,
        pre_og_g.reshape(width),
        pre_os_g.reshape(width),
        post_reduce_g,
        post_conv_g,
        post_expand_g,
        post_gain_g,
        post_shift_g,
        post_og_g.reshape(width),
        post_os_g.reshape(width),
        read_total,
        read_bias_g,
    )


def solution(mesh):
    images, strips = mesh.devices.shape
    split = jax.sharding.Mesh(
        mesh.devices.reshape(images // 2, 2, strips), ("im", "half", "row")
    )
    return jax.shard_map(
        shards,
        mesh=split,
        in_specs=(P(IMG, "row", None, None),)
        + (P(),) * 14
        + (P(None, "row"), P("row"), P(IMG, None, None, "row")),
        out_specs=(P(IMG, None, None, "row"), P(IMG, "row", None, None))
        + (P(),) * 14
        + (P(None, "row"), P("row")),
        check_vma=False,
    )
```
